32 devices in a mesh: groups: 2 (over y), replica: 4 (over z), tensor: 4 (over x, core).
Axes of the slice: x: 2, y: 2, z: 4, core: 2. Of those that a mesh axis runs over, the one named last changes fastest.
Arguments:
- x_new: bfloat16 [2048, 8192], P(('groups', 'replica'), 'tensor'), parts along dimension 0, may hold values from -6 to 6
- z_new: bfloat16 [2048, 8192], P(('groups', 'replica'), 'tensor'), parts along dimension 0, may hold values from -6 to 6
- conv_weight: bfloat16 [4, 8192], P(None, 'tensor'), may hold values from -3 to 3
- conv_bias: float32 [8192], P('tensor'), may hold values from -0.5 to 0.5
- x_proj_weight: bfloat16 [8192, 288], P('tensor'), may hold values from -0.0625 to 0.0625
- dt_proj_weight: bfloat16 [256, 8192], P(None, 'tensor'), may hold values from -0.75 to 0.75
- dt_bias: float32 [8192], P('tensor'), may hold values from -6 to -2.5
- a_log: float32 [16, 8192], P(None, 'tensor'), may hold values from 0 to 2.8
- d_skip: float32 [8192], P('tensor'), may hold values from 0.5 to 1.5
- cache_ssm: bfloat16 [16, 16, 8192], P(('groups', 'replica'), None, 'tensor'), parts along dimension 0, may hold values from -6 to 6
- cache_conv: bfloat16 [16, 3, 8192], P(('groups', 'replica'), None, 'tensor'), parts along dimension 0, may hold values from -6 to 6
- holder: int32 [64], P('groups'), parts along dimension 0, may hold values from 0 to 3, as said below
- slot_id: int32 [64], P('groups'), parts along dimension 0, may hold values from 0 to 1, as said below
- prefix_len: int32 [64], P('groups'), parts along dimension 0, may hold values from 0 to 4096, as said below
Outputs:
- gated_out: bfloat16 [2048, 8192], P(('groups', 'replica'), 'tensor'), parts along dimension 0
- new_state: bfloat16 [64, 16, 8192], P(('groups', 'replica'), None, 'tensor'), parts along dimension 0
The draws below stay inside these ranges and needn't reach their ends.
There are 2 independent parts, one for each index of `groups`. The reference program is written for one: setup_inputs(seed, part) draws one part's arguments, and reference() takes and returns one part's arrays. A program takes and returns all parts, laid end to end along the dimension named above; an argument that names none is the same for every part. Nothing has to cross between parts.
Inputs may be any that keep to these rules, and one draw needn't show every extreme that they name: `holder`: every replica holds some request's prefix. `slot_id`: slot among the holder's 2 slots. `prefix_len`: 0 means no cached prefix.
All inputs are finite; a program needn't handle non-finite values.
Results may differ from the reference program's by a relative error of at most 0.0077.
Values may be sent and summed in bfloat16 or wider, within the bound.
No kernel may reach another device: no remote copies, remote signals or barrier semaphores. Data moves between devices by JAX's collectives and lax.ppermute only.
A program may use at most 64 MiB of HBM per device.

```python
import jax
import jax.numpy as jnp
from jax import lax

E = 8192
NS = 16
DTR = 256
KC = 4
NEW = 32
SLOTS = 2
PREFIX_MOST = 4096
REQUESTS = 32
ROWS = 1024
SLOTS_ALL = 8
N_REPLICA = 4


def arrival_rank(key):
    order = jax.random.permutation(key, REQUESTS)
    return jnp.argsort(order).astype(jnp.int32)


def draw_holder(key, part):
    ranks = arrival_rank(key)
    key = jax.random.fold_in(key, 11)
    first_key, second_key, third_key = jax.random.split(key, 3)
    uniform_pick = jax.random.randint(first_key, (REQUESTS,), 0, N_REPLICA)
    skewed_pick = uniform_pick * uniform_pick // N_REPLICA
    coin_flip = jax.random.randint(second_key, (REQUESTS,), 0, 2)
    chosen = jnp.where(coin_flip == 1, skewed_pick, uniform_pick)
    relabel = jax.random.permutation(third_key, N_REPLICA)
    picked = jnp.take(relabel, chosen)
    return jnp.where(ranks < N_REPLICA, ranks, picked).astype(jnp.int32)


def draw_slot_id(key, part):
    ranks = arrival_rank(key)
    key = jax.random.fold_in(key, 23)
    drawn = jax.random.randint(key, (REQUESTS,), 0, SLOTS)
    drawn = jnp.where(ranks == 0, SLOTS - 1, drawn)
    return jnp.where(ranks == 1, 0, drawn).astype(jnp.int32)


def draw_prefix_len(key, part):
    ranks = arrival_rank(key)
    key = jax.random.fold_in(key, 37)
    first_key, second_key = jax.random.split(key, 2)
    kind_pick = jax.random.randint(first_key, (REQUESTS,), 0, 8)
    long_len = jax.random.randint(second_key, (REQUESTS,), 3, PREFIX_MOST + 1)
    lengths = jnp.where(kind_pick == 0, 0, jnp.where(kind_pick == 1, 1, jnp.where(kind_pick == 2, 2, long_len)))
    lengths = jnp.where(ranks == 2, PREFIX_MOST, lengths)
    return jnp.where(ranks == 3, 0, lengths).astype(jnp.int32)


def block_levels(key, extent, pieces, low, high):
    factor_of = 1.0
    for dim, shards_of in pieces:
        steps = jax.random.uniform(jax.random.fold_in(jax.random.fold_in(key, 6), dim), (shards_of,), jnp.float32, low / len(pieces), high / len(pieces))
        factor_of = factor_of * jnp.repeat(jnp.exp(steps), extent[dim] // shards_of).reshape((-1,) + (1,) * (len(extent) - 1 - dim))
    return factor_of


def bell_draw(key, dims, width, limit, cuts=(), kind=jnp.bfloat16):
    values = jax.random.normal(key, dims, jnp.float32) * width
    if len(cuts) > 0:
        values = block_levels(key, dims, cuts, -0.22, 0.18) * values
    return jnp.clip(values, min=-limit, max=limit).astype(kind)


def setup_inputs(seed: int = 0, part: int = 0) -> dict:
    seeds = jax.random.split(jax.random.key(seed), 15)
    part_splits = jax.random.split(jax.random.fold_in(seeds[14], part), 15)
    return {
        "x_new": bell_draw(part_splits[0], (ROWS, E), 1.0, 6.0, ((0, 4), (1, 4))),
        "z_new": bell_draw(part_splits[1], (ROWS, E), 1.0, 6.0, ((0, 4), (1, 4))),
        "conv_weight": bell_draw(seeds[2], (KC, E), KC ** -0.5, 3.0, ((1, 4),)),
        "conv_bias": jnp.clip(jax.random.uniform(seeds[3], (E,), jnp.float32, -0.5, 0.5) * block_levels(seeds[3], (E,), ((0, 4),), -0.4, 0.0), -0.5, 0.5),
        "x_proj_weight": bell_draw(seeds[4], (E, DTR + 2 * NS), E ** -0.5, 0.0625, ((0, 4),)),
        "dt_proj_weight": bell_draw(seeds[5], (DTR, E), (DTR // 4) ** -0.5, 0.75, ((1, 4),)),
        "dt_bias": jnp.clip(-6.0 + 3.5 * jax.random.uniform(seeds[6], (E,), jnp.float32) ** block_levels(seeds[6], (E,), ((0, 4),), -0.2, 0.2), -6.0, -2.5),
        "a_log": jnp.clip(2.8 * jax.random.uniform(seeds[7], (NS, E), jnp.float32) ** block_levels(seeds[7], (NS, E), ((1, 4),), -0.2, 0.2), 0.0, 2.8),
        "d_skip": jnp.clip(0.5 + 1.0 * jax.random.uniform(seeds[8], (E,), jnp.float32) ** block_levels(seeds[8], (E,), ((0, 4),), -0.2, 0.2), 0.5, 1.5),
        "cache_ssm": bell_draw(part_splits[9], (SLOTS_ALL, NS, E), 1.0, 6.0, ((0, 4), (2, 4))),
        "cache_conv": bell_draw(part_splits[10], (SLOTS_ALL, KC - 1, E), 1.0, 6.0, ((0, 4), (2, 4))),
        "holder": draw_holder(jax.random.fold_in(jax.random.fold_in(seeds[14], part), 71), part),
        "slot_id": draw_slot_id(jax.random.fold_in(jax.random.fold_in(seeds[14], part), 71), part),
        "prefix_len": draw_prefix_len(jax.random.fold_in(jax.random.fold_in(seeds[14], part), 71), part),
    }


def conv_mix(history, tokens_in, conv_weight, conv_bias):
    tap_count = conv_weight.shape[0]
    length = tokens_in.shape[1]
    joined = jnp.concatenate([history, tokens_in], axis=1)
    summed = jnp.zeros(tokens_in.shape, jnp.float32) + conv_bias
    for offset in range(tap_count):
        summed = summed + joined[:, offset:offset + length].astype(jnp.float32) * conv_weight[offset].astype(jnp.float32)
    return jax.nn.silu(summed).astype(jnp.bfloat16)


def time_major(values, requests):
    return values.reshape(requests, NEW, -1).transpose(1, 0, 2)


def reference(x_new, z_new, conv_weight, conv_bias, x_proj_weight, dt_proj_weight, dt_bias, a_log, d_skip, cache_ssm, cache_conv, holder, slot_id, prefix_len):
    requests = holder.shape[0]
    channels = x_new.shape[1]
    slot_index = (holder * SLOTS + slot_id).astype(jnp.int32)
    has_cache = prefix_len > 0
    fetched_ssm = jnp.take(cache_ssm, slot_index, axis=0).astype(jnp.float32)
    start_state = jnp.where(has_cache[:, None, None], fetched_ssm, jnp.zeros_like(fetched_ssm))
    row_age = (KC - 1) - jnp.arange(KC - 1, dtype=jnp.int32)
    conv_live = row_age[None, :] <= prefix_len[:, None]
    fetched_conv = jnp.take(cache_conv, slot_index, axis=0)
    history = jnp.where(conv_live[:, :, None], fetched_conv, jnp.zeros_like(fetched_conv))
    mixed = conv_mix(history, x_new.reshape(requests, NEW, channels), conv_weight, conv_bias)
    flat_rows = mixed.reshape(requests * NEW, channels)
    projected = jnp.dot(flat_rows, x_proj_weight, preferred_element_type=jnp.float32)
    dt_low = projected[:, :DTR].astype(jnp.bfloat16)
    b_rows = projected[:, DTR:DTR + NS]
    c_rows = projected[:, DTR + NS:]
    step_size = jax.nn.softplus(jnp.dot(dt_low, dt_proj_weight, preferred_element_type=jnp.float32) + dt_bias)
    a_matrix = -jnp.exp(a_log)
    mixed_float = flat_rows.astype(jnp.float32)
    driven = step_size * mixed_float

    def advance(state_now, token_data):
        step_now, drive_now, mixed_now, b_values, c_values = token_data
        state_now = jnp.exp(step_now[:, None, :] * a_matrix) * state_now + drive_now[:, None, :] * b_values[:, :, None]
        result = jnp.sum(c_values[:, :, None] * state_now, axis=1) + d_skip * mixed_now
        return state_now, result

    final_state, outputs = lax.scan(advance, start_state, (time_major(step_size, requests), time_major(driven, requests), time_major(mixed_float, requests), time_major(b_rows, requests), time_major(c_rows, requests)))
    ssm_out = outputs.transpose(1, 0, 2).reshape(requests * NEW, channels)
    gated_out = (ssm_out * jax.nn.silu(z_new.astype(jnp.float32))).astype(jnp.bfloat16)
    return gated_out, final_state.astype(jnp.bfloat16)
```

```python
import functools

import jax
import jax.numpy as jnp
from jax import lax
from jax.experimental import pallas as pl
from jax.experimental.pallas import tpu as pltpu
from jax.sharding import PartitionSpec as P

NEW = 32
LOG2E = 1.4426950408889634
VMEM_LIMIT = 40 * 1024 * 1024
NT = (((1,), (1,)), ((), ()))


def silu(v):
    half = 0.5 * v
    return half + half * jnp.tanh(half)


def softplus(v):
    u = jnp.exp(-jnp.abs(v))
    small = u * (1.0 - u * (0.5 - u * (1.0 / 3.0)))
    return jnp.maximum(v, 0.0) + jnp.where(u < 0.004, small, jnp.log(1.0 + u))


def one_hot_rows(count, outer, inner):
    row = lax.broadcasted_iota(jnp.int32, (count, count), 0)
    col = lax.broadcasted_iota(jnp.int32, (count, count), 1)
    source = lax.rem(row, outer) * inner + lax.div(row, outer)
    return jnp.where(col == source, 1.0, 0.0).astype(jnp.bfloat16)


def project_kernel(dims, holder, slot_id, prefix_len, *refs):
    per_dev, n_replica, slots, relative, n_pieces = dims
    x_ref, wt_ref, cw_ref, cb_ref = refs[:4]
    pieces = refs[4 : 4 + n_pieces]
    mixed_ref, part_ref = refs[4 + n_pieces : 6 + n_pieces]
    joined, order = refs[6 + n_pieces :]
    step = pl.program_id(0)
    me = lax.axis_index("replica")
    rows = per_dev * NEW
    taps = cw_ref.shape[0]
    piece_rows = pieces[0].shape[0]

    @pl.when(step == 0)
    def _():
        order[...] = one_hot_rows(rows, per_dev, NEW)

    for r in range(per_dev):
        request = me * per_dev + r
        base = me if relative else 0
        index = lax.rem(holder[request] - base + n_replica, n_replica) * slots + slot_id[request]
        length = prefix_len[request]
        value = jnp.zeros(pieces[0].shape[1:], jnp.float32)
        for p in range(n_pieces):
            row = jnp.clip(index - p * piece_rows, 0, piece_rows - 1)
            here = (index >= p * piece_rows) & (index < (p + 1) * piece_rows)
            value = jnp.where(here, pieces[p][row].astype(jnp.float32), value)
        for j in range(taps - 1):
            live = taps - 1 - j <= length
            line = value[j : j + 1, :]
            joined[j * per_dev + r : j * per_dev + r + 1, :] = jnp.where(live, line, jnp.zeros_like(line))

    joined[(taps - 1) * per_dev :, :] = jnp.dot(
        order[...], x_ref[...], preferred_element_type=jnp.float32
    )
    summed = jnp.broadcast_to(cb_ref[...], x_ref.shape)
    for k in range(taps):
        weight = cw_ref[k : k + 1, :].astype(jnp.float32)
        summed = summed + joined[k * per_dev : k * per_dev + rows, :] * weight
    mixed = silu(summed).astype(jnp.bfloat16)
    mixed_ref[...] = mixed
    part = lax.dot_general(mixed, wt_ref[...], NT, preferred_element_type=jnp.float32)

    @pl.when(step == 0)
    def _():
        part_ref[...] = part

    @pl.when(step > 0)
    def _():
        part_ref[...] += part


def scan_kernel(dims, holder, slot_id, prefix_len, *refs):
    per_dev, n_replica, slots, relative, n_pieces, n_parts = dims
    mixed_ref, z_ref, dtw_ref, dtb_ref, al_ref, skip_ref = refs[:6]
    parts = refs[6 : 6 + n_parts]
    pieces = refs[6 + n_parts : 6 + n_parts + n_pieces]
    out_ref, state_ref = refs[6 + n_parts + n_pieces : 8 + n_parts + n_pieces]
    (order, back, order_s, back_s, dt_low, b_tab, c_tab, dt_buf, gate_buf, y_buf, a_buf, start_rm, start_tm,
     final_tm, sems) = refs[8 + n_parts + n_pieces :]
    step = pl.program_id(0)
    me = lax.axis_index("replica")
    rows = per_dev * NEW
    states = al_ref.shape[0]
    rank = dtw_ref.shape[0]
    width = z_ref.shape[1]
    piece_rows = pieces[0].shape[0]

    def fetch(r, do):
        request = me * per_dev + r
        base = me if relative else 0
        index = lax.rem(holder[request] - base + n_replica, n_replica) * slots + slot_id[request]
        for p in range(n_pieces):
            row = jnp.clip(index - p * piece_rows, 0, piece_rows - 1)
            here = (index >= p * piece_rows) & (index < (p + 1) * piece_rows)

            @pl.when(here)
            def _():
                do(pltpu.make_async_copy(pieces[p].at[row], start_rm.at[r], sems.at[r]))

    @pl.when(step == 0)
    def _():
        for r in range(per_dev):
            fetch(r, lambda copy: copy.start())
        order[...] = one_hot_rows(rows, per_dev, NEW)
        back[...] = one_hot_rows(rows, NEW, per_dev)
        order_s[...] = one_hot_rows(per_dev * states, per_dev, states)
        back_s[...] = one_hot_rows(per_dev * states, states, per_dev)
        projected = parts[0][...]
        for p in range(1, n_parts):
            projected = projected + parts[p][...]
        dt_low[...] = projected[:, :rank].astype(jnp.bfloat16)
        for n in range(states):
            b_tab[n] = jnp.broadcast_to(projected[:, rank + n : rank + n + 1], (rows, 128))
            c_tab[n] = jnp.broadcast_to(
                projected[:, rank + states + n : rank + states + n + 1], (rows, 128)
            )
        for r in range(per_dev):
            fetch(r, lambda copy: copy.wait())
        for r in range(per_dev):
            has = prefix_len[me * per_dev + r] > 0
            value = start_rm[r]
            start_rm[r] = jnp.where(has, value, jnp.zeros_like(value))

    columns = pl.ds(pl.multiple_of(step * width, 128), width)
    dt_buf[...] = softplus(
        jnp.dot(dt_low[...], dtw_ref[...], preferred_element_type=jnp.float32) + dtb_ref[...]
    )
    gate_buf[...] = silu(jnp.dot(order[...], z_ref[...], preferred_element_type=jnp.float32))
    a_buf[...] = jnp.exp(al_ref[...]) * (-LOG2E)
    start = start_rm[:, :, columns].reshape(per_dev * states, width)
    start_tm[...] = jnp.dot(order_s[...], start, preferred_element_type=jnp.float32)

    for tile in range(width // 128):
        lanes = slice(tile * 128, (tile + 1) * 128)
        rates = [jnp.broadcast_to(a_buf[n : n + 1, lanes], (per_dev, 128)) for n in range(states)]
        skip = jnp.broadcast_to(skip_ref[:, lanes], (per_dev, 128))

        def advance(t, state):
            now = pl.ds(pl.multiple_of(t * per_dev, per_dev), per_dev)
            dt = dt_buf[now, lanes]
            mixed = mixed_ref[now, lanes].astype(jnp.float32)
            drive = dt * mixed
            later = []
            terms = []
            for n in range(states):
                value = jnp.exp2(dt * rates[n]) * state[n] + drive * b_tab[n, now, :]
                later.append(value)
                terms.append(value * c_tab[n, now, :])
            while len(terms) > 1:
                terms = [terms[i] + terms[i + 1] for i in range(0, len(terms) - 1, 2)] + (
                    [terms[-1]] if len(terms) % 2 else []
                )
            y_buf[now, lanes] = (terms[0] + skip * mixed) * gate_buf[now, lanes]
            return tuple(later)

        state = tuple(start_tm[n * per_dev : (n + 1) * per_dev, lanes] for n in range(states))
        state = lax.fori_loop(0, NEW, advance, state, unroll=2)
        for n in range(states):
            final_tm[n * per_dev : (n + 1) * per_dev, lanes] = state[n]

    out_ref[...] = jnp.dot(
        back[...], y_buf[...].astype(jnp.bfloat16), preferred_element_type=jnp.float32
    ).astype(jnp.bfloat16)
    final = jnp.dot(back_s[...], final_tm[...].astype(jnp.bfloat16), preferred_element_type=jnp.float32)
    state_ref[...] = final.astype(jnp.bfloat16).reshape(per_dev, states, width)


def from_offset(value, axis, size, offset):
    return lax.ppermute(value, axis, [((i + offset) % size, i) for i in range(size)])


def gather_pieces(value, axis, size):
    if size <= 8:
        return [value] + [from_offset(value, axis, size, k) for k in range(1, size)], True
    return [lax.all_gather(value, axis, axis=0, tiled=True)], False


def shards(mesh, x_new, z_new, conv_weight, conv_bias, x_proj_weight, dt_proj_weight, dt_bias, a_log, d_skip,
           cache_ssm, cache_conv, holder, slot_id, prefix_len):
    n_replica, n_tensor = mesh.shape["replica"], mesh.shape["tensor"]
    rows, channels = x_new.shape
    per_dev = rows // NEW
    states = a_log.shape[0]
    rank = dt_proj_weight.shape[0]
    taps = conv_weight.shape[0]
    slots = cache_ssm.shape[0]
    out_cols = x_proj_weight.shape[1]

    conv_pieces, relative = gather_pieces(cache_conv, "replica", n_replica)
    ssm_pieces, _ = gather_pieces(cache_ssm, "replica", n_replica)

    width = min(512, channels)
    smem = pl.BlockSpec(memory_space=pltpu.SMEM)

    def cols(count):
        return pl.BlockSpec((count, width), lambda i: (0, i))

    def whole(shape):
        return pl.BlockSpec(shape, lambda i: (0,) * len(shape))

    params = pltpu.CompilerParams(vmem_limit_bytes=VMEM_LIMIT)
    dims = (per_dev, n_replica, slots, relative, len(conv_pieces))
    mixed, part = pl.pallas_call(
        functools.partial(project_kernel, dims),
        grid=(channels // width,),
        in_specs=[smem] * 3
        + [cols(rows), cols(out_cols), cols(taps), cols(1)]
        + [pl.BlockSpec(piece.shape[:2] + (width,), lambda i: (0, 0, i)) for piece in conv_pieces],
        out_specs=[cols(rows), whole((rows, out_cols))],
        out_shape=[
            jax.ShapeDtypeStruct((rows, channels), jnp.bfloat16),
            jax.ShapeDtypeStruct((rows, out_cols), jnp.float32),
        ],
        scratch_shapes=[
            pltpu.VMEM((rows + (taps - 1) * per_dev, width), jnp.float32),
            pltpu.VMEM((rows, rows), jnp.bfloat16),
        ],
        compiler_params=params,
        name="conv_project",
    )(holder, slot_id, prefix_len, x_new, x_proj_weight.T, conv_weight, conv_bias[None, :], *conv_pieces)

    parts = [part] + [from_offset(part, "tensor", n_tensor, k) for k in range(1, n_tensor)]

    dims = (per_dev, n_replica, slots, relative, len(ssm_pieces), n_tensor)
    f32, bf16 = jnp.float32, jnp.bfloat16
    return pl.pallas_call(
        functools.partial(scan_kernel, dims),
        grid=(channels // width,),
        in_specs=[smem] * 3
        + [cols(rows), cols(rows), cols(rank), cols(1), cols(states), cols(1)]
        + [whole((rows, out_cols))] * n_tensor
        + [pl.BlockSpec(memory_space=pl.ANY)] * len(ssm_pieces),
        out_specs=[cols(rows), pl.BlockSpec((per_dev, states, width), lambda i: (0, 0, i))],
        out_shape=[
            jax.ShapeDtypeStruct((rows, channels), bf16),
            jax.ShapeDtypeStruct((per_dev, states, channels), bf16),
        ],
        scratch_shapes=[
            pltpu.VMEM((rows, rows), bf16),
            pltpu.VMEM((rows, rows), bf16),
            pltpu.VMEM((per_dev * states, per_dev * states), bf16),
            pltpu.VMEM((per_dev * states, per_dev * states), bf16),
            pltpu.VMEM((rows, rank), bf16),
            pltpu.VMEM((states, rows, 128), f32),
            pltpu.VMEM((states, rows, 128), f32),
            pltpu.VMEM((rows, width), f32),
            pltpu.VMEM((rows, width), f32),
            pltpu.VMEM((rows, width), f32),
            pltpu.VMEM((states, width), f32),
            pltpu.VMEM((per_dev, states, channels), bf16),
            pltpu.VMEM((per_dev * states, width), f32),
            pltpu.VMEM((per_dev * states, width), f32),
            pltpu.SemaphoreType.DMA((per_dev,)),
        ],
        compiler_params=params,
        name="dt_scan_gate",
    )(holder, slot_id, prefix_len, mixed, z_new, dt_proj_weight, dt_bias[None, :], a_log, d_skip[None, :],
      *parts, *ssm_pieces)


def solution(mesh):
    placed = (
        P(("groups", "replica"), "tensor"),
        P(("groups", "replica"), "tensor"),
        P(None, "tensor"),
        P("tensor"),
        P("tensor", None),
        P(None, "tensor"),
        P("tensor"),
        P(None, "tensor"),
        P("tensor"),
        P(("groups", "replica"), None, "tensor"),
        P(("groups", "replica"), None, "tensor"),
        P("groups"),
        P("groups"),
        P("groups"),
    )
    return jax.shard_map(
        functools.partial(shards, mesh),
        mesh=mesh,
        in_specs=placed,
        out_specs=(P(("groups", "replica"), "tensor"), P(("groups", "replica"), None, "tensor")),
        check_vma=False,
    )
```

```python
import functools

import jax
import jax.numpy as jnp
from jax import lax
from jax.experimental import pallas as pl
from jax.experimental.pallas import tpu as pltpu
from jax.sharding import PartitionSpec as P

NEW = 32
LANES = 128
LOG2E = 1.4426950408889634
VMEM_LIMIT = 60 * 1024 * 1024
UNROLL = 8
F32, BF16 = jnp.float32, jnp.bfloat16
NT = (((1,), (1,)), ((), ()))
TN = (((0,), (0,)), ((), ()))


def silu(v):
    half = 0.5 * v
    return half + half * jnp.tanh(half)


def softplus(v):
    u = jnp.exp(-jnp.abs(v))
    small = u * (1.0 - u * (0.5 - u * (1.0 / 3.0)))
    return jnp.maximum(v, 0.0) + jnp.where(u < 0.004, small, jnp.log(1.0 + u))


def split_index(value, inner):
    assert inner & (inner - 1) == 0
    return value >> (inner.bit_length() - 1), value & (inner - 1)


def one_hot_rows(outer, inner):
    count = outer * inner
    row = lax.broadcasted_iota(jnp.int32, (count, count), 0)
    col = lax.broadcasted_iota(jnp.int32, (count, count), 1)
    high, low = split_index(row, outer)
    return jnp.where(col == low * inner + high, 1.0, 0.0).astype(BF16)


def pick_rows(values, row_low, count):
    out = jnp.zeros(row_low.shape, jnp.int32)
    for r in range(count):
        out = jnp.where(row_low == r, values[r], out)
    return out


def request_slots(dims, ints, me):
    per_dev, n_replica, slots, relative = dims
    found, lengths = [], []
    for r in range(per_dev):
        request = me * per_dev + r
        base = me if relative else 0
        place = lax.rem(ints[0][request] - base + n_replica, n_replica)
        found.append(place * slots + ints[1][request])
        lengths.append(ints[2][request])
    return found, lengths


def project_kernel(dims, refs_in, refs_out, scratch):
    per_dev, n_replica, slots, _ = dims
    holder, slot_id, prefix_len, x_hbm, wt_hbm, cw_hbm, cb_hbm, conv_hbm = refs_in
    mixed_hbm, part_hbm = refs_out
    h_s, s_s, l_s, x_v, wt_v, cw_v, cb_v, conv_v, joined, mixed_v, part_f, part_v, sems, out_sems = scratch
    rows, channels = x_v.shape
    taps = cw_v.shape[0]
    copies = []
    for src, dst in ((holder, h_s), (slot_id, s_s), (prefix_len, l_s), (conv_hbm, conv_v), (cw_hbm, cw_v), (cb_hbm, cb_v)):
        copies.append(pltpu.make_async_copy(src, dst, sems.at[len(copies)]))
    small = len(copies)
    width = min(512, channels)
    chunks = [slice(c * width, (c + 1) * width) for c in range(channels // width)]
    for chunk in chunks:
        copies.append(pltpu.make_async_copy(x_hbm.at[:, chunk], x_v.at[:, chunk], sems.at[len(copies)]))
        copies.append(pltpu.make_async_copy(wt_hbm.at[:, chunk], wt_v.at[:, chunk], sems.at[len(copies)]))
    for copy in copies:
        copy.start()

    order = one_hot_rows(per_dev, NEW)
    for copy in copies[:small]:
        copy.wait()

    me = lax.axis_index("replica")
    found, lengths = request_slots(dims, (h_s, s_s, l_s), me)
    lines = (taps - 1) * per_dev
    shape = (per_dev * taps, conv_v.shape[0])
    tap, request = split_index(lax.broadcasted_iota(jnp.int32, shape, 0), per_dev)
    slot, col_tap = split_index(lax.broadcasted_iota(jnp.int32, shape, 1), taps)
    live = (taps - 1 - tap <= pick_rows(lengths, request, per_dev)) & (tap == col_tap)
    chosen = live & (slot == pick_rows(found, request, per_dev))
    select = jnp.where(chosen, 1.0, 0.0).astype(BF16)

    outs = []
    for c, chunk in enumerate(chunks):
        copies[small + 2 * c].wait()
        history = jnp.dot(select, conv_v[:, chunk], preferred_element_type=F32)
        joined[:lines, chunk] = history[:lines]
        joined[lines:, chunk] = jnp.dot(order, x_v[:, chunk], preferred_element_type=F32)
        summed = jnp.broadcast_to(cb_v[:, chunk], (rows, width))
        for k in range(taps):
            weight = cw_v[k : k + 1, chunk].astype(F32)
            summed = summed + joined[k * per_dev : k * per_dev + rows, chunk] * weight
        mixed = silu(summed).astype(BF16)
        mixed_v[:, chunk] = mixed
        copies[small + 2 * c + 1].wait()
        part = lax.dot_general(wt_v[:, chunk], mixed, NT, preferred_element_type=F32)
        if c == 0:
            part_f[...] = part
        else:
            part_f[...] += part
        outs.append(pltpu.make_async_copy(mixed_v.at[:, chunk], mixed_hbm.at[:, chunk], out_sems.at[c]))
        outs[-1].start()
    part_v[...] = part_f[...].astype(BF16)
    for k in range(part_hbm.shape[0]):
        outs.append(pltpu.make_async_copy(part_v, part_hbm.at[k], out_sems.at[len(outs)]))
        outs[-1].start()
    for copy in outs:
        copy.wait()


def scan_kernel(dims, refs_in, refs_out, scratch):
    per_dev, n_replica, slots, _ = dims
    holder, slot_id, prefix_len, mixed_hbm, z_hbm, dtw_hbm, dtb_hbm, al_hbm, skip_hbm, parts_hbm = refs_in[:10]
    pieces = refs_in[10:]
    out_hbm, state_hbm = refs_out
    (h_s, s_s, l_s, mixed_v, z_v, dtw_v, dtb_v, al_v, skip_v, parts_v, cache_v, b_tab, c_tab, dt_v, gate_v,
     a_v, start_tm, final_tm, y_v, out_v, state_v, sems, out_sems) = scratch
    rows, channels = z_v.shape
    states = al_v.shape[0]
    rank = dtw_v.shape[0]
    pairs = (
        (z_hbm, z_v), (parts_hbm, parts_v), (dtw_hbm, dtw_v), (dtb_hbm, dtb_v), (al_hbm, al_v), (holder, h_s),
        (slot_id, s_s), (prefix_len, l_s), (skip_hbm, skip_v), (mixed_hbm, mixed_v),
    )
    copies = [pltpu.make_async_copy(src, dst, sems.at[i]) for i, (src, dst) in enumerate(pairs)]
    piece_rows = cache_v.shape[0] // len(pieces)
    for p, piece in enumerate(pieces):
        target = cache_v.at[p * piece_rows : (p + 1) * piece_rows]
        copies.append(pltpu.make_async_copy(piece, target, sems.at[len(copies)]))
    for copy in copies:
        copy.start()

    order = one_hot_rows(per_dev, NEW)
    copies[0].wait()
    gate_v[...] = silu(jnp.dot(order, z_v[...], preferred_element_type=F32))

    copies[1].wait()
    projected = parts_v[0].astype(F32)
    for p in range(1, parts_v.shape[0]):
        projected = projected + parts_v[p].astype(F32)
    dt_low = projected[:rank].astype(BF16)
    late = projected[rank:].T
    for n in range(states):
        b_tab[n] = jnp.broadcast_to(late[:, n : n + 1], (rows, LANES))
        c_tab[n] = jnp.broadcast_to(late[:, states + n : states + n + 1], (rows, LANES))
    for copy in copies[2:]:
        copy.wait()
    dt_v[...] = softplus(
        lax.dot_general(dt_low, dtw_v[...], TN, preferred_element_type=F32) + dtb_v[...]
    )
    a_v[...] = jnp.exp(al_v[...]) * (-LOG2E)

    me = lax.axis_index("replica")
    found, lengths = request_slots(dims, (h_s, s_s, l_s), me)
    shape = (per_dev * states, cache_v.shape[0])
    state_id, request = split_index(lax.broadcasted_iota(jnp.int32, shape, 0), per_dev)
    slot, col_state = split_index(lax.broadcasted_iota(jnp.int32, shape, 1), states)
    chosen = (pick_rows(lengths, request, per_dev) > 0) & (state_id == col_state)
    chosen = chosen & (slot == pick_rows(found, request, per_dev))
    select = jnp.where(chosen, 1.0, 0.0).astype(BF16)
    start_tm[...] = jnp.dot(select, cache_v[...], preferred_element_type=F32)

    back = one_hot_rows(NEW, per_dev)
    back_s = one_hot_rows(states, per_dev)
    width = min(512, channels)
    outs = []
    for c in range(channels // width):

        def one_tile(i, carry):
            lanes = pl.ds(pl.multiple_of(c * width + i * LANES, LANES), LANES)
            rates = [jnp.broadcast_to(a_v[n : n + 1, lanes], (per_dev, LANES)) for n in range(states)]
            skip = jnp.broadcast_to(skip_v[:, lanes], (per_dev, LANES))

            def advance(block, state):
                state = list(state)
                for u in range(UNROLL):
                    now = pl.ds(pl.multiple_of((block * UNROLL + u) * per_dev, per_dev), per_dev)
                    dt = dt_v[now, lanes]
                    if u % 2 == 0:
                        both = pl.ds(pl.multiple_of((block * UNROLL + u) * per_dev, 2 * per_dev), 2 * per_dev)
                        pair = mixed_v[both, lanes].astype(F32)
                    mixed = pair[u % 2 * per_dev : (u % 2 + 1) * per_dev]
                    drive = dt * mixed
                    sums = [skip * mixed, None]
                    for n in range(states):
                        state[n] = jnp.exp2(dt * rates[n]) * state[n] + drive * b_tab[n, now, :]
                        term = state[n] * c_tab[n, now, :]
                        sums[n % 2] = term if sums[n % 2] is None else sums[n % 2] + term
                    y_v[now, lanes] = (sums[0] + sums[1]) * gate_v[now, lanes]
                return tuple(state)

            state = tuple(start_tm[n * per_dev : (n + 1) * per_dev, lanes] for n in range(states))
            state = lax.fori_loop(0, NEW // UNROLL, advance, state)
            for n in range(states):
                final_tm[n * per_dev : (n + 1) * per_dev, lanes] = state[n]
            return carry

        lax.fori_loop(0, width // LANES, one_tile, 0)
        chunk = slice(c * width, (c + 1) * width)
        gated = y_v[:, chunk].astype(BF16)
        out_v[:, chunk] = jnp.dot(back, gated, preferred_element_type=F32).astype(BF16)
        final = jnp.dot(back_s, final_tm[:, chunk].astype(BF16), preferred_element_type=F32)
        state_v[:, chunk] = final.astype(BF16)
        for src, dst in ((out_v, out_hbm), (state_v, state_hbm)):
            outs.append(pltpu.make_async_copy(src.at[:, chunk], dst.at[:, chunk], out_sems.at[len(outs)]))
            outs[-1].start()
    for copy in outs:
        copy.wait()


def split_refs(kernel, dims, n_in, n_out):
    def body(*refs):
        kernel(dims, refs[:n_in], refs[n_in : n_in + n_out], refs[n_in + n_out :])

    return body


def call(kernel, dims, name, ins, outs, scratch):
    hbm = pl.BlockSpec(memory_space=pltpu.HBM)
    anywhere = pl.BlockSpec(memory_space=pl.ANY)
    return pl.pallas_call(
        split_refs(kernel, dims, len(ins), len(outs)),
        in_specs=[hbm if fixed else anywhere for _, fixed in ins],
        out_specs=[anywhere] * len(outs),
        out_shape=[jax.ShapeDtypeStruct(*out) for out in outs],
        scratch_shapes=scratch,
        compiler_params=pltpu.CompilerParams(vmem_limit_bytes=VMEM_LIMIT),
        name=name,
    )(*[value for value, _ in ins])


def to_all(value, axis):
    return lax.all_to_all(value, axis, 0, 0)


def from_offset(value, axis, size, offset):
    return lax.ppermute(value, axis, [((i + offset) % size, i) for i in range(size)])


def shards(mesh, x_new, z_new, conv_weight, conv_bias, x_proj_weight, dt_proj_weight, dt_bias, a_log, d_skip,
           cache_ssm, cache_conv, holder, slot_id, prefix_len):
    n_replica, n_tensor = mesh.shape["replica"], mesh.shape["tensor"]
    rows, channels = x_new.shape
    per_dev = rows // NEW
    states = a_log.shape[0]
    rank = dt_proj_weight.shape[0]
    taps = conv_weight.shape[0]
    slots = cache_ssm.shape[0]
    out_cols = x_proj_weight.shape[1]
    requests = holder.shape[0]

    conv_rows = jnp.pad(cache_conv, ((0, 0), (0, 1), (0, 0))).reshape(slots * taps, channels)
    ssm_rows = cache_ssm.reshape(slots * states, channels)
    relative = n_replica <= 8
    if relative:
        conv_all = to_all(jnp.broadcast_to(conv_rows[None], (n_replica,) + conv_rows.shape), "replica")
        conv_all = conv_all.reshape(n_replica * slots * taps, channels)
        ssm_pieces = [ssm_rows] + [from_offset(ssm_rows, "replica", n_replica, k) for k in range(1, n_replica)]
    else:
        conv_all = lax.all_gather(conv_rows, "replica", axis=0, tiled=True)
        ssm_pieces = [lax.all_gather(ssm_rows, "replica", axis=0, tiled=True)]

    vmem, dma = pltpu.VMEM, pltpu.SemaphoreType.DMA
    ints = [pltpu.SMEM((requests,), jnp.int32)] * 3
    n_chunks = channels // min(512, channels)

    mixed, parts = call(
        project_kernel, (per_dev, n_replica, slots, False), "conv_project",
        [(holder, True), (slot_id, True), (prefix_len, True), (x_new, True), (x_proj_weight.T, True),
         (conv_weight, True), (conv_bias[None, :], True), (conv_all, False)],
        [((rows, channels), BF16), ((n_tensor, out_cols, rows), BF16)],
        ints + [
            vmem((rows, channels), BF16),
            vmem((out_cols, channels), BF16),
            vmem((taps, channels), BF16),
            vmem((1, channels), F32),
            vmem(conv_all.shape, BF16),
            vmem((rows + (taps - 1) * per_dev, channels), F32),
            vmem((rows, channels), BF16),
            vmem((out_cols, rows), F32),
            vmem((out_cols, rows), BF16),
            dma((6 + 2 * n_chunks,)),
            dma((n_chunks + n_tensor,)),
        ],
    )
    parts = to_all(parts, "tensor")

    out, state = call(
        scan_kernel, (per_dev, n_replica, slots, relative), "dt_scan_gate",
        [(holder, True), (slot_id, True), (prefix_len, True), (mixed, False), (z_new, True), (dt_proj_weight, True),
         (dt_bias[None, :], True), (a_log, True), (d_skip[None, :], True), (parts, False)]
        + [(piece, False) for piece in ssm_pieces],
        [((rows, channels), BF16), ((per_dev * states, channels), BF16)],
        ints + [
            vmem((rows, channels), BF16),
            vmem((rows, channels), BF16),
            vmem((rank, channels), BF16),
            vmem((1, channels), F32),
            vmem((states, channels), F32),
            vmem((1, channels), F32),
            vmem((n_tensor, out_cols, rows), BF16),
            vmem((n_replica * slots * states, channels), BF16),
            vmem((states, rows, LANES), F32),
            vmem((states, rows, LANES), F32),
            vmem((rows, channels), F32),
            vmem((rows, channels), F32),
            vmem((states, channels), F32),
            vmem((per_dev * states, channels), F32),
            vmem((per_dev * states, channels), F32),
            vmem((rows, channels), F32),
            vmem((rows, channels), BF16),
            vmem((per_dev * states, channels), BF16),
            dma((10 + len(ssm_pieces),)),
            dma((2 * n_chunks,)),
        ],
    )
    return out, state.reshape(per_dev, states, channels)


def solution(mesh):
    placed = (
        P(("groups", "replica"), "tensor"),
        P(("groups", "replica"), "tensor"),
        P(None, "tensor"),
        P("tensor"),
        P("tensor", None),
        P(None, "tensor"),
        P("tensor"),
        P(None, "tensor"),
        P("tensor"),
        P(("groups", "replica"), None, "tensor"),
        P(("groups", "replica"), None, "tensor"),
        P("groups"),
        P("groups"),
        P("groups"),
    )
    return jax.shard_map(
        functools.partial(shards, mesh),
        mesh=mesh,
        in_specs=placed,
        out_specs=(P(("groups", "replica"), "tensor"), P(("groups", "replica"), None, "tensor")),
        check_vma=False,
    )
```

```python
import functools

import jax
import jax.numpy as jnp
from jax import lax
from jax.experimental import pallas as pl
from jax.experimental.pallas import tpu as pltpu
from jax.sharding import PartitionSpec as P

NEW = 32
LANES = 128
LOG2E = 1.4426950408889634
MIB = 1024 * 1024
UNROLL = 8
F32, BF16 = jnp.float32, jnp.bfloat16
NT = (((1,), (1,)), ((), ()))
TN = (((0,), (0,)), ((), ()))


def silu(v):
    half = 0.5 * v
    return half + half * jnp.tanh(half)


def softplus(v):
    u = jnp.exp(-jnp.abs(v))
    small = u * (1.0 - u * (0.5 - u * (1.0 / 3.0)))
    return jnp.maximum(v, 0.0) + jnp.where(u < 0.004, small, jnp.log(1.0 + u))


def split_index(value, inner):
    assert inner & (inner - 1) == 0
    return value >> (inner.bit_length() - 1), value & (inner - 1)


def one_hot_rows(outer, inner):
    count = outer * inner
    row = lax.broadcasted_iota(jnp.int32, (count, count), 0)
    col = lax.broadcasted_iota(jnp.int32, (count, count), 1)
    high, low = split_index(row, outer)
    return jnp.where(col == low * inner + high, 1.0, 0.0).astype(BF16)


def pick_rows(values, row_low, count):
    out = jnp.zeros(row_low.shape, jnp.int32)
    for r in range(count):
        out = jnp.where(row_low == r, values[r], out)
    return out


def request_slots(dims, ints, me, gray):
    per_dev, n_replica, slots, relative = dims
    found, lengths = [], []
    for r in range(per_dev):
        request = me * per_dev + r
        place = ints[0][request]
        if relative:
            place = place ^ me
            place = place ^ (place >> 1) if gray else place
        found.append(place * slots + ints[1][request])
        lengths.append(ints[2][request])
    return found, lengths


def project_kernel(dims, refs_in, refs_out, scratch):
    per_dev, n_replica, slots, _ = dims
    holder, slot_id, prefix_len, x_hbm, wt_hbm, cw_hbm, cb_hbm = refs_in[:7]
    mixed_hbm, part_hbm = refs_out
    h_s, s_s, l_s, x_v, wt_v, cw_v, cb_v, conv_v, joined, mixed_v, part_f, part_v, sems, out_sems = scratch
    n_pieces = conv_v.shape[0]
    pieces = refs_in[7 : 7 + n_pieces]
    rows, channels = x_v.shape
    taps = cw_v.shape[0]
    copies = []
    pairs = [(cw_hbm, cw_v), (cb_hbm, cb_v), (holder, h_s), (slot_id, s_s), (prefix_len, l_s)]
    pairs += [(piece, conv_v.at[p]) for p, piece in enumerate(pieces)]
    for src, dst in pairs:
        copies.append(pltpu.make_async_copy(src, dst, sems.at[len(copies)]))
    small = len(copies)
    width = min(512, channels)
    chunks = [slice(c * width, (c + 1) * width) for c in range(channels // width)]
    for chunk in chunks:
        copies.append(pltpu.make_async_copy(x_hbm.at[:, chunk], x_v.at[:, chunk], sems.at[len(copies)]))
        copies.append(pltpu.make_async_copy(wt_hbm.at[:, chunk], wt_v.at[:, chunk], sems.at[len(copies)]))
    for copy in copies:
        copy.start()

    order = one_hot_rows(per_dev, NEW)
    for copy in copies[:small]:
        copy.wait()

    me = lax.axis_index("replica")
    found, lengths = request_slots(dims, (h_s, s_s, l_s), me, False)
    lines = (taps - 1) * per_dev
    piece_rows = conv_v.shape[1]
    shape = (per_dev * taps, n_pieces * piece_rows)
    tap, request = split_index(lax.broadcasted_iota(jnp.int32, shape, 0), per_dev)
    slot, col_tap = split_index(lax.broadcasted_iota(jnp.int32, shape, 1), taps)
    live = (taps - 1 - tap <= pick_rows(lengths, request, per_dev)) & (tap == col_tap)
    chosen = live & (slot == pick_rows(found, request, per_dev))
    select = jnp.where(chosen, 1.0, 0.0).astype(BF16)

    outs = []
    for c, chunk in enumerate(chunks):
        copies[small + 2 * c].wait()
        history = jnp.dot(select[:, :piece_rows], conv_v[0, :, chunk], preferred_element_type=F32)
        for p in range(1, n_pieces):
            picked = select[:, p * piece_rows : (p + 1) * piece_rows]
            history = history + jnp.dot(picked, conv_v[p, :, chunk], preferred_element_type=F32)
        joined[:lines, chunk] = history[:lines]
        joined[lines:, chunk] = jnp.dot(order, x_v[:, chunk], preferred_element_type=F32)
        summed = jnp.broadcast_to(cb_v[:, chunk], (rows, width))
        for k in range(taps):
            weight = cw_v[k : k + 1, chunk].astype(F32)
            summed = summed + joined[k * per_dev : k * per_dev + rows, chunk] * weight
        mixed = silu(summed).astype(BF16)
        mixed_v[:, chunk] = mixed
        copies[small + 2 * c + 1].wait()
        part = lax.dot_general(wt_v[:, chunk], mixed, NT, preferred_element_type=F32)
        if c == 0:
            part_f[...] = part
        else:
            part_f[...] += part
        outs.append(pltpu.make_async_copy(mixed_v.at[:, chunk], mixed_hbm.at[:, chunk], out_sems.at[c]))
        outs[-1].start()
    part_v[...] = part_f[...].astype(BF16)
    outs.append(pltpu.make_async_copy(part_v, part_hbm, out_sems.at[len(outs)]))
    outs[-1].start()
    for copy in outs:
        copy.wait()


def scan_kernel(dims, refs_in, refs_out, scratch):
    per_dev, n_replica, slots, _ = dims
    holder, slot_id, prefix_len, mixed_hbm, z_hbm, dtw_hbm, dtb_hbm, al_hbm, skip_hbm = refs_in[:9]
    out_hbm, state_hbm = refs_out
    (h_s, s_s, l_s, mixed_v, z_v, dtw_v, dtb_v, al_v, skip_v, parts_v, cache_v, b_tab, c_big, dt_v, gate_v,
     a_v, start_tm, final_tm, h_v, y_v, out_v, state_v, sems, out_sems) = scratch
    n_parts = parts_v.shape[0]
    parts, pieces = refs_in[9 : 9 + n_parts], refs_in[9 + n_parts :]
    rows, channels = z_v.shape
    states = al_v.shape[0]
    rank = dtw_v.shape[0]
    group = h_v.shape[2]
    pair_rows = 2 * per_dev
    depth = 2 * states * per_dev
    piece_rows = cache_v.shape[0] // len(pieces)
    pairs = [(z_hbm, z_v)] + [(part, parts_v.at[p]) for p, part in enumerate(parts)]
    pairs += [(dtw_hbm, dtw_v), (dtb_hbm, dtb_v), (al_hbm, al_v), (holder, h_s), (slot_id, s_s), (prefix_len, l_s),
              (skip_hbm, skip_v), (mixed_hbm, mixed_v)]
    pairs += [(piece, cache_v.at[p * piece_rows : (p + 1) * piece_rows]) for p, piece in enumerate(pieces)]
    copies = [pltpu.make_async_copy(src, dst, sems.at[i]) for i, (src, dst) in enumerate(pairs)]
    for copy in copies:
        copy.start()

    order = one_hot_rows(per_dev, NEW)
    copies[0].wait()
    gate_v[...] = silu(jnp.dot(order, z_v[...], preferred_element_type=F32))

    for copy in copies[1 : 1 + n_parts]:
        copy.wait()
    projected = parts_v[0].astype(F32)
    for p in range(1, n_parts):
        projected = projected + parts_v[p].astype(F32)
    dt_low = projected[:rank].astype(BF16)
    late = projected[rank:].T
    for n in range(states):
        b_tab[n] = jnp.broadcast_to(late[:, n : n + 1], (rows, LANES))
    shape = (states, depth)
    col_state = split_index(lax.broadcasted_iota(jnp.int32, shape, 1), per_dev)[0] & (states - 1)
    spread = jnp.where(lax.broadcasted_iota(jnp.int32, shape, 0) == col_state, 1.0, 0.0).astype(BF16)
    c_wide = jnp.dot(late[:, states:].astype(BF16), spread, preferred_element_type=F32)
    row = lax.broadcasted_iota(jnp.int32, (rows, depth), 0)
    col = lax.broadcasted_iota(jnp.int32, (rows, depth), 1)
    row_token, row_request = split_index(row, per_dev)
    col_token, col_rest = split_index(col, states * per_dev)
    fits = (row_request == (col_rest & (per_dev - 1))) & ((row_token & 1) == col_token)
    c_big[...] = jnp.where(fits, c_wide, 0.0).astype(BF16)

    for copy in copies[1 + n_parts :]:
        copy.wait()
    dt_v[...] = softplus(
        lax.dot_general(dt_low, dtw_v[...], TN, preferred_element_type=F32) + dtb_v[...]
    )
    a_v[...] = jnp.exp(al_v[...]) * (-LOG2E)

    me = lax.axis_index("replica")
    found, lengths = request_slots(dims, (h_s, s_s, l_s), me, True)
    shape = (per_dev * states, cache_v.shape[0])
    state_id, request = split_index(lax.broadcasted_iota(jnp.int32, shape, 0), per_dev)
    slot, col_state = split_index(lax.broadcasted_iota(jnp.int32, shape, 1), states)
    chosen = (pick_rows(lengths, request, per_dev) > 0) & (state_id == col_state)
    chosen = chosen & (slot == pick_rows(found, request, per_dev))
    select = jnp.where(chosen, 1.0, 0.0).astype(BF16)
    start_tm[...] = jnp.dot(select, cache_v[...], preferred_element_type=F32)

    n_groups = channels // group
    n_tiles = group // LANES
    n_blocks = NEW // UNROLL
    pairs_each = NEW // 2 // (n_tiles * n_blocks)

    def group_lanes(g):
        return pl.ds(pl.multiple_of(g * group, group), group)

    def finish_pair(g, pair):
        lanes = group_lanes(g)
        now = pl.ds(pl.multiple_of(pair * pair_rows, pair_rows), pair_rows)
        held = h_v[g & 1, pl.ds(pl.multiple_of(pair * depth, depth), depth), :]
        total = jnp.dot(c_big[now, :], held, preferred_element_type=F32)
        mixed = mixed_v[now, lanes].astype(F32)
        y_v[now, lanes] = ((total + skip_v[:, lanes] * mixed) * gate_v[now, lanes]).astype(BF16)

    def out_copies(g):
        lanes = group_lanes(g)
        return [
            pltpu.make_async_copy(src.at[:, lanes], dst.at[:, lanes], out_sems.at[i, g])
            for i, (src, dst) in enumerate(((out_v, out_hbm), (state_v, state_hbm)))
        ]

    def finish_group(g):
        lanes = group_lanes(g)
        back = one_hot_rows(NEW, per_dev)
        back_s = one_hot_rows(states, per_dev)
        out_v[:, lanes] = jnp.dot(back, y_v[:, lanes], preferred_element_type=F32).astype(BF16)
        final = jnp.dot(back_s, final_tm[:, lanes].astype(BF16), preferred_element_type=F32)
        state_v[:, lanes] = final.astype(BF16)
        for copy in out_copies(g):
            copy.start()

    def one_group(g, carry):
        before = jnp.maximum(g - 1, 0)

        def one_tile(i, carry):
            lanes = pl.ds(pl.multiple_of(g * group + i * LANES, LANES), LANES)
            part = pl.ds(pl.multiple_of(i * LANES, LANES), LANES)
            rates = [jnp.broadcast_to(a_v[n : n + 1, lanes], (per_dev, LANES)) for n in range(states)]

            def advance(block, state):
                state = list(state)
                for u in range(UNROLL):
                    t = block * UNROLL + u
                    now = pl.ds(pl.multiple_of(t * per_dev, per_dev), per_dev)
                    dt = dt_v[now, lanes]
                    if u % 2 == 0:
                        both = pl.ds(pl.multiple_of(t * per_dev, pair_rows), pair_rows)
                        pair = mixed_v[both, lanes].astype(F32)
                    drive = dt * pair[u % 2 * per_dev : (u % 2 + 1) * per_dev]
                    for n in range(states):
                        state[n] = jnp.exp2(dt * rates[n]) * state[n] + drive * b_tab[n, now, :]
                        if n % 2:
                            spot = pl.multiple_of((t * states + n - 1) * per_dev, pair_rows)
                            packed = jnp.concatenate([state[n - 1], state[n]], axis=0).astype(BF16)
                            h_v[g & 1, pl.ds(spot, pair_rows), part] = packed
                for k in range(pairs_each):
                    finish_pair(before, (i * n_blocks + block) * pairs_each + k)
                return tuple(state)

            state = tuple(start_tm[n * per_dev : (n + 1) * per_dev, lanes] for n in range(states))
            state = lax.fori_loop(0, n_blocks, advance, state)
            for n in range(states):
                final_tm[n * per_dev : (n + 1) * per_dev, lanes] = state[n]
            return carry

        lax.fori_loop(0, n_tiles, one_tile, 0)

        @pl.when(g > 0)
        def _():
            finish_group(before)

        return carry

    lax.fori_loop(0, n_groups, one_group, 0)

    def last_pair(pair, carry):
        finish_pair(n_groups - 1, pair)
        return carry

    lax.fori_loop(0, NEW // 2, last_pair, 0, unroll=4)
    finish_group(n_groups - 1)

    def last_wait(g, carry):
        for copy in out_copies(g):
            copy.wait()
        return carry

    lax.fori_loop(0, n_groups, last_wait, 0)


def split_refs(kernel, dims, n_in, n_out):
    def body(*refs):
        kernel(dims, refs[:n_in], refs[n_in : n_in + n_out], refs[n_in + n_out :])

    return body


def call(kernel, dims, name, limit, ins, outs, scratch):
    hbm = pl.BlockSpec(memory_space=pltpu.HBM)
    anywhere = pl.BlockSpec(memory_space=pl.ANY)
    return pl.pallas_call(
        split_refs(kernel, dims, len(ins), len(outs)),
        in_specs=[hbm if fixed else anywhere for _, fixed in ins],
        out_specs=[anywhere] * len(outs),
        out_shape=[jax.ShapeDtypeStruct(*out) for out in outs],
        scratch_shapes=scratch,
        compiler_params=pltpu.CompilerParams(vmem_limit_bytes=limit * MIB),
        name=name,
    )(*[value for value, _ in ins])


def swap(value, axis, size, mask):
    return lax.ppermute(value, axis, [(i, i ^ mask) for i in range(size)])


def shards(mesh, x_new, z_new, conv_weight, conv_bias, x_proj_weight, dt_proj_weight, dt_bias, a_log, d_skip,
           cache_ssm, cache_conv, holder, slot_id, prefix_len):
    n_replica, n_tensor = mesh.shape["replica"], mesh.shape["tensor"]
    rows, channels = x_new.shape
    per_dev = rows // NEW
    states = a_log.shape[0]
    rank = dt_proj_weight.shape[0]
    taps = conv_weight.shape[0]
    slots = cache_ssm.shape[0]
    out_cols = x_proj_weight.shape[1]
    requests = holder.shape[0]

    conv_rows = jnp.pad(cache_conv, ((0, 0), (0, 1), (0, 0))).reshape(slots * taps, channels)
    ssm_rows = cache_ssm.reshape(slots * states, channels)
    relative = n_replica == 4
    if relative:
        conv_pieces = [conv_rows] + [swap(conv_rows, "replica", n_replica, k) for k in range(1, n_replica)]
        early = [swap(ssm_rows, "replica", n_replica, 3), swap(ssm_rows, "replica", n_replica, 1)]
        ssm_pieces = [ssm_rows, early[1], early[0], swap(early[0], "replica", n_replica, 1)]
    else:
        conv_pieces = [lax.all_gather(conv_rows, "replica", axis=0, tiled=True)]
        ssm_pieces = [lax.all_gather(ssm_rows, "replica", axis=0, tiled=True)]
        early = []

    vmem, dma = pltpu.VMEM, pltpu.SemaphoreType.DMA
    ints = [pltpu.SMEM((requests,), jnp.int32)] * 3
    n_chunks = channels // min(512, channels)
    dims = (per_dev, n_replica, slots, relative)

    mixed, part = call(
        project_kernel, dims, "conv_project", 60,
        [(holder, True), (slot_id, True), (prefix_len, True), (x_new, True), (x_proj_weight.T, True),
         (conv_weight, True), (conv_bias[None, :], True)]
        + [(piece, False) for piece in conv_pieces + early],
        [((rows, channels), BF16), ((out_cols, rows), BF16)],
        ints + [
            vmem((rows, channels), BF16),
            vmem((out_cols, channels), BF16),
            vmem((taps, channels), BF16),
            vmem((1, channels), F32),
            vmem((len(conv_pieces),) + conv_pieces[0].shape, BF16),
            vmem((rows + (taps - 1) * per_dev, channels), F32),
            vmem((rows, channels), BF16),
            vmem((out_cols, rows), F32),
            vmem((out_cols, rows), BF16),
            dma((5 + len(conv_pieces) + 2 * n_chunks,)),
            dma((n_chunks + 1,)),
        ],
    )
    parts = [swap(part, "tensor", n_tensor, k) for k in reversed(range(1, n_tensor))] + [part]

    group = 2 * LANES
    out, state = call(
        scan_kernel, dims, "dt_scan_gate", 32,
        [(holder, True), (slot_id, True), (prefix_len, True), (mixed, False), (z_new, True), (dt_proj_weight, True),
         (dt_bias[None, :], True), (a_log, True), (d_skip[None, :], True)]
        + [(piece, False) for piece in parts + ssm_pieces],
        [((rows, channels), BF16), ((per_dev * states, channels), BF16)],
        ints + [
            vmem((rows, channels), BF16),
            vmem((rows, channels), BF16),
            vmem((rank, channels), BF16),
            vmem((1, channels), F32),
            vmem((states, channels), F32),
            vmem((1, channels), F32),
            vmem((n_tensor, out_cols, rows), BF16),
            vmem((n_replica * slots * states, channels), BF16),
            vmem((states, rows, LANES), F32),
            vmem((rows, 2 * states * per_dev), BF16),
            vmem((rows, channels), F32),
            vmem((rows, channels), F32),
            vmem((states, channels), F32),
            vmem((per_dev * states, channels), F32),
            vmem((per_dev * states, channels), F32),
            vmem((2, rows * states, group), BF16),
            vmem((rows, channels), BF16),
            vmem((rows, channels), BF16),
            vmem((per_dev * states, channels), BF16),
            dma((9 + n_tensor + len(ssm_pieces),)),
            dma((2, channels // group)),
        ],
    )
    return out, state.reshape(per_dev, states, channels)


def solution(mesh):
    placed = (
        P(("groups", "replica"), "tensor"),
        P(("groups", "replica"), "tensor"),
        P(None, "tensor"),
        P("tensor"),
        P("tensor", None),
        P(None, "tensor"),
        P("tensor"),
        P(None, "tensor"),
        P("tensor"),
        P(("groups", "replica"), None, "tensor"),
        P(("groups", "replica"), None, "tensor"),
        P("groups"),
        P("groups"),
        P("groups"),
    )
    return jax.shard_map(
        functools.partial(shards, mesh),
        mesh=mesh,
        in_specs=placed,
        out_specs=(P(("groups", "replica"), "tensor"), P(("groups", "replica"), None, "tensor")),
        check_vma=False,
    )
```

```python
import functools

import jax
import jax.numpy as jnp
from jax import lax
from jax.experimental import pallas as pl
from jax.experimental.pallas import tpu as pltpu
from jax.sharding import PartitionSpec as P

NEW = 32
LANES = 128
LOG2E = 1.4426950408889634
MIB = 1024 * 1024
UNROLL = 8
F32, BF16 = jnp.float32, jnp.bfloat16
NT = (((1,), (1,)), ((), ()))
TN = (((0,), (0,)), ((), ()))


def silu(v):
    half = 0.5 * v
    return half + half * jnp.tanh(half)


def softplus(v):
    u = jnp.exp(-jnp.abs(v))
    small = u * (1.0 - u * (0.5 - u * (1.0 / 3.0)))
    return jnp.maximum(v, 0.0) + jnp.where(u < 0.004, small, jnp.log(1.0 + u))


def split_index(value, inner):
    assert inner & (inner - 1) == 0
    return value >> (inner.bit_length() - 1), value & (inner - 1)


def one_hot_rows(outer, inner):
    count = outer * inner
    row = lax.broadcasted_iota(jnp.int32, (count, count), 0)
    col = lax.broadcasted_iota(jnp.int32, (count, count), 1)
    high, low = split_index(row, outer)
    return jnp.where(col == low * inner + high, 1.0, 0.0).astype(BF16)


def pick_rows(values, row_low, count):
    out = jnp.zeros(row_low.shape, jnp.int32)
    for r in range(count):
        out = jnp.where(row_low == r, values[r], out)
    return out


def request_places(dims, ints, me):
    per_dev, n_replica, _, relative = dims
    places, slot_ids, lengths = [], [], []
    for r in range(per_dev):
        request = me * per_dev + r
        place = ints[0][request]
        if relative:
            place = place ^ me
            place = place ^ (place >> 1)
        places.append(place)
        slot_ids.append(ints[1][request])
        lengths.append(ints[2][request])
    return places, slot_ids, lengths


def fetch_rows(target, live, pieces):
    total = None
    for first, value in pieces:
        col = lax.broadcasted_iota(jnp.int32, (target.shape[0], value.shape[0]), 1) + first
        select = jnp.where((col == target) & live, 1.0, 0.0).astype(BF16)
        part = jnp.dot(select, value, preferred_element_type=F32)
        total = part if total is None else total + part
    return total


def project_kernel(dims, refs_in, refs_out, scratch):
    dims, block, firsts = dims
    per_dev, n_replica, slots, _ = dims
    holder, slot_id, prefix_len, x_hbm, wt_hbm, cw_hbm, cb_hbm = refs_in[:7]
    mixed_hbm, part_hbm = refs_out
    h_s, s_s, l_s, x_v, wt_v, cw_v, cb_v, joined, mixed_v, part_f, part_v, sems, out_sems = scratch[:13]
    held = scratch[13:]
    pieces = refs_in[7:]
    rows, channels = x_v.shape
    taps = cw_v.shape[0]
    copies = []
    pairs = [(cw_hbm, cw_v), (cb_hbm, cb_v), (holder, h_s), (slot_id, s_s), (prefix_len, l_s)]
    pairs += list(zip(pieces, held))
    for src, dst in pairs:
        copies.append(pltpu.make_async_copy(src, dst, sems.at[len(copies)]))
    small = len(copies)
    width = min(512, channels)
    chunks = [slice(c * width, (c + 1) * width) for c in range(channels // width)]
    for chunk in chunks:
        copies.append(pltpu.make_async_copy(x_hbm.at[:, chunk], x_v.at[:, chunk], sems.at[len(copies)]))
        copies.append(pltpu.make_async_copy(wt_hbm.at[:, chunk], wt_v.at[:, chunk], sems.at[len(copies)]))
    for copy in copies:
        copy.start()

    order = one_hot_rows(per_dev, NEW)
    for copy in copies[:small]:
        copy.wait()

    me = lax.axis_index("replica")
    places, slot_ids, lengths = request_places(dims, (h_s, s_s, l_s), me)
    lines = (taps - 1) * per_dev
    tap, request = split_index(lax.broadcasted_iota(jnp.int32, (per_dev * taps, 1), 0), per_dev)
    starts = [places[r] * block + (block - slots * taps) + slot_ids[r] * taps for r in range(per_dev)]
    target = pick_rows(starts, request, per_dev) + tap
    live = (tap < taps - 1) & (taps - 1 - tap <= pick_rows(lengths, request, per_dev))

    outs = []
    for c, chunk in enumerate(chunks):
        copies[small + 2 * c].wait()
        found = [(first, ref[:, chunk]) for first, ref in zip(firsts, held)]
        history = fetch_rows(target, live, found)
        joined[:lines, chunk] = history[:lines]
        joined[lines:, chunk] = jnp.dot(order, x_v[:, chunk], preferred_element_type=F32)
        summed = jnp.broadcast_to(cb_v[:, chunk], (rows, width))
        for k in range(taps):
            weight = cw_v[k : k + 1, chunk].astype(F32)
            summed = summed + joined[k * per_dev : k * per_dev + rows, chunk] * weight
        mixed = silu(summed).astype(BF16)
        mixed_v[:, chunk] = mixed
        copies[small + 2 * c + 1].wait()
        part = lax.dot_general(wt_v[:, chunk], mixed, NT, preferred_element_type=F32)
        if c == 0:
            part_f[...] = part
        else:
            part_f[...] += part
        outs.append(pltpu.make_async_copy(mixed_v.at[:, chunk], mixed_hbm.at[:, chunk], out_sems.at[c]))
        outs[-1].start()
    part_v[...] = part_f[...].astype(BF16)
    outs.append(pltpu.make_async_copy(part_v, part_hbm, out_sems.at[len(outs)]))
    outs[-1].start()
    for copy in outs:
        copy.wait()


def scan_kernel(dims, refs_in, refs_out, scratch):
    dims, block = dims
    per_dev, n_replica, slots, _ = dims
    holder, slot_id, prefix_len, mixed_hbm, z_hbm, dtw_hbm, dtb_hbm, al_hbm, skip_hbm = refs_in[:9]
    out_hbm, state_hbm = refs_out
    (h_s, s_s, l_s, mixed_v, z_v, dtw_v, dtb_v, al_v, skip_v, parts_v, cache_v, b_tab, c_tab, dt_v, drive_v, gate_v,
     a_v, start_tm, final_tm, y_v, out_v, state_v, sems, out_sems) = scratch
    n_parts, n_pieces = parts_v.shape[0], cache_v.shape[0]
    parts, pieces = refs_in[9 : 9 + n_parts], refs_in[9 + n_parts :]
    rows, channels = z_v.shape
    states = al_v.shape[0]
    rank = dtw_v.shape[0]
    pairs = [(z_hbm, z_v)] + [(part, parts_v.at[p]) for p, part in enumerate(parts)]
    pairs += [(dtw_hbm, dtw_v), (dtb_hbm, dtb_v), (al_hbm, al_v), (holder, h_s), (slot_id, s_s), (prefix_len, l_s),
              (skip_hbm, skip_v), (mixed_hbm, mixed_v)]
    pairs += [(piece, cache_v.at[p]) for p, piece in enumerate(pieces)]
    copies = [pltpu.make_async_copy(src, dst, sems.at[i]) for i, (src, dst) in enumerate(pairs)]
    for copy in copies:
        copy.start()

    order = one_hot_rows(per_dev, NEW)
    copies[0].wait()
    gate_v[...] = silu(jnp.dot(order, z_v[...], preferred_element_type=F32))

    for copy in copies[1 : 1 + n_parts]:
        copy.wait()
    projected = parts_v[0].astype(F32)
    for p in range(1, n_parts):
        projected = projected + parts_v[p].astype(F32)
    dt_low = projected[:rank].astype(BF16)
    late = projected[rank:].T
    for n in range(states):
        b_tab[n] = jnp.broadcast_to(late[:, n : n + 1], (rows, LANES))
        c_tab[n] = jnp.broadcast_to(late[:, states + n : states + n + 1], (rows, LANES))
    for copy in copies[1 + n_parts :]:
        copy.wait()
    dt = softplus(lax.dot_general(dt_low, dtw_v[...], TN, preferred_element_type=F32) + dtb_v[...])
    dt_v[...] = dt
    drive_v[...] = dt * mixed_v[...].astype(F32)
    a_v[...] = jnp.exp(al_v[...]) * (-LOG2E)

    me = lax.axis_index("replica")
    places, slot_ids, lengths = request_places(dims, (h_s, s_s, l_s), me)
    state_id, request = split_index(lax.broadcasted_iota(jnp.int32, (per_dev * states, 1), 0), per_dev)
    starts = [places[r] * block + slot_ids[r] * states for r in range(per_dev)]
    target = pick_rows(starts, request, per_dev) + state_id
    live = pick_rows(lengths, request, per_dev) > 0
    found = [(p * cache_v.shape[1], cache_v[p]) for p in range(n_pieces)]
    start_tm[...] = fetch_rows(target, live, found)

    tiles = 2
    half = states // 2
    width = 2 * tiles * LANES
    n_chunks = channels // width

    def out_copies(c):
        lanes = pl.ds(pl.multiple_of(c * width, width), width)
        return [
            pltpu.make_async_copy(src.at[:, lanes], dst.at[:, lanes], out_sems.at[i, c])
            for i, (src, dst) in enumerate(((out_v, out_hbm), (state_v, state_hbm)))
        ]

    def scan_group(g, carry):
        lanes = [pl.ds(pl.multiple_of((g * tiles + j) * LANES, LANES), LANES) for j in range(tiles)]
        for first in range(0, states, half):
            ids = range(first, first + half)
            rates = [[jnp.broadcast_to(a_v[n : n + 1, lane], (per_dev, LANES)) for n in ids] for lane in lanes]

            def advance(step, state):
                state = list(state)
                for u in range(UNROLL):
                    now = pl.ds(pl.multiple_of((step * UNROLL + u) * per_dev, per_dev), per_dev)
                    dt = [dt_v[now, lane] for lane in lanes]
                    drive = [drive_v[now, lane] for lane in lanes]
                    sums = [None] * tiles
                    for k, n in enumerate(ids):
                        b, c = b_tab[n, now, :], c_tab[n, now, :]
                        for j in range(tiles):
                            i = j * half + k
                            state[i] = jnp.exp2(dt[j] * rates[j][k]) * state[i] + drive[j] * b
                            term = state[i] * c
                            sums[j] = term if sums[j] is None else sums[j] + term
                    for j, lane in enumerate(lanes):
                        y_v[now, lane] = sums[j] if first == 0 else y_v[now, lane] + sums[j]
                return tuple(state)

            state = tuple(start_tm[n * per_dev : (n + 1) * per_dev, lane] for lane in lanes for n in ids)
            state = lax.fori_loop(0, NEW // UNROLL, advance, state)
            for j, lane in enumerate(lanes):
                for k, n in enumerate(ids):
                    final_tm[n * per_dev : (n + 1) * per_dev, lane] = state[j * half + k]
        return carry

    def one_chunk(c, carry):
        lax.fori_loop(c * 2, c * 2 + 2, scan_group, 0)
        lanes = pl.ds(pl.multiple_of(c * width, width), width)
        total = y_v[:, lanes] + skip_v[:, lanes] * mixed_v[:, lanes].astype(F32)
        gated = (total * gate_v[:, lanes]).astype(BF16)
        back = one_hot_rows(NEW, per_dev)
        back_s = one_hot_rows(states, per_dev)
        out_v[:, lanes] = jnp.dot(back, gated, preferred_element_type=F32).astype(BF16)
        final = jnp.dot(back_s, final_tm[:, lanes].astype(BF16), preferred_element_type=F32)
        state_v[:, lanes] = final.astype(BF16)
        for copy in out_copies(c):
            copy.start()
        return carry

    lax.fori_loop(0, n_chunks, one_chunk, 0)

    def last_wait(c, carry):
        for copy in out_copies(c):
            copy.wait()
        return carry

    lax.fori_loop(0, n_chunks, last_wait, 0)


def split_refs(kernel, dims, n_in, n_out):
    def body(*refs):
        kernel(dims, refs[:n_in], refs[n_in : n_in + n_out], refs[n_in + n_out :])

    return body


def call(kernel, dims, name, limit, ins, outs, scratch):
    hbm = pl.BlockSpec(memory_space=pltpu.HBM)
    anywhere = pl.BlockSpec(memory_space=pl.ANY)
    return pl.pallas_call(
        split_refs(kernel, dims, len(ins), len(outs)),
        in_specs=[hbm if fixed else anywhere for _, fixed in ins],
        out_specs=[anywhere] * len(outs),
        out_shape=[jax.ShapeDtypeStruct(*out) for out in outs],
        scratch_shapes=scratch,
        compiler_params=pltpu.CompilerParams(vmem_limit_bytes=limit * MIB),
        name=name,
    )(*[value for value, _ in ins])


def swap(value, axis, size, mask):
    return lax.ppermute(value, axis, [(i, i ^ mask) for i in range(size)])


def shards(mesh, x_new, z_new, conv_weight, conv_bias, x_proj_weight, dt_proj_weight, dt_bias, a_log, d_skip,
           cache_ssm, cache_conv, holder, slot_id, prefix_len):
    n_replica, n_tensor = mesh.shape["replica"], mesh.shape["tensor"]
    rows, channels = x_new.shape
    per_dev = rows // NEW
    states = a_log.shape[0]
    rank = dt_proj_weight.shape[0]
    taps = conv_weight.shape[0]
    slots = cache_ssm.shape[0]
    out_cols = x_proj_weight.shape[1]
    requests = holder.shape[0]

    conv_rows = jnp.pad(cache_conv, ((0, 0), (0, 1), (0, 0))).reshape(slots * taps, channels)
    rows_all = jnp.concatenate([cache_ssm.reshape(slots * states, channels), conv_rows])
    block = rows_all.shape[0]
    relative = n_replica == 4
    if relative:
        far = swap(rows_all, "replica", n_replica, 3)
        near = swap(rows_all, "replica", n_replica, 1)
        conv_two = swap(conv_rows, "replica", n_replica, 2)
        conv_pieces = [rows_all, near, far, conv_two]
        firsts = (0, block, 2 * block, 4 * block - slots * taps)
        ssm_pieces = [rows_all, near, far, swap(far, "replica", n_replica, 1)]
    else:
        ssm_pieces = [lax.all_gather(rows_all, "replica", axis=0, tiled=True)]
        conv_pieces, firsts = ssm_pieces, (0,)

    vmem, dma = pltpu.VMEM, pltpu.SemaphoreType.DMA
    ints = [pltpu.SMEM((requests,), jnp.int32)] * 3
    n_chunks = channels // min(512, channels)
    dims = (per_dev, n_replica, slots, relative)

    mixed, part = call(
        project_kernel, (dims, block, firsts), "conv_project", 60,
        [(holder, True), (slot_id, True), (prefix_len, True), (x_new, True), (x_proj_weight.T, True),
         (conv_weight, True), (conv_bias[None, :], True)]
        + [(piece, False) for piece in conv_pieces],
        [((rows, channels), BF16), ((out_cols, rows), BF16)],
        ints + [
            vmem((rows, channels), BF16),
            vmem((out_cols, channels), BF16),
            vmem((taps, channels), BF16),
            vmem((1, channels), F32),
            vmem((rows + (taps - 1) * per_dev, channels), F32),
            vmem((rows, channels), BF16),
            vmem((out_cols, rows), F32),
            vmem((out_cols, rows), BF16),
            dma((5 + len(conv_pieces) + 2 * n_chunks,)),
            dma((n_chunks + 1,)),
        ] + [vmem(piece.shape, BF16) for piece in conv_pieces],
    )
    parts = [swap(part, "tensor", n_tensor, k) for k in reversed(range(1, n_tensor))] + [part]

    blocks = (len(ssm_pieces),) + ssm_pieces[0].shape
    out, state = call(
        scan_kernel, (dims, block), "dt_scan_gate", 60,
        [(holder, True), (slot_id, True), (prefix_len, True), (mixed, False), (z_new, True), (dt_proj_weight, True),
         (dt_bias[None, :], True), (a_log, True), (d_skip[None, :], True)]
        + [(piece, False) for piece in parts + ssm_pieces],
        [((rows, channels), BF16), ((per_dev * states, channels), BF16)],
        ints + [
            vmem((rows, channels), BF16),
            vmem((rows, channels), BF16),
            vmem((rank, channels), BF16),
            vmem((1, channels), F32),
            vmem((states, channels), F32),
            vmem((1, channels), F32),
            vmem((n_tensor, out_cols, rows), BF16),
            vmem(blocks, BF16),
            vmem((states, rows, LANES), F32),
            vmem((states, rows, LANES), F32),
            vmem((rows, channels), F32),
            vmem((rows, channels), F32),
            vmem((rows, channels), F32),
            vmem((states, channels), F32),
            vmem((per_dev * states, channels), F32),
            vmem((per_dev * states, channels), F32),
            vmem((rows, channels), F32),
            vmem((rows, channels), BF16),
            vmem((per_dev * states, channels), BF16),
            dma((9 + n_tensor + len(ssm_pieces),)),
            dma((2, n_chunks)),
        ],
    )
    return out, state.reshape(per_dev, states, channels)


def solution(mesh):
    placed = (
        P(("groups", "replica"), "tensor"),
        P(("groups", "replica"), "tensor"),
        P(None, "tensor"),
        P("tensor"),
        P("tensor", None),
        P(None, "tensor"),
        P("tensor"),
        P(None, "tensor"),
        P("tensor"),
        P(("groups", "replica"), None, "tensor"),
        P(("groups", "replica"), None, "tensor"),
        P("groups"),
        P("groups"),
        P("groups"),
    )
    return jax.shard_map(
        functools.partial(shards, mesh),
        mesh=mesh,
        in_specs=placed,
        out_specs=(P(("groups", "replica"), "tensor"), P(("groups", "replica"), None, "tensor")),
        check_vma=False,
    )
```

```python
import functools

import jax
import jax.numpy as jnp
from jax import lax
from jax.experimental import pallas as pl
from jax.experimental.pallas import tpu as pltpu
from jax.sharding import PartitionSpec as P

NEW = 32
LANES = 128
MIB = 1024 * 1024
UNROLL = 8
F32, BF16 = jnp.float32, jnp.bfloat16
NT = (((1,), (1,)), ((), ()))
TN = (((0,), (0,)), ((), ()))


def silu(v):
    half = 0.5 * v
    return half + half * jnp.tanh(half)


def softplus(v):
    u = jnp.exp(-jnp.abs(v))
    small = u * (1.0 - u * (0.5 - u * (1.0 / 3.0)))
    return jnp.maximum(v, 0.0) + jnp.where(u < 0.004, small, jnp.log(1.0 + u))


def split_index(value, inner):
    assert inner & (inner - 1) == 0
    return value >> (inner.bit_length() - 1), value & (inner - 1)


def one_hot_rows(outer, inner):
    count = outer * inner
    row = lax.broadcasted_iota(jnp.int32, (count, count), 0)
    col = lax.broadcasted_iota(jnp.int32, (count, count), 1)
    high, low = split_index(row, outer)
    return jnp.where(col == low * inner + high, 1.0, 0.0).astype(BF16)


def pick_rows(values, row_low, count):
    out = jnp.zeros(row_low.shape, jnp.int32)
    for r in range(count):
        out = jnp.where(row_low == r, values[r], out)
    return out


def request_places(dims, ints, me):
    per_dev, n_replica, _, relative = dims
    places, slot_ids, lengths = [], [], []
    for r in range(per_dev):
        request = me * per_dev + r
        place = ints[0][request]
        if relative:
            place = place ^ me
            place = place ^ (place >> 1)
        places.append(place)
        slot_ids.append(ints[1][request])
        lengths.append(ints[2][request])
    return places, slot_ids, lengths


def fetch_rows(target, live, pieces):
    total = None
    for first, value in pieces:
        col = lax.broadcasted_iota(jnp.int32, (target.shape[0], value.shape[0]), 1) + first
        select = jnp.where((col == target) & live, 1.0, 0.0).astype(BF16)
        part = jnp.dot(select, value, preferred_element_type=F32)
        total = part if total is None else total + part
    return total


def project_kernel(dims, refs_in, refs_out, scratch):
    per_dev = dims
    x_hbm, wt_hbm, cw_hbm, cb_hbm = refs_in
    mixed_hbm, head_hbm, part_hbm = refs_out
    x_v, wt_v, cw_v, cb_v, joined, mixed_v, head_v, part_f, part_v, sems, out_sems = scratch
    rows, channels = x_v.shape
    taps = cw_v.shape[0]
    lines = (taps - 1) * per_dev
    pairs = [(cw_hbm, cw_v), (cb_hbm, cb_v)]
    width = min(512, channels)
    chunks = [slice(c * width, (c + 1) * width) for c in range(channels // width)]
    for chunk in chunks:
        pairs += [(x_hbm.at[:, chunk], x_v.at[:, chunk]), (wt_hbm.at[:, chunk], wt_v.at[:, chunk])]
    copies = [pltpu.make_async_copy(src, dst, sems.at[i]) for i, (src, dst) in enumerate(pairs)]
    for copy in copies:
        copy.start()

    order = one_hot_rows(per_dev, NEW)
    joined[:lines, :] = jnp.zeros((lines, channels), F32)
    copies[0].wait()
    copies[1].wait()
    outs = []
    for c, chunk in enumerate(chunks):
        copies[2 + 2 * c].wait()
        joined[lines:, chunk] = jnp.dot(order, x_v[:, chunk], preferred_element_type=F32)
        summed = jnp.broadcast_to(cb_v[:, chunk], (rows, width))
        for k in range(taps):
            weight = cw_v[k : k + 1, chunk].astype(F32)
            summed = summed + joined[k * per_dev : k * per_dev + rows, chunk] * weight
        head_v[:, chunk] = summed[: head_v.shape[0]]
        mixed = silu(summed).astype(BF16)
        mixed_v[:, chunk] = mixed
        copies[3 + 2 * c].wait()
        part = lax.dot_general(wt_v[:, chunk], mixed, NT, preferred_element_type=F32)
        if c == 0:
            part_f[...] = part
        else:
            part_f[...] += part
        outs.append(pltpu.make_async_copy(mixed_v.at[:, chunk], mixed_hbm.at[:, chunk], out_sems.at[c]))
        outs[-1].start()
    part_v[...] = part_f[...].astype(BF16)
    for src, dst in ((part_v, part_hbm), (head_v, head_hbm)):
        outs.append(pltpu.make_async_copy(src, dst, out_sems.at[len(outs)]))
        outs[-1].start()
    for copy in outs:
        copy.wait()


def history_kernel(dims, refs_in, refs_out, scratch):
    dims, block, firsts = dims
    per_dev, n_replica, slots, _ = dims
    holder, slot_id, prefix_len, head_hbm, part_hbm, wt_hbm, cw_hbm = refs_in[:7]
    pieces = refs_in[7:]
    mixed_hbm, fixed_hbm = refs_out
    h_s, s_s, l_s, head_v, part_v, wt_v, cw_v, mixed_v, sems, out_sems = scratch[:10]
    held = scratch[10:]
    taps = cw_v.shape[0]
    pairs = [(holder, h_s), (slot_id, s_s), (prefix_len, l_s), (cw_hbm, cw_v), (head_hbm, head_v)]
    pairs += list(zip(pieces, held)) + [(wt_hbm, wt_v), (part_hbm, part_v)]
    copies = [pltpu.make_async_copy(src, dst, sems.at[i]) for i, (src, dst) in enumerate(pairs)]
    for copy in copies:
        copy.start()
    for copy in copies[:-2]:
        copy.wait()

    me = lax.axis_index("replica")
    places, slot_ids, lengths = request_places(dims, (h_s, s_s, l_s), me)
    tap, request = split_index(lax.broadcasted_iota(jnp.int32, (per_dev * taps, 1), 0), per_dev)
    starts = [places[r] * block + (block - slots * taps) + slot_ids[r] * taps for r in range(per_dev)]
    target = pick_rows(starts, request, per_dev) + tap
    live = (tap < taps - 1) & (taps - 1 - tap <= pick_rows(lengths, request, per_dev))
    history = fetch_rows(target, live, [(first, ref[...]) for first, ref in zip(firsts, held)])
    for t in range(taps - 1):
        now = slice(t * per_dev, (t + 1) * per_dev)
        summed = head_v[now]
        for k in range(taps - 1 - t):
            weight = cw_v[k : k + 1].astype(F32)
            summed = summed + history[(t + k) * per_dev : (t + k + 1) * per_dev] * weight
        head_v[now] = summed
    mixed = silu(head_v[...]).astype(BF16)
    mixed_v[...] = mixed
    mixed_out = pltpu.make_async_copy(mixed_v, mixed_hbm, out_sems.at[0])
    mixed_out.start()
    copies[-2].wait()
    part = lax.dot_general(wt_v[...], mixed, NT, preferred_element_type=F32).astype(BF16)
    copies[-1].wait()
    part_v[:, : per_dev * taps] = part
    part_out = pltpu.make_async_copy(part_v, fixed_hbm, out_sems.at[1])
    part_out.start()
    mixed_out.wait()
    part_out.wait()


def scan_kernel(dims, refs_in, refs_out, scratch):
    dims, block = dims
    per_dev, n_replica, slots, _ = dims
    holder, slot_id, prefix_len, mixed_hbm, head_hbm, z_hbm, dtw_hbm, dtb_hbm, al_hbm, skip_hbm = refs_in[:10]
    out_hbm, state_hbm = refs_out
    (h_s, s_s, l_s, mixed_v, z_v, dtw_v, dtb_v, al_v, skip_v, parts_v, cache_v, b_tab, c_tab, dt_v, drive_v, gate_v,
     a_v, start_tm, final_tm, y_v, out_v, state_v, sems, out_sems) = scratch
    n_parts, n_pieces = parts_v.shape[0], cache_v.shape[0]
    parts, pieces = refs_in[10 : 10 + n_parts], refs_in[10 + n_parts :]
    head = head_hbm.shape[0]
    rows, channels = z_v.shape
    states = al_v.shape[0]
    rank = dtw_v.shape[0]
    pairs = [(z_hbm, z_v)] + [(part, parts_v.at[p]) for p, part in enumerate(parts)]
    pairs += [(dtw_hbm, dtw_v), (dtb_hbm, dtb_v), (al_hbm, al_v), (holder, h_s), (slot_id, s_s), (prefix_len, l_s),
              (skip_hbm, skip_v), (head_hbm, mixed_v.at[:head]), (mixed_hbm.at[head:], mixed_v.at[head:])]
    pairs += [(piece, cache_v.at[p]) for p, piece in enumerate(pieces)]
    copies = [pltpu.make_async_copy(src, dst, sems.at[i]) for i, (src, dst) in enumerate(pairs)]
    for copy in copies:
        copy.start()

    order = one_hot_rows(per_dev, NEW)
    copies[0].wait()
    gate_v[...] = silu(jnp.dot(order, z_v[...], preferred_element_type=F32))

    for copy in copies[1 : 1 + n_parts]:
        copy.wait()
    projected = parts_v[0].astype(F32)
    for p in range(1, n_parts):
        projected = projected + parts_v[p].astype(F32)
    dt_low = projected[:rank].astype(BF16)
    late = projected[rank:].T
    for n in range(states):
        b_tab[n] = jnp.broadcast_to(late[:, n : n + 1], (rows, LANES))
        c_tab[n] = jnp.broadcast_to(late[:, states + n : states + n + 1], (rows, LANES))
    for copy in copies[1 + n_parts :]:
        copy.wait()
    dt = softplus(lax.dot_general(dt_low, dtw_v[...], TN, preferred_element_type=F32) + dtb_v[...])
    dt_v[...] = dt
    drive_v[...] = dt * mixed_v[...].astype(F32)
    a_v[...] = -jnp.exp(al_v[...])

    me = lax.axis_index("replica")
    places, slot_ids, lengths = request_places(dims, (h_s, s_s, l_s), me)
    state_id, request = split_index(lax.broadcasted_iota(jnp.int32, (per_dev * states, 1), 0), per_dev)
    starts = [places[r] * block + slot_ids[r] * states for r in range(per_dev)]
    target = pick_rows(starts, request, per_dev) + state_id
    live = pick_rows(lengths, request, per_dev) > 0
    found = [(p * cache_v.shape[1], cache_v[p]) for p in range(n_pieces)]
    start_tm[...] = fetch_rows(target, live, found)

    tiles = 2
    half = states // 2
    width = 2 * tiles * LANES
    n_chunks = channels // width

    def out_copies(c):
        lanes = pl.ds(pl.multiple_of(c * width, width), width)
        return [
            pltpu.make_async_copy(src.at[:, lanes], dst.at[:, lanes], out_sems.at[i, c])
            for i, (src, dst) in enumerate(((out_v, out_hbm), (state_v, state_hbm)))
        ]

    def scan_group(g, carry):
        lanes = [pl.ds(pl.multiple_of((g * tiles + j) * LANES, LANES), LANES) for j in range(tiles)]
        for first in range(0, states, half):
            ids = range(first, first + half)
            rates = [[jnp.broadcast_to(a_v[n : n + 1, lane], (per_dev, LANES)) for n in ids] for lane in lanes]

            def advance(step, state):
                state = list(state)
                for u in range(UNROLL):
                    now = pl.ds(pl.multiple_of((step * UNROLL + u) * per_dev, per_dev), per_dev)
                    dt = [dt_v[now, lane] for lane in lanes]
                    drive = [drive_v[now, lane] for lane in lanes]
                    sums = [None] * tiles
                    for k, n in enumerate(ids):
                        b, c = b_tab[n, now, :], c_tab[n, now, :]
                        for j in range(tiles):
                            i = j * half + k
                            state[i] = jnp.exp(dt[j] * rates[j][k]) * state[i] + drive[j] * b
                            term = state[i] * c
                            sums[j] = term if sums[j] is None else sums[j] + term
                    for j, lane in enumerate(lanes):
                        y_v[now, lane] = sums[j] if first == 0 else y_v[now, lane] + sums[j]
                return tuple(state)

            state = tuple(start_tm[n * per_dev : (n + 1) * per_dev, lane] for lane in lanes for n in ids)
            state = lax.fori_loop(0, NEW // UNROLL, advance, state)
            for j, lane in enumerate(lanes):
                for k, n in enumerate(ids):
                    final_tm[n * per_dev : (n + 1) * per_dev, lane] = state[j * half + k]
        return carry

    def one_chunk(c, carry):
        lax.fori_loop(c * 2, c * 2 + 2, scan_group, 0)
        lanes = pl.ds(pl.multiple_of(c * width, width), width)
        total = y_v[:, lanes] + skip_v[:, lanes] * mixed_v[:, lanes].astype(F32)
        gated = (total * gate_v[:, lanes]).astype(BF16)
        back = one_hot_rows(NEW, per_dev)
        back_s = one_hot_rows(states, per_dev)
        out_v[:, lanes] = jnp.dot(back, gated, preferred_element_type=F32).astype(BF16)
        final = jnp.dot(back_s, final_tm[:, lanes].astype(BF16), preferred_element_type=F32)
        state_v[:, lanes] = final.astype(BF16)
        for copy in out_copies(c):
            copy.start()
        return carry

    lax.fori_loop(0, n_chunks, one_chunk, 0)

    def last_wait(c, carry):
        for copy in out_copies(c):
            copy.wait()
        return carry

    lax.fori_loop(0, n_chunks, last_wait, 0)


def split_refs(kernel, dims, n_in, n_out):
    def body(*refs):
        kernel(dims, refs[:n_in], refs[n_in : n_in + n_out], refs[n_in + n_out :])

    return body


def call(kernel, dims, name, limit, ins, outs, scratch):
    hbm = pl.BlockSpec(memory_space=pltpu.HBM)
    anywhere = pl.BlockSpec(memory_space=pl.ANY)
    return pl.pallas_call(
        split_refs(kernel, dims, len(ins), len(outs)),
        in_specs=[hbm if fixed else anywhere for _, fixed in ins],
        out_specs=[anywhere] * len(outs),
        out_shape=[jax.ShapeDtypeStruct(*out) for out in outs],
        scratch_shapes=scratch,
        compiler_params=pltpu.CompilerParams(vmem_limit_bytes=limit * MIB),
        name=name,
    )(*[value for value, _ in ins])


def swap(value, axis, size, mask):
    return lax.ppermute(value, axis, [(i, i ^ mask) for i in range(size)])


def shards(mesh, x_new, z_new, conv_weight, conv_bias, x_proj_weight, dt_proj_weight, dt_bias, a_log, d_skip,
           cache_ssm, cache_conv, holder, slot_id, prefix_len):
    n_replica, n_tensor = mesh.shape["replica"], mesh.shape["tensor"]
    rows, channels = x_new.shape
    per_dev = rows // NEW
    states = a_log.shape[0]
    rank = dt_proj_weight.shape[0]
    taps = conv_weight.shape[0]
    slots = cache_ssm.shape[0]
    out_cols = x_proj_weight.shape[1]
    requests = holder.shape[0]

    conv_rows = jnp.pad(cache_conv, ((0, 0), (0, 1), (0, 0))).reshape(slots * taps, channels)
    rows_all = jnp.concatenate([cache_ssm.reshape(slots * states, channels), conv_rows])
    block = rows_all.shape[0]
    relative = n_replica == 4
    if relative:
        far = swap(rows_all, "replica", n_replica, 3)
        near = swap(rows_all, "replica", n_replica, 1)
        conv_two = swap(conv_rows, "replica", n_replica, 2)
        conv_pieces = [rows_all, near, far, conv_two]
        firsts = (0, block, 2 * block, 4 * block - slots * taps)
        ssm_pieces = [rows_all, near, far, swap(far, "replica", n_replica, 1)]
    else:
        ssm_pieces = [lax.all_gather(rows_all, "replica", axis=0, tiled=True)]
        conv_pieces, firsts = ssm_pieces, (0,)

    vmem, dma = pltpu.VMEM, pltpu.SemaphoreType.DMA
    ints = [pltpu.SMEM((requests,), jnp.int32)] * 3
    n_chunks = channels // min(512, channels)
    dims = (per_dev, n_replica, slots, relative)

    head = per_dev * taps
    weights = x_proj_weight.T
    mixed, head_sums, part = call(
        project_kernel, per_dev, "conv_project", 60,
        [(x_new, True), (weights, True), (conv_weight, True), (conv_bias[None, :], True)],
        [((rows, channels), BF16), ((head, channels), F32), ((out_cols, rows), BF16)],
        [
            vmem((rows, channels), BF16),
            vmem((out_cols, channels), BF16),
            vmem((taps, channels), BF16),
            vmem((1, channels), F32),
            vmem((rows + (taps - 1) * per_dev, channels), F32),
            vmem((rows, channels), BF16),
            vmem((head, channels), F32),
            vmem((out_cols, rows), F32),
            vmem((out_cols, rows), BF16),
            dma((2 + 2 * n_chunks,)),
            dma((n_chunks + 2,)),
        ],
    )
    mixed_head, part = call(
        history_kernel, (dims, block, firsts), "history", 60,
        [(holder, True), (slot_id, True), (prefix_len, True), (head_sums, False), (part, False), (weights, True),
         (conv_weight, True)]
        + [(piece, False) for piece in conv_pieces],
        [((head, channels), BF16), ((out_cols, rows), BF16)],
        ints + [
            vmem((head, channels), F32),
            vmem((out_cols, rows), BF16),
            vmem((out_cols, channels), BF16),
            vmem((taps, channels), BF16),
            vmem((head, channels), BF16),
            dma((7 + len(conv_pieces),)),
            dma((2,)),
        ] + [vmem(piece.shape, BF16) for piece in conv_pieces],
    )
    parts = [part]
    mask = n_tensor // 2
    while mask:
        parts = parts + [swap(value, "tensor", n_tensor, mask) for value in reversed(parts)]
        mask //= 2

    blocks = (len(ssm_pieces),) + ssm_pieces[0].shape
    out, state = call(
        scan_kernel, (dims, block), "dt_scan_gate", 60,
        [(holder, True), (slot_id, True), (prefix_len, True), (mixed, False), (mixed_head, False), (z_new, True), (dt_proj_weight, True),
         (dt_bias[None, :], True), (a_log, True), (d_skip[None, :], True)]
        + [(piece, False) for piece in parts + ssm_pieces],
        [((rows, channels), BF16), ((per_dev * states, channels), BF16)],
        ints + [
            vmem((rows, channels), BF16),
            vmem((rows, channels), BF16),
            vmem((rank, channels), BF16),
            vmem((1, channels), F32),
            vmem((states, channels), F32),
            vmem((1, channels), F32),
            vmem((n_tensor, out_cols, rows), BF16),
            vmem(blocks, BF16),
            vmem((states, rows, LANES), F32),
            vmem((states, rows, LANES), F32),
            vmem((rows, channels), F32),
            vmem((rows, channels), F32),
            vmem((rows, channels), F32),
            vmem((states, channels), F32),
            vmem((per_dev * states, channels), F32),
            vmem((per_dev * states, channels), F32),
            vmem((rows, channels), F32),
            vmem((rows, channels), BF16),
            vmem((per_dev * states, channels), BF16),
            dma((10 + n_tensor + len(ssm_pieces),)),
            dma((2, n_chunks)),
        ],
    )
    return out, state.reshape(per_dev, states, channels)


def solution(mesh):
    placed = (
        P(("groups", "replica"), "tensor"),
        P(("groups", "replica"), "tensor"),
        P(None, "tensor"),
        P("tensor"),
        P("tensor", None),
        P(None, "tensor"),
        P("tensor"),
        P(None, "tensor"),
        P("tensor"),
        P(("groups", "replica"), None, "tensor"),
        P(("groups", "replica"), None, "tensor"),
        P("groups"),
        P("groups"),
        P("groups"),
    )
    return jax.shard_map(
        functools.partial(shards, mesh),
        mesh=mesh,
        in_specs=placed,
        out_specs=(P(("groups", "replica"), "tensor"), P(("groups", "replica"), None, "tensor")),
        check_vma=False,
    )
```

```python
import functools

import jax
import jax.numpy as jnp
from jax import lax
from jax.experimental import pallas as pl
from jax.experimental.pallas import tpu as pltpu
from jax.sharding import PartitionSpec as P

NEW = 32
LANES = 128
MIB = 1024 * 1024
UNROLL = 8
LOG2E = 1.4426950408889634
F32, BF16 = jnp.float32, jnp.bfloat16
NT = (((1,), (1,)), ((), ()))
TN = (((0,), (0,)), ((), ()))


def silu(v):
    half = 0.5 * v
    return half + half * jnp.tanh(half)


def softplus(v):
    u = jnp.exp(-jnp.abs(v))
    small = u * (1.0 - u * (0.5 - u * (1.0 / 3.0)))
    return jnp.maximum(v, 0.0) + jnp.where(u < 0.004, small, jnp.log(1.0 + u))


def split_index(value, inner):
    assert inner & (inner - 1) == 0
    return value >> (inner.bit_length() - 1), value & (inner - 1)


def pick_rows(values, row_low, count):
    out = jnp.zeros(row_low.shape, jnp.int32)
    for r in range(count):
        out = jnp.where(row_low == r, values[r], out)
    return out


def request_places(dims, ints, me):
    per_dev, n_replica, _, relative = dims
    places, slot_ids, lengths = [], [], []
    for r in range(per_dev):
        request = me * per_dev + r
        place = ints[0][request]
        if relative:
            place = place ^ me
            place = place ^ (place >> 1)
        places.append(place)
        slot_ids.append(ints[1][request])
        lengths.append(ints[2][request])
    return places, slot_ids, lengths


def fetch_rows(target, live, pieces):
    total = None
    for first, value in pieces:
        col = lax.broadcasted_iota(jnp.int32, (target.shape[0], value.shape[0]), 1) + first
        select = jnp.where((col == target) & live, 1.0, 0.0).astype(BF16)
        part = jnp.dot(select, value, preferred_element_type=F32)
        total = part if total is None else total + part
    return total


def project_kernel(dims, refs_in, refs_out, scratch):
    per_dev = dims
    x_hbm, wt_hbm, cw_hbm, cb_hbm = refs_in
    mixed_hbm, head_hbm, part_hbm = refs_out
    x_v, wt_v, cw_v, cb_v, joined, mixed_v, head_v, part_f, part_v, sems, out_sems = scratch
    rows, channels = x_v.shape
    taps = cw_v.shape[0]
    lines = (taps - 1) * per_dev
    pairs = [(cw_hbm, cw_v), (cb_hbm, cb_v)]
    width = min(512, channels)
    chunks = [slice(c * width, (c + 1) * width) for c in range(channels // width)]
    for chunk in chunks:
        pairs += [(x_hbm.at[:, chunk], x_v.at[:, chunk]), (wt_hbm.at[:, chunk], wt_v.at[:, chunk])]
    copies = [pltpu.make_async_copy(src, dst, sems.at[i]) for i, (src, dst) in enumerate(pairs)]
    for copy in copies:
        copy.start()

    joined[:, :lines, :] = jnp.zeros((channels // LANES, lines, LANES), F32)
    copies[0].wait()
    copies[1].wait()
    outs = []
    for c, chunk in enumerate(chunks):
        copies[2 + 2 * c].wait()
        sums = []
        for tile in range(c * width // LANES, (c + 1) * width // LANES):
            lanes = slice(tile * LANES, (tile + 1) * LANES)
            for r in range(per_dev):
                tokens = x_v[r * NEW : (r + 1) * NEW, lanes].astype(F32)
                joined[tile, pl.ds(lines + r, NEW, stride=per_dev), :] = tokens
            summed = jnp.broadcast_to(cb_v[:, lanes], (rows, LANES))
            for k in range(taps):
                weight = cw_v[k : k + 1, lanes].astype(F32)
                summed = summed + joined[tile, k * per_dev : k * per_dev + rows, :] * weight
            sums.append(summed)
        summed = jnp.concatenate(sums, axis=1)
        head_v[:, chunk] = summed[: head_v.shape[0]]
        mixed = silu(summed).astype(BF16)
        mixed_v[:, chunk] = mixed
        copies[3 + 2 * c].wait()
        part = lax.dot_general(wt_v[:, chunk], mixed, NT, preferred_element_type=F32)
        if c == 0:
            part_f[...] = part
        else:
            part_f[...] += part
        outs.append(pltpu.make_async_copy(mixed_v.at[:, chunk], mixed_hbm.at[:, chunk], out_sems.at[c]))
        outs[-1].start()
    part_v[...] = part_f[...].astype(BF16)
    for src, dst in ((part_v, part_hbm), (head_v, head_hbm)):
        outs.append(pltpu.make_async_copy(src, dst, out_sems.at[len(outs)]))
        outs[-1].start()
    for copy in outs:
        copy.wait()


def history_kernel(dims, refs_in, refs_out, scratch):
    dims, block, firsts = dims
    per_dev, n_replica, slots, _ = dims
    holder, slot_id, prefix_len, head_hbm, part_hbm, wt_hbm, cw_hbm = refs_in[:7]
    pieces = refs_in[7:]
    mixed_hbm, fixed_hbm = refs_out
    h_s, s_s, l_s, head_v, part_v, wt_v, cw_v, mixed_v, sems, out_sems = scratch[:10]
    held = scratch[10:]
    taps = cw_v.shape[0]
    pairs = [(holder, h_s), (slot_id, s_s), (prefix_len, l_s), (cw_hbm, cw_v), (head_hbm, head_v)]
    pairs += list(zip(pieces, held)) + [(wt_hbm, wt_v), (part_hbm, part_v)]
    copies = [pltpu.make_async_copy(src, dst, sems.at[i]) for i, (src, dst) in enumerate(pairs)]
    for copy in copies:
        copy.start()
    for copy in copies[:-2]:
        copy.wait()

    me = lax.axis_index("replica")
    places, slot_ids, lengths = request_places(dims, (h_s, s_s, l_s), me)
    tap, request = split_index(lax.broadcasted_iota(jnp.int32, (per_dev * taps, 1), 0), per_dev)
    starts = [places[r] * block + (block - slots * taps) + slot_ids[r] * taps for r in range(per_dev)]
    target = pick_rows(starts, request, per_dev) + tap
    live = (tap < taps - 1) & (taps - 1 - tap <= pick_rows(lengths, request, per_dev))
    history = fetch_rows(target, live, [(first, ref[...]) for first, ref in zip(firsts, held)])
    for t in range(taps - 1):
        now = slice(t * per_dev, (t + 1) * per_dev)
        summed = head_v[now]
        for k in range(taps - 1 - t):
            weight = cw_v[k : k + 1].astype(F32)
            summed = summed + history[(t + k) * per_dev : (t + k + 1) * per_dev] * weight
        head_v[now] = summed
    mixed = silu(head_v[...]).astype(BF16)
    mixed_v[...] = mixed
    mixed_out = pltpu.make_async_copy(mixed_v, mixed_hbm, out_sems.at[0])
    mixed_out.start()
    copies[-2].wait()
    part = lax.dot_general(wt_v[...], mixed, NT, preferred_element_type=F32).astype(BF16)
    copies[-1].wait()
    part_v[:, : per_dev * taps] = part
    part_out = pltpu.make_async_copy(part_v, fixed_hbm, out_sems.at[1])
    part_out.start()
    mixed_out.wait()
    part_out.wait()


def scan_kernel(dims, refs_in, refs_out, scratch):
    per_dev = dims[0]
    holder, slot_id, prefix_len, mixed_hbm, head_hbm, z_hbm, dtw_hbm, dtb_hbm, al_hbm, skip_hbm = refs_in[:10]
    out_hbm, state_hbm = refs_out
    (h_s, s_s, l_s, mixed_v, z_v, dtw_v, dtb_v, al_v, skip_v, parts_v, cache_v, b_tab, c_tab, dt_v, drive_v,
     a_v, start_tm, final_tm, y_v, out_v, state_v, sems, out_sems) = scratch
    n_parts = parts_v.shape[0]
    parts, pieces = refs_in[10 : 10 + n_parts], refs_in[10 + n_parts :]
    head = head_hbm.shape[0]
    rows, channels = z_v.shape
    states = al_v.shape[0]
    rank = dtw_v.shape[0]
    pairs = [(part, parts_v.at[p]) for p, part in enumerate(parts)]
    pairs += [(dtw_hbm, dtw_v), (dtb_hbm, dtb_v), (head_hbm, mixed_v.at[:head]), (mixed_hbm.at[head:], mixed_v.at[head:]),
              (skip_hbm, skip_v), (al_hbm, al_v), (holder, h_s), (slot_id, s_s), (prefix_len, l_s)]
    if len(pieces) == 1:
        pairs.append((pieces[0], cache_v))
    else:
        pairs += [(piece, cache_v.at[p]) for p, piece in enumerate(pieces)]
    pairs.append((z_hbm, z_v))
    copies = [pltpu.make_async_copy(src, dst, sems.at[i]) for i, (src, dst) in enumerate(pairs)]
    for copy in copies:
        copy.start()

    for copy in copies[:n_parts]:
        copy.wait()
    projected = parts_v[0].astype(F32)
    for p in range(1, n_parts):
        projected = projected + parts_v[p].astype(F32)
    dt_low = projected[:rank].astype(BF16)
    late = projected[rank:].T
    for n in range(states):
        b_tab[n] = jnp.broadcast_to(late[:, n : n + 1], (rows, LANES))
        c_tab[n] = jnp.broadcast_to(late[:, states + n : states + n + 1], (rows, LANES))
    for copy in copies[n_parts:-1]:
        copy.wait()
    n_tiles = channels // LANES
    dt_all = softplus(lax.dot_general(dt_low, dtw_v[...], TN, preferred_element_type=F32) + dtb_v[...])
    for tile in range(n_tiles):
        lanes = slice(tile * LANES, (tile + 1) * LANES)
        dt = dt_all[:, lanes]
        mixed = mixed_v[:, lanes].astype(F32)
        dt_v[tile] = dt
        drive_v[tile] = dt * mixed
        y_v[tile, :rows, :] = skip_v[:, lanes] * mixed
    a_v[...] = jnp.exp(al_v[...]) * (-LOG2E)

    me = lax.axis_index("replica")
    places, slot_ids, lengths = request_places(dims, (h_s, s_s, l_s), me)
    for r in range(per_dev):
        spot = pl.ds(pl.multiple_of(slot_ids[r] * states, states), states)
        for tile in range(n_tiles):
            value = cache_v[places[r], spot, tile * LANES : (tile + 1) * LANES].astype(F32)
            value = jnp.where(lengths[r] > 0, value, jnp.zeros_like(value))
            start_tm[tile, pl.ds(r, states, stride=per_dev), :] = value
    copies[-1].wait()

    tiles = 2
    half = states // 2
    width = 2 * tiles * LANES
    n_chunks = channels // width

    def out_copies(c):
        lanes = pl.ds(pl.multiple_of(c * width, width), width)
        return [
            pltpu.make_async_copy(src.at[:, lanes], dst.at[:, lanes], out_sems.at[i, c])
            for i, (src, dst) in enumerate(((out_v, out_hbm), (state_v, state_hbm)))
        ]

    def scan_group(g, carry):
        group = [g * tiles + j for j in range(tiles)]
        lanes = [pl.ds(pl.multiple_of(tile * LANES, LANES), LANES) for tile in group]
        for first in range(0, states, half):
            ids = range(first, first + half)
            rates = [[jnp.broadcast_to(a_v[n : n + 1, lane], (per_dev, LANES)) for n in ids] for lane in lanes]

            def advance(step, state):
                state = list(state)
                for u in range(UNROLL):
                    now = pl.ds(pl.multiple_of((step * UNROLL + u) * per_dev, per_dev), per_dev)
                    dt = [dt_v[tile, now, :] for tile in group]
                    drive = [drive_v[tile, now, :] for tile in group]
                    sums = [None] * tiles
                    for k, n in enumerate(ids):
                        b, c = b_tab[n, now, :], c_tab[n, now, :]
                        for j in range(tiles):
                            i = j * half + k
                            state[i] = jnp.exp2(dt[j] * rates[j][k]) * state[i] + drive[j] * b
                            term = state[i] * c
                            sums[j] = term if sums[j] is None else sums[j] + term
                    for j, tile in enumerate(group):
                        y_v[tile, now, :] += sums[j]
                return tuple(state)

            state = tuple(start_tm[tile, n * per_dev : (n + 1) * per_dev, :] for tile in group for n in ids)
            state = lax.fori_loop(0, NEW // UNROLL, advance, state)
            for j, tile in enumerate(group):
                for k, n in enumerate(ids):
                    final_tm[tile, n * per_dev : (n + 1) * per_dev, :] = state[j * half + k]
        return carry

    def one_chunk(c, carry):
        lax.fori_loop(c * 2, c * 2 + 2, scan_group, 0)
        for j in range(width // LANES):
            tile = c * (width // LANES) + j
            lanes = pl.ds(pl.multiple_of(tile * LANES, LANES), LANES)
            for r in range(per_dev):
                here = slice(r * NEW, (r + 1) * NEW)
                value = y_v[tile, pl.ds(r, NEW, stride=per_dev), :] * silu(z_v[here, lanes].astype(F32))
                out_v[here, lanes] = value.astype(BF16)
                final = final_tm[tile, pl.ds(r, states, stride=per_dev), :]
                state_v[r * states : (r + 1) * states, lanes] = final.astype(BF16)
        for copy in out_copies(c):
            copy.start()
        return carry

    lax.fori_loop(0, n_chunks, one_chunk, 0)

    def last_wait(c, carry):
        for copy in out_copies(c):
            copy.wait()
        return carry

    lax.fori_loop(0, n_chunks, last_wait, 0)


def split_refs(kernel, dims, n_in, n_out):
    def body(*refs):
        kernel(dims, refs[:n_in], refs[n_in : n_in + n_out], refs[n_in + n_out :])

    return body


def call(kernel, dims, name, limit, ins, outs, scratch):
    hbm = pl.BlockSpec(memory_space=pltpu.HBM)
    anywhere = pl.BlockSpec(memory_space=pl.ANY)
    return pl.pallas_call(
        split_refs(kernel, dims, len(ins), len(outs)),
        in_specs=[hbm if fixed else anywhere for _, fixed in ins],
        out_specs=[anywhere] * len(outs),
        out_shape=[jax.ShapeDtypeStruct(*out) for out in outs],
        scratch_shapes=scratch,
        compiler_params=pltpu.CompilerParams(vmem_limit_bytes=limit * MIB),
        name=name,
    )(*[value for value, _ in ins])


def swap(value, axis, size, mask):
    return lax.ppermute(value, axis, [(i, i ^ mask) for i in range(size)])


def shards(mesh, x_new, z_new, conv_weight, conv_bias, x_proj_weight, dt_proj_weight, dt_bias, a_log, d_skip,
           cache_ssm, cache_conv, holder, slot_id, prefix_len):
    n_replica, n_tensor = mesh.shape["replica"], mesh.shape["tensor"]
    rows, channels = x_new.shape
    per_dev = rows // NEW
    states = a_log.shape[0]
    rank = dt_proj_weight.shape[0]
    taps = conv_weight.shape[0]
    slots = cache_ssm.shape[0]
    out_cols = x_proj_weight.shape[1]
    requests = holder.shape[0]

    conv_rows = jnp.pad(cache_conv, ((0, 0), (0, 1), (0, 0))).reshape(slots * taps, channels)
    rows_all = jnp.concatenate([cache_ssm.reshape(slots * states, channels), conv_rows])
    block = rows_all.shape[0]
    relative = n_replica == 4
    if relative:
        far = swap(rows_all, "replica", n_replica, 3)
        near = swap(rows_all, "replica", n_replica, 1)
        conv_two = swap(conv_rows, "replica", n_replica, 2)
        conv_pieces = [rows_all, near, far, conv_two]
        firsts = (0, block, 2 * block, 4 * block - slots * taps)
        ssm_pieces = [rows_all, near, far, swap(far, "replica", n_replica, 1)]
    else:
        ssm_pieces = [lax.all_gather(rows_all, "replica")]
        conv_pieces, firsts = [ssm_pieces[0].reshape(-1, channels)], (0,)

    vmem, dma = pltpu.VMEM, pltpu.SemaphoreType.DMA
    ints = [pltpu.SMEM((requests,), jnp.int32)] * 3
    n_chunks = channels // min(512, channels)
    dims = (per_dev, n_replica, slots, relative)

    head = per_dev * taps
    weights = x_proj_weight.T
    mixed, head_sums, part = call(
        project_kernel, per_dev, "conv_project", 60,
        [(x_new, True), (weights, True), (conv_weight, True), (conv_bias[None, :], True)],
        [((rows, channels), BF16), ((head, channels), F32), ((out_cols, rows), BF16)],
        [
            vmem((rows, channels), BF16),
            vmem((out_cols, channels), BF16),
            vmem((taps, channels), BF16),
            vmem((1, channels), F32),
            vmem((channels // LANES, rows + taps * per_dev, LANES), F32),
            vmem((rows, channels), BF16),
            vmem((head, channels), F32),
            vmem((out_cols, rows), F32),
            vmem((out_cols, rows), BF16),
            dma((2 + 2 * n_chunks,)),
            dma((n_chunks + 2,)),
        ],
    )
    mixed_head, part = call(
        history_kernel, (dims, block, firsts), "history", 60,
        [(holder, True), (slot_id, True), (prefix_len, True), (head_sums, False), (part, False), (weights, True),
         (conv_weight, True)]
        + [(piece, False) for piece in conv_pieces],
        [((head, channels), BF16), ((out_cols, rows), BF16)],
        ints + [
            vmem((head, channels), F32),
            vmem((out_cols, rows), BF16),
            vmem((out_cols, channels), BF16),
            vmem((taps, channels), BF16),
            vmem((head, channels), BF16),
            dma((7 + len(conv_pieces),)),
            dma((2,)),
        ] + [vmem(piece.shape, BF16) for piece in conv_pieces],
    )
    parts = [part]
    mask = n_tensor // 2
    while mask:
        parts = parts + [swap(value, "tensor", n_tensor, mask) for value in reversed(parts)]
        mask //= 2

    blocks = (n_replica, block, channels)
    n_tiles = channels // LANES
    out, state = call(
        scan_kernel, dims, "dt_scan_gate", 60,
        [(holder, True), (slot_id, True), (prefix_len, True), (mixed, False), (mixed_head, False), (z_new, True), (dt_proj_weight, True),
         (dt_bias[None, :], True), (a_log, True), (d_skip[None, :], True)]
        + [(piece, False) for piece in parts + ssm_pieces],
        [((rows, channels), BF16), ((per_dev * states, channels), BF16)],
        ints + [
            vmem((rows, channels), BF16),
            vmem((rows, channels), BF16),
            vmem((rank, channels), BF16),
            vmem((1, channels), F32),
            vmem((states, channels), F32),
            vmem((1, channels), F32),
            vmem((n_tensor, out_cols, rows), BF16),
            vmem(blocks, BF16),
            vmem((states, rows, LANES), F32),
            vmem((states, rows, LANES), F32),
            vmem((n_tiles, rows, LANES), F32),
            vmem((n_tiles, rows, LANES), F32),
            vmem((states, channels), F32),
            vmem((n_tiles, per_dev * (states + 1), LANES), F32),
            vmem((n_tiles, per_dev * (states + 1), LANES), F32),
            vmem((n_tiles, rows + per_dev, LANES), F32),
            vmem((rows, channels), BF16),
            vmem((per_dev * states, channels), BF16),
            dma((10 + n_tensor + len(ssm_pieces),)),
            dma((2, n_chunks)),
        ],
    )
    return out, state.reshape(per_dev, states, channels)


def solution(mesh):
    placed = (
        P(("groups", "replica"), "tensor"),
        P(("groups", "replica"), "tensor"),
        P(None, "tensor"),
        P("tensor"),
        P("tensor", None),
        P(None, "tensor"),
        P("tensor"),
        P(None, "tensor"),
        P("tensor"),
        P(("groups", "replica"), None, "tensor"),
        P(("groups", "replica"), None, "tensor"),
        P("groups"),
        P("groups"),
        P("groups"),
    )
    return jax.shard_map(
        functools.partial(shards, mesh),
        mesh=mesh,
        in_specs=placed,
        out_specs=(P(("groups", "replica"), "tensor"), P(("groups", "replica"), None, "tensor")),
        check_vma=False,
    )
```

```python
import functools

import jax
import jax.numpy as jnp
from jax import lax
from jax.experimental import pallas as pl
from jax.experimental.pallas import tpu as pltpu
from jax.sharding import PartitionSpec as P

NEW = 32
LANES = 128
MIB = 1024 * 1024
UNROLL = 8
LOG2E = 1.4426950408889634
F32, BF16 = jnp.float32, jnp.bfloat16
NT = (((1,), (1,)), ((), ()))
TN = (((0,), (0,)), ((), ()))


def silu(v):
    half = 0.5 * v
    return half + half * jnp.tanh(half)


def softplus(v):
    u = jnp.exp(-jnp.abs(v))
    small = u * (1.0 - u * (0.5 - u * (1.0 / 3.0)))
    return jnp.maximum(v, 0.0) + jnp.where(u < 0.004, small, jnp.log(1.0 + u))


def split_index(value, inner):
    assert inner & (inner - 1) == 0
    return value >> (inner.bit_length() - 1), value & (inner - 1)


def pick_rows(values, row_low, count):
    out = jnp.zeros(row_low.shape, jnp.int32)
    for r in range(count):
        out = jnp.where(row_low == r, values[r], out)
    return out


def request_places(dims, ints, me):
    per_dev, n_replica, _, relative = dims
    places, slot_ids, lengths = [], [], []
    for r in range(per_dev):
        request = me * per_dev + r
        place = ints[0][request]
        if relative:
            place = place ^ me
            place = place ^ (place >> 1)
        places.append(place)
        slot_ids.append(ints[1][request])
        lengths.append(ints[2][request])
    return places, slot_ids, lengths


def fetch_rows(target, live, pieces):
    total = None
    for first, value in pieces:
        col = lax.broadcasted_iota(jnp.int32, (target.shape[0], value.shape[0]), 1) + first
        select = jnp.where((col == target) & live, 1.0, 0.0).astype(BF16)
        part = jnp.dot(select, value, preferred_element_type=F32)
        total = part if total is None else total + part
    return total


def project_kernel(dims, refs_in, refs_out, scratch):
    per_dev = dims
    x_hbm, wt_hbm, cw_hbm, cb_hbm = refs_in
    mixed_hbm, head_hbm, part_hbm = refs_out
    x_v, wt_v, cw_v, cb_v, joined, mixed_v, head_v, part_f, part_v, sems, out_sems = scratch
    rows, channels = x_v.shape
    taps = cw_v.shape[0]
    lines = (taps - 1) * per_dev
    pairs = [(cw_hbm, cw_v), (cb_hbm, cb_v)]
    width = min(512, channels)
    chunks = [slice(c * width, (c + 1) * width) for c in range(channels // width)]
    for chunk in chunks:
        pairs += [(x_hbm.at[:, chunk], x_v.at[:, chunk]), (wt_hbm.at[:, chunk], wt_v.at[:, chunk])]
    copies = [pltpu.make_async_copy(src, dst, sems.at[i]) for i, (src, dst) in enumerate(pairs)]
    for copy in copies:
        copy.start()

    joined[:, :lines, :] = jnp.zeros((channels // LANES, lines, LANES), F32)
    copies[0].wait()
    copies[1].wait()
    outs = []
    for c, chunk in enumerate(chunks):
        copies[2 + 2 * c].wait()
        for tile in range(c * width // LANES, (c + 1) * width // LANES):
            lanes = slice(tile * LANES, (tile + 1) * LANES)
            for r in range(per_dev):
                tokens = x_v[r * NEW : (r + 1) * NEW, lanes].astype(F32)
                joined[tile, pl.ds(lines + r, NEW, stride=per_dev), :] = tokens
            weight = [cw_v[k : k + 1, lanes].astype(F32) for k in range(taps)]
            bias = cb_v[:, lanes]
            for first in range(0, rows, LANES):
                summed = bias + joined[tile, first : first + LANES, :] * weight[0]
                for k in range(1, taps):
                    begin = first + k * per_dev
                    summed = summed + joined[tile, begin : begin + LANES, :] * weight[k]
                if first == 0:
                    head_v[:, lanes] = summed[: head_v.shape[0]]
                mixed_v[first : first + LANES, lanes] = silu(summed).astype(BF16)
        copies[3 + 2 * c].wait()
        part = lax.dot_general(wt_v[:, chunk], mixed_v[:, chunk], NT, preferred_element_type=F32)
        if c == 0:
            part_f[...] = part
        else:
            part_f[...] += part
        outs.append(pltpu.make_async_copy(mixed_v.at[:, chunk], mixed_hbm.at[:, chunk], out_sems.at[c]))
        outs[-1].start()
    part_v[...] = part_f[...].astype(BF16)
    for src, dst in ((part_v, part_hbm), (head_v, head_hbm)):
        outs.append(pltpu.make_async_copy(src, dst, out_sems.at[len(outs)]))
        outs[-1].start()
    for copy in outs:
        copy.wait()


def history_kernel(dims, refs_in, refs_out, scratch):
    dims, block, firsts = dims
    per_dev, n_replica, slots, _ = dims
    holder, slot_id, prefix_len, head_hbm, part_hbm, wt_hbm, cw_hbm = refs_in[:7]
    pieces = refs_in[7:]
    mixed_hbm, fixed_hbm = refs_out
    h_s, s_s, l_s, head_v, part_v, wt_v, cw_v, mixed_v, sems, out_sems = scratch[:10]
    held = scratch[10:]
    taps = cw_v.shape[0]
    pairs = [(holder, h_s), (slot_id, s_s), (prefix_len, l_s), (cw_hbm, cw_v), (head_hbm, head_v)]
    pairs += list(zip(pieces, held)) + [(wt_hbm, wt_v), (part_hbm, part_v)]
    copies = [pltpu.make_async_copy(src, dst, sems.at[i]) for i, (src, dst) in enumerate(pairs)]
    for copy in copies:
        copy.start()
    for copy in copies[:-2]:
        copy.wait()

    me = lax.axis_index("replica")
    places, slot_ids, lengths = request_places(dims, (h_s, s_s, l_s), me)
    tap, request = split_index(lax.broadcasted_iota(jnp.int32, (per_dev * taps, 1), 0), per_dev)
    starts = [places[r] * block + (block - slots * taps) + slot_ids[r] * taps for r in range(per_dev)]
    target = pick_rows(starts, request, per_dev) + tap
    live = (tap < taps - 1) & (taps - 1 - tap <= pick_rows(lengths, request, per_dev))
    history = fetch_rows(target, live, [(first, ref[...]) for first, ref in zip(firsts, held)])
    for t in range(taps - 1):
        now = slice(t * per_dev, (t + 1) * per_dev)
        summed = head_v[now]
        for k in range(taps - 1 - t):
            weight = cw_v[k : k + 1].astype(F32)
            summed = summed + history[(t + k) * per_dev : (t + k + 1) * per_dev] * weight
        head_v[now] = summed
    mixed = silu(head_v[...]).astype(BF16)
    mixed_v[...] = mixed
    mixed_out = pltpu.make_async_copy(mixed_v, mixed_hbm, out_sems.at[0])
    mixed_out.start()
    copies[-2].wait()
    part = lax.dot_general(wt_v[...], mixed, NT, preferred_element_type=F32).astype(BF16)
    copies[-1].wait()
    part_v[:, : per_dev * taps] = part
    part_out = pltpu.make_async_copy(part_v, fixed_hbm, out_sems.at[1])
    part_out.start()
    mixed_out.wait()
    part_out.wait()


def scan_kernel(dims, refs_in, refs_out, scratch):
    per_dev = dims[0]
    holder, slot_id, prefix_len, mixed_hbm, head_hbm, z_hbm, dtw_hbm, dtb_hbm, al_hbm, skip_hbm = refs_in[:10]
    out_hbm, state_hbm = refs_out
    (h_s, s_s, l_s, mixed_v, z_v, dtw_v, dtb_v, al_v, skip_v, parts_v, cache_v, b_tab, c_tab, dt_v, drive_v,
     a_v, start_tm, final_tm, y_v, out_v, state_v, sems, out_sems) = scratch
    n_parts = parts_v.shape[0]
    parts, pieces = refs_in[10 : 10 + n_parts], refs_in[10 + n_parts :]
    head = head_hbm.shape[0]
    rows, channels = z_v.shape
    states = al_v.shape[0]
    rank = dtw_v.shape[0]
    pairs = [(part, parts_v.at[p]) for p, part in enumerate(parts)]
    pairs += [(dtw_hbm, dtw_v), (dtb_hbm, dtb_v), (head_hbm, mixed_v.at[:head]), (mixed_hbm.at[head:], mixed_v.at[head:]),
              (skip_hbm, skip_v), (al_hbm, al_v), (holder, h_s), (slot_id, s_s), (prefix_len, l_s)]
    if len(pieces) == 1:
        pairs.append((pieces[0], cache_v))
    else:
        pairs += [(piece, cache_v.at[p]) for p, piece in enumerate(pieces)]
    pairs.append((z_hbm, z_v))
    copies = [pltpu.make_async_copy(src, dst, sems.at[i]) for i, (src, dst) in enumerate(pairs)]
    for copy in copies:
        copy.start()

    for copy in copies[: n_parts + 5]:
        copy.wait()
    projected = parts_v[0].astype(F32)
    for p in range(1, n_parts):
        projected = projected + parts_v[p].astype(F32)
    dt_low = projected[:rank].astype(BF16)
    late = projected[rank:].T
    n_tiles = channels // LANES
    wide = min(4, n_tiles)
    per_chunk = 2 * states * wide // n_tiles
    for c in range(n_tiles // wide):
        for n in range(c * per_chunk, (c + 1) * per_chunk):
            table = b_tab if n < states else c_tab
            table[n % states] = jnp.broadcast_to(late[:, n : n + 1], (rows, LANES))
        weights = dtw_v[:, c * wide * LANES : (c + 1) * wide * LANES]
        raw = lax.dot_general(dt_low, weights, TN, preferred_element_type=F32)
        for j in range(wide):
            tile = c * wide + j
            lanes = slice(tile * LANES, (tile + 1) * LANES)
            for first in range(0, rows, LANES):
                here = slice(first, first + LANES)
                dt = softplus(raw[here, j * LANES : (j + 1) * LANES] + dtb_v[:, lanes])
                mixed = mixed_v[here, lanes].astype(F32)
                dt_v[tile, here, :] = dt
                drive_v[tile, here, :] = dt * mixed
                y_v[tile, here, :] = skip_v[:, lanes] * mixed
    for copy in copies[n_parts + 5 : -1]:
        copy.wait()
    a_v[...] = jnp.exp(al_v[...]) * (-LOG2E)

    me = lax.axis_index("replica")
    places, slot_ids, lengths = request_places(dims, (h_s, s_s, l_s), me)
    for r in range(per_dev):
        spot = pl.ds(pl.multiple_of(slot_ids[r] * states, states), states)
        for tile in range(n_tiles):
            value = cache_v[places[r], spot, tile * LANES : (tile + 1) * LANES].astype(F32)
            value = jnp.where(lengths[r] > 0, value, jnp.zeros_like(value))
            start_tm[tile, pl.ds(r, states, stride=per_dev), :] = value
    copies[-1].wait()

    tiles = 2
    half = states // 2
    width = 2 * tiles * LANES
    n_chunks = channels // width

    def out_copies(c):
        lanes = pl.ds(pl.multiple_of(c * width, width), width)
        return [
            pltpu.make_async_copy(src.at[:, lanes], dst.at[:, lanes], out_sems.at[i, c])
            for i, (src, dst) in enumerate(((out_v, out_hbm), (state_v, state_hbm)))
        ]

    def scan_group(g, carry):
        group = [g * tiles + j for j in range(tiles)]
        lanes = [pl.ds(pl.multiple_of(tile * LANES, LANES), LANES) for tile in group]
        for first in range(0, states, half):
            ids = range(first, first + half)
            rates = [[jnp.broadcast_to(a_v[n : n + 1, lane], (per_dev, LANES)) for n in ids] for lane in lanes]

            def advance(step, state):
                state = list(state)
                for u in range(UNROLL):
                    now = pl.ds(pl.multiple_of((step * UNROLL + u) * per_dev, per_dev), per_dev)
                    dt = [dt_v[tile, now, :] for tile in group]
                    drive = [drive_v[tile, now, :] for tile in group]
                    sums = [None] * tiles
                    for k, n in enumerate(ids):
                        b, c = b_tab[n, now, :], c_tab[n, now, :]
                        for j in range(tiles):
                            i = j * half + k
                            state[i] = jnp.exp2(dt[j] * rates[j][k]) * state[i] + drive[j] * b
                            term = state[i] * c
                            sums[j] = term if sums[j] is None else sums[j] + term
                    for j, tile in enumerate(group):
                        y_v[tile, now, :] += sums[j]
                return tuple(state)

            state = tuple(start_tm[tile, n * per_dev : (n + 1) * per_dev, :] for tile in group for n in ids)
            state = lax.fori_loop(0, NEW // UNROLL, advance, state)
            for j, tile in enumerate(group):
                for k, n in enumerate(ids):
                    final_tm[tile, n * per_dev : (n + 1) * per_dev, :] = state[j * half + k]
        return carry

    def one_chunk(c, carry):
        lax.fori_loop(c * 2, c * 2 + 2, scan_group, 0)
        for j in range(width // LANES):
            tile = c * (width // LANES) + j
            lanes = pl.ds(pl.multiple_of(tile * LANES, LANES), LANES)
            for r in range(per_dev):
                here = slice(r * NEW, (r + 1) * NEW)
                value = y_v[tile, pl.ds(r, NEW, stride=per_dev), :] * silu(z_v[here, lanes].astype(F32))
                out_v[here, lanes] = value.astype(BF16)
                final = final_tm[tile, pl.ds(r, states, stride=per_dev), :]
                state_v[r * states : (r + 1) * states, lanes] = final.astype(BF16)
        for copy in out_copies(c):
            copy.start()
        return carry

    lax.fori_loop(0, n_chunks, one_chunk, 0)

    def last_wait(c, carry):
        for copy in out_copies(c):
            copy.wait()
        return carry

    lax.fori_loop(0, n_chunks, last_wait, 0)


def split_refs(kernel, dims, n_in, n_out):
    def body(*refs):
        kernel(dims, refs[:n_in], refs[n_in : n_in + n_out], refs[n_in + n_out :])

    return body


def call(kernel, dims, name, limit, ins, outs, scratch):
    hbm = pl.BlockSpec(memory_space=pltpu.HBM)
    anywhere = pl.BlockSpec(memory_space=pl.ANY)
    return pl.pallas_call(
        split_refs(kernel, dims, len(ins), len(outs)),
        in_specs=[hbm if fixed else anywhere for _, fixed in ins],
        out_specs=[anywhere] * len(outs),
        out_shape=[jax.ShapeDtypeStruct(*out) for out in outs],
        scratch_shapes=scratch,
        compiler_params=pltpu.CompilerParams(vmem_limit_bytes=limit * MIB),
        name=name,
    )(*[value for value, _ in ins])


def swap(value, axis, size, mask):
    return lax.ppermute(value, axis, [(i, i ^ mask) for i in range(size)])


def shards(mesh, x_new, z_new, conv_weight, conv_bias, x_proj_weight, dt_proj_weight, dt_bias, a_log, d_skip,
           cache_ssm, cache_conv, holder, slot_id, prefix_len):
    n_replica, n_tensor = mesh.shape["replica"], mesh.shape["tensor"]
    rows, channels = x_new.shape
    per_dev = rows // NEW
    states = a_log.shape[0]
    rank = dt_proj_weight.shape[0]
    taps = conv_weight.shape[0]
    slots = cache_ssm.shape[0]
    out_cols = x_proj_weight.shape[1]
    requests = holder.shape[0]

    conv_rows = jnp.pad(cache_conv, ((0, 0), (0, 1), (0, 0))).reshape(slots * taps, channels)
    rows_all = jnp.concatenate([cache_ssm.reshape(slots * states, channels), conv_rows])
    block = rows_all.shape[0]
    relative = n_replica == 4
    if relative:
        far = swap(rows_all, "replica", n_replica, 3)
        near = swap(rows_all, "replica", n_replica, 1)
        conv_two = swap(conv_rows, "replica", n_replica, 2)
        conv_pieces = [rows_all, near, far, conv_two]
        firsts = (0, block, 2 * block, 4 * block - slots * taps)
        ssm_pieces = [rows_all, near, far, swap(far, "replica", n_replica, 1)]
    else:
        ssm_pieces = [lax.all_gather(rows_all, "replica")]
        conv_pieces, firsts = [ssm_pieces[0].reshape(-1, channels)], (0,)

    vmem, dma = pltpu.VMEM, pltpu.SemaphoreType.DMA
    ints = [pltpu.SMEM((requests,), jnp.int32)] * 3
    n_chunks = channels // min(512, channels)
    dims = (per_dev, n_replica, slots, relative)

    head = per_dev * taps
    weights = x_proj_weight.T
    mixed, head_sums, part = call(
        project_kernel, per_dev, "conv_project", 60,
        [(x_new, True), (weights, True), (conv_weight, True), (conv_bias[None, :], True)],
        [((rows, channels), BF16), ((head, channels), F32), ((out_cols, rows), BF16)],
        [
            vmem((rows, channels), BF16),
            vmem((out_cols, channels), BF16),
            vmem((taps, channels), BF16),
            vmem((1, channels), F32),
            vmem((channels // LANES, rows + taps * per_dev, LANES), F32),
            vmem((rows, channels), BF16),
            vmem((head, channels), F32),
            vmem((out_cols, rows), F32),
            vmem((out_cols, rows), BF16),
            dma((2 + 2 * n_chunks,)),
            dma((n_chunks + 2,)),
        ],
    )
    mixed_head, part = call(
        history_kernel, (dims, block, firsts), "history", 60,
        [(holder, True), (slot_id, True), (prefix_len, True), (head_sums, False), (part, False), (weights, True),
         (conv_weight, True)]
        + [(piece, False) for piece in conv_pieces],
        [((head, channels), BF16), ((out_cols, rows), BF16)],
        ints + [
            vmem((head, channels), F32),
            vmem((out_cols, rows), BF16),
            vmem((out_cols, channels), BF16),
            vmem((taps, channels), BF16),
            vmem((head, channels), BF16),
            dma((7 + len(conv_pieces),)),
            dma((2,)),
        ] + [vmem(piece.shape, BF16) for piece in conv_pieces],
    )
    parts = [part]
    mask = n_tensor // 2
    while mask:
        parts = parts + [swap(value, "tensor", n_tensor, mask) for value in reversed(parts)]
        mask //= 2

    blocks = (n_replica, block, channels)
    n_tiles = channels // LANES
    out, state = call(
        scan_kernel, dims, "dt_scan_gate", 60,
        [(holder, True), (slot_id, True), (prefix_len, True), (mixed, False), (mixed_head, False), (z_new, True), (dt_proj_weight, True),
         (dt_bias[None, :], True), (a_log, True), (d_skip[None, :], True)]
        + [(piece, False) for piece in parts + ssm_pieces],
        [((rows, channels), BF16), ((per_dev * states, channels), BF16)],
        ints + [
            vmem((rows, channels), BF16),
            vmem((rows, channels), BF16),
            vmem((rank, channels), BF16),
            vmem((1, channels), F32),
            vmem((states, channels), F32),
            vmem((1, channels), F32),
            vmem((n_tensor, out_cols, rows), BF16),
            vmem(blocks, BF16),
            vmem((states, rows, LANES), F32),
            vmem((states, rows, LANES), F32),
            vmem((n_tiles, rows, LANES), F32),
            vmem((n_tiles, rows, LANES), F32),
            vmem((states, channels), F32),
            vmem((n_tiles, per_dev * (states + 1), LANES), F32),
            vmem((n_tiles, per_dev * (states + 1), LANES), F32),
            vmem((n_tiles, rows + per_dev, LANES), F32),
            vmem((rows, channels), BF16),
            vmem((per_dev * states, channels), BF16),
            dma((10 + n_tensor + len(ssm_pieces),)),
            dma((2, n_chunks)),
        ],
    )
    return out, state.reshape(per_dev, states, channels)


def solution(mesh):
    placed = (
        P(("groups", "replica"), "tensor"),
        P(("groups", "replica"), "tensor"),
        P(None, "tensor"),
        P("tensor"),
        P("tensor", None),
        P(None, "tensor"),
        P("tensor"),
        P(None, "tensor"),
        P("tensor"),
        P(("groups", "replica"), None, "tensor"),
        P(("groups", "replica"), None, "tensor"),
        P("groups"),
        P("groups"),
        P("groups"),
    )
    return jax.shard_map(
        functools.partial(shards, mesh),
        mesh=mesh,
        in_specs=placed,
        out_specs=(P(("groups", "replica"), "tensor"), P(("groups", "replica"), None, "tensor")),
        check_vma=False,
    )
```

```python
import functools

import jax
import jax.numpy as jnp
from jax import lax
from jax.experimental import pallas as pl
from jax.experimental.pallas import tpu as pltpu
from jax.sharding import PartitionSpec as P

NEW = 32
LANES = 128
MIB = 1024 * 1024
UNROLL = 16
LOG2E = 1.4426950408889634
F32, BF16 = jnp.float32, jnp.bfloat16
NT = (((1,), (1,)), ((), ()))
TN = (((0,), (0,)), ((), ()))


def silu(v):
    half = 0.5 * v
    return half + half * jnp.tanh(half)


def softplus(v):
    u = jnp.exp(-jnp.abs(v))
    small = u * (1.0 - u * (0.5 - u * (1.0 / 3.0)))
    return jnp.maximum(v, 0.0) + jnp.where(u < 0.004, small, jnp.log(1.0 + u))


def split_index(value, inner):
    assert inner & (inner - 1) == 0
    return value >> (inner.bit_length() - 1), value & (inner - 1)


def pick_rows(values, row_low, count):
    out = jnp.zeros(row_low.shape, jnp.int32)
    for r in range(count):
        out = jnp.where(row_low == r, values[r], out)
    return out


def request_places(dims, ints, me):
    per_dev, n_replica, _, relative = dims
    places, slot_ids, lengths = [], [], []
    for r in range(per_dev):
        request = me * per_dev + r
        place = ints[0][request]
        if relative:
            place = place ^ me
            place = place ^ (place >> 1)
        places.append(place)
        slot_ids.append(ints[1][request])
        lengths.append(ints[2][request])
    return places, slot_ids, lengths


def fetch_rows(target, live, pieces):
    total = None
    for first, value in pieces:
        col = lax.broadcasted_iota(jnp.int32, (target.shape[0], value.shape[0]), 1) + first
        select = jnp.where((col == target) & live, 1.0, 0.0).astype(BF16)
        part = jnp.dot(select, value, preferred_element_type=F32)
        total = part if total is None else total + part
    return total


def project_kernel(dims, refs_in, refs_out, scratch):
    per_dev = dims
    x_hbm, wt_hbm, cw_hbm, cb_hbm = refs_in
    mixed_hbm, head_hbm, part_hbm = refs_out
    x_v, wt_v, cw_v, cb_v, joined, mixed_v, head_v, part_f, part_v, sems, out_sems = scratch
    rows, channels = x_v.shape
    taps = cw_v.shape[0]
    lines = (taps - 1) * per_dev
    pairs = [(cw_hbm, cw_v), (cb_hbm, cb_v)]
    width = min(512, channels)
    chunks = [slice(c * width, (c + 1) * width) for c in range(channels // width)]
    for chunk in chunks:
        pairs += [(x_hbm.at[:, chunk], x_v.at[:, chunk]), (wt_hbm.at[:, chunk], wt_v.at[:, chunk])]
    copies = [pltpu.make_async_copy(src, dst, sems.at[i]) for i, (src, dst) in enumerate(pairs)]
    for copy in copies:
        copy.start()

    joined[:, :lines, :] = jnp.zeros((channels // LANES, lines, LANES), F32)
    copies[0].wait()
    copies[1].wait()
    outs = []
    for c, chunk in enumerate(chunks):
        copies[2 + 2 * c].wait()
        for tile in range(c * width // LANES, (c + 1) * width // LANES):
            lanes = slice(tile * LANES, (tile + 1) * LANES)
            for r in range(per_dev):
                tokens = x_v[r * NEW : (r + 1) * NEW, lanes].astype(F32)
                joined[tile, pl.ds(lines + r, NEW, stride=per_dev), :] = tokens
            weight = [cw_v[k : k + 1, lanes].astype(F32) for k in range(taps)]
            bias = cb_v[:, lanes]
            for first in range(0, rows, LANES):
                summed = bias + joined[tile, first : first + LANES, :] * weight[0]
                for k in range(1, taps):
                    begin = first + k * per_dev
                    summed = summed + joined[tile, begin : begin + LANES, :] * weight[k]
                if first == 0:
                    head_v[:, lanes] = summed[: head_v.shape[0]]
                mixed_v[first : first + LANES, lanes] = silu(summed).astype(BF16)
        copies[3 + 2 * c].wait()
        part = lax.dot_general(wt_v[:, chunk], mixed_v[:, chunk], NT, preferred_element_type=F32)
        if c == 0:
            part_f[...] = part
        else:
            part_f[...] += part
        outs.append(pltpu.make_async_copy(mixed_v.at[:, chunk], mixed_hbm.at[:, chunk], out_sems.at[c]))
        outs[-1].start()
    part_v[...] = part_f[...].astype(BF16)
    for src, dst in ((part_v, part_hbm), (head_v, head_hbm)):
        outs.append(pltpu.make_async_copy(src, dst, out_sems.at[len(outs)]))
        outs[-1].start()
    for copy in outs:
        copy.wait()


def history_kernel(dims, refs_in, refs_out, scratch):
    dims, block, firsts = dims
    per_dev, n_replica, slots, _ = dims
    holder, slot_id, prefix_len, head_hbm, wt_hbm, cw_hbm = refs_in[:6]
    pieces = refs_in[6:]
    mixed_hbm, part_hbm = refs_out
    h_s, s_s, l_s, head_v, wt_v, cw_v, mixed_v, part_v, sems, out_sems = scratch[:10]
    held = scratch[10:]
    taps = cw_v.shape[0]
    pairs = [(holder, h_s), (slot_id, s_s), (prefix_len, l_s), (cw_hbm, cw_v), (head_hbm, head_v)]
    pairs += list(zip(pieces, held)) + [(wt_hbm, wt_v)]
    copies = [pltpu.make_async_copy(src, dst, sems.at[i]) for i, (src, dst) in enumerate(pairs)]
    for copy in copies:
        copy.start()
    for copy in copies[:-1]:
        copy.wait()

    me = lax.axis_index("replica")
    places, slot_ids, lengths = request_places(dims, (h_s, s_s, l_s), me)
    tap, request = split_index(lax.broadcasted_iota(jnp.int32, (per_dev * taps, 1), 0), per_dev)
    starts = [places[r] * block + (block - slots * taps) + slot_ids[r] * taps for r in range(per_dev)]
    target = pick_rows(starts, request, per_dev) + tap
    live = (tap < taps - 1) & (taps - 1 - tap <= pick_rows(lengths, request, per_dev))
    history = fetch_rows(target, live, [(first, ref[...]) for first, ref in zip(firsts, held)])
    for t in range(taps - 1):
        now = slice(t * per_dev, (t + 1) * per_dev)
        summed = head_v[now]
        for k in range(taps - 1 - t):
            weight = cw_v[k : k + 1].astype(F32)
            summed = summed + history[(t + k) * per_dev : (t + k + 1) * per_dev] * weight
        head_v[now] = summed
    mixed = silu(head_v[...]).astype(BF16)
    mixed_v[...] = mixed
    mixed_out = pltpu.make_async_copy(mixed_v, mixed_hbm, out_sems.at[0])
    mixed_out.start()
    copies[-1].wait()
    part_v[...] = lax.dot_general(wt_v[...], mixed, NT, preferred_element_type=F32).T.astype(BF16)
    part_out = pltpu.make_async_copy(part_v, part_hbm, out_sems.at[1])
    part_out.start()
    mixed_out.wait()
    part_out.wait()


def scan_kernel(dims, refs_in, refs_out, scratch):
    per_dev = dims[0]
    holder, slot_id, prefix_len, mixed_hbm, head_hbm, z_hbm, dtw_hbm, dtb_hbm, al_hbm, skip_hbm = refs_in[:10]
    out_hbm, state_hbm = refs_out
    (h_s, s_s, l_s, mixed_v, z_v, dtw_v, dtb_v, al_v, skip_v, parts_v, fixes_v, proj_v, cache_v, b_tab, c_tab, dt_v, drive_v,
     a_v, start_tm, final_tm, y_v, out_v, state_v, sems, out_sems) = scratch
    n_parts = parts_v.shape[0]
    parts, fixes, pieces = refs_in[10 : 10 + n_parts], refs_in[10 + n_parts : 10 + 2 * n_parts], refs_in[10 + 2 * n_parts :]
    head = head_hbm.shape[0]
    rows, channels = z_v.shape
    states = al_v.shape[0]
    rank = dtw_v.shape[0]
    pairs = [(part, parts_v.at[p]) for p, part in enumerate(parts)]
    pairs += [(fix, fixes_v.at[p]) for p, fix in enumerate(fixes)]
    pairs += [(dtw_hbm, dtw_v), (dtb_hbm, dtb_v), (head_hbm, mixed_v.at[:head]), (mixed_hbm.at[head:], mixed_v.at[head:]),
              (skip_hbm, skip_v), (al_hbm, al_v), (holder, h_s), (slot_id, s_s), (prefix_len, l_s)]
    if len(pieces) == 1:
        pairs.append((pieces[0], cache_v))
    else:
        pairs += [(piece, cache_v.at[p]) for p, piece in enumerate(pieces)]
    pairs.append((z_hbm, z_v))
    copies = [pltpu.make_async_copy(src, dst, sems.at[i]) for i, (src, dst) in enumerate(pairs)]
    for copy in copies:
        copy.start()

    for copy in copies[: 2 * n_parts + 5]:
        copy.wait()
    projected = parts_v[0].astype(F32)
    for p in range(1, n_parts):
        projected = projected + parts_v[p].astype(F32)
    fixed = fixes_v[0].astype(F32)
    for p in range(1, n_parts):
        fixed = fixed + fixes_v[p].astype(F32)
    proj_v[...] = projected
    proj_v[:, :head] = fixed.T
    projected = proj_v[...]
    dt_low = projected[:rank].astype(BF16)
    late = projected[rank:].T
    n_tiles = channels // LANES
    wide = min(4, n_tiles)
    per_chunk = 2 * states * wide // n_tiles
    for c in range(n_tiles // wide):
        for n in range(c * per_chunk, (c + 1) * per_chunk):
            table = b_tab if n < states else c_tab
            table[n % states] = jnp.broadcast_to(late[:, n : n + 1], (rows, LANES))
        weights = dtw_v[:, c * wide * LANES : (c + 1) * wide * LANES]
        raw = lax.dot_general(dt_low, weights, TN, preferred_element_type=F32)
        for j in range(wide):
            tile = c * wide + j
            lanes = slice(tile * LANES, (tile + 1) * LANES)
            for first in range(0, rows, LANES):
                here = slice(first, first + LANES)
                dt = softplus(raw[here, j * LANES : (j + 1) * LANES] + dtb_v[:, lanes])
                mixed = mixed_v[here, lanes].astype(F32)
                dt_v[tile, here, :] = dt
                drive_v[tile, here, :] = dt * mixed
                y_v[tile, here, :] = skip_v[:, lanes] * mixed
    for copy in copies[2 * n_parts + 5 : -1]:
        copy.wait()
    a_v[...] = jnp.exp(al_v[...]) * (-LOG2E)

    me = lax.axis_index("replica")
    places, slot_ids, lengths = request_places(dims, (h_s, s_s, l_s), me)
    for r in range(per_dev):
        spot = pl.ds(pl.multiple_of(slot_ids[r] * states, states), states)
        for tile in range(n_tiles):
            value = cache_v[places[r], spot, tile * LANES : (tile + 1) * LANES].astype(F32)
            value = jnp.where(lengths[r] > 0, value, jnp.zeros_like(value))
            start_tm[tile, pl.ds(r, states, stride=per_dev), :] = value
    copies[-1].wait()

    tiles = 2
    half = states // 2
    width = 2 * tiles * LANES
    n_chunks = channels // width

    def out_copies(c):
        lanes = pl.ds(pl.multiple_of(c * width, width), width)
        return [
            pltpu.make_async_copy(src.at[:, lanes], dst.at[:, lanes], out_sems.at[i, c])
            for i, (src, dst) in enumerate(((out_v, out_hbm), (state_v, state_hbm)))
        ]

    def scan_group(g, carry):
        group = [g * tiles + j for j in range(tiles)]
        lanes = [pl.ds(pl.multiple_of(tile * LANES, LANES), LANES) for tile in group]
        for first in range(0, states, half):
            ids = range(first, first + half)
            rates = [[jnp.broadcast_to(a_v[n : n + 1, lane], (per_dev, LANES)) for n in ids] for lane in lanes]

            def advance(step, state):
                state = list(state)
                for u in range(UNROLL):
                    now = pl.ds(pl.multiple_of((step * UNROLL + u) * per_dev, per_dev), per_dev)
                    dt = [dt_v[tile, now, :] for tile in group]
                    drive = [drive_v[tile, now, :] for tile in group]
                    sums = [None] * tiles
                    for k, n in enumerate(ids):
                        b, c = b_tab[n, now, :], c_tab[n, now, :]
                        for j in range(tiles):
                            i = j * half + k
                            state[i] = jnp.exp2(dt[j] * rates[j][k]) * state[i] + drive[j] * b
                            term = state[i] * c
                            sums[j] = term if sums[j] is None else sums[j] + term
                    for j, tile in enumerate(group):
                        y_v[tile, now, :] += sums[j]
                return tuple(state)

            state = tuple(start_tm[tile, n * per_dev : (n + 1) * per_dev, :] for tile in group for n in ids)
            state = lax.fori_loop(0, NEW // UNROLL, advance, state)
            for j, tile in enumerate(group):
                for k, n in enumerate(ids):
                    final_tm[tile, n * per_dev : (n + 1) * per_dev, :] = state[j * half + k]
        return carry

    def one_chunk(c, carry):
        lax.fori_loop(c * 2, c * 2 + 2, scan_group, 0)
        for j in range(width // LANES):
            tile = c * (width // LANES) + j
            lanes = pl.ds(pl.multiple_of(tile * LANES, LANES), LANES)
            for r in range(per_dev):
                here = slice(r * NEW, (r + 1) * NEW)
                value = y_v[tile, pl.ds(r, NEW, stride=per_dev), :] * silu(z_v[here, lanes].astype(F32))
                out_v[here, lanes] = value.astype(BF16)
                final = final_tm[tile, pl.ds(r, states, stride=per_dev), :]
                state_v[r * states : (r + 1) * states, lanes] = final.astype(BF16)
        for copy in out_copies(c):
            copy.start()
        return carry

    lax.fori_loop(0, n_chunks, one_chunk, 0)

    def last_wait(c, carry):
        for copy in out_copies(c):
            copy.wait()
        return carry

    lax.fori_loop(0, n_chunks, last_wait, 0)


def split_refs(kernel, dims, n_in, n_out):
    def body(*refs):
        kernel(dims, refs[:n_in], refs[n_in : n_in + n_out], refs[n_in + n_out :])

    return body


def call(kernel, dims, name, limit, ins, outs, scratch):
    hbm = pl.BlockSpec(memory_space=pltpu.HBM)
    anywhere = pl.BlockSpec(memory_space=pl.ANY)
    return pl.pallas_call(
        split_refs(kernel, dims, len(ins), len(outs)),
        in_specs=[hbm if fixed else anywhere for _, fixed in ins],
        out_specs=[anywhere] * len(outs),
        out_shape=[jax.ShapeDtypeStruct(*out) for out in outs],
        scratch_shapes=scratch,
        compiler_params=pltpu.CompilerParams(vmem_limit_bytes=limit * MIB),
        name=name,
    )(*[pltpu.with_memory_space_constraint(value, pltpu.HBM) if fixed else value for value, fixed in ins])


def swap(value, axis, size, mask):
    return lax.ppermute(value, axis, [(i, i ^ mask) for i in range(size)])


def shards(mesh, x_new, z_new, conv_weight, conv_bias, x_proj_weight, dt_proj_weight, dt_bias, a_log, d_skip,
           cache_ssm, cache_conv, holder, slot_id, prefix_len):
    n_replica, n_tensor = mesh.shape["replica"], mesh.shape["tensor"]
    rows, channels = x_new.shape
    per_dev = rows // NEW
    states = a_log.shape[0]
    rank = dt_proj_weight.shape[0]
    taps = conv_weight.shape[0]
    slots = cache_ssm.shape[0]
    out_cols = x_proj_weight.shape[1]
    requests = holder.shape[0]

    conv_rows = jnp.pad(cache_conv, ((0, 0), (0, 1), (0, 0))).reshape(slots * taps, channels)
    rows_all = jnp.concatenate([cache_ssm.reshape(slots * states, channels), conv_rows])
    block = rows_all.shape[0]
    relative = n_replica == 4
    if relative:
        far = swap(rows_all, "replica", n_replica, 3)
        near = swap(rows_all, "replica", n_replica, 1)
        conv_two = swap(conv_rows, "replica", n_replica, 2)
        conv_pieces = [rows_all, near, far, conv_two]
        firsts = (0, block, 2 * block, 4 * block - slots * taps)
        ssm_pieces = [rows_all, near, far, swap(far, "replica", n_replica, 1)]
    else:
        ssm_pieces = [lax.all_gather(rows_all, "replica")]
        conv_pieces, firsts = [ssm_pieces[0].reshape(-1, channels)], (0,)

    vmem, dma = pltpu.VMEM, pltpu.SemaphoreType.DMA
    ints = [pltpu.SMEM((requests,), jnp.int32)] * 3
    n_chunks = channels // min(512, channels)
    dims = (per_dev, n_replica, slots, relative)

    head = per_dev * taps
    weights = x_proj_weight.T
    mixed, head_sums, part = call(
        project_kernel, per_dev, "conv_project", 40,
        [(x_new, True), (weights, True), (conv_weight, True), (conv_bias[None, :], True)],
        [((rows, channels), BF16), ((head, channels), F32), ((out_cols, rows), BF16)],
        [
            vmem((rows, channels), BF16),
            vmem((out_cols, channels), BF16),
            vmem((taps, channels), BF16),
            vmem((1, channels), F32),
            vmem((channels // LANES, rows + taps * per_dev, LANES), F32),
            vmem((rows, channels), BF16),
            vmem((head, channels), F32),
            vmem((out_cols, rows), F32),
            vmem((out_cols, rows), BF16),
            dma((2 + 2 * n_chunks,)),
            dma((n_chunks + 2,)),
        ],
    )
    mixed_head, fix = call(
        history_kernel, (dims, block, firsts), "history", 40,
        [(holder, True), (slot_id, True), (prefix_len, True), (head_sums, False), (weights, True),
         (conv_weight, True)]
        + [(piece, False) for piece in conv_pieces],
        [((head, channels), BF16), ((head, out_cols), BF16)],
        ints + [
            vmem((head, channels), F32),
            vmem((out_cols, channels), BF16),
            vmem((taps, channels), BF16),
            vmem((head, channels), BF16),
            vmem((head, out_cols), BF16),
            dma((6 + len(conv_pieces),)),
            dma((2,)),
        ] + [vmem(piece.shape, BF16) for piece in conv_pieces],
    )
    parts = [part]
    mask = n_tensor // 2
    while mask:
        parts = parts + [swap(value, "tensor", n_tensor, mask) for value in reversed(parts)]
        mask //= 2
    fixes = [fix] + [swap(fix, "tensor", n_tensor, k) for k in range(1, n_tensor)]

    blocks = (n_replica, block, channels)
    n_tiles = channels // LANES
    out, state = call(
        scan_kernel, dims, "dt_scan_gate", 40,
        [(holder, True), (slot_id, True), (prefix_len, True), (mixed, False), (mixed_head, False), (z_new, True), (dt_proj_weight, True),
         (dt_bias[None, :], True), (a_log, True), (d_skip[None, :], True)]
        + [(piece, False) for piece in parts + fixes + ssm_pieces],
        [((rows, channels), BF16), ((per_dev * states, channels), BF16)],
        ints + [
            vmem((rows, channels), BF16),
            vmem((rows, channels), BF16),
            vmem((rank, channels), BF16),
            vmem((1, channels), F32),
            vmem((states, channels), F32),
            vmem((1, channels), F32),
            vmem((n_tensor, out_cols, rows), BF16),
            vmem((n_tensor, head, out_cols), BF16),
            vmem((out_cols, rows), F32),
            vmem(blocks, BF16),
            vmem((states, rows, LANES), F32),
            vmem((states, rows, LANES), F32),
            vmem((n_tiles, rows, LANES), F32),
            vmem((n_tiles, rows, LANES), F32),
            vmem((states, channels), F32),
            vmem((n_tiles, per_dev * (states + 1), LANES), F32),
            vmem((n_tiles, per_dev * (states + 1), LANES), F32),
            vmem((n_tiles, rows + per_dev, LANES), F32),
            vmem((rows, channels), BF16),
            vmem((per_dev * states, channels), BF16),
            dma((10 + 2 * n_tensor + len(ssm_pieces),)),
            dma((2, n_chunks)),
        ],
    )
    return out, state.reshape(per_dev, states, channels)


def solution(mesh):
    placed = (
        P(("groups", "replica"), "tensor"),
        P(("groups", "replica"), "tensor"),
        P(None, "tensor"),
        P("tensor"),
        P("tensor", None),
        P(None, "tensor"),
        P("tensor"),
        P(None, "tensor"),
        P("tensor"),
        P(("groups", "replica"), None, "tensor"),
        P(("groups", "replica"), None, "tensor"),
        P("groups"),
        P("groups"),
        P("groups"),
    )
    return jax.shard_map(
        functools.partial(shards, mesh),
        mesh=mesh,
        in_specs=placed,
        out_specs=(P(("groups", "replica"), "tensor"), P(("groups", "replica"), None, "tensor")),
        check_vma=False,
    )
```

```python
import functools

import jax
import jax.numpy as jnp
from jax import lax
from jax.experimental import pallas as pl
from jax.experimental.pallas import tpu as pltpu
from jax.sharding import PartitionSpec as P

NEW = 32
LANES = 128
MIB = 1024 * 1024
UNROLL = 8
LOG2E = 1.4426950408889634
F32, BF16 = jnp.float32, jnp.bfloat16
NT = (((1,), (1,)), ((), ()))
TN = (((0,), (0,)), ((), ()))


def silu(v):
    half = 0.5 * v
    return half + half * jnp.tanh(half)


def softplus(v):
    u = jnp.exp(-jnp.abs(v))
    small = u * (1.0 - u * (0.5 - u * (1.0 / 3.0)))
    return jnp.maximum(v, 0.0) + jnp.where(u < 0.004, small, jnp.log(1.0 + u))


def split_index(value, inner):
    assert inner & (inner - 1) == 0
    return value >> (inner.bit_length() - 1), value & (inner - 1)


def pick_rows(values, row_low, count):
    out = jnp.zeros(row_low.shape, jnp.int32)
    for r in range(count):
        out = jnp.where(row_low == r, values[r], out)
    return out


def request_places(dims, ints, me):
    per_dev, n_replica, _, relative = dims
    places, slot_ids, lengths = [], [], []
    for r in range(per_dev):
        request = me * per_dev + r
        place = ints[0][request]
        if relative:
            place = place ^ me
            place = place ^ (place >> 1)
        places.append(place)
        slot_ids.append(ints[1][request])
        lengths.append(ints[2][request])
    return places, slot_ids, lengths


def fetch_rows(target, live, pieces):
    total = None
    for first, value in pieces:
        col = lax.broadcasted_iota(jnp.int32, (target.shape[0], value.shape[0]), 1) + first
        select = jnp.where((col == target) & live, 1.0, 0.0).astype(BF16)
        part = jnp.dot(select, value, preferred_element_type=F32)
        total = part if total is None else total + part
    return total


def project_kernel(dims, refs_in, refs_out, scratch):
    per_dev = dims
    x_hbm, wt_hbm, cw_hbm, cb_hbm = refs_in[:4]
    mixed_hbm, head_hbm, part_hbm = refs_out
    x_v, wt_v, cw_v, cb_v, joined, mixed_v, head_v, part_f, part_v, sems, out_sems = scratch
    rows, channels = x_v.shape
    taps = cw_v.shape[0]
    lines = (taps - 1) * per_dev
    pairs = [(cw_hbm, cw_v), (cb_hbm, cb_v)]
    width = min(512, channels)
    chunks = [slice(c * width, (c + 1) * width) for c in range(channels // width)]
    for chunk in chunks:
        pairs += [(x_hbm.at[:, chunk], x_v.at[:, chunk]), (wt_hbm.at[:, chunk], wt_v.at[:, chunk])]
    copies = [pltpu.make_async_copy(src, dst, sems.at[i]) for i, (src, dst) in enumerate(pairs)]
    for copy in copies:
        copy.start()

    joined[:, :lines, :] = jnp.zeros((channels // LANES, lines, LANES), F32)
    copies[0].wait()
    copies[1].wait()
    outs = []
    for c, chunk in enumerate(chunks):
        copies[2 + 2 * c].wait()
        for tile in range(c * width // LANES, (c + 1) * width // LANES):
            lanes = slice(tile * LANES, (tile + 1) * LANES)
            for r in range(per_dev):
                tokens = x_v[r * NEW : (r + 1) * NEW, lanes].astype(F32)
                joined[tile, pl.ds(lines + r, NEW, stride=per_dev), :] = tokens
            weight = [cw_v[k : k + 1, lanes].astype(F32) for k in range(taps)]
            bias = cb_v[:, lanes]
            for first in range(0, rows, LANES):
                summed = bias + joined[tile, first : first + LANES, :] * weight[0]
                for k in range(1, taps):
                    begin = first + k * per_dev
                    summed = summed + joined[tile, begin : begin + LANES, :] * weight[k]
                if first == 0:
                    head_v[:, lanes] = summed[: head_v.shape[0]]
                mixed_v[first : first + LANES, lanes] = silu(summed).astype(BF16)
        copies[3 + 2 * c].wait()
        part = lax.dot_general(wt_v[:, chunk], mixed_v[:, chunk], NT, preferred_element_type=F32)
        if c == 0:
            part_f[...] = part
        else:
            part_f[...] += part
        outs.append(pltpu.make_async_copy(mixed_v.at[:, chunk], mixed_hbm.at[:, chunk], out_sems.at[c]))
        outs[-1].start()
    part_v[...] = part_f[...].astype(BF16)
    for src, dst in ((part_v, part_hbm), (head_v, head_hbm)):
        outs.append(pltpu.make_async_copy(src, dst, out_sems.at[len(outs)]))
        outs[-1].start()
    for copy in outs:
        copy.wait()


def history_kernel(dims, refs_in, refs_out, scratch):
    dims, block, firsts = dims
    per_dev, n_replica, slots, _ = dims
    holder, slot_id, prefix_len, head_hbm, wt_hbm, cw_hbm = refs_in[:6]
    pieces = refs_in[6:]
    mixed_hbm, part_hbm = refs_out
    h_s, s_s, l_s, head_v, wt_v, cw_v, mixed_v, part_v, sems, out_sems = scratch[:10]
    held = scratch[10:]
    taps = cw_v.shape[0]
    pairs = [(holder, h_s), (slot_id, s_s), (prefix_len, l_s), (cw_hbm, cw_v), (head_hbm, head_v)]
    pairs += list(zip(pieces, held)) + [(wt_hbm, wt_v)]
    copies = [pltpu.make_async_copy(src, dst, sems.at[i]) for i, (src, dst) in enumerate(pairs)]
    for copy in copies:
        copy.start()
    for copy in copies[:-1]:
        copy.wait()

    me = lax.axis_index("replica")
    places, slot_ids, lengths = request_places(dims, (h_s, s_s, l_s), me)
    tap, request = split_index(lax.broadcasted_iota(jnp.int32, (per_dev * taps, 1), 0), per_dev)
    starts = [places[r] * block + (block - slots * taps) + slot_ids[r] * taps for r in range(per_dev)]
    target = pick_rows(starts, request, per_dev) + tap
    live = (tap < taps - 1) & (taps - 1 - tap <= pick_rows(lengths, request, per_dev))
    history = fetch_rows(target, live, [(first, ref[...]) for first, ref in zip(firsts, held)])
    for t in range(taps - 1):
        now = slice(t * per_dev, (t + 1) * per_dev)
        summed = head_v[now]
        for k in range(taps - 1 - t):
            weight = cw_v[k : k + 1].astype(F32)
            summed = summed + history[(t + k) * per_dev : (t + k + 1) * per_dev] * weight
        head_v[now] = summed
    mixed = silu(head_v[...]).astype(BF16)
    mixed_v[...] = mixed
    mixed_out = pltpu.make_async_copy(mixed_v, mixed_hbm, out_sems.at[0])
    mixed_out.start()
    copies[-1].wait()
    part_v[...] = lax.dot_general(wt_v[...], mixed, NT, preferred_element_type=F32).T.astype(BF16)
    part_out = pltpu.make_async_copy(part_v, part_hbm, out_sems.at[1])
    part_out.start()
    mixed_out.wait()
    part_out.wait()


def scan_kernel(dims, refs_in, refs_out, scratch):
    per_dev = dims[0]
    holder, slot_id, prefix_len, mixed_hbm, head_hbm, z_hbm, dtw_hbm, dtb_hbm, al_hbm, skip_hbm = refs_in[:10]
    out_hbm, state_hbm = refs_out
    (h_s, s_s, l_s, mixed_v, z_v, dtw_v, dtb_v, al_v, skip_v, parts_v, fixes_v, proj_v, cache_v, b_tab, c_tab, dt_v, drive_v,
     a_v, start_tm, final_tm, y_v, out_v, state_v, sems, out_sems) = scratch
    n_parts = parts_v.shape[0]
    parts, fixes, pieces = refs_in[10 : 10 + n_parts], refs_in[10 + n_parts : 10 + 2 * n_parts], refs_in[10 + 2 * n_parts :]
    head = head_hbm.shape[0]
    rows, channels = z_v.shape
    states = al_v.shape[0]
    rank = dtw_v.shape[0]
    pairs = [(part, parts_v.at[p]) for p, part in enumerate(parts)]
    pairs += [(fix, fixes_v.at[p]) for p, fix in enumerate(fixes)]
    pairs += [(dtw_hbm, dtw_v), (dtb_hbm, dtb_v), (head_hbm, mixed_v.at[:head]), (mixed_hbm.at[head:], mixed_v.at[head:]),
              (skip_hbm, skip_v), (al_hbm, al_v), (holder, h_s), (slot_id, s_s), (prefix_len, l_s)]
    if len(pieces) == 1:
        pairs.append((pieces[0], cache_v))
    else:
        pairs += [(piece, cache_v.at[p]) for p, piece in enumerate(pieces)]
    pairs.append((z_hbm, z_v))
    copies = [pltpu.make_async_copy(src, dst, sems.at[i]) for i, (src, dst) in enumerate(pairs)]
    for copy in copies:
        copy.start()

    for copy in copies[: 2 * n_parts + 5]:
        copy.wait()
    projected = parts_v[0].astype(F32)
    for p in range(1, n_parts):
        projected = projected + parts_v[p].astype(F32)
    fixed = fixes_v[0].astype(F32)
    for p in range(1, n_parts):
        fixed = fixed + fixes_v[p].astype(F32)
    proj_v[...] = projected
    proj_v[:, :head] = fixed.T
    projected = proj_v[...]
    dt_low = projected[:rank].astype(BF16)
    late = projected[rank:].T
    n_tiles = channels // LANES
    wide = min(4, n_tiles)
    per_chunk = 2 * states * wide // n_tiles
    for c in range(n_tiles // wide):
        for n in range(c * per_chunk, (c + 1) * per_chunk):
            table = b_tab if n < states else c_tab
            table[n % states] = jnp.broadcast_to(late[:, n : n + 1], (rows, LANES))
        weights = dtw_v[:, c * wide * LANES : (c + 1) * wide * LANES]
        raw = lax.dot_general(dt_low, weights, TN, preferred_element_type=F32)
        for j in range(wide):
            tile = c * wide + j
            lanes = slice(tile * LANES, (tile + 1) * LANES)
            for first in range(0, rows, LANES):
                here = slice(first, first + LANES)
                dt = softplus(raw[here, j * LANES : (j + 1) * LANES] + dtb_v[:, lanes])
                mixed = mixed_v[here, lanes].astype(F32)
                dt_v[tile, here, :] = dt
                drive_v[tile, here, :] = dt * mixed
                y_v[tile, here, :] = skip_v[:, lanes] * mixed
    for copy in copies[2 * n_parts + 5 : -1]:
        copy.wait()
    a_v[...] = jnp.exp(al_v[...]) * (-LOG2E)

    me = lax.axis_index("replica")
    places, slot_ids, lengths = request_places(dims, (h_s, s_s, l_s), me)
    for r in range(per_dev):
        spot = pl.ds(pl.multiple_of(slot_ids[r] * states, states), states)
        for tile in range(n_tiles):
            value = cache_v[places[r], spot, tile * LANES : (tile + 1) * LANES].astype(F32)
            value = jnp.where(lengths[r] > 0, value, jnp.zeros_like(value))
            start_tm[tile, pl.ds(r, states, stride=per_dev), :] = value
    copies[-1].wait()

    tiles = 2
    half = states // 2
    width = 2 * tiles * LANES
    n_chunks = channels // width

    def out_copies(c):
        lanes = pl.ds(pl.multiple_of(c * width, width), width)
        return [
            pltpu.make_async_copy(src.at[:, lanes], dst.at[:, lanes], out_sems.at[i, c])
            for i, (src, dst) in enumerate(((out_v, out_hbm), (state_v, state_hbm)))
        ]

    def scan_group(g, carry):
        group = [g * tiles + j for j in range(tiles)]
        lanes = [pl.ds(pl.multiple_of(tile * LANES, LANES), LANES) for tile in group]
        for first in range(0, states, half):
            ids = range(first, first + half)
            rates = [[jnp.broadcast_to(a_v[n : n + 1, lane], (per_dev, LANES)) for n in ids] for lane in lanes]

            def advance(step, state):
                state = list(state)
                for u in range(UNROLL):
                    now = pl.ds(pl.multiple_of((step * UNROLL + u) * per_dev, per_dev), per_dev)
                    dt = [dt_v[tile, now, :] for tile in group]
                    drive = [drive_v[tile, now, :] for tile in group]
                    sums = [None] * tiles
                    for k, n in enumerate(ids):
                        b, c = b_tab[n, now, :], c_tab[n, now, :]
                        for j in range(tiles):
                            i = j * half + k
                            state[i] = jnp.exp2(dt[j] * rates[j][k]) * state[i] + drive[j] * b
                            term = state[i] * c
                            sums[j] = term if sums[j] is None else sums[j] + term
                    for j, tile in enumerate(group):
                        y_v[tile, now, :] += sums[j]
                return tuple(state)

            state = tuple(start_tm[tile, n * per_dev : (n + 1) * per_dev, :] for tile in group for n in ids)
            state = lax.fori_loop(0, NEW // UNROLL, advance, state)
            for j, tile in enumerate(group):
                for k, n in enumerate(ids):
                    final_tm[tile, n * per_dev : (n + 1) * per_dev, :] = state[j * half + k]
        return carry

    def one_chunk(c, carry):
        lax.fori_loop(c * 2, c * 2 + 2, scan_group, 0)
        for j in range(width // LANES):
            tile = c * (width // LANES) + j
            lanes = pl.ds(pl.multiple_of(tile * LANES, LANES), LANES)
            for r in range(per_dev):
                here = slice(r * NEW, (r + 1) * NEW)
                value = y_v[tile, pl.ds(r, NEW, stride=per_dev), :] * silu(z_v[here, lanes].astype(F32))
                out_v[here, lanes] = value.astype(BF16)
                final = final_tm[tile, pl.ds(r, states, stride=per_dev), :]
                state_v[r * states : (r + 1) * states, lanes] = final.astype(BF16)
        for copy in out_copies(c):
            copy.start()
        return carry

    lax.fori_loop(0, n_chunks, one_chunk, 0)

    def last_wait(c, carry):
        for copy in out_copies(c):
            copy.wait()
        return carry

    lax.fori_loop(0, n_chunks, last_wait, 0)


def split_refs(kernel, dims, n_in, n_out):
    def body(*refs):
        kernel(dims, refs[:n_in], refs[n_in : n_in + n_out], refs[n_in + n_out :])

    return body


def call(kernel, dims, name, limit, ins, outs, scratch):
    hbm = pl.BlockSpec(memory_space=pltpu.HBM)
    anywhere = pl.BlockSpec(memory_space=pl.ANY)
    return pl.pallas_call(
        split_refs(kernel, dims, len(ins), len(outs)),
        in_specs=[hbm if fixed else anywhere for _, fixed in ins],
        out_specs=[anywhere] * len(outs),
        out_shape=[jax.ShapeDtypeStruct(*out) for out in outs],
        scratch_shapes=scratch,
        compiler_params=pltpu.CompilerParams(vmem_limit_bytes=limit * MIB),
        name=name,
    )(*[pltpu.with_memory_space_constraint(value, pltpu.HBM) if fixed else value for value, fixed in ins])


def swap(value, axis, size, mask):
    return lax.ppermute(value, axis, [(i, i ^ mask) for i in range(size)])


def shards(mesh, x_new, z_new, conv_weight, conv_bias, x_proj_weight, dt_proj_weight, dt_bias, a_log, d_skip,
           cache_ssm, cache_conv, holder, slot_id, prefix_len):
    n_replica, n_tensor = mesh.shape["replica"], mesh.shape["tensor"]
    rows, channels = x_new.shape
    per_dev = rows // NEW
    states = a_log.shape[0]
    rank = dt_proj_weight.shape[0]
    taps = conv_weight.shape[0]
    slots = cache_ssm.shape[0]
    out_cols = x_proj_weight.shape[1]
    requests = holder.shape[0]

    conv_rows = jnp.pad(cache_conv, ((0, 0), (0, 1), (0, 0))).reshape(slots * taps, channels)
    rows_all = jnp.concatenate([cache_ssm.reshape(slots * states, channels), conv_rows])
    block = rows_all.shape[0]
    relative = n_replica == 4
    if relative:
        far = swap(rows_all, "replica", n_replica, 3)
        near = swap(rows_all, "replica", n_replica, 1)
        conv_two = swap(conv_rows, "replica", n_replica, 2)
        conv_pieces = [rows_all, near, far, conv_two]
        firsts = (0, block, 2 * block, 4 * block - slots * taps)
        first_pieces = [conv_two]
        ssm_pieces = [rows_all, near, far, swap(far, "replica", n_replica, 1)]
    else:
        ssm_pieces = [lax.all_gather(rows_all, "replica")]
        conv_pieces, firsts, first_pieces = [ssm_pieces[0].reshape(-1, channels)], (0,), []

    vmem, dma = pltpu.VMEM, pltpu.SemaphoreType.DMA
    ints = [pltpu.SMEM((requests,), jnp.int32)] * 3
    n_chunks = channels // min(512, channels)
    dims = (per_dev, n_replica, slots, relative)

    head = per_dev * taps
    weights = x_proj_weight.T
    mixed, head_sums, part = call(
        project_kernel, per_dev, "conv_project", 40,
        [(x_new, True), (weights, True), (conv_weight, True), (conv_bias[None, :], True)]
        + [(piece, False) for piece in first_pieces],
        [((rows, channels), BF16), ((head, channels), F32), ((out_cols, rows), BF16)],
        [
            vmem((rows, channels), BF16),
            vmem((out_cols, channels), BF16),
            vmem((taps, channels), BF16),
            vmem((1, channels), F32),
            vmem((channels // LANES, rows + taps * per_dev, LANES), F32),
            vmem((rows, channels), BF16),
            vmem((head, channels), F32),
            vmem((out_cols, rows), F32),
            vmem((out_cols, rows), BF16),
            dma((2 + 2 * n_chunks,)),
            dma((n_chunks + 2,)),
        ],
    )
    mixed_head, fix = call(
        history_kernel, (dims, block, firsts), "history", 40,
        [(holder, False), (slot_id, False), (prefix_len, False), (head_sums, False), (weights, False),
         (conv_weight, False)]
        + [(piece, False) for piece in conv_pieces],
        [((head, channels), BF16), ((head, out_cols), BF16)],
        ints + [
            vmem((head, channels), F32),
            vmem((out_cols, channels), BF16),
            vmem((taps, channels), BF16),
            vmem((head, channels), BF16),
            vmem((head, out_cols), BF16),
            dma((6 + len(conv_pieces),)),
            dma((2,)),
        ] + [vmem(piece.shape, BF16) for piece in conv_pieces],
    )
    parts = [part]
    mask = n_tensor // 2
    while mask:
        parts = parts + [swap(value, "tensor", n_tensor, mask) for value in reversed(parts)]
        mask //= 2
    fixes = [fix] + [swap(fix, "tensor", n_tensor, k) for k in range(1, n_tensor)]

    blocks = (n_replica, block, channels)
    n_tiles = channels // LANES
    out, state = call(
        scan_kernel, dims, "dt_scan_gate", 40,
        [(holder, False), (slot_id, False), (prefix_len, False), (mixed, False), (mixed_head, False), (z_new, False), (dt_proj_weight, False),
         (dt_bias[None, :], False), (a_log, False), (d_skip[None, :], False)]
        + [(piece, False) for piece in parts + fixes + ssm_pieces],
        [((rows, channels), BF16), ((per_dev * states, channels), BF16)],
        ints + [
            vmem((rows, channels), BF16),
            vmem((rows, channels), BF16),
            vmem((rank, channels), BF16),
            vmem((1, channels), F32),
            vmem((states, channels), F32),
            vmem((1, channels), F32),
            vmem((n_tensor, out_cols, rows), BF16),
            vmem((n_tensor, head, out_cols), BF16),
            vmem((out_cols, rows), F32),
            vmem(blocks, BF16),
            vmem((states, rows, LANES), F32),
            vmem((states, rows, LANES), F32),
            vmem((n_tiles, rows, LANES), F32),
            vmem((n_tiles, rows, LANES), F32),
            vmem((states, channels), F32),
            vmem((n_tiles, per_dev * (states + 1), LANES), F32),
            vmem((n_tiles, per_dev * (states + 1), LANES), F32),
            vmem((n_tiles, rows + per_dev, LANES), F32),
            vmem((rows, channels), BF16),
            vmem((per_dev * states, channels), BF16),
            dma((10 + 2 * n_tensor + len(ssm_pieces),)),
            dma((2, n_chunks)),
        ],
    )
    return out, state.reshape(per_dev, states, channels)


def solution(mesh):
    placed = (
        P(("groups", "replica"), "tensor"),
        P(("groups", "replica"), "tensor"),
        P(None, "tensor"),
        P("tensor"),
        P("tensor", None),
        P(None, "tensor"),
        P("tensor"),
        P(None, "tensor"),
        P("tensor"),
        P(("groups", "replica"), None, "tensor"),
        P(("groups", "replica"), None, "tensor"),
        P("groups"),
        P("groups"),
        P("groups"),
    )
    return jax.shard_map(
        functools.partial(shards, mesh),
        mesh=mesh,
        in_specs=placed,
        out_specs=(P(("groups", "replica"), "tensor"), P(("groups", "replica"), None, "tensor")),
        check_vma=False,
    )
```

```python
import functools

import jax
import jax.numpy as jnp
from jax import lax
from jax.experimental import pallas as pl
from jax.experimental.pallas import tpu as pltpu
from jax.sharding import PartitionSpec as P

NEW = 32
LANES = 128
MIB = 1024 * 1024
UNROLL = 8
LOG2E = 1.4426950408889634
F32, BF16 = jnp.float32, jnp.bfloat16
NT = (((1,), (1,)), ((), ()))
TN = (((0,), (0,)), ((), ()))


def silu(v):
    half = 0.5 * v
    return half + half * jnp.tanh(half)


def softplus(v):
    u = jnp.exp(-jnp.abs(v))
    small = u * (1.0 - u * (0.5 - u * (1.0 / 3.0)))
    return jnp.maximum(v, 0.0) + jnp.where(u < 0.004, small, jnp.log(1.0 + u))


def split_index(value, inner):
    assert inner & (inner - 1) == 0
    return value >> (inner.bit_length() - 1), value & (inner - 1)


def pick_rows(values, row_low, count):
    out = jnp.zeros(row_low.shape, jnp.int32)
    for r in range(count):
        out = jnp.where(row_low == r, values[r], out)
    return out


def request_places(dims, ints, me):
    per_dev, n_replica, _, relative = dims
    places, slot_ids, lengths = [], [], []
    for r in range(per_dev):
        request = me * per_dev + r
        place = ints[0][request]
        if relative:
            place = place ^ me
            place = place ^ (place >> 1)
        places.append(place)
        slot_ids.append(ints[1][request])
        lengths.append(ints[2][request])
    return places, slot_ids, lengths


def fetch_rows(target, live, pieces):
    total = None
    for first, value in pieces:
        col = lax.broadcasted_iota(jnp.int32, (target.shape[0], value.shape[0]), 1) + first
        select = jnp.where((col == target) & live, 1.0, 0.0).astype(BF16)
        part = jnp.dot(select, value, preferred_element_type=F32)
        total = part if total is None else total + part
    return total


def project_kernel(dims, refs_in, refs_out, scratch):
    per_dev = dims
    x_hbm, wt_hbm, cw_hbm, cb_hbm = refs_in
    mixed_hbm, head_hbm, part_hbm = refs_out
    x_v, wt_v, cw_v, cb_v, joined, mixed_v, head_v, part_f, part_v, sems, out_sems = scratch
    rows, channels = x_v.shape
    taps = cw_v.shape[0]
    lines = (taps - 1) * per_dev
    pairs = [(cw_hbm, cw_v), (cb_hbm, cb_v)]
    width = min(512, channels)
    chunks = [slice(c * width, (c + 1) * width) for c in range(channels // width)]
    for chunk in chunks:
        pairs += [(x_hbm.at[:, chunk], x_v.at[:, chunk]), (wt_hbm.at[:, chunk], wt_v.at[:, chunk])]
    copies = [pltpu.make_async_copy(src, dst, sems.at[i]) for i, (src, dst) in enumerate(pairs)]
    for copy in copies:
        copy.start()

    joined[:, :lines, :] = jnp.zeros((channels // LANES, lines, LANES), F32)
    copies[0].wait()
    copies[1].wait()
    outs = []
    for c, chunk in enumerate(chunks):
        copies[2 + 2 * c].wait()
        for tile in range(c * width // LANES, (c + 1) * width // LANES):
            lanes = slice(tile * LANES, (tile + 1) * LANES)
            for r in range(per_dev):
                tokens = x_v[r * NEW : (r + 1) * NEW, lanes].astype(F32)
                joined[tile, pl.ds(lines + r, NEW, stride=per_dev), :] = tokens
            weight = [cw_v[k : k + 1, lanes].astype(F32) for k in range(taps)]
            bias = cb_v[:, lanes]
            for first in range(0, rows, LANES):
                summed = bias + joined[tile, first : first + LANES, :] * weight[0]
                for k in range(1, taps):
                    begin = first + k * per_dev
                    summed = summed + joined[tile, begin : begin + LANES, :] * weight[k]
                if first == 0:
                    head_v[:, lanes] = summed[: head_v.shape[0]]
                mixed_v[first : first + LANES, lanes] = silu(summed).astype(BF16)
        copies[3 + 2 * c].wait()
        part = lax.dot_general(wt_v[:, chunk], mixed_v[:, chunk], NT, preferred_element_type=F32)
        if c == 0:
            part_f[...] = part
        else:
            part_f[...] += part
        outs.append(pltpu.make_async_copy(mixed_v.at[:, chunk], mixed_hbm.at[:, chunk], out_sems.at[c]))
        outs[-1].start()
    part_v[...] = part_f[...].astype(BF16)
    for src, dst in ((part_v, part_hbm), (head_v, head_hbm)):
        outs.append(pltpu.make_async_copy(src, dst, out_sems.at[len(outs)]))
        outs[-1].start()
    for copy in outs:
        copy.wait()


def history_kernel(dims, refs_in, refs_out, scratch):
    dims, block, firsts = dims
    per_dev, n_replica, slots, _ = dims
    holder, slot_id, prefix_len, head_ref, part_ref, wt_ref, cw_ref = refs_in[:7]
    pieces = refs_in[7:]
    mixed_ref, fixed_ref = refs_out
    taps = cw_ref.shape[0]
    me = lax.axis_index("replica")
    places, slot_ids, lengths = request_places(dims, (holder, slot_id, prefix_len), me)
    tap, request = split_index(lax.broadcasted_iota(jnp.int32, (per_dev * taps, 1), 0), per_dev)
    starts = [places[r] * block + (block - slots * taps) + slot_ids[r] * taps for r in range(per_dev)]
    target = pick_rows(starts, request, per_dev) + tap
    live = (tap < taps - 1) & (taps - 1 - tap <= pick_rows(lengths, request, per_dev))
    history = fetch_rows(target, live, [(first, ref[...]) for first, ref in zip(firsts, pieces)])
    sums = []
    for t in range(taps):
        summed = head_ref[t * per_dev : (t + 1) * per_dev]
        for k in range(taps - 1 - t):
            weight = cw_ref[k : k + 1].astype(F32)
            summed = summed + history[(t + k) * per_dev : (t + k + 1) * per_dev] * weight
        sums.append(summed)
    mixed = silu(jnp.concatenate(sums, axis=0)).astype(BF16)
    mixed_ref[...] = mixed
    part = lax.dot_general(wt_ref[...], mixed, NT, preferred_element_type=F32)
    fixed_ref[...] = part_ref[...]
    fixed_ref[:, : per_dev * taps] = part.astype(BF16)


def scan_kernel(dims, refs_in, refs_out, scratch):
    per_dev, n_replica, _, _ = dims
    holder, slot_id, prefix_len, mixed_ref, head_ref, z_ref, dtw_ref, dtb_ref, al_ref, skip_ref = refs_in[:10]
    out_hbm, state_hbm = refs_out
    b_tab, c_tab, dt_v, drive_v, a_v, start_tm, final_tm, y_v, out_v, state_v, out_sems = scratch
    n_pieces = sum(1 for ref in refs_in[10:] if ref.shape[-1] == z_ref.shape[1])
    parts, pieces = refs_in[10:-n_pieces], refs_in[-n_pieces:]
    rows, channels = z_ref.shape
    states = al_ref.shape[0]
    rank = dtw_ref.shape[0]
    head = head_ref.shape[0]

    projected = parts[0][...].astype(F32)
    for part in parts[1:]:
        projected = projected + part[...].astype(F32)
    dt_low = projected[:rank].astype(BF16)
    late = projected[rank:].T
    n_tiles = channels // LANES
    wide = min(4, n_tiles)
    per_chunk = 2 * states * wide // n_tiles
    for c in range(n_tiles // wide):
        for n in range(c * per_chunk, (c + 1) * per_chunk):
            table = b_tab if n < states else c_tab
            table[n % states] = jnp.broadcast_to(late[:, n : n + 1], (rows, LANES))
        weights = dtw_ref[:, c * wide * LANES : (c + 1) * wide * LANES]
        raw = lax.dot_general(dt_low, weights, TN, preferred_element_type=F32)
        for j in range(wide):
            tile = c * wide + j
            lanes = slice(tile * LANES, (tile + 1) * LANES)
            for first in range(0, rows, LANES):
                here = slice(first, first + LANES)
                dt = softplus(raw[here, j * LANES : (j + 1) * LANES] + dtb_ref[:, lanes])
                mixed = mixed_ref[here, lanes]
                if first == 0:
                    mixed = jnp.concatenate([head_ref[:, lanes], mixed[head:]], axis=0)
                mixed = mixed.astype(F32)
                dt_v[tile, here, :] = dt
                drive_v[tile, here, :] = dt * mixed
                y_v[tile, here, :] = skip_ref[:, lanes] * mixed
    a_v[...] = jnp.exp(al_ref[...]) * (-LOG2E)

    me = lax.axis_index("replica")
    places, slot_ids, lengths = request_places(dims, (holder, slot_id, prefix_len), me)
    for r in range(per_dev):
        spot = pl.ds(pl.multiple_of(slot_ids[r] * states, states), states)
        for tile in range(n_tiles):
            lanes = slice(tile * LANES, (tile + 1) * LANES)
            if n_pieces == 1:
                value = pieces[0][places[r], spot, lanes]
            else:
                value = pieces[0][spot, lanes]
                for p in range(1, n_pieces):
                    value = jnp.where(places[r] == p, pieces[p][spot, lanes], value)
            value = value.astype(F32)
            value = jnp.where(lengths[r] > 0, value, jnp.zeros_like(value))
            start_tm[tile, pl.ds(r, states, stride=per_dev), :] = value

    tiles = 2
    half = states // 2
    width = 2 * tiles * LANES
    n_chunks = channels // width

    def out_copies(c):
        lanes = pl.ds(pl.multiple_of(c * width, width), width)
        return [
            pltpu.make_async_copy(src.at[:, lanes], dst.at[:, lanes], out_sems.at[i, c])
            for i, (src, dst) in enumerate(((out_v, out_hbm), (state_v, state_hbm)))
        ]

    def scan_group(g, carry):
        group = [g * tiles + j for j in range(tiles)]
        lanes = [pl.ds(pl.multiple_of(tile * LANES, LANES), LANES) for tile in group]
        for first in range(0, states, half):
            ids = range(first, first + half)
            rates = [[jnp.broadcast_to(a_v[n : n + 1, lane], (per_dev, LANES)) for n in ids] for lane in lanes]

            def advance(step, state):
                state = list(state)
                for u in range(UNROLL):
                    now = pl.ds(pl.multiple_of((step * UNROLL + u) * per_dev, per_dev), per_dev)
                    dt = [dt_v[tile, now, :] for tile in group]
                    drive = [drive_v[tile, now, :] for tile in group]
                    sums = [None] * tiles
                    for k, n in enumerate(ids):
                        b, c = b_tab[n, now, :], c_tab[n, now, :]
                        for j in range(tiles):
                            i = j * half + k
                            state[i] = jnp.exp2(dt[j] * rates[j][k]) * state[i] + drive[j] * b
                            term = state[i] * c
                            sums[j] = term if sums[j] is None else sums[j] + term
                    for j, tile in enumerate(group):
                        y_v[tile, now, :] += sums[j]
                return tuple(state)

            state = tuple(start_tm[tile, n * per_dev : (n + 1) * per_dev, :] for tile in group for n in ids)
            state = lax.fori_loop(0, NEW // UNROLL, advance, state)
            for j, tile in enumerate(group):
                for k, n in enumerate(ids):
                    final_tm[tile, n * per_dev : (n + 1) * per_dev, :] = state[j * half + k]
        return carry

    def one_chunk(c, carry):
        lax.fori_loop(c * 2, c * 2 + 2, scan_group, 0)
        for j in range(width // LANES):
            tile = c * (width // LANES) + j
            lanes = pl.ds(pl.multiple_of(tile * LANES, LANES), LANES)
            for r in range(per_dev):
                here = slice(r * NEW, (r + 1) * NEW)
                value = y_v[tile, pl.ds(r, NEW, stride=per_dev), :] * silu(z_ref[here, lanes].astype(F32))
                out_v[here, lanes] = value.astype(BF16)
                final = final_tm[tile, pl.ds(r, states, stride=per_dev), :]
                state_v[r * states : (r + 1) * states, lanes] = final.astype(BF16)
        for copy in out_copies(c):
            copy.start()
        return carry

    lax.fori_loop(0, n_chunks, one_chunk, 0)

    def last_wait(c, carry):
        for copy in out_copies(c):
            copy.wait()
        return carry

    lax.fori_loop(0, n_chunks, last_wait, 0)


def split_refs(kernel, dims, n_in, n_out):
    def body(*refs):
        kernel(dims, refs[:n_in], refs[n_in : n_in + n_out], refs[n_in + n_out :])

    return body


def call(kernel, dims, name, limit, ins, outs, scratch):
    spaces = {"hbm": pltpu.HBM, "any": pl.ANY, "vmem": pltpu.VMEM, "smem": pltpu.SMEM}
    values = [
        pltpu.with_memory_space_constraint(value, pltpu.HBM) if place == "hbm" else value for value, place in ins
    ]
    return pl.pallas_call(
        split_refs(kernel, dims, len(ins), len(outs)),
        in_specs=[pl.BlockSpec(memory_space=spaces[place]) for _, place in ins],
        out_specs=[pl.BlockSpec(memory_space=spaces[place]) for _, _, place in outs],
        out_shape=[jax.ShapeDtypeStruct(shape, dtype) for shape, dtype, _ in outs],
        scratch_shapes=scratch,
        compiler_params=pltpu.CompilerParams(vmem_limit_bytes=limit * MIB),
        name=name,
    )(*values)


def swap(value, axis, size, mask):
    return lax.ppermute(value, axis, [(i, i ^ mask) for i in range(size)])


def shards(mesh, x_new, z_new, conv_weight, conv_bias, x_proj_weight, dt_proj_weight, dt_bias, a_log, d_skip,
           cache_ssm, cache_conv, holder, slot_id, prefix_len):
    n_replica, n_tensor = mesh.shape["replica"], mesh.shape["tensor"]
    rows, channels = x_new.shape
    per_dev = rows // NEW
    states = a_log.shape[0]
    rank = dt_proj_weight.shape[0]
    taps = conv_weight.shape[0]
    slots = cache_ssm.shape[0]
    out_cols = x_proj_weight.shape[1]
    requests = holder.shape[0]

    conv_rows = jnp.pad(cache_conv, ((0, 0), (0, 1), (0, 0))).reshape(slots * taps, channels)
    rows_all = jnp.concatenate([cache_ssm.reshape(slots * states, channels), conv_rows])
    block = rows_all.shape[0]
    relative = n_replica == 4
    if relative:
        far = swap(rows_all, "replica", n_replica, 3)
        near = swap(rows_all, "replica", n_replica, 1)
        conv_two = swap(conv_rows, "replica", n_replica, 2)
        conv_pieces = [rows_all, near, far, conv_two]
        firsts = (0, block, 2 * block, 4 * block - slots * taps)
        ssm_pieces = [rows_all, near, far, swap(far, "replica", n_replica, 1)]
    else:
        ssm_pieces = [lax.all_gather(rows_all, "replica")]
        conv_pieces, firsts = [ssm_pieces[0].reshape(-1, channels)], (0,)

    vmem, dma = pltpu.VMEM, pltpu.SemaphoreType.DMA
    n_chunks = channels // min(512, channels)
    dims = (per_dev, n_replica, slots, relative)
    head = per_dev * taps
    weights = x_proj_weight.T
    requests = [(holder, "smem"), (slot_id, "smem"), (prefix_len, "smem")]

    mixed, head_sums, part = call(
        project_kernel, per_dev, "conv_project", 40,
        [(x_new, "hbm"), (weights, "hbm"), (conv_weight, "hbm"), (conv_bias[None, :], "hbm")],
        [((rows, channels), BF16, "any"), ((head, channels), F32, "any"), ((out_cols, rows), BF16, "any")],
        [
            vmem((rows, channels), BF16),
            vmem((out_cols, channels), BF16),
            vmem((taps, channels), BF16),
            vmem((1, channels), F32),
            vmem((channels // LANES, rows + taps * per_dev, LANES), F32),
            vmem((rows, channels), BF16),
            vmem((head, channels), F32),
            vmem((out_cols, rows), F32),
            vmem((out_cols, rows), BF16),
            dma((2 + 2 * n_chunks,)),
            dma((n_chunks + 2,)),
        ],
    )
    mixed_head, part = call(
        history_kernel, (dims, block, firsts), "history", 20,
        requests
        + [(value, "vmem") for value in [head_sums, part, weights, conv_weight] + conv_pieces],
        [((head, channels), BF16, "vmem"), ((out_cols, rows), BF16, "vmem")],
        [],
    )
    parts = [part]
    mask = n_tensor // 2
    while mask:
        parts = parts + [swap(value, "tensor", n_tensor, mask) for value in reversed(parts)]
        mask //= 2

    n_tiles = channels // LANES
    operands = [mixed, mixed_head, z_new, dt_proj_weight, dt_bias[None, :], a_log, d_skip[None, :]]
    out, state = call(
        scan_kernel, dims, "dt_scan_gate", 40,
        requests + [(value, "vmem") for value in operands + parts + ssm_pieces],
        [((rows, channels), BF16, "any"), ((per_dev * states, channels), BF16, "any")],
        [
            vmem((states, rows, LANES), F32),
            vmem((states, rows, LANES), F32),
            vmem((n_tiles, rows, LANES), F32),
            vmem((n_tiles, rows, LANES), F32),
            vmem((states, channels), F32),
            vmem((n_tiles, per_dev * (states + 1), LANES), F32),
            vmem((n_tiles, per_dev * (states + 1), LANES), F32),
            vmem((n_tiles, rows + per_dev, LANES), F32),
            vmem((rows, channels), BF16),
            vmem((per_dev * states, channels), BF16),
            dma((2, n_chunks)),
        ],
    )
    return out, state.reshape(per_dev, states, channels)


def solution(mesh):
    placed = (
        P(("groups", "replica"), "tensor"),
        P(("groups", "replica"), "tensor"),
        P(None, "tensor"),
        P("tensor"),
        P("tensor", None),
        P(None, "tensor"),
        P("tensor"),
        P(None, "tensor"),
        P("tensor"),
        P(("groups", "replica"), None, "tensor"),
        P(("groups", "replica"), None, "tensor"),
        P("groups"),
        P("groups"),
        P("groups"),
    )
    return jax.shard_map(
        functools.partial(shards, mesh),
        mesh=mesh,
        in_specs=placed,
        out_specs=(P(("groups", "replica"), "tensor"), P(("groups", "replica"), None, "tensor")),
        check_vma=False,
    )
```

```python
import functools

import jax
import jax.numpy as jnp
from jax import lax
from jax.experimental import pallas as pl
from jax.experimental.pallas import tpu as pltpu
from jax.sharding import PartitionSpec as P

NEW = 32
LANES = 128
MIB = 1024 * 1024
UNROLL = 8
LOG2E = 1.4426950408889634
F32, BF16 = jnp.float32, jnp.bfloat16
NT = (((1,), (1,)), ((), ()))


def silu(v):
    half = 0.5 * v
    return half + half * jnp.tanh(half)


def softplus(v):
    u = jnp.exp2(jnp.abs(v) * -LOG2E)
    return jnp.maximum(v, 0.0) + jnp.where(u < 2.0**-10, u - 0.5 * (u * u), jnp.log(1.0 + u))


def split_index(value, inner):
    assert inner & (inner - 1) == 0
    return value >> (inner.bit_length() - 1), value & (inner - 1)


def pick_rows(values, row_low, count):
    out = jnp.zeros(row_low.shape, jnp.int32)
    for r in range(count):
        out = jnp.where(row_low == r, values[r], out)
    return out


def request_places(dims, ints, me):
    per_dev, n_replica, _, relative = dims
    places, slot_ids, lengths = [], [], []
    for r in range(per_dev):
        request = me * per_dev + r
        place = ints[0][request]
        if relative:
            place = place ^ me
            place = place ^ (place >> 1)
        places.append(place)
        slot_ids.append(ints[1][request])
        lengths.append(ints[2][request])
    return places, slot_ids, lengths


def fetch_rows(target, live, pieces):
    total = None
    for first, value in pieces:
        col = lax.broadcasted_iota(jnp.int32, (target.shape[0], value.shape[0]), 1) + first
        select = jnp.where((col == target) & live, 1.0, 0.0).astype(BF16)
        part = jnp.dot(select, value, preferred_element_type=F32)
        total = part if total is None else total + part
    return total


def pack_kernel(dims, refs_in, refs_out, scratch):
    slots, taps = dims
    ssm_hbm, conv_hbm = refs_in
    block_ref, conv_ref = refs_out
    conv_v, sems = scratch
    states = pltpu.make_async_copy(ssm_hbm, block_ref.at[: ssm_hbm.shape[0]], sems.at[0])
    inputs = pltpu.make_async_copy(conv_hbm, conv_v, sems.at[1])
    states.start()
    inputs.start()
    inputs.wait()
    lines = []
    for slot in range(slots):
        for tap in range(taps):
            line = conv_v[min(tap, taps - 2)].astype(F32)[slot : slot + 1]
            lines.append(line if tap < taps - 1 else jnp.zeros_like(line))
    rows = jnp.concatenate(lines, axis=0).astype(BF16)
    conv_ref[...] = rows
    block_ref[ssm_hbm.shape[0] :, :] = rows
    states.wait()


def project_kernel(dims, refs_in, refs_out, scratch):
    per_dev = dims
    x_hbm, wt_hbm, cw_hbm, cb_hbm = refs_in
    mixed_hbm, head_hbm, part_hbm = refs_out
    x_v, wt_v, cw_v, cb_v, joined, mixed_v, head_v, part_f, part_v, sems, out_sems = scratch
    rows, channels = x_v.shape
    taps = cw_v.shape[0]
    lines = (taps - 1) * per_dev
    pairs = [(cw_hbm, cw_v), (cb_hbm, cb_v)]
    width = min(512, channels)
    chunks = [slice(c * width, (c + 1) * width) for c in range(channels // width)]
    for chunk in chunks:
        pairs += [(x_hbm.at[:, chunk], x_v.at[:, chunk]), (wt_hbm.at[:, chunk], wt_v.at[:, chunk])]
    copies = [pltpu.make_async_copy(src, dst, sems.at[i]) for i, (src, dst) in enumerate(pairs)]
    for copy in copies:
        copy.start()

    joined[:, :lines, :] = jnp.zeros((channels // LANES, lines, LANES), F32)
    copies[0].wait()
    copies[1].wait()
    outs = []
    for c, chunk in enumerate(chunks):
        copies[2 + 2 * c].wait()
        for tile in range(c * width // LANES, (c + 1) * width // LANES):
            lanes = slice(tile * LANES, (tile + 1) * LANES)
            for r in range(per_dev):
                tokens = x_v[r * NEW : (r + 1) * NEW, lanes].astype(F32)
                joined[tile, pl.ds(lines + r, NEW, stride=per_dev), :] = tokens
            weight = [cw_v[k : k + 1, lanes].astype(F32) for k in range(taps)]
            bias = cb_v[:, lanes]
            for first in range(0, rows, LANES):
                summed = bias + joined[tile, first : first + LANES, :] * weight[0]
                for k in range(1, taps):
                    begin = first + k * per_dev
                    summed = summed + joined[tile, begin : begin + LANES, :] * weight[k]
                if first == 0:
                    head_v[:, lanes] = summed[: head_v.shape[0]]
                mixed_v[first : first + LANES, lanes] = silu(summed).astype(BF16)
        copies[3 + 2 * c].wait()
        part = lax.dot_general(wt_v[:, chunk], mixed_v[:, chunk], NT, preferred_element_type=F32)
        if c == 0:
            part_f[...] = part
        else:
            part_f[...] += part
        outs.append(pltpu.make_async_copy(mixed_v.at[:, chunk], mixed_hbm.at[:, chunk], out_sems.at[c]))
        outs[-1].start()
    part_v[...] = part_f[...].astype(BF16)
    for src, dst in ((part_v, part_hbm), (head_v, head_hbm)):
        outs.append(pltpu.make_async_copy(src, dst, out_sems.at[len(outs)]))
        outs[-1].start()
    for copy in outs:
        copy.wait()


def history_kernel(dims, refs_in, refs_out, scratch):
    dims, block, firsts = dims
    per_dev, n_replica, slots, _ = dims
    holder, slot_id, prefix_len, head_ref, part_ref, wt_ref, cw_ref = refs_in[:7]
    pieces = refs_in[7:]
    mixed_ref, fixed_ref = refs_out
    taps = cw_ref.shape[0]
    me = lax.axis_index("replica")
    places, slot_ids, lengths = request_places(dims, (holder, slot_id, prefix_len), me)
    tap, request = split_index(lax.broadcasted_iota(jnp.int32, (per_dev * taps, 1), 0), per_dev)
    starts = [places[r] * block + (block - slots * taps) + slot_ids[r] * taps for r in range(per_dev)]
    target = pick_rows(starts, request, per_dev) + tap
    live = (tap < taps - 1) & (taps - 1 - tap <= pick_rows(lengths, request, per_dev))
    history = fetch_rows(target, live, [(first, ref[...]) for first, ref in zip(firsts, pieces)])
    sums = []
    for t in range(taps):
        summed = head_ref[t * per_dev : (t + 1) * per_dev]
        for k in range(taps - 1 - t):
            weight = cw_ref[k : k + 1].astype(F32)
            summed = summed + history[(t + k) * per_dev : (t + k + 1) * per_dev] * weight
        sums.append(summed)
    mixed = silu(jnp.concatenate(sums, axis=0)).astype(BF16)
    mixed_ref[...] = mixed
    part = lax.dot_general(wt_ref[...], mixed, NT, preferred_element_type=F32)
    fixed_ref[...] = part_ref[...]
    fixed_ref[:, : per_dev * taps] = part.astype(BF16)


def scan_kernel(dims, refs_in, refs_out, scratch):
    per_dev, n_replica, _, _ = dims
    mixed_ref, head_ref, z_ref, dtw_ref, dtb_ref, al_ref, skip_ref = refs_in[3:10]
    out_hbm, state_hbm = refs_out
    b_tab, c_tab, dt_v, drive_v, a_v, start_tm, final_tm, y_v, out_v, state_v, out_sems, int_sems = scratch[:12]
    ints = scratch[12:]
    int_copies = [pltpu.make_async_copy(refs_in[i], ints[i], int_sems.at[i]) for i in range(len(ints))]
    for copy in int_copies:
        copy.start()
    n_pieces = sum(1 for ref in refs_in[10:] if ref.shape[-1] == z_ref.shape[1])
    parts, pieces = refs_in[10:-n_pieces], refs_in[-n_pieces:]
    rows, channels = z_ref.shape
    states = al_ref.shape[0]
    rank = dtw_ref.shape[0]
    head = head_ref.shape[0]

    projected = parts[0][...].astype(F32)
    for part in parts[1:]:
        projected = projected + part[...].astype(F32)
    projected = projected.T
    dt_low = projected[:, :rank].astype(BF16)
    late = projected[:, rank:]
    n_tiles = channels // LANES
    wide = min(4, n_tiles)
    per_chunk = 2 * states * wide // n_tiles
    for c in range(n_tiles // wide):
        for n in range(c * per_chunk, (c + 1) * per_chunk):
            table = b_tab if n < states else c_tab
            table[n % states] = jnp.broadcast_to(late[:, n : n + 1], (rows, LANES))
        weights = dtw_ref[:, c * wide * LANES : (c + 1) * wide * LANES]
        raw = jnp.dot(dt_low, weights, preferred_element_type=F32)
        for j in range(wide):
            tile = c * wide + j
            lanes = slice(tile * LANES, (tile + 1) * LANES)
            for first in range(0, rows, LANES):
                here = slice(first, first + LANES)
                dt = softplus(raw[here, j * LANES : (j + 1) * LANES] + dtb_ref[:, lanes])
                mixed = mixed_ref[here, lanes]
                if first == 0:
                    mixed = jnp.concatenate([head_ref[:, lanes], mixed[head:]], axis=0)
                mixed = mixed.astype(F32)
                dt_v[tile, here, :] = dt
                drive_v[tile, here, :] = dt * mixed
                y_v[tile, here, :] = skip_ref[:, lanes] * mixed
    a_v[...] = jnp.exp(al_ref[...]) * (-LOG2E)

    me = lax.axis_index("replica")
    for copy in int_copies:
        copy.wait()
    places, slot_ids, lengths = request_places(dims, ints, me)
    for r in range(per_dev):
        spot = pl.ds(pl.multiple_of(slot_ids[r] * states, states), states)
        for tile in range(n_tiles):
            lanes = slice(tile * LANES, (tile + 1) * LANES)
            if n_pieces == 1:
                value = pieces[0][places[r], spot, lanes]
            else:
                value = pieces[0][spot, lanes]
                for p in range(1, n_pieces):
                    value = jnp.where(places[r] == p, pieces[p][spot, lanes], value)
            value = value.astype(F32)
            value = jnp.where(lengths[r] > 0, value, jnp.zeros_like(value))
            start_tm[tile, pl.ds(r, states, stride=per_dev), :] = value

    tiles = 2
    half = states // 2
    width = 2 * tiles * LANES
    n_chunks = channels // width

    def out_copies(c):
        lanes = pl.ds(pl.multiple_of(c * width, width), width)
        return [
            pltpu.make_async_copy(src.at[:, lanes], dst.at[:, lanes], out_sems.at[i, c])
            for i, (src, dst) in enumerate(((out_v, out_hbm), (state_v, state_hbm)))
        ]

    def scan_group(g, carry):
        group = [g * tiles + j for j in range(tiles)]
        lanes = [pl.ds(pl.multiple_of(tile * LANES, LANES), LANES) for tile in group]
        for first in range(0, states, half):
            ids = range(first, first + half)
            rates = [[jnp.broadcast_to(a_v[n : n + 1, lane], (per_dev, LANES)) for n in ids] for lane in lanes]

            def advance(step, state):
                state = list(state)
                for u in range(UNROLL):
                    now = pl.ds(pl.multiple_of((step * UNROLL + u) * per_dev, per_dev), per_dev)
                    dt = [dt_v[tile, now, :] for tile in group]
                    drive = [drive_v[tile, now, :] for tile in group]
                    sums = [None] * tiles
                    for k, n in enumerate(ids):
                        b, c = b_tab[n, now, :], c_tab[n, now, :]
                        for j in range(tiles):
                            i = j * half + k
                            state[i] = jnp.exp2(dt[j] * rates[j][k]) * state[i] + drive[j] * b
                            term = state[i] * c
                            sums[j] = term if sums[j] is None else sums[j] + term
                    for j, tile in enumerate(group):
                        y_v[tile, now, :] += sums[j]
                return tuple(state)

            state = tuple(start_tm[tile, n * per_dev : (n + 1) * per_dev, :] for tile in group for n in ids)
            state = lax.fori_loop(0, NEW // UNROLL, advance, state)
            for j, tile in enumerate(group):
                for k, n in enumerate(ids):
                    final_tm[tile, n * per_dev : (n + 1) * per_dev, :] = state[j * half + k]
        return carry

    def one_chunk(c, carry):
        lax.fori_loop(c * 2, c * 2 + 2, scan_group, 0)
        for j in range(width // LANES):
            tile = c * (width // LANES) + j
            lanes = pl.ds(pl.multiple_of(tile * LANES, LANES), LANES)
            for r in range(per_dev):
                here = slice(r * NEW, (r + 1) * NEW)
                value = y_v[tile, pl.ds(r, NEW, stride=per_dev), :] * silu(z_ref[here, lanes].astype(F32))
                out_v[here, lanes] = value.astype(BF16)
                final = final_tm[tile, pl.ds(r, states, stride=per_dev), :]
                state_v[r * states : (r + 1) * states, lanes] = final.astype(BF16)
        for copy in out_copies(c):
            copy.start()
        return carry

    lax.fori_loop(0, n_chunks, one_chunk, 0)

    def last_wait(c, carry):
        for copy in out_copies(c):
            copy.wait()
        return carry

    lax.fori_loop(0, n_chunks, last_wait, 0)


def split_refs(kernel, dims, n_in, n_out):
    def body(*refs):
        kernel(dims, refs[:n_in], refs[n_in : n_in + n_out], refs[n_in + n_out :])

    return body


def call(kernel, dims, name, limit, ins, outs, scratch):
    spaces = {"hbm": pltpu.HBM, "any": pl.ANY, "vmem": pltpu.VMEM, "smem": pltpu.SMEM}
    values = [
        pltpu.with_memory_space_constraint(value, pltpu.HBM) if place == "hbm" else value for value, place in ins
    ]
    return pl.pallas_call(
        split_refs(kernel, dims, len(ins), len(outs)),
        in_specs=[pl.BlockSpec(memory_space=spaces[place]) for _, place in ins],
        out_specs=[pl.BlockSpec(memory_space=spaces[place]) for _, _, place in outs],
        out_shape=[jax.ShapeDtypeStruct(shape, dtype) for shape, dtype, _ in outs],
        scratch_shapes=scratch,
        compiler_params=pltpu.CompilerParams(vmem_limit_bytes=limit * MIB),
        name=name,
    )(*values)


def swap(value, axis, size, mask):
    return lax.ppermute(value, axis, [(i, i ^ mask) for i in range(size)])


def shards(mesh, x_new, z_new, conv_weight, conv_bias, x_proj_weight, dt_proj_weight, dt_bias, a_log, d_skip,
           cache_ssm, cache_conv, holder, slot_id, prefix_len):
    n_replica, n_tensor = mesh.shape["replica"], mesh.shape["tensor"]
    rows, channels = x_new.shape
    per_dev = rows // NEW
    states = a_log.shape[0]
    rank = dt_proj_weight.shape[0]
    taps = conv_weight.shape[0]
    slots = cache_ssm.shape[0]
    out_cols = x_proj_weight.shape[1]
    requests = holder.shape[0]

    vmem, dma = pltpu.VMEM, pltpu.SemaphoreType.DMA
    ssm_rows = slots * states
    rows_all, conv_rows = call(
        pack_kernel, (slots, taps), "pack", 20,
        [(cache_ssm.reshape(ssm_rows, channels), "hbm"), (cache_conv.transpose(1, 0, 2), "hbm")],
        [((ssm_rows + slots * taps, channels), BF16, "vmem"), ((slots * taps, channels), BF16, "vmem")],
        [vmem((taps - 1, slots, channels), BF16), dma((2,))],
    )
    block = rows_all.shape[0]
    relative = n_replica == 4
    if relative:
        far = swap(rows_all, "replica", n_replica, 3)
        near = swap(rows_all, "replica", n_replica, 1)
        conv_two = swap(conv_rows, "replica", n_replica, 2)
        conv_pieces = [rows_all, near, far, conv_two]
        firsts = (0, block, 2 * block, 4 * block - slots * taps)
        ssm_pieces = [rows_all, near, far, swap(far, "replica", n_replica, 1)]
    else:
        ssm_pieces = [lax.all_gather(rows_all, "replica")]
        conv_pieces, firsts = [ssm_pieces[0].reshape(-1, channels)], (0,)

    n_chunks = channels // min(512, channels)
    dims = (per_dev, n_replica, slots, relative)
    head = per_dev * taps
    weights = x_proj_weight.T
    requests = [(holder, "smem"), (slot_id, "smem"), (prefix_len, "smem")]

    mixed, head_sums, part = call(
        project_kernel, per_dev, "conv_project", 40,
        [(x_new, "hbm"), (weights, "hbm"), (conv_weight, "hbm"), (conv_bias[None, :], "hbm")],
        [((rows, channels), BF16, "any"), ((head, channels), F32, "any"), ((out_cols, rows), BF16, "any")],
        [
            vmem((rows, channels), BF16),
            vmem((out_cols, channels), BF16),
            vmem((taps, channels), BF16),
            vmem((1, channels), F32),
            vmem((channels // LANES, rows + taps * per_dev, LANES), F32),
            vmem((rows, channels), BF16),
            vmem((head, channels), F32),
            vmem((out_cols, rows), F32),
            vmem((out_cols, rows), BF16),
            dma((2 + 2 * n_chunks,)),
            dma((n_chunks + 2,)),
        ],
    )
    mixed_head, part = call(
        history_kernel, (dims, block, firsts), "history", 20,
        requests
        + [(value, "vmem") for value in [head_sums, part, weights, conv_weight] + conv_pieces],
        [((head, channels), BF16, "vmem"), ((out_cols, rows), BF16, "vmem")],
        [],
    )
    parts = [part]
    mask = n_tensor // 2
    while mask:
        parts = parts + [swap(value, "tensor", n_tensor, mask) for value in reversed(parts)]
        mask //= 2

    n_tiles = channels // LANES
    operands = [mixed, mixed_head, z_new, dt_proj_weight, dt_bias[None, :], a_log, d_skip[None, :]]
    out, state = call(
        scan_kernel, dims, "dt_scan_gate", 40,
        [(value, "any") for value, _ in requests] + [(value, "vmem") for value in operands + parts + ssm_pieces],
        [((rows, channels), BF16, "any"), ((per_dev * states, channels), BF16, "any")],
        [
            vmem((states, rows, LANES), F32),
            vmem((states, rows, LANES), F32),
            vmem((n_tiles, rows, LANES), F32),
            vmem((n_tiles, rows, LANES), F32),
            vmem((states, channels), F32),
            vmem((n_tiles, per_dev * (states + 1), LANES), F32),
            vmem((n_tiles, per_dev * (states + 1), LANES), F32),
            vmem((n_tiles, rows + per_dev, LANES), F32),
            vmem((rows, channels), BF16),
            vmem((per_dev * states, channels), BF16),
            dma((2, n_chunks)),
            dma((3,)),
        ] + [pltpu.SMEM(holder.shape, jnp.int32)] * 3,
    )
    return out, state.reshape(per_dev, states, channels)


def solution(mesh):
    placed = (
        P(("groups", "replica"), "tensor"),
        P(("groups", "replica"), "tensor"),
        P(None, "tensor"),
        P("tensor"),
        P("tensor", None),
        P(None, "tensor"),
        P("tensor"),
        P(None, "tensor"),
        P("tensor"),
        P(("groups", "replica"), None, "tensor"),
        P(("groups", "replica"), None, "tensor"),
        P("groups"),
        P("groups"),
        P("groups"),
    )
    return jax.shard_map(
        functools.partial(shards, mesh),
        mesh=mesh,
        in_specs=placed,
        out_specs=(P(("groups", "replica"), "tensor"), P(("groups", "replica"), None, "tensor")),
        check_vma=False,
    )
```

```python
import functools

import jax
import jax.numpy as jnp
from jax import lax
from jax.experimental import pallas as pl
from jax.experimental.pallas import tpu as pltpu
from jax.sharding import PartitionSpec as P

NEW = 32
LANES = 128
MIB = 1024 * 1024
UNROLL = 32
LOG2E = 1.4426950408889634
F32, BF16 = jnp.float32, jnp.bfloat16
NT = (((1,), (1,)), ((), ()))


def silu(v):
    half = 0.5 * v
    return half + half * jnp.tanh(half)


def softplus(v):
    u = jnp.exp2(jnp.abs(v) * -LOG2E)
    return jnp.maximum(v, 0.0) + jnp.where(u < 2.0**-10, u - 0.5 * (u * u), jnp.log(1.0 + u))


def split_index(value, inner):
    assert inner & (inner - 1) == 0
    return value >> (inner.bit_length() - 1), value & (inner - 1)


def pick_rows(values, row_low, count):
    out = jnp.zeros(row_low.shape, jnp.int32)
    for r in range(count):
        out = jnp.where(row_low == r, values[r], out)
    return out


def request_places(dims, ints, me):
    per_dev, n_replica, _, relative = dims
    places, slot_ids, lengths = [], [], []
    for r in range(per_dev):
        request = me * per_dev + r
        place = ints[0][request]
        if relative:
            place = place ^ me
            place = place ^ (place >> 1)
        places.append(place)
        slot_ids.append(ints[1][request])
        lengths.append(ints[2][request])
    return places, slot_ids, lengths


def fetch_rows(target, live, pieces):
    total = None
    for first, value in pieces:
        col = lax.broadcasted_iota(jnp.int32, (target.shape[0], value.shape[0]), 1) + first
        select = jnp.where((col == target) & live, 1.0, 0.0).astype(BF16)
        part = jnp.dot(select, value, preferred_element_type=F32)
        total = part if total is None else total + part
    return total


def pack_kernel(dims, refs_in, refs_out, scratch):
    slots, taps = dims
    ssm_hbm, conv_hbm = refs_in
    block_ref, conv_ref = refs_out
    conv_v, sems = scratch
    states = pltpu.make_async_copy(ssm_hbm, block_ref.at[: ssm_hbm.shape[0]], sems.at[0])
    inputs = pltpu.make_async_copy(conv_hbm, conv_v, sems.at[1])
    states.start()
    inputs.start()
    inputs.wait()
    lines = []
    for slot in range(slots):
        for tap in range(taps):
            line = conv_v[min(tap, taps - 2)].astype(F32)[slot : slot + 1]
            lines.append(line if tap < taps - 1 else jnp.zeros_like(line))
    rows = jnp.concatenate(lines, axis=0).astype(BF16)
    conv_ref[...] = rows
    block_ref[ssm_hbm.shape[0] :, :] = rows
    states.wait()


def project_kernel(dims, refs_in, refs_out, scratch):
    per_dev = dims
    x_hbm, wt_hbm, cw_hbm, cb_hbm = refs_in
    mixed_hbm, head_hbm, part_hbm = refs_out
    x_v, wt_v, cw_v, cb_v, joined, mixed_v, head_v, part_f, part_v, sems, out_sems = scratch
    rows, channels = x_v.shape
    taps = cw_v.shape[0]
    lines = (taps - 1) * per_dev
    pairs = [(cw_hbm, cw_v), (cb_hbm, cb_v)]
    width = min(512, channels)
    chunks = [slice(c * width, (c + 1) * width) for c in range(channels // width)]
    for chunk in chunks:
        pairs += [(x_hbm.at[:, chunk], x_v.at[:, chunk]), (wt_hbm.at[:, chunk], wt_v.at[:, chunk])]
    copies = [pltpu.make_async_copy(src, dst, sems.at[i]) for i, (src, dst) in enumerate(pairs)]
    for copy in copies:
        copy.start()

    joined[:, :lines, :] = jnp.zeros((channels // LANES, lines, LANES), F32)
    copies[0].wait()
    copies[1].wait()
    outs = []
    for c, chunk in enumerate(chunks):
        copies[2 + 2 * c].wait()
        for tile in range(c * width // LANES, (c + 1) * width // LANES):
            lanes = slice(tile * LANES, (tile + 1) * LANES)
            for r in range(per_dev):
                tokens = x_v[r * NEW : (r + 1) * NEW, lanes].astype(F32)
                joined[tile, pl.ds(lines + r, NEW, stride=per_dev), :] = tokens
            weight = [cw_v[k : k + 1, lanes].astype(F32) for k in range(taps)]
            bias = cb_v[:, lanes]
            for first in range(0, rows, LANES):
                summed = bias + joined[tile, first : first + LANES, :] * weight[0]
                for k in range(1, taps):
                    begin = first + k * per_dev
                    summed = summed + joined[tile, begin : begin + LANES, :] * weight[k]
                if first == 0:
                    head_v[:, lanes] = summed[: head_v.shape[0]]
                mixed_v[first : first + LANES, lanes] = silu(summed).astype(BF16)
        copies[3 + 2 * c].wait()
        part = lax.dot_general(wt_v[:, chunk], mixed_v[:, chunk], NT, preferred_element_type=F32)
        if c == 0:
            part_f[...] = part
        else:
            part_f[...] += part
        outs.append(pltpu.make_async_copy(mixed_v.at[:, chunk], mixed_hbm.at[:, chunk], out_sems.at[c]))
        outs[-1].start()
    part_v[...] = part_f[...].astype(BF16)
    for src, dst in ((part_v, part_hbm), (head_v, head_hbm)):
        outs.append(pltpu.make_async_copy(src, dst, out_sems.at[len(outs)]))
        outs[-1].start()
    for copy in outs:
        copy.wait()


def history_kernel(dims, refs_in, refs_out, scratch):
    dims, block, firsts = dims
    per_dev, n_replica, slots, _ = dims
    holder, slot_id, prefix_len, head_ref, part_ref, wt_ref, cw_ref = refs_in[:7]
    pieces = refs_in[7:]
    mixed_ref, fixed_ref = refs_out
    taps = cw_ref.shape[0]
    me = lax.axis_index("replica")
    places, slot_ids, lengths = request_places(dims, (holder, slot_id, prefix_len), me)
    tap, request = split_index(lax.broadcasted_iota(jnp.int32, (per_dev * taps, 1), 0), per_dev)
    starts = [places[r] * block + (block - slots * taps) + slot_ids[r] * taps for r in range(per_dev)]
    target = pick_rows(starts, request, per_dev) + tap
    live = (tap < taps - 1) & (taps - 1 - tap <= pick_rows(lengths, request, per_dev))
    history = fetch_rows(target, live, [(first, ref[...]) for first, ref in zip(firsts, pieces)])
    sums = []
    for t in range(taps):
        summed = head_ref[t * per_dev : (t + 1) * per_dev]
        for k in range(taps - 1 - t):
            weight = cw_ref[k : k + 1].astype(F32)
            summed = summed + history[(t + k) * per_dev : (t + k + 1) * per_dev] * weight
        sums.append(summed)
    mixed = silu(jnp.concatenate(sums, axis=0)).astype(BF16)
    mixed_ref[...] = mixed
    part = lax.dot_general(wt_ref[...], mixed, NT, preferred_element_type=F32)
    fixed_ref[...] = part_ref[...]
    fixed_ref[:, : per_dev * taps] = part.astype(BF16)


def scan_kernel(dims, refs_in, refs_out, scratch):
    per_dev, n_replica, _, _ = dims
    mixed_ref, head_ref, z_ref, dtw_ref, dtb_ref, al_ref, skip_ref = refs_in[3:10]
    out_hbm, state_hbm = refs_out
    b_tab, c_tab, dt_v, drive_v, a_v, start_tm, final_tm, y_v, out_v, state_v, out_sems, int_sems = scratch[:12]
    ints = scratch[12:]
    int_copies = [pltpu.make_async_copy(refs_in[i], ints[i], int_sems.at[i]) for i in range(len(ints))]
    for copy in int_copies:
        copy.start()
    n_pieces = sum(1 for ref in refs_in[10:] if ref.shape[-1] == z_ref.shape[1])
    parts, pieces = refs_in[10:-n_pieces], refs_in[-n_pieces:]
    rows, channels = z_ref.shape
    states = al_ref.shape[0]
    rank = dtw_ref.shape[0]
    head = head_ref.shape[0]

    projected = parts[0][...].astype(F32)
    for part in parts[1:]:
        projected = projected + part[...].astype(F32)
    projected = projected.T
    dt_low = projected[:, :rank].astype(BF16)
    late = projected[:, rank:]
    n_tiles = channels // LANES
    wide = min(4, n_tiles)
    per_chunk = 2 * states * wide // n_tiles
    for c in range(n_tiles // wide):
        for n in range(c * per_chunk, (c + 1) * per_chunk):
            table = b_tab if n < states else c_tab
            table[n % states] = jnp.broadcast_to(late[:, n : n + 1], (rows, LANES))
        weights = dtw_ref[:, c * wide * LANES : (c + 1) * wide * LANES]
        raw = jnp.dot(dt_low, weights, preferred_element_type=F32)
        for j in range(wide):
            tile = c * wide + j
            lanes = slice(tile * LANES, (tile + 1) * LANES)
            for first in range(0, rows, LANES):
                here = slice(first, first + LANES)
                dt = softplus(raw[here, j * LANES : (j + 1) * LANES] + dtb_ref[:, lanes])
                mixed = mixed_ref[here, lanes]
                if first == 0:
                    mixed = jnp.concatenate([head_ref[:, lanes], mixed[head:]], axis=0)
                mixed = mixed.astype(F32)
                dt_v[tile, here, :] = dt
                drive_v[tile, here, :] = dt * mixed
                y_v[tile, here, :] = skip_ref[:, lanes] * mixed
    a_v[...] = jnp.exp(al_ref[...]) * (-LOG2E)

    me = lax.axis_index("replica")
    for copy in int_copies:
        copy.wait()
    places, slot_ids, lengths = request_places(dims, ints, me)
    for r in range(per_dev):
        spot = pl.ds(pl.multiple_of(slot_ids[r] * states, states), states)
        for tile in range(n_tiles):
            lanes = slice(tile * LANES, (tile + 1) * LANES)
            if n_pieces == 1:
                value = pieces[0][places[r], spot, lanes]
            else:
                value = pieces[0][spot, lanes]
                for p in range(1, n_pieces):
                    value = jnp.where(places[r] == p, pieces[p][spot, lanes], value)
            value = value.astype(F32)
            value = jnp.where(lengths[r] > 0, value, jnp.zeros_like(value))
            start_tm[tile, pl.ds(r, states, stride=per_dev), :] = value

    tiles = 2
    half = states // 2
    width = tiles * LANES
    n_groups = n_tiles // tiles

    def out_copies(g):
        lanes = pl.ds(pl.multiple_of(g * width, width), width)
        return [
            pltpu.make_async_copy(src.at[:, lanes], dst.at[:, lanes], out_sems.at[i, g])
            for i, (src, dst) in enumerate(((out_v, out_hbm), (state_v, state_hbm)))
        ]

    def finish(g):
        for j in range(tiles):
            tile = g * tiles + j
            lanes = pl.ds(pl.multiple_of(tile * LANES, LANES), LANES)
            for r in range(per_dev):
                here = slice(r * NEW, (r + 1) * NEW)
                value = y_v[tile, pl.ds(r, NEW, stride=per_dev), :] * silu(z_ref[here, lanes].astype(F32))
                out_v[here, lanes] = value.astype(BF16)
                final = final_tm[tile, pl.ds(r, states, stride=per_dev), :]
                state_v[r * states : (r + 1) * states, lanes] = final.astype(BF16)

    def scan_group(g):
        group = [g * tiles + j for j in range(tiles)]
        lanes = [pl.ds(pl.multiple_of(tile * LANES, LANES), LANES) for tile in group]
        for first in range(0, states, half):
            ids = range(first, first + half)
            rates = [[jnp.broadcast_to(a_v[n : n + 1, lane], (per_dev, LANES)) for n in ids] for lane in lanes]

            def advance(step, state):
                state = list(state)
                for u in range(UNROLL):
                    now = pl.ds(pl.multiple_of((step * UNROLL + u) * per_dev, per_dev), per_dev)
                    dt = [dt_v[tile, now, :] for tile in group]
                    drive = [drive_v[tile, now, :] for tile in group]
                    sums = [None] * tiles
                    for k, n in enumerate(ids):
                        b, c = b_tab[n, now, :], c_tab[n, now, :]
                        for j in range(tiles):
                            i = j * half + k
                            state[i] = jnp.exp2(dt[j] * rates[j][k]) * state[i] + drive[j] * b
                            term = state[i] * c
                            sums[j] = term if sums[j] is None else sums[j] + term
                    for j, tile in enumerate(group):
                        y_v[tile, now, :] += sums[j]
                return tuple(state)

            state = tuple(start_tm[tile, n * per_dev : (n + 1) * per_dev, :] for tile in group for n in ids)
            if NEW == UNROLL:
                state = advance(0, state)
            else:
                state = lax.fori_loop(0, NEW // UNROLL, advance, state)
            for j, tile in enumerate(group):
                for k, n in enumerate(ids):
                    final_tm[tile, n * per_dev : (n + 1) * per_dev, :] = state[j * half + k]

    def one_group(g, carry):
        before = jnp.maximum(g - 1, 0)
        finish(before)
        scan_group(g)

        @pl.when(g > 0)
        def _():
            for copy in out_copies(before):
                copy.start()

        return carry

    final_tm[:tiles] = jnp.zeros((tiles,) + final_tm.shape[1:], F32)
    lax.fori_loop(0, n_groups, one_group, 0)
    finish(n_groups - 1)
    for copy in out_copies(n_groups - 1):
        copy.start()

    def last_wait(g, carry):
        for copy in out_copies(g):
            copy.wait()
        return carry

    lax.fori_loop(0, n_groups, last_wait, 0)


def split_refs(kernel, dims, n_in, n_out):
    def body(*refs):
        kernel(dims, refs[:n_in], refs[n_in : n_in + n_out], refs[n_in + n_out :])

    return body


def call(kernel, dims, name, limit, ins, outs, scratch):
    spaces = {"hbm": pltpu.HBM, "any": pl.ANY, "vmem": pltpu.VMEM, "smem": pltpu.SMEM}
    values = [
        pltpu.with_memory_space_constraint(value, pltpu.HBM) if place == "hbm" else value for value, place in ins
    ]
    return pl.pallas_call(
        split_refs(kernel, dims, len(ins), len(outs)),
        in_specs=[pl.BlockSpec(memory_space=spaces[place]) for _, place in ins],
        out_specs=[pl.BlockSpec(memory_space=spaces[place]) for _, _, place in outs],
        out_shape=[jax.ShapeDtypeStruct(shape, dtype) for shape, dtype, _ in outs],
        scratch_shapes=scratch,
        compiler_params=pltpu.CompilerParams(vmem_limit_bytes=limit * MIB),
        name=name,
    )(*values)


def swap(value, axis, size, mask):
    return lax.ppermute(value, axis, [(i, i ^ mask) for i in range(size)])


def shards(mesh, x_new, z_new, conv_weight, conv_bias, x_proj_weight, dt_proj_weight, dt_bias, a_log, d_skip,
           cache_ssm, cache_conv, holder, slot_id, prefix_len):
    n_replica, n_tensor = mesh.shape["replica"], mesh.shape["tensor"]
    rows, channels = x_new.shape
    per_dev = rows // NEW
    states = a_log.shape[0]
    rank = dt_proj_weight.shape[0]
    taps = conv_weight.shape[0]
    slots = cache_ssm.shape[0]
    out_cols = x_proj_weight.shape[1]
    requests = holder.shape[0]

    vmem, dma = pltpu.VMEM, pltpu.SemaphoreType.DMA
    ssm_rows = slots * states
    rows_all, conv_rows = call(
        pack_kernel, (slots, taps), "pack", 20,
        [(cache_ssm.reshape(ssm_rows, channels), "hbm"), (cache_conv.transpose(1, 0, 2), "hbm")],
        [((ssm_rows + slots * taps, channels), BF16, "vmem"), ((slots * taps, channels), BF16, "vmem")],
        [vmem((taps - 1, slots, channels), BF16), dma((2,))],
    )
    block = rows_all.shape[0]
    relative = n_replica == 4
    if relative:
        far = swap(rows_all, "replica", n_replica, 3)
        near = swap(rows_all, "replica", n_replica, 1)
        conv_two = swap(conv_rows, "replica", n_replica, 2)
        conv_pieces = [rows_all, near, far, conv_two]
        firsts = (0, block, 2 * block, 4 * block - slots * taps)
        ssm_pieces = [rows_all, near, far, swap(far, "replica", n_replica, 1)]
    else:
        ssm_pieces = [lax.all_gather(rows_all, "replica")]
        conv_pieces, firsts = [ssm_pieces[0].reshape(-1, channels)], (0,)

    n_chunks = channels // min(512, channels)
    dims = (per_dev, n_replica, slots, relative)
    head = per_dev * taps
    weights = x_proj_weight.T
    requests = [(holder, "smem"), (slot_id, "smem"), (prefix_len, "smem")]

    mixed, head_sums, part = call(
        project_kernel, per_dev, "conv_project", 40,
        [(x_new, "hbm"), (weights, "hbm"), (conv_weight, "hbm"), (conv_bias[None, :], "hbm")],
        [((rows, channels), BF16, "any"), ((head, channels), F32, "any"), ((out_cols, rows), BF16, "any")],
        [
            vmem((rows, channels), BF16),
            vmem((out_cols, channels), BF16),
            vmem((taps, channels), BF16),
            vmem((1, channels), F32),
            vmem((channels // LANES, rows + taps * per_dev, LANES), F32),
            vmem((rows, channels), BF16),
            vmem((head, channels), F32),
            vmem((out_cols, rows), F32),
            vmem((out_cols, rows), BF16),
            dma((2 + 2 * n_chunks,)),
            dma((n_chunks + 2,)),
        ],
    )
    mixed_head, part = call(
        history_kernel, (dims, block, firsts), "history", 20,
        requests
        + [(value, "vmem") for value in [head_sums, part, weights, conv_weight] + conv_pieces],
        [((head, channels), BF16, "vmem"), ((out_cols, rows), BF16, "vmem")],
        [],
    )
    parts = [part]
    mask = n_tensor // 2
    while mask:
        parts = parts + [swap(value, "tensor", n_tensor, mask) for value in reversed(parts)]
        mask //= 2

    n_tiles = channels // LANES
    operands = [mixed, mixed_head, z_new, dt_proj_weight, dt_bias[None, :], a_log, d_skip[None, :]]
    out, state = call(
        scan_kernel, dims, "dt_scan_gate", 40,
        [(value, "any") for value, _ in requests] + [(value, "vmem") for value in operands + parts + ssm_pieces],
        [((rows, channels), BF16, "any"), ((per_dev * states, channels), BF16, "any")],
        [
            vmem((states, rows, LANES), F32),
            vmem((states, rows, LANES), F32),
            vmem((n_tiles, rows, LANES), F32),
            vmem((n_tiles, rows, LANES), F32),
            vmem((states, channels), F32),
            vmem((n_tiles, per_dev * (states + 1), LANES), F32),
            vmem((n_tiles, per_dev * (states + 1), LANES), F32),
            vmem((n_tiles, rows + per_dev, LANES), F32),
            vmem((rows, channels), BF16),
            vmem((per_dev * states, channels), BF16),
            dma((2, n_tiles // 2)),
            dma((3,)),
        ] + [pltpu.SMEM(holder.shape, jnp.int32)] * 3,
    )
    return out, state.reshape(per_dev, states, channels)


def solution(mesh):
    placed = (
        P(("groups", "replica"), "tensor"),
        P(("groups", "replica"), "tensor"),
        P(None, "tensor"),
        P("tensor"),
        P("tensor", None),
        P(None, "tensor"),
        P("tensor"),
        P(None, "tensor"),
        P("tensor"),
        P(("groups", "replica"), None, "tensor"),
        P(("groups", "replica"), None, "tensor"),
        P("groups"),
        P("groups"),
        P("groups"),
    )
    return jax.shard_map(
        functools.partial(shards, mesh),
        mesh=mesh,
        in_specs=placed,
        out_specs=(P(("groups", "replica"), "tensor"), P(("groups", "replica"), None, "tensor")),
        check_vma=False,
    )
```

```python
import functools

import jax
import jax.numpy as jnp
from jax import lax
from jax.experimental import pallas as pl
from jax.experimental.pallas import tpu as pltpu
from jax.sharding import PartitionSpec as P

NEW = 32
LANES = 128
MIB = 1024 * 1024
UNROLL = 32
LOG2E = 1.4426950408889634
F32, BF16 = jnp.float32, jnp.bfloat16
NT = (((1,), (1,)), ((), ()))


def silu(v):
    half = 0.5 * v
    return half + half * jnp.tanh(half)


def softplus(v):
    u = jnp.exp2(jnp.abs(v) * -LOG2E)
    return jnp.maximum(v, 0.0) + jnp.where(u < 2.0**-10, u - 0.5 * (u * u), jnp.log(1.0 + u))


def split_index(value, inner):
    assert inner & (inner - 1) == 0
    return value >> (inner.bit_length() - 1), value & (inner - 1)


def pick_rows(values, row_low, count):
    out = jnp.zeros(row_low.shape, jnp.int32)
    for r in range(count):
        out = jnp.where(row_low == r, values[r], out)
    return out


def request_places(dims, ints, me):
    per_dev, n_replica, _, relative = dims
    places, slot_ids, lengths = [], [], []
    for r in range(per_dev):
        request = me * per_dev + r
        place = ints[0][request]
        if relative:
            place = place ^ me
            place = place ^ (place >> 1)
        places.append(place)
        slot_ids.append(ints[1][request])
        lengths.append(ints[2][request])
    return places, slot_ids, lengths


def fetch_rows(target, live, pieces):
    total = None
    for first, value in pieces:
        col = lax.broadcasted_iota(jnp.int32, (target.shape[0], value.shape[0]), 1) + first
        select = jnp.where((col == target) & live, 1.0, 0.0).astype(BF16)
        part = jnp.dot(select, value, preferred_element_type=F32)
        total = part if total is None else total + part
    return total


def pack_kernel(dims, refs_in, refs_out, scratch):
    slots, taps = dims
    ssm_hbm, conv_hbm = refs_in
    block_ref, conv_ref = refs_out
    conv_v, sems = scratch
    states = pltpu.make_async_copy(ssm_hbm, block_ref.at[: ssm_hbm.shape[0]], sems.at[0])
    inputs = pltpu.make_async_copy(conv_hbm, conv_v, sems.at[1])
    states.start()
    inputs.start()
    inputs.wait()
    lines = []
    for slot in range(slots):
        for tap in range(taps):
            line = conv_v[min(tap, taps - 2)].astype(F32)[slot : slot + 1]
            lines.append(line if tap < taps - 1 else jnp.zeros_like(line))
    rows = jnp.concatenate(lines, axis=0).astype(BF16)
    conv_ref[...] = rows
    block_ref[ssm_hbm.shape[0] :, :] = rows
    states.wait()


def project_kernel(dims, refs_in, refs_out, scratch):
    per_dev = dims
    x_hbm, wt_hbm, cw_hbm, cb_hbm = refs_in
    mixed_hbm, head_hbm, part_hbm = refs_out
    x_v, wt_v, cw_v, cb_v, joined, mixed_v, head_v, part_f, part_v, sems, out_sems = scratch
    rows, channels = x_v.shape
    taps = cw_v.shape[0]
    lines = (taps - 1) * per_dev
    pairs = [(cw_hbm, cw_v), (cb_hbm, cb_v)]
    width = min(512, channels)
    chunks = [slice(c * width, (c + 1) * width) for c in range(channels // width)]
    for chunk in chunks:
        pairs += [(x_hbm.at[:, chunk], x_v.at[:, chunk]), (wt_hbm.at[:, chunk], wt_v.at[:, chunk])]
    copies = [pltpu.make_async_copy(src, dst, sems.at[i]) for i, (src, dst) in enumerate(pairs)]
    for copy in copies:
        copy.start()

    joined[:, :lines, :] = jnp.zeros((channels // LANES, lines, LANES), F32)
    copies[0].wait()
    copies[1].wait()
    outs = []
    for c, chunk in enumerate(chunks):
        copies[2 + 2 * c].wait()
        for tile in range(c * width // LANES, (c + 1) * width // LANES):
            lanes = slice(tile * LANES, (tile + 1) * LANES)
            for r in range(per_dev):
                tokens = x_v[r * NEW : (r + 1) * NEW, lanes].astype(F32)
                joined[tile, pl.ds(lines + r, NEW, stride=per_dev), :] = tokens
            weight = [cw_v[k : k + 1, lanes].astype(F32) for k in range(taps)]
            bias = cb_v[:, lanes]
            for first in range(0, rows, LANES):
                summed = bias + joined[tile, first : first + LANES, :] * weight[0]
                for k in range(1, taps):
                    begin = first + k * per_dev
                    summed = summed + joined[tile, begin : begin + LANES, :] * weight[k]
                if first == 0:
                    head_v[:, lanes] = summed[: head_v.shape[0]]
                mixed_v[first : first + LANES, lanes] = silu(summed).astype(BF16)
        copies[3 + 2 * c].wait()
        part = lax.dot_general(wt_v[:, chunk], mixed_v[:, chunk], NT, preferred_element_type=F32)
        if c == 0:
            part_f[...] = part
        else:
            part_f[...] += part
        outs.append(pltpu.make_async_copy(mixed_v.at[:, chunk], mixed_hbm.at[:, chunk], out_sems.at[c]))
        outs[-1].start()
    part_v[...] = part_f[...].astype(BF16)
    for src, dst in ((part_v, part_hbm), (head_v, head_hbm)):
        outs.append(pltpu.make_async_copy(src, dst, out_sems.at[len(outs)]))
        outs[-1].start()
    for copy in outs:
        copy.wait()


def history_kernel(dims, refs_in, refs_out, scratch):
    dims, block, firsts = dims
    per_dev, n_replica, slots, _ = dims
    holder, slot_id, prefix_len, head_ref, wt_ref, cw_ref = refs_in[:6]
    pieces = refs_in[6:]
    mixed_ref, part_ref = refs_out
    taps = cw_ref.shape[0]
    me = lax.axis_index("replica")
    places, slot_ids, lengths = request_places(dims, (holder, slot_id, prefix_len), me)
    tap, request = split_index(lax.broadcasted_iota(jnp.int32, (per_dev * taps, 1), 0), per_dev)
    starts = [places[r] * block + (block - slots * taps) + slot_ids[r] * taps for r in range(per_dev)]
    target = pick_rows(starts, request, per_dev) + tap
    live = (tap < taps - 1) & (taps - 1 - tap <= pick_rows(lengths, request, per_dev))
    history = fetch_rows(target, live, [(first, ref[...]) for first, ref in zip(firsts, pieces)])
    sums = []
    for t in range(taps):
        summed = head_ref[t * per_dev : (t + 1) * per_dev]
        for k in range(taps - 1 - t):
            weight = cw_ref[k : k + 1].astype(F32)
            summed = summed + history[(t + k) * per_dev : (t + k + 1) * per_dev] * weight
        sums.append(summed)
    mixed = silu(jnp.concatenate(sums, axis=0)).astype(BF16)
    mixed_ref[...] = mixed
    part = lax.dot_general(wt_ref[...], mixed, NT, preferred_element_type=F32)
    part_ref[...] = part.T.astype(BF16)


def merge_kernel(dims, refs_in, refs_out, scratch):
    part_ref, across_ref, head_ref, head_across_ref = refs_in
    (sum_ref,) = refs_out
    head = head_ref[...].astype(F32) + head_across_ref[...].astype(F32)
    sum_ref[...] = (part_ref[...].astype(F32) + across_ref[...].astype(F32)).astype(BF16)
    sum_ref[:, : head_ref.shape[0]] = head.T.astype(BF16)


def scan_kernel(dims, refs_in, refs_out, scratch):
    per_dev, n_replica, _, _ = dims
    mixed_ref, head_ref, z_ref, dtw_ref, dtb_ref, al_ref, skip_ref = refs_in[3:10]
    out_hbm, state_hbm = refs_out
    b_tab, c_tab, dt_v, drive_v, a_v, start_tm, final_tm, y_v, out_v, state_v, out_sems, int_sems = scratch[:12]
    ints = scratch[12:]
    int_copies = [pltpu.make_async_copy(refs_in[i], ints[i], int_sems.at[i]) for i in range(len(ints))]
    for copy in int_copies:
        copy.start()
    n_pieces = sum(1 for ref in refs_in[10:] if ref.shape[-1] == z_ref.shape[1])
    parts, pieces = refs_in[10:-n_pieces], refs_in[-n_pieces:]
    rows, channels = z_ref.shape
    states = al_ref.shape[0]
    rank = dtw_ref.shape[0]
    head = head_ref.shape[0]

    projected = parts[0][...].astype(F32)
    for part in parts[1:]:
        projected = projected + part[...].astype(F32)
    projected = projected.T
    dt_low = projected[:, :rank].astype(BF16)
    late = projected[:, rank:]
    n_tiles = channels // LANES
    wide = min(4, n_tiles)
    per_chunk = 2 * states * wide // n_tiles
    for c in range(n_tiles // wide):
        for n in range(c * per_chunk, (c + 1) * per_chunk):
            table = b_tab if n < states else c_tab
            table[n % states] = jnp.broadcast_to(late[:, n : n + 1], (rows, LANES))
        weights = dtw_ref[:, c * wide * LANES : (c + 1) * wide * LANES]
        raw = jnp.dot(dt_low, weights, preferred_element_type=F32)
        for j in range(wide):
            tile = c * wide + j
            lanes = slice(tile * LANES, (tile + 1) * LANES)
            for first in range(0, rows, LANES):
                here = slice(first, first + LANES)
                dt = softplus(raw[here, j * LANES : (j + 1) * LANES] + dtb_ref[:, lanes])
                mixed = mixed_ref[here, lanes]
                if first == 0:
                    mixed = jnp.concatenate([head_ref[:, lanes], mixed[head:]], axis=0)
                mixed = mixed.astype(F32)
                dt_v[tile, here, :] = dt
                drive_v[tile, here, :] = dt * mixed
                y_v[tile, here, :] = skip_ref[:, lanes] * mixed
    a_v[...] = jnp.exp(al_ref[...]) * (-LOG2E)

    me = lax.axis_index("replica")
    for copy in int_copies:
        copy.wait()
    places, slot_ids, lengths = request_places(dims, ints, me)
    for r in range(per_dev):
        spot = pl.ds(pl.multiple_of(slot_ids[r] * states, states), states)
        for tile in range(n_tiles):
            lanes = slice(tile * LANES, (tile + 1) * LANES)
            if n_pieces == 1:
                value = pieces[0][places[r], spot, lanes]
            else:
                value = pieces[0][spot, lanes]
                for p in range(1, n_pieces):
                    value = jnp.where(places[r] == p, pieces[p][spot, lanes], value)
            value = value.astype(F32)
            value = jnp.where(lengths[r] > 0, value, jnp.zeros_like(value))
            start_tm[tile, pl.ds(r, states, stride=per_dev), :] = value

    tiles = 2
    half = states // 2
    width = tiles * LANES
    n_groups = n_tiles // tiles

    def out_copies(g):
        lanes = pl.ds(pl.multiple_of(g * width, width), width)
        return [
            pltpu.make_async_copy(src.at[:, lanes], dst.at[:, lanes], out_sems.at[i, g])
            for i, (src, dst) in enumerate(((out_v, out_hbm), (state_v, state_hbm)))
        ]

    def finish(g):
        for j in range(tiles):
            tile = g * tiles + j
            lanes = pl.ds(pl.multiple_of(tile * LANES, LANES), LANES)
            for r in range(per_dev):
                here = slice(r * NEW, (r + 1) * NEW)
                value = y_v[tile, pl.ds(r, NEW, stride=per_dev), :] * silu(z_ref[here, lanes].astype(F32))
                out_v[here, lanes] = value.astype(BF16)
                final = final_tm[tile, pl.ds(r, states, stride=per_dev), :]
                state_v[r * states : (r + 1) * states, lanes] = final.astype(BF16)

    def scan_group(g):
        group = [g * tiles + j for j in range(tiles)]
        lanes = [pl.ds(pl.multiple_of(tile * LANES, LANES), LANES) for tile in group]
        for first in range(0, states, half):
            ids = range(first, first + half)
            rates = [[jnp.broadcast_to(a_v[n : n + 1, lane], (per_dev, LANES)) for n in ids] for lane in lanes]

            def advance(step, state):
                state = list(state)
                for u in range(UNROLL):
                    now = pl.ds(pl.multiple_of((step * UNROLL + u) * per_dev, per_dev), per_dev)
                    dt = [dt_v[tile, now, :] for tile in group]
                    drive = [drive_v[tile, now, :] for tile in group]
                    sums = [None] * tiles
                    for k, n in enumerate(ids):
                        b, c = b_tab[n, now, :], c_tab[n, now, :]
                        for j in range(tiles):
                            i = j * half + k
                            state[i] = jnp.exp2(dt[j] * rates[j][k]) * state[i] + drive[j] * b
                            term = state[i] * c
                            sums[j] = term if sums[j] is None else sums[j] + term
                    for j, tile in enumerate(group):
                        y_v[tile, now, :] += sums[j]
                return tuple(state)

            state = tuple(start_tm[tile, n * per_dev : (n + 1) * per_dev, :] for tile in group for n in ids)
            if NEW == UNROLL:
                state = advance(0, state)
            else:
                state = lax.fori_loop(0, NEW // UNROLL, advance, state)
            for j, tile in enumerate(group):
                for k, n in enumerate(ids):
                    final_tm[tile, n * per_dev : (n + 1) * per_dev, :] = state[j * half + k]

    def one_group(g, carry):
        before = jnp.maximum(g - 1, 0)
        finish(before)
        scan_group(g)

        @pl.when(g > 0)
        def _():
            for copy in out_copies(before):
                copy.start()

        return carry

    final_tm[:tiles] = jnp.zeros((tiles,) + final_tm.shape[1:], F32)
    lax.fori_loop(0, n_groups, one_group, 0)
    finish(n_groups - 1)
    for copy in out_copies(n_groups - 1):
        copy.start()

    def last_wait(g, carry):
        for copy in out_copies(g):
            copy.wait()
        return carry

    lax.fori_loop(0, n_groups, last_wait, 0)


def split_refs(kernel, dims, n_in, n_out):
    def body(*refs):
        kernel(dims, refs[:n_in], refs[n_in : n_in + n_out], refs[n_in + n_out :])

    return body


def call(kernel, dims, name, limit, ins, outs, scratch):
    spaces = {"hbm": pltpu.HBM, "any": pl.ANY, "vmem": pltpu.VMEM, "smem": pltpu.SMEM}
    values = [
        pltpu.with_memory_space_constraint(value, pltpu.HBM) if place == "hbm" else value for value, place in ins
    ]
    return pl.pallas_call(
        split_refs(kernel, dims, len(ins), len(outs)),
        in_specs=[pl.BlockSpec(memory_space=spaces[place]) for _, place in ins],
        out_specs=[pl.BlockSpec(memory_space=spaces[place]) for _, _, place in outs],
        out_shape=[jax.ShapeDtypeStruct(shape, dtype) for shape, dtype, _ in outs],
        scratch_shapes=scratch,
        compiler_params=pltpu.CompilerParams(vmem_limit_bytes=limit * MIB),
        name=name,
    )(*values)


def swap(value, axis, size, mask):
    return lax.ppermute(value, axis, [(i, i ^ mask) for i in range(size)])


def shards(mesh, x_new, z_new, conv_weight, conv_bias, x_proj_weight, dt_proj_weight, dt_bias, a_log, d_skip,
           cache_ssm, cache_conv, holder, slot_id, prefix_len):
    n_replica, n_tensor = mesh.shape["replica"], mesh.shape["tensor"]
    rows, channels = x_new.shape
    per_dev = rows // NEW
    states = a_log.shape[0]
    rank = dt_proj_weight.shape[0]
    taps = conv_weight.shape[0]
    slots = cache_ssm.shape[0]
    out_cols = x_proj_weight.shape[1]
    requests = holder.shape[0]

    vmem, dma = pltpu.VMEM, pltpu.SemaphoreType.DMA
    ssm_rows = slots * states
    rows_all, conv_rows = call(
        pack_kernel, (slots, taps), "pack", 20,
        [(cache_ssm.reshape(ssm_rows, channels), "hbm"), (cache_conv.transpose(1, 0, 2), "hbm")],
        [((ssm_rows + slots * taps, channels), BF16, "vmem"), ((slots * taps, channels), BF16, "vmem")],
        [vmem((taps - 1, slots, channels), BF16), dma((2,))],
    )
    block = rows_all.shape[0]
    relative = n_replica == 4
    if relative:
        far = swap(rows_all, "replica", n_replica, 3)
        near = swap(rows_all, "replica", n_replica, 1)
        conv_two = swap(conv_rows, "replica", n_replica, 2)
        conv_pieces = [rows_all, near, far, conv_two]
        firsts = (0, block, 2 * block, 4 * block - slots * taps)
        ssm_pieces = [rows_all, near, far, swap(far, "replica", n_replica, 1)]
    else:
        ssm_pieces = [lax.all_gather(rows_all, "replica")]
        conv_pieces, firsts = [ssm_pieces[0].reshape(-1, channels)], (0,)

    n_chunks = channels // min(512, channels)
    dims = (per_dev, n_replica, slots, relative)
    head = per_dev * taps
    weights = x_proj_weight.T
    requests = [(holder, "smem"), (slot_id, "smem"), (prefix_len, "smem")]

    mixed, head_sums, part = call(
        project_kernel, per_dev, "conv_project", 40,
        [(x_new, "hbm"), (weights, "hbm"), (conv_weight, "hbm"), (conv_bias[None, :], "hbm")],
        [((rows, channels), BF16, "any"), ((head, channels), F32, "any"), ((out_cols, rows), BF16, "any")],
        [
            vmem((rows, channels), BF16),
            vmem((out_cols, channels), BF16),
            vmem((taps, channels), BF16),
            vmem((1, channels), F32),
            vmem((channels // LANES, rows + taps * per_dev, LANES), F32),
            vmem((rows, channels), BF16),
            vmem((head, channels), F32),
            vmem((out_cols, rows), F32),
            vmem((out_cols, rows), BF16),
            dma((2 + 2 * n_chunks,)),
            dma((n_chunks + 2,)),
        ],
    )
    mixed_head, part_head = call(
        history_kernel, (dims, block, firsts), "history", 20,
        requests + [(value, "vmem") for value in [head_sums, weights, conv_weight] + conv_pieces],
        [((head, channels), BF16, "vmem"), ((head, out_cols), BF16, "vmem")],
        [],
    )
    mask = n_tensor // 2
    pairs = [part, swap(part, "tensor", n_tensor, mask), part_head, swap(part_head, "tensor", n_tensor, mask)]
    (merged,) = call(
        merge_kernel, None, "merge", 20,
        [(value, "vmem") for value in pairs],
        [((out_cols, rows), BF16, "vmem")],
        [],
    )
    parts = [merged] + [swap(merged, "tensor", n_tensor, k) for k in range(1, mask)]

    n_tiles = channels // LANES
    operands = [mixed, mixed_head, z_new, dt_proj_weight, dt_bias[None, :], a_log, d_skip[None, :]]
    out, state = call(
        scan_kernel, dims, "dt_scan_gate", 40,
        [(value, "any") for value, _ in requests] + [(value, "vmem") for value in operands + parts + ssm_pieces],
        [((rows, channels), BF16, "any"), ((per_dev * states, channels), BF16, "any")],
        [
            vmem((states, rows, LANES), F32),
            vmem((states, rows, LANES), F32),
            vmem((n_tiles, rows, LANES), F32),
            vmem((n_tiles, rows, LANES), F32),
            vmem((states, channels), F32),
            vmem((n_tiles, per_dev * (states + 1), LANES), F32),
            vmem((n_tiles, per_dev * (states + 1), LANES), F32),
            vmem((n_tiles, rows + per_dev, LANES), F32),
            vmem((rows, channels), BF16),
            vmem((per_dev * states, channels), BF16),
            dma((2, n_tiles // 2)),
            dma((3,)),
        ] + [pltpu.SMEM(holder.shape, jnp.int32)] * 3,
    )
    return out, state.reshape(per_dev, states, channels)


def solution(mesh):
    placed = (
        P(("groups", "replica"), "tensor"),
        P(("groups", "replica"), "tensor"),
        P(None, "tensor"),
        P("tensor"),
        P("tensor", None),
        P(None, "tensor"),
        P("tensor"),
        P(None, "tensor"),
        P("tensor"),
        P(("groups", "replica"), None, "tensor"),
        P(("groups", "replica"), None, "tensor"),
        P("groups"),
        P("groups"),
        P("groups"),
    )
    return jax.shard_map(
        functools.partial(shards, mesh),
        mesh=mesh,
        in_specs=placed,
        out_specs=(P(("groups", "replica"), "tensor"), P(("groups", "replica"), None, "tensor")),
        check_vma=False,
    )
```

```python
import functools

import jax
import jax.numpy as jnp
from jax import lax
from jax.experimental import pallas as pl
from jax.experimental.pallas import tpu as pltpu
from jax.sharding import PartitionSpec as P

NEW = 32
LANES = 128
MIB = 1024 * 1024
UNROLL = 32
LOG2E = 1.4426950408889634
F32, BF16 = jnp.float32, jnp.bfloat16
NT = (((1,), (1,)), ((), ()))


def silu(v):
    half = 0.5 * v
    return half + half * jnp.tanh(half)


def softplus(v):
    u = jnp.exp2(jnp.abs(v) * -LOG2E)
    return jnp.maximum(v, 0.0) + jnp.where(u < 2.0**-10, u - 0.5 * (u * u), jnp.log(1.0 + u))


def split_index(value, inner):
    assert inner & (inner - 1) == 0
    return value >> (inner.bit_length() - 1), value & (inner - 1)


def pick_rows(values, row_low, count):
    out = jnp.zeros(row_low.shape, jnp.int32)
    for r in range(count):
        out = jnp.where(row_low == r, values[r], out)
    return out


def request_places(dims, ints, me):
    per_dev, n_replica, _, relative = dims
    places, slot_ids, lengths = [], [], []
    for r in range(per_dev):
        request = me * per_dev + r
        place = ints[0][request]
        if relative:
            place = place ^ me
            place = place ^ (place >> 1)
        places.append(place)
        slot_ids.append(ints[1][request])
        lengths.append(ints[2][request])
    return places, slot_ids, lengths


def fetch_rows(target, live, pieces):
    total = None
    for first, value in pieces:
        col = lax.broadcasted_iota(jnp.int32, (target.shape[0], value.shape[0]), 1) + first
        select = jnp.where((col == target) & live, 1.0, 0.0).astype(BF16)
        part = jnp.dot(select, value, preferred_element_type=F32)
        total = part if total is None else total + part
    return total


def pack_kernel(dims, refs_in, refs_out, scratch):
    slots, taps = dims
    ssm_hbm, conv_hbm = refs_in
    block_ref, conv_ref = refs_out
    conv_v, sems = scratch
    states = pltpu.make_async_copy(ssm_hbm, block_ref.at[: ssm_hbm.shape[0]], sems.at[0])
    inputs = pltpu.make_async_copy(conv_hbm, conv_v, sems.at[1])
    states.start()
    inputs.start()
    inputs.wait()
    lines = []
    for slot in range(slots):
        for tap in range(taps):
            line = conv_v[min(tap, taps - 2)].astype(F32)[slot : slot + 1]
            lines.append(line if tap < taps - 1 else jnp.zeros_like(line))
    rows = jnp.concatenate(lines, axis=0).astype(BF16)
    conv_ref[...] = rows
    block_ref[ssm_hbm.shape[0] :, :] = rows
    states.wait()


def project_kernel(dims, refs_in, refs_out, scratch):
    per_dev = dims
    x_hbm, wt_hbm, cw_hbm, cb_hbm = refs_in
    mixed_hbm, head_hbm, part_hbm = refs_out
    x_v, wt_v, cw_v, cb_v, joined, mixed_v, head_v, part_f, part_v, sems, out_sems = scratch
    rows, channels = x_v.shape
    taps = cw_v.shape[0]
    lines = (taps - 1) * per_dev
    pairs = [(cw_hbm, cw_v), (cb_hbm, cb_v)]
    width = min(512, channels)
    chunks = [slice(c * width, (c + 1) * width) for c in range(channels // width)]
    for chunk in chunks:
        pairs += [(x_hbm.at[:, chunk], x_v.at[:, chunk]), (wt_hbm.at[:, chunk], wt_v.at[:, chunk])]
    copies = [pltpu.make_async_copy(src, dst, sems.at[i]) for i, (src, dst) in enumerate(pairs)]
    for copy in copies:
        copy.start()

    joined[:, :lines, :] = jnp.zeros((channels // LANES, lines, LANES), F32)
    copies[0].wait()
    copies[1].wait()
    outs = []
    for c, chunk in enumerate(chunks):
        copies[2 + 2 * c].wait()
        for tile in range(c * width // LANES, (c + 1) * width // LANES):
            lanes = slice(tile * LANES, (tile + 1) * LANES)
            for r in range(per_dev):
                tokens = x_v[r * NEW : (r + 1) * NEW, lanes].astype(F32)
                joined[tile, pl.ds(lines + r, NEW, stride=per_dev), :] = tokens
            weight = [cw_v[k : k + 1, lanes].astype(F32) for k in range(taps)]
            bias = cb_v[:, lanes]
            for first in range(0, rows, LANES):
                summed = bias + joined[tile, first : first + LANES, :] * weight[0]
                for k in range(1, taps):
                    begin = first + k * per_dev
                    summed = summed + joined[tile, begin : begin + LANES, :] * weight[k]
                if first == 0:
                    head_v[:, lanes] = summed[: head_v.shape[0]]
                mixed_v[first : first + LANES, lanes] = silu(summed).astype(BF16)
        copies[3 + 2 * c].wait()
        part = lax.dot_general(wt_v[:, chunk], mixed_v[:, chunk], NT, preferred_element_type=F32)
        if c == 0:
            part_f[...] = part
        else:
            part_f[...] += part
        outs.append(pltpu.make_async_copy(mixed_v.at[:, chunk], mixed_hbm.at[:, chunk], out_sems.at[c]))
        outs[-1].start()
    part_v[...] = part_f[...].astype(BF16)
    for src, dst in ((part_v, part_hbm), (head_v, head_hbm)):
        outs.append(pltpu.make_async_copy(src, dst, out_sems.at[len(outs)]))
        outs[-1].start()
    for copy in outs:
        copy.wait()


def history_kernel(dims, refs_in, refs_out, scratch):
    dims, block, firsts = dims
    per_dev, n_replica, slots, _ = dims
    holder, slot_id, prefix_len, head_ref, part_ref, wt_ref, cw_ref = refs_in[:7]
    pieces = refs_in[7:]
    mixed_ref, fixed_ref = refs_out
    taps = cw_ref.shape[0]
    me = lax.axis_index("replica")
    places, slot_ids, lengths = request_places(dims, (holder, slot_id, prefix_len), me)
    tap, request = split_index(lax.broadcasted_iota(jnp.int32, (per_dev * taps, 1), 0), per_dev)
    starts = [places[r] * block + (block - slots * taps) + slot_ids[r] * taps for r in range(per_dev)]
    target = pick_rows(starts, request, per_dev) + tap
    live = (tap < taps - 1) & (taps - 1 - tap <= pick_rows(lengths, request, per_dev))
    history = fetch_rows(target, live, [(first, ref[...]) for first, ref in zip(firsts, pieces)])
    sums = []
    for t in range(taps):
        summed = head_ref[t * per_dev : (t + 1) * per_dev]
        for k in range(taps - 1 - t):
            weight = cw_ref[k : k + 1].astype(F32)
            summed = summed + history[(t + k) * per_dev : (t + k + 1) * per_dev] * weight
        sums.append(summed)
    mixed = silu(jnp.concatenate(sums, axis=0)).astype(BF16)
    mixed_ref[...] = mixed
    part = lax.dot_general(wt_ref[...], mixed, NT, preferred_element_type=F32)
    fixed_ref[...] = part_ref[...]
    fixed_ref[:, : per_dev * taps] = part.astype(BF16)


def scan_kernel(dims, refs_in, refs_out, scratch):
    per_dev, n_replica, _, _ = dims
    mixed_ref, head_ref, z_ref, dtw_ref, dtb_ref, al_ref, skip_ref = refs_in[3:10]
    out_hbm, state_hbm = refs_out
    b_tab, c_tab, dt_v, drive_v, a_v, start_tm, final_tm, y_v, out_v, state_v, out_sems, int_sems = scratch[:12]
    ints = scratch[12:]
    int_copies = [pltpu.make_async_copy(refs_in[i], ints[i], int_sems.at[i]) for i in range(len(ints))]
    for copy in int_copies:
        copy.start()
    n_pieces = sum(1 for ref in refs_in[10:] if ref.shape[-1] == z_ref.shape[1])
    parts, pieces = refs_in[10:-n_pieces], refs_in[-n_pieces:]
    rows, channels = z_ref.shape
    states = al_ref.shape[0]
    rank = dtw_ref.shape[0]
    head = head_ref.shape[0]

    projected = parts[0][...].astype(F32)
    for part in parts[1:]:
        projected = projected + part[...].astype(F32)
    c_part = projected[rank + states :]
    c_high = c_part.astype(BF16).astype(F32)
    shape = (2 * states, states * LANES)
    term = lax.broadcasted_iota(jnp.int32, shape, 0) & (states - 1)
    lane_group, _ = split_index(lax.broadcasted_iota(jnp.int32, shape, 1), LANES)
    spread = jnp.where(term == lane_group, 1.0, 0.0).astype(BF16)
    c_terms = jnp.concatenate([c_high, c_part - c_high], axis=0).T.astype(BF16)
    projected = projected[: rank + states].T
    dt_low = projected[:, :rank].astype(BF16)
    late = projected[:, rank:]
    n_tiles = channels // LANES
    wide = min(4, n_tiles)
    per_chunk = states * wide // n_tiles
    for c in range(n_tiles // wide):
        for n in range(c * per_chunk, (c + 1) * per_chunk):
            b_tab[n] = jnp.broadcast_to(late[:, n : n + 1], (rows, LANES))
        lanes = slice(c * per_chunk * LANES, (c + 1) * per_chunk * LANES)
        repeated = jnp.dot(c_terms, spread[:, lanes], preferred_element_type=F32)
        for n in range(per_chunk):
            c_tab[c * per_chunk + n] = repeated[:, n * LANES : (n + 1) * LANES]
        weights = dtw_ref[:, c * wide * LANES : (c + 1) * wide * LANES]
        raw = jnp.dot(dt_low, weights, preferred_element_type=F32)
        for j in range(wide):
            tile = c * wide + j
            lanes = slice(tile * LANES, (tile + 1) * LANES)
            for first in range(0, rows, LANES):
                here = slice(first, first + LANES)
                dt = softplus(raw[here, j * LANES : (j + 1) * LANES] + dtb_ref[:, lanes])
                mixed = mixed_ref[here, lanes]
                if first == 0:
                    mixed = jnp.concatenate([head_ref[:, lanes], mixed[head:]], axis=0)
                mixed = mixed.astype(F32)
                dt_v[tile, here, :] = dt
                drive_v[tile, here, :] = dt * mixed
                y_v[tile, here, :] = skip_ref[:, lanes] * mixed
    a_v[...] = jnp.exp(al_ref[...]) * (-LOG2E)

    me = lax.axis_index("replica")
    for copy in int_copies:
        copy.wait()
    places, slot_ids, lengths = request_places(dims, ints, me)
    for r in range(per_dev):
        spot = pl.ds(pl.multiple_of(slot_ids[r] * states, states), states)
        for tile in range(n_tiles):
            lanes = slice(tile * LANES, (tile + 1) * LANES)
            if n_pieces == 1:
                value = pieces[0][places[r], spot, lanes]
            else:
                value = pieces[0][spot, lanes]
                for p in range(1, n_pieces):
                    value = jnp.where(places[r] == p, pieces[p][spot, lanes], value)
            value = value.astype(F32)
            value = jnp.where(lengths[r] > 0, value, jnp.zeros_like(value))
            start_tm[tile, pl.ds(r, states, stride=per_dev), :] = value

    tiles = 2
    half = states // 2
    width = tiles * LANES
    n_groups = n_tiles // tiles

    def out_copies(g):
        lanes = pl.ds(pl.multiple_of(g * width, width), width)
        return [
            pltpu.make_async_copy(src.at[:, lanes], dst.at[:, lanes], out_sems.at[i, g])
            for i, (src, dst) in enumerate(((out_v, out_hbm), (state_v, state_hbm)))
        ]

    def finish(g):
        for j in range(tiles):
            tile = g * tiles + j
            lanes = pl.ds(pl.multiple_of(tile * LANES, LANES), LANES)
            for r in range(per_dev):
                here = slice(r * NEW, (r + 1) * NEW)
                value = y_v[tile, pl.ds(r, NEW, stride=per_dev), :] * silu(z_ref[here, lanes].astype(F32))
                out_v[here, lanes] = value.astype(BF16)
                final = final_tm[tile, pl.ds(r, states, stride=per_dev), :]
                state_v[r * states : (r + 1) * states, lanes] = final.astype(BF16)

    def scan_group(g):
        group = [g * tiles + j for j in range(tiles)]
        lanes = [pl.ds(pl.multiple_of(tile * LANES, LANES), LANES) for tile in group]
        for first in range(0, states, half):
            ids = range(first, first + half)
            rates = [[jnp.broadcast_to(a_v[n : n + 1, lane], (per_dev, LANES)) for n in ids] for lane in lanes]

            def advance(step, state):
                state = list(state)
                for u in range(UNROLL):
                    now = pl.ds(pl.multiple_of((step * UNROLL + u) * per_dev, per_dev), per_dev)
                    dt = [dt_v[tile, now, :] for tile in group]
                    drive = [drive_v[tile, now, :] for tile in group]
                    sums = [None] * tiles
                    for k, n in enumerate(ids):
                        b, c = b_tab[n, now, :], c_tab[n, now, :]
                        for j in range(tiles):
                            i = j * half + k
                            state[i] = jnp.exp2(dt[j] * rates[j][k]) * state[i] + drive[j] * b
                            term = state[i] * c
                            sums[j] = term if sums[j] is None else sums[j] + term
                    for j, tile in enumerate(group):
                        y_v[tile, now, :] += sums[j]
                return tuple(state)

            state = tuple(start_tm[tile, n * per_dev : (n + 1) * per_dev, :] for tile in group for n in ids)
            if NEW == UNROLL:
                state = advance(0, state)
            else:
                state = lax.fori_loop(0, NEW // UNROLL, advance, state)
            for j, tile in enumerate(group):
                for k, n in enumerate(ids):
                    final_tm[tile, n * per_dev : (n + 1) * per_dev, :] = state[j * half + k]

    def one_group(g, carry):
        before = jnp.maximum(g - 1, 0)
        finish(before)
        scan_group(g)

        @pl.when(g > 0)
        def _():
            for copy in out_copies(before):
                copy.start()

        return carry

    final_tm[:tiles] = jnp.zeros((tiles,) + final_tm.shape[1:], F32)
    lax.fori_loop(0, n_groups, one_group, 0)
    finish(n_groups - 1)
    for copy in out_copies(n_groups - 1):
        copy.start()

    def last_wait(g, carry):
        for copy in out_copies(g):
            copy.wait()
        return carry

    lax.fori_loop(0, n_groups, last_wait, 0)


def split_refs(kernel, dims, n_in, n_out):
    def body(*refs):
        kernel(dims, refs[:n_in], refs[n_in : n_in + n_out], refs[n_in + n_out :])

    return body


def call(kernel, dims, name, limit, ins, outs, scratch):
    spaces = {"hbm": pltpu.HBM, "any": pl.ANY, "vmem": pltpu.VMEM, "smem": pltpu.SMEM}
    values = [
        pltpu.with_memory_space_constraint(value, pltpu.HBM) if place == "hbm" else value for value, place in ins
    ]
    return pl.pallas_call(
        split_refs(kernel, dims, len(ins), len(outs)),
        in_specs=[pl.BlockSpec(memory_space=spaces[place]) for _, place in ins],
        out_specs=[pl.BlockSpec(memory_space=spaces[place]) for _, _, place in outs],
        out_shape=[jax.ShapeDtypeStruct(shape, dtype) for shape, dtype, _ in outs],
        scratch_shapes=scratch,
        compiler_params=pltpu.CompilerParams(vmem_limit_bytes=limit * MIB),
        name=name,
    )(*values)


def swap(value, axis, size, mask):
    return lax.ppermute(value, axis, [(i, i ^ mask) for i in range(size)])


def shards(mesh, x_new, z_new, conv_weight, conv_bias, x_proj_weight, dt_proj_weight, dt_bias, a_log, d_skip,
           cache_ssm, cache_conv, holder, slot_id, prefix_len):
    n_replica, n_tensor = mesh.shape["replica"], mesh.shape["tensor"]
    rows, channels = x_new.shape
    per_dev = rows // NEW
    states = a_log.shape[0]
    rank = dt_proj_weight.shape[0]
    taps = conv_weight.shape[0]
    slots = cache_ssm.shape[0]
    out_cols = x_proj_weight.shape[1]
    requests = holder.shape[0]

    vmem, dma = pltpu.VMEM, pltpu.SemaphoreType.DMA
    ssm_rows = slots * states
    rows_all, conv_rows = call(
        pack_kernel, (slots, taps), "pack", 20,
        [(cache_ssm.reshape(ssm_rows, channels), "hbm"), (cache_conv.transpose(1, 0, 2), "hbm")],
        [((ssm_rows + slots * taps, channels), BF16, "vmem"), ((slots * taps, channels), BF16, "vmem")],
        [vmem((taps - 1, slots, channels), BF16), dma((2,))],
    )
    block = rows_all.shape[0]
    relative = n_replica == 4
    if relative:
        far = swap(rows_all, "replica", n_replica, 3)
        near = swap(rows_all, "replica", n_replica, 1)
        conv_two = swap(conv_rows, "replica", n_replica, 2)
        conv_pieces = [rows_all, near, far, conv_two]
        firsts = (0, block, 2 * block, 4 * block - slots * taps)
        ssm_pieces = [rows_all, near, far, swap(far, "replica", n_replica, 1)]
    else:
        ssm_pieces = [lax.all_gather(rows_all, "replica")]
        conv_pieces, firsts = [ssm_pieces[0].reshape(-1, channels)], (0,)

    n_chunks = channels // min(512, channels)
    dims = (per_dev, n_replica, slots, relative)
    head = per_dev * taps
    weights = x_proj_weight.T
    requests = [(holder, "smem"), (slot_id, "smem"), (prefix_len, "smem")]

    mixed, head_sums, part = call(
        project_kernel, per_dev, "conv_project", 40,
        [(x_new, "hbm"), (weights, "hbm"), (conv_weight, "hbm"), (conv_bias[None, :], "hbm")],
        [((rows, channels), BF16, "any"), ((head, channels), F32, "any"), ((out_cols, rows), BF16, "any")],
        [
            vmem((rows, channels), BF16),
            vmem((out_cols, channels), BF16),
            vmem((taps, channels), BF16),
            vmem((1, channels), F32),
            vmem((channels // LANES, rows + taps * per_dev, LANES), F32),
            vmem((rows, channels), BF16),
            vmem((head, channels), F32),
            vmem((out_cols, rows), F32),
            vmem((out_cols, rows), BF16),
            dma((2 + 2 * n_chunks,)),
            dma((n_chunks + 2,)),
        ],
    )
    mixed_head, part = call(
        history_kernel, (dims, block, firsts), "history", 20,
        requests
        + [(value, "vmem") for value in [head_sums, part, weights, conv_weight] + conv_pieces],
        [((head, channels), BF16, "vmem"), ((out_cols, rows), BF16, "vmem")],
        [],
    )
    parts = [part]
    mask = n_tensor // 2
    while mask:
        parts = parts + [swap(value, "tensor", n_tensor, mask) for value in reversed(parts)]
        mask //= 2

    n_tiles = channels // LANES
    operands = [mixed, mixed_head, z_new, dt_proj_weight, dt_bias[None, :], a_log, d_skip[None, :]]
    out, state = call(
        scan_kernel, dims, "dt_scan_gate", 40,
        [(value, "any") for value, _ in requests] + [(value, "vmem") for value in operands + parts + ssm_pieces],
        [((rows, channels), BF16, "any"), ((per_dev * states, channels), BF16, "any")],
        [
            vmem((states, rows, LANES), F32),
            vmem((states, rows, LANES), F32),
            vmem((n_tiles, rows, LANES), F32),
            vmem((n_tiles, rows, LANES), F32),
            vmem((states, channels), F32),
            vmem((n_tiles, per_dev * (states + 1), LANES), F32),
            vmem((n_tiles, per_dev * (states + 1), LANES), F32),
            vmem((n_tiles, rows + per_dev, LANES), F32),
            vmem((rows, channels), BF16),
            vmem((per_dev * states, channels), BF16),
            dma((2, n_tiles // 2)),
            dma((3,)),
        ] + [pltpu.SMEM(holder.shape, jnp.int32)] * 3,
    )
    return out, state.reshape(per_dev, states, channels)


def solution(mesh):
    placed = (
        P(("groups", "replica"), "tensor"),
        P(("groups", "replica"), "tensor"),
        P(None, "tensor"),
        P("tensor"),
        P("tensor", None),
        P(None, "tensor"),
        P("tensor"),
        P(None, "tensor"),
        P("tensor"),
        P(("groups", "replica"), None, "tensor"),
        P(("groups", "replica"), None, "tensor"),
        P("groups"),
        P("groups"),
        P("groups"),
    )
    return jax.shard_map(
        functools.partial(shards, mesh),
        mesh=mesh,
        in_specs=placed,
        out_specs=(P(("groups", "replica"), "tensor"), P(("groups", "replica"), None, "tensor")),
        check_vma=False,
    )
```

```python
import functools

import jax
import jax.numpy as jnp
from jax import lax
from jax.experimental import pallas as pl
from jax.experimental.pallas import tpu as pltpu
from jax.sharding import PartitionSpec as P

NEW = 32
LANES = 128
MIB = 1024 * 1024
UNROLL = 32
LOG2E = 1.4426950408889634
F32, BF16 = jnp.float32, jnp.bfloat16
NT = (((1,), (1,)), ((), ()))


def silu(v):
    half = 0.5 * v
    return half + half * jnp.tanh(half)


def softplus(v):
    u = jnp.exp2(jnp.abs(v) * -LOG2E)
    return jnp.maximum(v, 0.0) + jnp.where(u < 2.0**-10, u - 0.5 * (u * u), jnp.log(1.0 + u))


def split_index(value, inner):
    assert inner & (inner - 1) == 0
    return value >> (inner.bit_length() - 1), value & (inner - 1)


def pick_rows(values, row_low, count):
    out = jnp.zeros(row_low.shape, jnp.int32)
    for r in range(count):
        out = jnp.where(row_low == r, values[r], out)
    return out


def request_places(dims, ints, me):
    per_dev, n_replica, _, relative = dims
    places, slot_ids, lengths = [], [], []
    for r in range(per_dev):
        request = me * per_dev + r
        place = ints[0][request]
        if relative:
            place = place ^ me
            place = place ^ (place >> 1)
        places.append(place)
        slot_ids.append(ints[1][request])
        lengths.append(ints[2][request])
    return places, slot_ids, lengths


def fetch_rows(target, live, pieces):
    total = None
    for first, value in pieces:
        col = lax.broadcasted_iota(jnp.int32, (target.shape[0], value.shape[0]), 1) + first
        select = jnp.where((col == target) & live, 1.0, 0.0).astype(BF16)
        part = jnp.dot(select, value, preferred_element_type=F32)
        total = part if total is None else total + part
    return total


def pack_kernel(dims, refs_in, refs_out, scratch):
    slots, taps = dims
    ssm_hbm, conv_hbm = refs_in
    block_ref, conv_ref = refs_out
    conv_v, sems = scratch
    states = pltpu.make_async_copy(ssm_hbm, block_ref.at[: ssm_hbm.shape[0]], sems.at[0])
    inputs = pltpu.make_async_copy(conv_hbm, conv_v, sems.at[1])
    states.start()
    inputs.start()
    inputs.wait()
    lines = []
    for slot in range(slots):
        for tap in range(taps):
            line = conv_v[min(tap, taps - 2)].astype(F32)[slot : slot + 1]
            lines.append(line if tap < taps - 1 else jnp.zeros_like(line))
    rows = jnp.concatenate(lines, axis=0).astype(BF16)
    conv_ref[...] = rows
    block_ref[ssm_hbm.shape[0] :, :] = rows
    states.wait()


def project_kernel(dims, refs_in, refs_out, scratch):
    per_dev = dims
    x_hbm, wt_hbm, cw_hbm, cb_hbm = refs_in
    mixed_hbm, head_hbm, part_hbm = refs_out
    x_v, wt_v, cw_v, cb_v, joined, mixed_v, head_v, part_f, part_v, sems, out_sems = scratch
    rows, channels = x_v.shape
    taps = cw_v.shape[0]
    lines = (taps - 1) * per_dev
    pairs = [(cw_hbm, cw_v), (cb_hbm, cb_v)]
    width = min(512, channels)
    chunks = [slice(c * width, (c + 1) * width) for c in range(channels // width)]
    for chunk in chunks:
        pairs += [(x_hbm.at[:, chunk], x_v.at[:, chunk]), (wt_hbm.at[:, chunk], wt_v.at[:, chunk])]
    copies = [pltpu.make_async_copy(src, dst, sems.at[i]) for i, (src, dst) in enumerate(pairs)]
    for copy in copies:
        copy.start()

    joined[:, :lines, :] = jnp.zeros((channels // LANES, lines, LANES), F32)
    copies[0].wait()
    copies[1].wait()
    outs = []
    for c, chunk in enumerate(chunks):
        copies[2 + 2 * c].wait()
        for tile in range(c * width // LANES, (c + 1) * width // LANES):
            lanes = slice(tile * LANES, (tile + 1) * LANES)
            for r in range(per_dev):
                tokens = x_v[r * NEW : (r + 1) * NEW, lanes].astype(F32)
                joined[tile, pl.ds(lines + r, NEW, stride=per_dev), :] = tokens
            weight = [cw_v[k : k + 1, lanes].astype(F32) for k in range(taps)]
            bias = cb_v[:, lanes]
            for first in range(0, rows, LANES):
                summed = bias + joined[tile, first : first + LANES, :] * weight[0]
                for k in range(1, taps):
                    begin = first + k * per_dev
                    summed = summed + joined[tile, begin : begin + LANES, :] * weight[k]
                if first == 0:
                    head_v[:, lanes] = summed[: head_v.shape[0]]
                mixed_v[first : first + LANES, lanes] = silu(summed).astype(BF16)
        copies[3 + 2 * c].wait()
        part = lax.dot_general(wt_v[:, chunk], mixed_v[:, chunk], NT, preferred_element_type=F32)
        if c == 0:
            part_f[...] = part
        else:
            part_f[...] += part
        outs.append(pltpu.make_async_copy(mixed_v.at[:, chunk], mixed_hbm.at[:, chunk], out_sems.at[c]))
        outs[-1].start()
    part_v[...] = part_f[...].astype(BF16)
    for src, dst in ((part_v, part_hbm), (head_v, head_hbm)):
        outs.append(pltpu.make_async_copy(src, dst, out_sems.at[len(outs)]))
        outs[-1].start()
    for copy in outs:
        copy.wait()


def history_kernel(dims, refs_in, refs_out, scratch):
    dims, block, firsts = dims
    per_dev, n_replica, slots, _ = dims
    holder, slot_id, prefix_len, head_ref, part_ref, wt_ref, cw_ref = refs_in[:7]
    pieces = refs_in[7:]
    mixed_ref, fixed_ref = refs_out
    taps = cw_ref.shape[0]
    me = lax.axis_index("replica")
    places, slot_ids, lengths = request_places(dims, (holder, slot_id, prefix_len), me)
    tap, request = split_index(lax.broadcasted_iota(jnp.int32, (per_dev * taps, 1), 0), per_dev)
    starts = [places[r] * block + (block - slots * taps) + slot_ids[r] * taps for r in range(per_dev)]
    target = pick_rows(starts, request, per_dev) + tap
    live = (tap < taps - 1) & (taps - 1 - tap <= pick_rows(lengths, request, per_dev))
    history = fetch_rows(target, live, [(first, ref[...]) for first, ref in zip(firsts, pieces)])
    sums = []
    for t in range(taps):
        summed = head_ref[t * per_dev : (t + 1) * per_dev]
        for k in range(taps - 1 - t):
            weight = cw_ref[k : k + 1].astype(F32)
            summed = summed + history[(t + k) * per_dev : (t + k + 1) * per_dev] * weight
        sums.append(summed)
    mixed = silu(jnp.concatenate(sums, axis=0)).astype(BF16)
    mixed_ref[...] = mixed
    part = lax.dot_general(wt_ref[...], mixed, NT, preferred_element_type=F32)
    fixed_ref[...] = part_ref[...]
    fixed_ref[:, : per_dev * taps] = part.astype(BF16)


def scan_kernel(dims, refs_in, refs_out, scratch):
    per_dev, n_replica, _, _ = dims
    mixed_ref, head_ref, z_ref, dtw_ref, dtb_ref, al_ref, skip_ref = refs_in[3:10]
    out_hbm, state_hbm = refs_out
    b_tab, c_tab, dt_v, drive_v, a_v, start_tm, final_tm, y_v, out_v, state_v, out_sems, int_sems = scratch[:12]
    ints = scratch[12:]
    int_copies = [pltpu.make_async_copy(refs_in[i], ints[i], int_sems.at[i]) for i in range(len(ints))]
    for copy in int_copies:
        copy.start()
    n_pieces = sum(1 for ref in refs_in[10:] if ref.shape[-1] == z_ref.shape[1])
    parts, pieces = refs_in[10:-n_pieces], refs_in[-n_pieces:]
    rows, channels = z_ref.shape
    states = al_ref.shape[0]
    rank = dtw_ref.shape[0]
    head = head_ref.shape[0]

    projected = parts[0][...].astype(F32)
    for part in parts[1:]:
        projected = projected + part[...].astype(F32)
    late = projected[rank:]
    high = late.astype(BF16).astype(F32)
    low = late - high
    shape = (2 * states, states * LANES)
    term = lax.broadcasted_iota(jnp.int32, shape, 0) & (states - 1)
    lane_group, _ = split_index(lax.broadcasted_iota(jnp.int32, shape, 1), LANES)
    spread = jnp.where(term == lane_group, 1.0, 0.0).astype(BF16)
    b_terms = jnp.concatenate([high[:states], low[:states]], axis=0).T.astype(BF16)
    c_terms = jnp.concatenate([high[states:], low[states:]], axis=0).T.astype(BF16)
    dt_low = projected[:rank].T.astype(BF16)
    n_tiles = channels // LANES
    wide = min(4, n_tiles)
    per_chunk = states * wide // n_tiles
    for c in range(n_tiles // wide):
        lanes = slice(c * per_chunk * LANES, (c + 1) * per_chunk * LANES)
        for table, terms in ((b_tab, b_terms), (c_tab, c_terms)):
            repeated = jnp.dot(terms, spread[:, lanes], preferred_element_type=F32)
            for n in range(per_chunk):
                table[c * per_chunk + n] = repeated[:, n * LANES : (n + 1) * LANES]
        weights = dtw_ref[:, c * wide * LANES : (c + 1) * wide * LANES]
        raw = jnp.dot(dt_low, weights, preferred_element_type=F32)
        for j in range(wide):
            tile = c * wide + j
            lanes = slice(tile * LANES, (tile + 1) * LANES)
            for first in range(0, rows, LANES):
                here = slice(first, first + LANES)
                dt = softplus(raw[here, j * LANES : (j + 1) * LANES] + dtb_ref[:, lanes])
                mixed = mixed_ref[here, lanes]
                if first == 0:
                    mixed = jnp.concatenate([head_ref[:, lanes], mixed[head:]], axis=0)
                mixed = mixed.astype(F32)
                dt_v[tile, here, :] = dt
                drive_v[tile, here, :] = dt * mixed
                y_v[tile, here, :] = skip_ref[:, lanes] * mixed
    a_v[...] = jnp.exp(al_ref[...]) * (-LOG2E)

    me = lax.axis_index("replica")
    for copy in int_copies:
        copy.wait()
    places, slot_ids, lengths = request_places(dims, ints, me)
    for r in range(per_dev):
        spot = pl.ds(pl.multiple_of(slot_ids[r] * states, states), states)
        for tile in range(n_tiles):
            lanes = slice(tile * LANES, (tile + 1) * LANES)
            if n_pieces == 1:
                value = pieces[0][places[r], spot, lanes]
            else:
                value = pieces[0][spot, lanes]
                for p in range(1, n_pieces):
                    value = jnp.where(places[r] == p, pieces[p][spot, lanes], value)
            value = value.astype(F32)
            value = jnp.where(lengths[r] > 0, value, jnp.zeros_like(value))
            start_tm[tile, pl.ds(r, states, stride=per_dev), :] = value

    tiles = 2
    half = states // 2
    width = tiles * LANES
    n_groups = n_tiles // tiles

    def out_copies(g):
        lanes = pl.ds(pl.multiple_of(g * width, width), width)
        return [
            pltpu.make_async_copy(src.at[:, lanes], dst.at[:, lanes], out_sems.at[i, g])
            for i, (src, dst) in enumerate(((out_v, out_hbm), (state_v, state_hbm)))
        ]

    def finish(g):
        for j in range(tiles):
            tile = g * tiles + j
            lanes = pl.ds(pl.multiple_of(tile * LANES, LANES), LANES)
            for r in range(per_dev):
                here = slice(r * NEW, (r + 1) * NEW)
                value = y_v[tile, pl.ds(r, NEW, stride=per_dev), :] * silu(z_ref[here, lanes].astype(F32))
                out_v[here, lanes] = value.astype(BF16)
                final = final_tm[tile, pl.ds(r, states, stride=per_dev), :]
                state_v[r * states : (r + 1) * states, lanes] = final.astype(BF16)

    def scan_group(g):
        group = [g * tiles + j for j in range(tiles)]
        lanes = [pl.ds(pl.multiple_of(tile * LANES, LANES), LANES) for tile in group]
        for first in range(0, states, half):
            ids = range(first, first + half)
            rates = [[jnp.broadcast_to(a_v[n : n + 1, lane], (per_dev, LANES)) for n in ids] for lane in lanes]

            def advance(step, state):
                state = list(state)
                for u in range(UNROLL):
                    now = pl.ds(pl.multiple_of((step * UNROLL + u) * per_dev, per_dev), per_dev)
                    dt = [dt_v[tile, now, :] for tile in group]
                    drive = [drive_v[tile, now, :] for tile in group]
                    sums = [None] * tiles
                    for k, n in enumerate(ids):
                        b, c = b_tab[n, now, :], c_tab[n, now, :]
                        for j in range(tiles):
                            i = j * half + k
                            state[i] = jnp.exp2(dt[j] * rates[j][k]) * state[i] + drive[j] * b
                            term = state[i] * c
                            sums[j] = term if sums[j] is None else sums[j] + term
                    for j, tile in enumerate(group):
                        y_v[tile, now, :] += sums[j]
                return tuple(state)

            state = tuple(start_tm[tile, n * per_dev : (n + 1) * per_dev, :] for tile in group for n in ids)
            if NEW == UNROLL:
                state = advance(0, state)
            else:
                state = lax.fori_loop(0, NEW // UNROLL, advance, state)
            for j, tile in enumerate(group):
                for k, n in enumerate(ids):
                    final_tm[tile, n * per_dev : (n + 1) * per_dev, :] = state[j * half + k]

    def one_group(g, carry):
        before = jnp.maximum(g - 1, 0)
        finish(before)
        scan_group(g)

        @pl.when(g > 0)
        def _():
            for copy in out_copies(before):
                copy.start()

        return carry

    final_tm[:tiles] = jnp.zeros((tiles,) + final_tm.shape[1:], F32)
    lax.fori_loop(0, n_groups, one_group, 0)
    finish(n_groups - 1)
    for copy in out_copies(n_groups - 1):
        copy.start()

    def last_wait(g, carry):
        for copy in out_copies(g):
            copy.wait()
        return carry

    lax.fori_loop(0, n_groups, last_wait, 0)


def split_refs(kernel, dims, n_in, n_out):
    def body(*refs):
        kernel(dims, refs[:n_in], refs[n_in : n_in + n_out], refs[n_in + n_out :])

    return body


def call(kernel, dims, name, limit, ins, outs, scratch):
    spaces = {"hbm": pltpu.HBM, "any": pl.ANY, "vmem": pltpu.VMEM, "smem": pltpu.SMEM}
    values = [
        pltpu.with_memory_space_constraint(value, pltpu.HBM) if place == "hbm" else value for value, place in ins
    ]
    return pl.pallas_call(
        split_refs(kernel, dims, len(ins), len(outs)),
        in_specs=[pl.BlockSpec(memory_space=spaces[place]) for _, place in ins],
        out_specs=[pl.BlockSpec(memory_space=spaces[place]) for _, _, place in outs],
        out_shape=[jax.ShapeDtypeStruct(shape, dtype) for shape, dtype, _ in outs],
        scratch_shapes=scratch,
        compiler_params=pltpu.CompilerParams(vmem_limit_bytes=limit * MIB),
        name=name,
    )(*values)


def swap(value, axis, size, mask):
    return lax.ppermute(value, axis, [(i, i ^ mask) for i in range(size)])


def shards(mesh, x_new, z_new, conv_weight, conv_bias, x_proj_weight, dt_proj_weight, dt_bias, a_log, d_skip,
           cache_ssm, cache_conv, holder, slot_id, prefix_len):
    n_replica, n_tensor = mesh.shape["replica"], mesh.shape["tensor"]
    rows, channels = x_new.shape
    per_dev = rows // NEW
    states = a_log.shape[0]
    rank = dt_proj_weight.shape[0]
    taps = conv_weight.shape[0]
    slots = cache_ssm.shape[0]
    out_cols = x_proj_weight.shape[1]
    requests = holder.shape[0]

    vmem, dma = pltpu.VMEM, pltpu.SemaphoreType.DMA
    ssm_rows = slots * states
    rows_all, conv_rows = call(
        pack_kernel, (slots, taps), "pack", 20,
        [(cache_ssm.reshape(ssm_rows, channels), "hbm"), (cache_conv.transpose(1, 0, 2), "hbm")],
        [((ssm_rows + slots * taps, channels), BF16, "vmem"), ((slots * taps, channels), BF16, "vmem")],
        [vmem((taps - 1, slots, channels), BF16), dma((2,))],
    )
    block = rows_all.shape[0]
    relative = n_replica == 4
    if relative:
        far = swap(rows_all, "replica", n_replica, 3)
        near = swap(rows_all, "replica", n_replica, 1)
        conv_two = swap(conv_rows, "replica", n_replica, 2)
        conv_pieces = [rows_all, near, far, conv_two]
        firsts = (0, block, 2 * block, 4 * block - slots * taps)
        ssm_pieces = [rows_all, near, far, swap(far, "replica", n_replica, 1)]
    else:
        ssm_pieces = [lax.all_gather(rows_all, "replica")]
        conv_pieces, firsts = [ssm_pieces[0].reshape(-1, channels)], (0,)

    n_chunks = channels // min(512, channels)
    dims = (per_dev, n_replica, slots, relative)
    head = per_dev * taps
    weights = x_proj_weight.T
    requests = [(holder, "smem"), (slot_id, "smem"), (prefix_len, "smem")]

    mixed, head_sums, part = call(
        project_kernel, per_dev, "conv_project", 40,
        [(x_new, "hbm"), (weights, "hbm"), (conv_weight, "hbm"), (conv_bias[None, :], "hbm")],
        [((rows, channels), BF16, "any"), ((head, channels), F32, "any"), ((out_cols, rows), BF16, "any")],
        [
            vmem((rows, channels), BF16),
            vmem((out_cols, channels), BF16),
            vmem((taps, channels), BF16),
            vmem((1, channels), F32),
            vmem((channels // LANES, rows + taps * per_dev, LANES), F32),
            vmem((rows, channels), BF16),
            vmem((head, channels), F32),
            vmem((out_cols, rows), F32),
            vmem((out_cols, rows), BF16),
            dma((2 + 2 * n_chunks,)),
            dma((n_chunks + 2,)),
        ],
    )
    mixed_head, part = call(
        history_kernel, (dims, block, firsts), "history", 20,
        requests
        + [(value, "vmem") for value in [head_sums, part, weights, conv_weight] + conv_pieces],
        [((head, channels), BF16, "vmem"), ((out_cols, rows), BF16, "vmem")],
        [],
    )
    parts = [part]
    mask = n_tensor // 2
    while mask:
        parts = parts + [swap(value, "tensor", n_tensor, mask) for value in reversed(parts)]
        mask //= 2

    n_tiles = channels // LANES
    operands = [mixed, mixed_head, z_new, dt_proj_weight, dt_bias[None, :], a_log, d_skip[None, :]]
    out, state = call(
        scan_kernel, dims, "dt_scan_gate", 40,
        [(value, "any") for value, _ in requests] + [(value, "vmem") for value in operands + parts + ssm_pieces],
        [((rows, channels), BF16, "any"), ((per_dev * states, channels), BF16, "any")],
        [
            vmem((states, rows, LANES), F32),
            vmem((states, rows, LANES), F32),
            vmem((n_tiles, rows, LANES), F32),
            vmem((n_tiles, rows, LANES), F32),
            vmem((states, channels), F32),
            vmem((n_tiles, per_dev * (states + 1), LANES), F32),
            vmem((n_tiles, per_dev * (states + 1), LANES), F32),
            vmem((n_tiles, rows + per_dev, LANES), F32),
            vmem((rows, channels), BF16),
            vmem((per_dev * states, channels), BF16),
            dma((2, n_tiles // 2)),
            dma((3,)),
        ] + [pltpu.SMEM(holder.shape, jnp.int32)] * 3,
    )
    return out, state.reshape(per_dev, states, channels)


def solution(mesh):
    placed = (
        P(("groups", "replica"), "tensor"),
        P(("groups", "replica"), "tensor"),
        P(None, "tensor"),
        P("tensor"),
        P("tensor", None),
        P(None, "tensor"),
        P("tensor"),
        P(None, "tensor"),
        P("tensor"),
        P(("groups", "replica"), None, "tensor"),
        P(("groups", "replica"), None, "tensor"),
        P("groups"),
        P("groups"),
        P("groups"),
    )
    return jax.shard_map(
        functools.partial(shards, mesh),
        mesh=mesh,
        in_specs=placed,
        out_specs=(P(("groups", "replica"), "tensor"), P(("groups", "replica"), None, "tensor")),
        check_vma=False,
    )
```

```python
import functools

import jax
import jax.numpy as jnp
from jax import lax
from jax.experimental import pallas as pl
from jax.experimental.pallas import tpu as pltpu
from jax.sharding import PartitionSpec as P

NEW = 32
LANES = 128
MIB = 1024 * 1024
UNROLL = 32
LOG2E = 1.4426950408889634
F32, BF16 = jnp.float32, jnp.bfloat16
NT = (((1,), (1,)), ((), ()))


def silu(v):
    half = 0.5 * v
    return half + half * jnp.tanh(half)


def softplus(v):
    u = jnp.exp2(jnp.abs(v) * -LOG2E)
    return jnp.maximum(v, 0.0) + jnp.where(u < 2.0**-10, u - 0.5 * (u * u), jnp.log(1.0 + u))


def split_index(value, inner):
    assert inner & (inner - 1) == 0
    return value >> (inner.bit_length() - 1), value & (inner - 1)


def pick_rows(values, row_low, count):
    out = jnp.zeros(row_low.shape, jnp.int32)
    for r in range(count):
        out = jnp.where(row_low == r, values[r], out)
    return out


def request_places(dims, ints, me):
    per_dev, n_replica, _, relative = dims
    places, slot_ids, lengths = [], [], []
    for r in range(per_dev):
        request = me * per_dev + r
        place = ints[0][request]
        if relative:
            place = place ^ me
            place = place ^ (place >> 1)
        places.append(place)
        slot_ids.append(ints[1][request])
        lengths.append(ints[2][request])
    return places, slot_ids, lengths


def fetch_rows(target, live, pieces):
    total = None
    for first, value in pieces:
        col = lax.broadcasted_iota(jnp.int32, (target.shape[0], value.shape[0]), 1) + first
        select = jnp.where((col == target) & live, 1.0, 0.0).astype(BF16)
        part = jnp.dot(select, value, preferred_element_type=F32)
        total = part if total is None else total + part
    return total


def pack_kernel(dims, refs_in, refs_out, scratch):
    slots, taps = dims
    ssm_hbm, conv_hbm = refs_in
    block_ref, conv_ref = refs_out
    conv_v, sems = scratch
    states = pltpu.make_async_copy(ssm_hbm, block_ref.at[: ssm_hbm.shape[0]], sems.at[0])
    inputs = pltpu.make_async_copy(conv_hbm, conv_v, sems.at[1])
    states.start()
    inputs.start()
    inputs.wait()
    lines = []
    for slot in range(slots):
        for tap in range(taps):
            line = conv_v[min(tap, taps - 2)].astype(F32)[slot : slot + 1]
            lines.append(line if tap < taps - 1 else jnp.zeros_like(line))
    rows = jnp.concatenate(lines, axis=0).astype(BF16)
    conv_ref[...] = rows
    block_ref[ssm_hbm.shape[0] :, :] = rows
    states.wait()


def project_kernel(dims, refs_in, refs_out, scratch):
    per_dev = dims
    x_hbm, wt_hbm, cw_hbm, cb_hbm = refs_in
    mixed_hbm, head_hbm, part_hbm = refs_out
    x_v, wt_v, cw_v, cb_v, joined, mixed_v, head_v, part_f, part_v, sems, out_sems = scratch
    rows, channels = x_v.shape
    taps = cw_v.shape[0]
    lines = (taps - 1) * per_dev
    pairs = [(cw_hbm, cw_v), (cb_hbm, cb_v)]
    width = min(512, channels)
    chunks = [slice(c * width, (c + 1) * width) for c in range(channels // width)]
    for chunk in chunks:
        pairs += [(x_hbm.at[:, chunk], x_v.at[:, chunk]), (wt_hbm.at[:, chunk], wt_v.at[:, chunk])]
    copies = [pltpu.make_async_copy(src, dst, sems.at[i]) for i, (src, dst) in enumerate(pairs)]
    for copy in copies:
        copy.start()

    joined[:, :lines, :] = jnp.zeros((channels // LANES, lines, LANES), F32)
    copies[0].wait()
    copies[1].wait()
    outs = []
    for c, chunk in enumerate(chunks):
        copies[2 + 2 * c].wait()
        for tile in range(c * width // LANES, (c + 1) * width // LANES):
            lanes = slice(tile * LANES, (tile + 1) * LANES)
            for r in range(per_dev):
                tokens = x_v[r * NEW : (r + 1) * NEW, lanes].astype(F32)
                joined[tile, pl.ds(lines + r, NEW, stride=per_dev), :] = tokens
            weight = [cw_v[k : k + 1, lanes].astype(F32) for k in range(taps)]
            bias = cb_v[:, lanes]
            for first in range(0, rows, LANES):
                summed = bias + joined[tile, first : first + LANES, :] * weight[0]
                for k in range(1, taps):
                    begin = first + k * per_dev
                    summed = summed + joined[tile, begin : begin + LANES, :] * weight[k]
                if first == 0:
                    head_v[:, lanes] = summed[: head_v.shape[0]]
                mixed_v[first : first + LANES, lanes] = silu(summed).astype(BF16)
        copies[3 + 2 * c].wait()
        part = lax.dot_general(wt_v[:, chunk], mixed_v[:, chunk], NT, preferred_element_type=F32)
        if c == 0:
            part_f[...] = part
        else:
            part_f[...] += part
        outs.append(pltpu.make_async_copy(mixed_v.at[:, chunk], mixed_hbm.at[:, chunk], out_sems.at[c]))
        outs[-1].start()
    part_v[...] = part_f[...].astype(BF16)
    for src, dst in ((part_v, part_hbm), (head_v, head_hbm)):
        outs.append(pltpu.make_async_copy(src, dst, out_sems.at[len(outs)]))
        outs[-1].start()
    for copy in outs:
        copy.wait()


def history_kernel(dims, refs_in, refs_out, scratch):
    dims, block, firsts = dims
    per_dev, n_replica, slots, _ = dims
    holder, slot_id, prefix_len, head_ref, part_ref, wt_ref, cw_ref = refs_in[:7]
    pieces = refs_in[7:]
    mixed_ref, fixed_ref = refs_out
    taps = cw_ref.shape[0]
    me = lax.axis_index("replica")
    places, slot_ids, lengths = request_places(dims, (holder, slot_id, prefix_len), me)
    tap, request = split_index(lax.broadcasted_iota(jnp.int32, (per_dev * taps, 1), 0), per_dev)
    starts = [places[r] * block + (block - slots * taps) + slot_ids[r] * taps for r in range(per_dev)]
    target = pick_rows(starts, request, per_dev) + tap
    live = (tap < taps - 1) & (taps - 1 - tap <= pick_rows(lengths, request, per_dev))
    history = fetch_rows(target, live, [(first, ref[...]) for first, ref in zip(firsts, pieces)])
    sums = []
    for t in range(taps):
        summed = head_ref[t * per_dev : (t + 1) * per_dev]
        for k in range(taps - 1 - t):
            weight = cw_ref[k : k + 1].astype(F32)
            summed = summed + history[(t + k) * per_dev : (t + k + 1) * per_dev] * weight
        sums.append(summed)
    mixed = silu(jnp.concatenate(sums, axis=0)).astype(BF16)
    mixed_ref[...] = mixed
    part = lax.dot_general(wt_ref[...], mixed, NT, preferred_element_type=F32)
    fixed_ref[...] = part_ref[...]
    fixed_ref[:, : per_dev * taps] = part.astype(BF16)


def prepare_kernel(dims, refs_in, refs_out, scratch):
    mixed_ref, head_ref, z_ref, al_ref, skip_ref = refs_in
    gate_ref, skipped_ref, rate_ref = refs_out
    rows, channels = z_ref.shape
    head = head_ref.shape[0]
    gate_ref[...] = silu(z_ref[...].astype(F32))
    rate_ref[...] = jnp.exp(al_ref[...]) * (-LOG2E)
    for tile in range(channels // LANES):
        lanes = slice(tile * LANES, (tile + 1) * LANES)
        skipped_ref[tile, :head, :] = skip_ref[:, lanes] * head_ref[:, lanes].astype(F32)
        skipped_ref[tile, head:, :] = skip_ref[:, lanes] * mixed_ref[head:, lanes].astype(F32)


def scan_kernel(dims, refs_in, refs_out, scratch):
    per_dev, n_replica, _, _ = dims
    mixed_ref, head_ref, dtw_ref, dtb_ref, gate_ref, skipped_ref, rate_ref = refs_in[3:10]
    out_hbm, state_hbm = refs_out
    b_tab, c_tab, dt_v, drive_v, start_tm, final_tm, y_v, out_v, state_v, out_sems, int_sems = scratch[:11]
    ints = scratch[11:]
    int_copies = [pltpu.make_async_copy(refs_in[i], ints[i], int_sems.at[i]) for i in range(len(ints))]
    for copy in int_copies:
        copy.start()
    n_pieces = sum(1 for ref in refs_in[10:] if ref.shape[-1] == gate_ref.shape[1])
    parts, pieces = refs_in[10:-n_pieces], refs_in[-n_pieces:]
    rows, channels = gate_ref.shape
    states = rate_ref.shape[0]
    rank = dtw_ref.shape[0]
    head = head_ref.shape[0]

    projected = parts[0][...].astype(F32)
    for part in parts[1:]:
        projected = projected + part[...].astype(F32)
    c_part = projected[rank + states :]
    c_high = c_part.astype(BF16).astype(F32)
    shape = (2 * states, states * LANES)
    term = lax.broadcasted_iota(jnp.int32, shape, 0) & (states - 1)
    lane_group, _ = split_index(lax.broadcasted_iota(jnp.int32, shape, 1), LANES)
    spread = jnp.where(term == lane_group, 1.0, 0.0).astype(BF16)
    c_terms = jnp.concatenate([c_high, c_part - c_high], axis=0).T.astype(BF16)
    projected = projected[: rank + states].T
    dt_low = projected[:, :rank].astype(BF16)
    late = projected[:, rank:]
    n_tiles = channels // LANES
    wide = min(4, n_tiles)
    per_chunk = states * wide // n_tiles
    for c in range(n_tiles // wide):
        for n in range(c * per_chunk, (c + 1) * per_chunk):
            b_tab[n] = jnp.broadcast_to(late[:, n : n + 1], (rows, LANES))
        lanes = slice(c * per_chunk * LANES, (c + 1) * per_chunk * LANES)
        repeated = jnp.dot(c_terms, spread[:, lanes], preferred_element_type=F32)
        for n in range(per_chunk):
            c_tab[c * per_chunk + n] = repeated[:, n * LANES : (n + 1) * LANES]
        weights = dtw_ref[:, c * wide * LANES : (c + 1) * wide * LANES]
        raw = jnp.dot(dt_low, weights, preferred_element_type=F32)
        for j in range(wide):
            tile = c * wide + j
            lanes = slice(tile * LANES, (tile + 1) * LANES)
            for first in range(0, rows, LANES):
                here = slice(first, first + LANES)
                dt = softplus(raw[here, j * LANES : (j + 1) * LANES] + dtb_ref[:, lanes])
                mixed = mixed_ref[here, lanes]
                if first == 0:
                    mixed = jnp.concatenate([head_ref[:, lanes], mixed[head:]], axis=0)
                mixed = mixed.astype(F32)
                dt_v[tile, here, :] = dt
                drive_v[tile, here, :] = dt * mixed

    me = lax.axis_index("replica")
    for copy in int_copies:
        copy.wait()
    places, slot_ids, lengths = request_places(dims, ints, me)
    for r in range(per_dev):
        spot = pl.ds(pl.multiple_of(slot_ids[r] * states, states), states)
        for tile in range(n_tiles):
            lanes = slice(tile * LANES, (tile + 1) * LANES)
            if n_pieces == 1:
                value = pieces[0][places[r], spot, lanes]
            else:
                value = pieces[0][spot, lanes]
                for p in range(1, n_pieces):
                    value = jnp.where(places[r] == p, pieces[p][spot, lanes], value)
            value = value.astype(F32)
            value = jnp.where(lengths[r] > 0, value, jnp.zeros_like(value))
            start_tm[tile, pl.ds(r, states, stride=per_dev), :] = value

    tiles = 2
    half = states // 2
    width = tiles * LANES
    n_groups = n_tiles // tiles

    def out_copies(g):
        lanes = pl.ds(pl.multiple_of(g * width, width), width)
        return [
            pltpu.make_async_copy(src.at[:, lanes], dst.at[:, lanes], out_sems.at[i, g])
            for i, (src, dst) in enumerate(((out_v, out_hbm), (state_v, state_hbm)))
        ]

    def finish(g):
        for j in range(tiles):
            tile = g * tiles + j
            lanes = pl.ds(pl.multiple_of(tile * LANES, LANES), LANES)
            for r in range(per_dev):
                here = slice(r * NEW, (r + 1) * NEW)
                value = y_v[tile, pl.ds(r, NEW, stride=per_dev), :] * gate_ref[here, lanes]
                out_v[here, lanes] = value.astype(BF16)
                final = final_tm[tile, pl.ds(r, states, stride=per_dev), :]
                state_v[r * states : (r + 1) * states, lanes] = final.astype(BF16)

    def scan_group(g):
        group = [g * tiles + j for j in range(tiles)]
        lanes = [pl.ds(pl.multiple_of(tile * LANES, LANES), LANES) for tile in group]
        for first in range(0, states, half):
            ids = range(first, first + half)
            rates = [[jnp.broadcast_to(rate_ref[n : n + 1, lane], (per_dev, LANES)) for n in ids] for lane in lanes]

            def advance(step, state):
                state = list(state)
                for u in range(UNROLL):
                    now = pl.ds(pl.multiple_of((step * UNROLL + u) * per_dev, per_dev), per_dev)
                    dt = [dt_v[tile, now, :] for tile in group]
                    drive = [drive_v[tile, now, :] for tile in group]
                    sums = [None] * tiles
                    for k, n in enumerate(ids):
                        b, c = b_tab[n, now, :], c_tab[n, now, :]
                        for j in range(tiles):
                            i = j * half + k
                            state[i] = jnp.exp2(dt[j] * rates[j][k]) * state[i] + drive[j] * b
                            term = state[i] * c
                            sums[j] = term if sums[j] is None else sums[j] + term
                    for j, tile in enumerate(group):
                        before = skipped_ref[tile, now, :] if first == 0 else y_v[tile, now, :]
                        y_v[tile, now, :] = before + sums[j]
                return tuple(state)

            state = tuple(start_tm[tile, n * per_dev : (n + 1) * per_dev, :] for tile in group for n in ids)
            if NEW == UNROLL:
                state = advance(0, state)
            else:
                state = lax.fori_loop(0, NEW // UNROLL, advance, state)
            for j, tile in enumerate(group):
                for k, n in enumerate(ids):
                    final_tm[tile, n * per_dev : (n + 1) * per_dev, :] = state[j * half + k]

    def one_group(g, carry):
        before = jnp.maximum(g - 1, 0)
        finish(before)
        scan_group(g)

        @pl.when(g > 0)
        def _():
            for copy in out_copies(before):
                copy.start()

        return carry

    final_tm[:tiles] = jnp.zeros((tiles,) + final_tm.shape[1:], F32)
    y_v[:tiles] = jnp.zeros((tiles,) + y_v.shape[1:], F32)
    lax.fori_loop(0, n_groups, one_group, 0)
    finish(n_groups - 1)
    for copy in out_copies(n_groups - 1):
        copy.start()

    def last_wait(g, carry):
        for copy in out_copies(g):
            copy.wait()
        return carry

    lax.fori_loop(0, n_groups, last_wait, 0)


def split_refs(kernel, dims, n_in, n_out):
    def body(*refs):
        kernel(dims, refs[:n_in], refs[n_in : n_in + n_out], refs[n_in + n_out :])

    return body


def call(kernel, dims, name, limit, ins, outs, scratch):
    spaces = {"hbm": pltpu.HBM, "any": pl.ANY, "vmem": pltpu.VMEM, "smem": pltpu.SMEM}
    values = [
        pltpu.with_memory_space_constraint(value, pltpu.HBM) if place == "hbm" else value for value, place in ins
    ]
    return pl.pallas_call(
        split_refs(kernel, dims, len(ins), len(outs)),
        in_specs=[pl.BlockSpec(memory_space=spaces[place]) for _, place in ins],
        out_specs=[pl.BlockSpec(memory_space=spaces[place]) for _, _, place in outs],
        out_shape=[jax.ShapeDtypeStruct(shape, dtype) for shape, dtype, _ in outs],
        scratch_shapes=scratch,
        compiler_params=pltpu.CompilerParams(vmem_limit_bytes=limit * MIB),
        name=name,
    )(*values)


def swap(value, axis, size, mask):
    return lax.ppermute(value, axis, [(i, i ^ mask) for i in range(size)])


def shards(mesh, x_new, z_new, conv_weight, conv_bias, x_proj_weight, dt_proj_weight, dt_bias, a_log, d_skip,
           cache_ssm, cache_conv, holder, slot_id, prefix_len):
    n_replica, n_tensor = mesh.shape["replica"], mesh.shape["tensor"]
    rows, channels = x_new.shape
    per_dev = rows // NEW
    states = a_log.shape[0]
    rank = dt_proj_weight.shape[0]
    taps = conv_weight.shape[0]
    slots = cache_ssm.shape[0]
    out_cols = x_proj_weight.shape[1]
    requests = holder.shape[0]

    vmem, dma = pltpu.VMEM, pltpu.SemaphoreType.DMA
    ssm_rows = slots * states
    rows_all, conv_rows = call(
        pack_kernel, (slots, taps), "pack", 20,
        [(cache_ssm.reshape(ssm_rows, channels), "hbm"), (cache_conv.transpose(1, 0, 2), "hbm")],
        [((ssm_rows + slots * taps, channels), BF16, "vmem"), ((slots * taps, channels), BF16, "vmem")],
        [vmem((taps - 1, slots, channels), BF16), dma((2,))],
    )
    block = rows_all.shape[0]
    relative = n_replica == 4
    if relative:
        far = swap(rows_all, "replica", n_replica, 3)
        near = swap(rows_all, "replica", n_replica, 1)
        conv_two = swap(conv_rows, "replica", n_replica, 2)
        conv_pieces = [rows_all, near, far, conv_two]
        firsts = (0, block, 2 * block, 4 * block - slots * taps)
        ssm_pieces = [rows_all, near, far, swap(far, "replica", n_replica, 1)]
    else:
        ssm_pieces = [lax.all_gather(rows_all, "replica")]
        conv_pieces, firsts = [ssm_pieces[0].reshape(-1, channels)], (0,)

    n_chunks = channels // min(512, channels)
    dims = (per_dev, n_replica, slots, relative)
    head = per_dev * taps
    weights = x_proj_weight.T
    requests = [(holder, "smem"), (slot_id, "smem"), (prefix_len, "smem")]

    mixed, head_sums, part = call(
        project_kernel, per_dev, "conv_project", 40,
        [(x_new, "hbm"), (weights, "hbm"), (conv_weight, "hbm"), (conv_bias[None, :], "hbm")],
        [((rows, channels), BF16, "any"), ((head, channels), F32, "any"), ((out_cols, rows), BF16, "any")],
        [
            vmem((rows, channels), BF16),
            vmem((out_cols, channels), BF16),
            vmem((taps, channels), BF16),
            vmem((1, channels), F32),
            vmem((channels // LANES, rows + taps * per_dev, LANES), F32),
            vmem((rows, channels), BF16),
            vmem((head, channels), F32),
            vmem((out_cols, rows), F32),
            vmem((out_cols, rows), BF16),
            dma((2 + 2 * n_chunks,)),
            dma((n_chunks + 2,)),
        ],
    )
    mixed_head, part = call(
        history_kernel, (dims, block, firsts), "history", 20,
        requests
        + [(value, "vmem") for value in [head_sums, part, weights, conv_weight] + conv_pieces],
        [((head, channels), BF16, "vmem"), ((out_cols, rows), BF16, "vmem")],
        [],
    )
    parts = [part]
    mask = n_tensor // 2
    while mask:
        parts = parts + [swap(value, "tensor", n_tensor, mask) for value in reversed(parts)]
        mask //= 2

    n_tiles = channels // LANES
    prepared = call(
        prepare_kernel, None, "prepare", 40,
        [(value, "vmem") for value in (mixed, mixed_head, z_new, a_log, d_skip[None, :])],
        [((rows, channels), F32, "vmem"), ((n_tiles, rows, LANES), F32, "vmem"), ((states, channels), F32, "vmem")],
        [],
    )
    operands = [mixed, mixed_head, dt_proj_weight, dt_bias[None, :], *prepared]
    out, state = call(
        scan_kernel, dims, "dt_scan_gate", 40,
        [(value, "any") for value, _ in requests] + [(value, "vmem") for value in operands + parts + ssm_pieces],
        [((rows, channels), BF16, "any"), ((per_dev * states, channels), BF16, "any")],
        [
            vmem((states, rows, LANES), F32),
            vmem((states, rows, LANES), F32),
            vmem((n_tiles, rows, LANES), F32),
            vmem((n_tiles, rows, LANES), F32),
            vmem((n_tiles, per_dev * (states + 1), LANES), F32),
            vmem((n_tiles, per_dev * (states + 1), LANES), F32),
            vmem((n_tiles, rows + per_dev, LANES), F32),
            vmem((rows, channels), BF16),
            vmem((per_dev * states, channels), BF16),
            dma((2, n_tiles // 2)),
            dma((3,)),
        ] + [pltpu.SMEM(holder.shape, jnp.int32)] * 3,
    )
    return out, state.reshape(per_dev, states, channels)


def solution(mesh):
    placed = (
        P(("groups", "replica"), "tensor"),
        P(("groups", "replica"), "tensor"),
        P(None, "tensor"),
        P("tensor"),
        P("tensor", None),
        P(None, "tensor"),
        P("tensor"),
        P(None, "tensor"),
        P("tensor"),
        P(("groups", "replica"), None, "tensor"),
        P(("groups", "replica"), None, "tensor"),
        P("groups"),
        P("groups"),
        P("groups"),
    )
    return jax.shard_map(
        functools.partial(shards, mesh),
        mesh=mesh,
        in_specs=placed,
        out_specs=(P(("groups", "replica"), "tensor"), P(("groups", "replica"), None, "tensor")),
        check_vma=False,
    )
```

```python
import functools

import jax
import jax.numpy as jnp
from jax import lax
from jax.experimental import pallas as pl
from jax.experimental.pallas import tpu as pltpu
from jax.sharding import PartitionSpec as P

NEW = 32
LANES = 128
MIB = 1024 * 1024
LOG2E = 1.4426950408889634
F32, BF16 = jnp.float32, jnp.bfloat16
NT = (((1,), (1,)), ((), ()))


def silu(v):
    half = 0.5 * v
    return half + half * jnp.tanh(half)


def softplus(v):
    u = jnp.exp2(jnp.abs(v) * -LOG2E)
    return jnp.maximum(v, 0.0) + jnp.where(u < 2.0**-10, u - 0.5 * (u * u), jnp.log(1.0 + u))


def split_index(value, inner):
    assert inner & (inner - 1) == 0
    return value >> (inner.bit_length() - 1), value & (inner - 1)


def pick_rows(values, row_low, count):
    out = jnp.zeros(row_low.shape, jnp.int32)
    for r in range(count):
        out = jnp.where(row_low == r, values[r], out)
    return out


def request_places(dims, ints, me):
    per_dev, n_replica, _, relative = dims
    places, slot_ids, lengths = [], [], []
    for r in range(per_dev):
        request = me * per_dev + r
        place = ints[0][request]
        if relative:
            place = place ^ me
            place = place ^ (place >> 1)
        places.append(place)
        slot_ids.append(ints[1][request])
        lengths.append(ints[2][request])
    return places, slot_ids, lengths


def fetch_rows(target, live, pieces):
    total = None
    for first, value in pieces:
        col = lax.broadcasted_iota(jnp.int32, (target.shape[0], value.shape[0]), 1) + first
        select = jnp.where((col == target) & live, 1.0, 0.0).astype(BF16)
        part = jnp.dot(select, value, preferred_element_type=F32)
        total = part if total is None else total + part
    return total


def pack_kernel(dims, refs_in, refs_out, scratch):
    slots, taps = dims
    ssm_hbm, conv_hbm = refs_in
    block_ref, conv_ref = refs_out
    conv_v, sems = scratch
    states = pltpu.make_async_copy(ssm_hbm, block_ref.at[: ssm_hbm.shape[0]], sems.at[0])
    inputs = pltpu.make_async_copy(conv_hbm, conv_v, sems.at[1])
    states.start()
    inputs.start()
    inputs.wait()
    lines = []
    for slot in range(slots):
        for tap in range(taps):
            line = conv_v[min(tap, taps - 2)].astype(F32)[slot : slot + 1]
            lines.append(line if tap < taps - 1 else jnp.zeros_like(line))
    rows = jnp.concatenate(lines, axis=0).astype(BF16)
    conv_ref[...] = rows
    block_ref[ssm_hbm.shape[0] :, :] = rows
    states.wait()


def project_kernel(dims, refs_in, refs_out, scratch):
    per_dev = dims
    x_hbm, wt_hbm, cw_hbm, cb_hbm = refs_in
    mixed_hbm, head_hbm, part_hbm = refs_out
    x_v, wt_v, cw_v, cb_v, joined, mixed_v, head_v, part_f, part_v, sems, out_sems = scratch
    rows, channels = x_v.shape
    taps = cw_v.shape[0]
    lines = (taps - 1) * per_dev
    pairs = [(cw_hbm, cw_v), (cb_hbm, cb_v)]
    width = min(512, channels)
    chunks = [slice(c * width, (c + 1) * width) for c in range(channels // width)]
    for chunk in chunks:
        pairs += [(x_hbm.at[:, chunk], x_v.at[:, chunk]), (wt_hbm.at[:, chunk], wt_v.at[:, chunk])]
    copies = [pltpu.make_async_copy(src, dst, sems.at[i]) for i, (src, dst) in enumerate(pairs)]
    for copy in copies:
        copy.start()

    joined[:, :lines, :] = jnp.zeros((channels // LANES, lines, LANES), F32)
    copies[0].wait()
    copies[1].wait()
    outs = []
    for c, chunk in enumerate(chunks):
        copies[2 + 2 * c].wait()
        for tile in range(c * width // LANES, (c + 1) * width // LANES):
            lanes = slice(tile * LANES, (tile + 1) * LANES)
            for r in range(per_dev):
                tokens = x_v[r * NEW : (r + 1) * NEW, lanes].astype(F32)
                joined[tile, pl.ds(lines + r, NEW, stride=per_dev), :] = tokens
            weight = [cw_v[k : k + 1, lanes].astype(F32) for k in range(taps)]
            bias = cb_v[:, lanes]
            for first in range(0, rows, LANES):
                summed = bias + joined[tile, first : first + LANES, :] * weight[0]
                for k in range(1, taps):
                    begin = first + k * per_dev
                    summed = summed + joined[tile, begin : begin + LANES, :] * weight[k]
                if first == 0:
                    head_v[:, lanes] = summed[: head_v.shape[0]]
                mixed_v[first : first + LANES, lanes] = silu(summed).astype(BF16)
        copies[3 + 2 * c].wait()
        part = lax.dot_general(wt_v[:, chunk], mixed_v[:, chunk], NT, preferred_element_type=F32)
        if c == 0:
            part_f[...] = part
        else:
            part_f[...] += part
        outs.append(pltpu.make_async_copy(mixed_v.at[:, chunk], mixed_hbm.at[:, chunk], out_sems.at[c]))
        outs[-1].start()
    part_v[...] = part_f[...].astype(BF16)
    for src, dst in ((part_v, part_hbm), (head_v, head_hbm)):
        outs.append(pltpu.make_async_copy(src, dst, out_sems.at[len(outs)]))
        outs[-1].start()
    for copy in outs:
        copy.wait()


def history_kernel(dims, refs_in, refs_out, scratch):
    dims, block, firsts = dims
    per_dev, n_replica, slots, _ = dims
    holder, slot_id, prefix_len, head_ref, part_ref, wt_ref, cw_ref = refs_in[:7]
    pieces = refs_in[7:]
    mixed_ref, fixed_ref = refs_out
    taps = cw_ref.shape[0]
    me = lax.axis_index("replica")
    places, slot_ids, lengths = request_places(dims, (holder, slot_id, prefix_len), me)
    tap, request = split_index(lax.broadcasted_iota(jnp.int32, (per_dev * taps, 1), 0), per_dev)
    starts = [places[r] * block + (block - slots * taps) + slot_ids[r] * taps for r in range(per_dev)]
    target = pick_rows(starts, request, per_dev) + tap
    live = (tap < taps - 1) & (taps - 1 - tap <= pick_rows(lengths, request, per_dev))
    history = fetch_rows(target, live, [(first, ref[...]) for first, ref in zip(firsts, pieces)])
    sums = []
    for t in range(taps):
        summed = head_ref[t * per_dev : (t + 1) * per_dev]
        for k in range(taps - 1 - t):
            weight = cw_ref[k : k + 1].astype(F32)
            summed = summed + history[(t + k) * per_dev : (t + k + 1) * per_dev] * weight
        sums.append(summed)
    mixed = silu(jnp.concatenate(sums, axis=0)).astype(BF16)
    mixed_ref[...] = mixed
    part = lax.dot_general(wt_ref[...], mixed, NT, preferred_element_type=F32)
    fixed_ref[...] = part_ref[...]
    fixed_ref[:, : per_dev * taps] = part.astype(BF16)


def prepare_kernel(dims, refs_in, refs_out, scratch):
    mixed_ref, head_ref, z_ref, al_ref, skip_ref = refs_in
    gate_ref, skipped_ref, rate_ref = refs_out
    rows, channels = z_ref.shape
    head = head_ref.shape[0]
    gate_ref[...] = silu(z_ref[...].astype(F32))
    rate_ref[...] = jnp.exp(al_ref[...]) * (-LOG2E)
    for tile in range(channels // LANES):
        lanes = slice(tile * LANES, (tile + 1) * LANES)
        skipped_ref[tile, :head, :] = skip_ref[:, lanes] * head_ref[:, lanes].astype(F32)
        skipped_ref[tile, head:, :] = skip_ref[:, lanes] * mixed_ref[head:, lanes].astype(F32)


def scan_kernel(dims, refs_in, refs_out, scratch):
    per_dev, n_replica, _, _ = dims
    mixed_ref, head_ref, dtw_ref, dtb_ref, gate_ref, skipped_ref, rate_ref = refs_in[3:10]
    out_hbm, state_hbm = refs_out
    b_tab, c_tab, low_v, start_tm, out_v, state_v, out_sems, int_sems = scratch[:8]
    even, odd, ints = scratch[8:12], scratch[12:16], scratch[16:]
    int_copies = [pltpu.make_async_copy(refs_in[i], ints[i], int_sems.at[i]) for i in range(len(ints))]
    for copy in int_copies:
        copy.start()
    n_pieces = sum(1 for ref in refs_in[10:] if ref.shape[-1] == gate_ref.shape[1])
    parts, pieces = refs_in[10:-n_pieces], refs_in[-n_pieces:]
    rows, channels = gate_ref.shape
    states = rate_ref.shape[0]
    rank = dtw_ref.shape[0]
    head = head_ref.shape[0]

    projected = parts[0][...].astype(F32)
    for part in parts[1:]:
        projected = projected + part[...].astype(F32)
    c_part = projected[rank + states :]
    c_high = c_part.astype(BF16).astype(F32)
    shape = (2 * states, states * LANES)
    term = lax.broadcasted_iota(jnp.int32, shape, 0) & (states - 1)
    lane_group, _ = split_index(lax.broadcasted_iota(jnp.int32, shape, 1), LANES)
    spread = jnp.where(term == lane_group, 1.0, 0.0).astype(BF16)
    c_terms = jnp.concatenate([c_high, c_part - c_high], axis=0).T.astype(BF16)
    projected = projected[: rank + states].T
    dt_low = projected[:, :rank].astype(BF16)
    late = projected[:, rank:]
    n_tiles = channels // LANES
    tiles = 2
    half = states // 2
    width = tiles * LANES
    n_groups = n_tiles // tiles
    low_v[...] = dt_low

    def group_lanes(g):
        return pl.ds(pl.multiple_of(g * width, width), width)

    def tile_lanes(g, j):
        return pl.ds(pl.multiple_of((g * tiles + j) * LANES, LANES), LANES)

    def steps(g, held):
        dt_v, drive_v = held[:2]
        raw = jnp.dot(low_v[...], dtw_ref[:, group_lanes(g)], preferred_element_type=F32)
        for j in range(tiles):
            lanes = tile_lanes(g, j)
            bias = dtb_ref[:, lanes]
            for first in range(0, rows, LANES):
                here = slice(first, first + LANES)
                dt = softplus(raw[here, j * LANES : (j + 1) * LANES] + bias)
                mixed = mixed_ref[here, lanes]
                if first == 0:
                    mixed = jnp.concatenate([head_ref[:, lanes], mixed[head:]], axis=0)
                dt_v[j, here, :] = dt
                drive_v[j, here, :] = dt * mixed.astype(F32)

    wide = 4
    for c in range(0, states, wide):
        for n in range(c, c + wide):
            b_tab[n] = jnp.broadcast_to(late[:, n : n + 1], (rows, LANES))
        repeated = jnp.dot(c_terms, spread[:, c * LANES : (c + wide) * LANES], preferred_element_type=F32)
        for n in range(wide):
            c_tab[c + n] = repeated[:, n * LANES : (n + 1) * LANES]
    steps(0, even)

    me = lax.axis_index("replica")
    for copy in int_copies:
        copy.wait()
    places, slot_ids, lengths = request_places(dims, ints, me)
    for r in range(per_dev):
        spot = pl.ds(pl.multiple_of(slot_ids[r] * states, states), states)
        for tile in range(n_tiles):
            lanes = slice(tile * LANES, (tile + 1) * LANES)
            if n_pieces == 1:
                value = pieces[0][places[r], spot, lanes]
            else:
                value = pieces[0][spot, lanes]
                for p in range(1, n_pieces):
                    value = jnp.where(places[r] == p, pieces[p][spot, lanes], value)
            value = value.astype(F32)
            value = jnp.where(lengths[r] > 0, value, jnp.zeros_like(value))
            start_tm[tile, pl.ds(r, states, stride=per_dev), :] = value

    def out_copies(g):
        lanes = group_lanes(g)
        return [
            pltpu.make_async_copy(src.at[:, lanes], dst.at[:, lanes], out_sems.at[i, g])
            for i, (src, dst) in enumerate(((out_v, out_hbm), (state_v, state_hbm)))
        ]

    def finish(g, held):
        y_v, final_tm = held[2:]
        for j in range(tiles):
            lanes = tile_lanes(g, j)
            for r in range(per_dev):
                here = slice(r * NEW, (r + 1) * NEW)
                value = y_v[j, pl.ds(r, NEW, stride=per_dev), :] * gate_ref[here, lanes]
                out_v[here, lanes] = value.astype(BF16)
                final = final_tm[j, pl.ds(r, states, stride=per_dev), :]
                state_v[r * states : (r + 1) * states, lanes] = final.astype(BF16)

    def scan(g, held):
        dt_v, drive_v, y_v, final_tm = held
        for first in range(0, states, half):
            ids = range(first, first + half)
            rates, state = {}, {}
            for j in range(tiles):
                for n in ids:
                    rates[j, n] = jnp.broadcast_to(rate_ref[n : n + 1, tile_lanes(g, j)], (per_dev, LANES))
                    state[j, n] = start_tm[g * tiles + j, n * per_dev : (n + 1) * per_dev, :]
            for t in range(NEW):
                now = slice(t * per_dev, (t + 1) * per_dev)
                dt = [dt_v[j, now, :] for j in range(tiles)]
                drive = [drive_v[j, now, :] for j in range(tiles)]
                sums = [skipped_ref[g * tiles + j, now, :] if first == 0 else y_v[j, now, :] for j in range(tiles)]
                for n in ids:
                    b, c = b_tab[n, now, :], c_tab[n, now, :]
                    for j in range(tiles):
                        state[j, n] = jnp.exp2(dt[j] * rates[j, n]) * state[j, n] + drive[j] * b
                        sums[j] = sums[j] + state[j, n] * c
                for j in range(tiles):
                    y_v[j, now, :] = sums[j]
            for j in range(tiles):
                for n in ids:
                    final_tm[j, n * per_dev : (n + 1) * per_dev, :] = state[j, n]

    def two_groups(i, carry):
        g = 2 * i
        before = jnp.maximum(g - 1, 0)
        finish(before, odd)
        scan(g, even)
        steps(g + 1, odd)
        finish(g, even)
        scan(g + 1, odd)
        steps(jnp.minimum(g + 2, n_groups - 1), even)
        for copy in out_copies(g):
            copy.start()

        @pl.when(i > 0)
        def _():
            for copy in out_copies(before):
                copy.start()

        return carry

    for ref in odd[2:]:
        ref[...] = jnp.zeros(ref.shape, F32)
    lax.fori_loop(0, n_groups // 2, two_groups, 0)
    finish(n_groups - 1, odd)
    for copy in out_copies(n_groups - 1):
        copy.start()

    def last_wait(g, carry):
        for copy in out_copies(g):
            copy.wait()
        return carry

    lax.fori_loop(0, n_groups, last_wait, 0)


def split_refs(kernel, dims, n_in, n_out):
    def body(*refs):
        kernel(dims, refs[:n_in], refs[n_in : n_in + n_out], refs[n_in + n_out :])

    return body


def call(kernel, dims, name, limit, ins, outs, scratch):
    spaces = {"hbm": pltpu.HBM, "any": pl.ANY, "vmem": pltpu.VMEM, "smem": pltpu.SMEM}
    values = [
        pltpu.with_memory_space_constraint(value, pltpu.HBM) if place == "hbm" else value for value, place in ins
    ]
    return pl.pallas_call(
        split_refs(kernel, dims, len(ins), len(outs)),
        in_specs=[pl.BlockSpec(memory_space=spaces[place]) for _, place in ins],
        out_specs=[pl.BlockSpec(memory_space=spaces[place]) for _, _, place in outs],
        out_shape=[jax.ShapeDtypeStruct(shape, dtype) for shape, dtype, _ in outs],
        scratch_shapes=scratch,
        compiler_params=pltpu.CompilerParams(vmem_limit_bytes=limit * MIB),
        name=name,
    )(*values)


def swap(value, axis, size, mask):
    return lax.ppermute(value, axis, [(i, i ^ mask) for i in range(size)])


def shards(mesh, x_new, z_new, conv_weight, conv_bias, x_proj_weight, dt_proj_weight, dt_bias, a_log, d_skip,
           cache_ssm, cache_conv, holder, slot_id, prefix_len):
    n_replica, n_tensor = mesh.shape["replica"], mesh.shape["tensor"]
    rows, channels = x_new.shape
    per_dev = rows // NEW
    states = a_log.shape[0]
    rank = dt_proj_weight.shape[0]
    taps = conv_weight.shape[0]
    slots = cache_ssm.shape[0]
    out_cols = x_proj_weight.shape[1]
    requests = holder.shape[0]

    vmem, dma = pltpu.VMEM, pltpu.SemaphoreType.DMA
    ssm_rows = slots * states
    rows_all, conv_rows = call(
        pack_kernel, (slots, taps), "pack", 20,
        [(cache_ssm.reshape(ssm_rows, channels), "hbm"), (cache_conv.transpose(1, 0, 2), "hbm")],
        [((ssm_rows + slots * taps, channels), BF16, "vmem"), ((slots * taps, channels), BF16, "vmem")],
        [vmem((taps - 1, slots, channels), BF16), dma((2,))],
    )
    block = rows_all.shape[0]
    relative = n_replica == 4
    if relative:
        far = swap(rows_all, "replica", n_replica, 3)
        near = swap(rows_all, "replica", n_replica, 1)
        conv_two = swap(conv_rows, "replica", n_replica, 2)
        conv_pieces = [rows_all, near, far, conv_two]
        firsts = (0, block, 2 * block, 4 * block - slots * taps)
        ssm_pieces = [rows_all, near, far, swap(far, "replica", n_replica, 1)]
    else:
        ssm_pieces = [lax.all_gather(rows_all, "replica")]
        conv_pieces, firsts = [ssm_pieces[0].reshape(-1, channels)], (0,)

    n_chunks = channels // min(512, channels)
    dims = (per_dev, n_replica, slots, relative)
    head = per_dev * taps
    weights = x_proj_weight.T
    requests = [(holder, "smem"), (slot_id, "smem"), (prefix_len, "smem")]

    mixed, head_sums, part = call(
        project_kernel, per_dev, "conv_project", 40,
        [(x_new, "hbm"), (weights, "hbm"), (conv_weight, "hbm"), (conv_bias[None, :], "hbm")],
        [((rows, channels), BF16, "any"), ((head, channels), F32, "any"), ((out_cols, rows), BF16, "any")],
        [
            vmem((rows, channels), BF16),
            vmem((out_cols, channels), BF16),
            vmem((taps, channels), BF16),
            vmem((1, channels), F32),
            vmem((channels // LANES, rows + taps * per_dev, LANES), F32),
            vmem((rows, channels), BF16),
            vmem((head, channels), F32),
            vmem((out_cols, rows), F32),
            vmem((out_cols, rows), BF16),
            dma((2 + 2 * n_chunks,)),
            dma((n_chunks + 2,)),
        ],
    )
    mixed_head, part = call(
        history_kernel, (dims, block, firsts), "history", 20,
        requests
        + [(value, "vmem") for value in [head_sums, part, weights, conv_weight] + conv_pieces],
        [((head, channels), BF16, "vmem"), ((out_cols, rows), BF16, "vmem")],
        [],
    )
    parts = [part]
    mask = n_tensor // 2
    while mask:
        parts = parts + [swap(value, "tensor", n_tensor, mask) for value in reversed(parts)]
        mask //= 2

    n_tiles = channels // LANES
    prepared = call(
        prepare_kernel, None, "prepare", 40,
        [(value, "vmem") for value in (mixed, mixed_head, z_new, a_log, d_skip[None, :])],
        [((rows, channels), F32, "vmem"), ((n_tiles, rows, LANES), F32, "vmem"), ((states, channels), F32, "vmem")],
        [],
    )
    operands = [mixed, mixed_head, dt_proj_weight, dt_bias[None, :], *prepared]
    out, state = call(
        scan_kernel, dims, "dt_scan_gate", 40,
        [(value, "any") for value, _ in requests] + [(value, "vmem") for value in operands + parts + ssm_pieces],
        [((rows, channels), BF16, "any"), ((per_dev * states, channels), BF16, "any")],
        [
            vmem((states, rows, LANES), F32),
            vmem((states, rows, LANES), F32),
            vmem((rows, rank), BF16),
            vmem((n_tiles, per_dev * (states + 1), LANES), F32),
            vmem((rows, channels), BF16),
            vmem((per_dev * states, channels), BF16),
            dma((2, n_tiles // 2)),
            dma((3,)),
        ]
        + [
            vmem((2, rows, LANES), F32),
            vmem((2, rows, LANES), F32),
            vmem((2, rows + per_dev, LANES), F32),
            vmem((2, per_dev * (states + 1), LANES), F32),
        ] * 2
        + [pltpu.SMEM(holder.shape, jnp.int32)] * 3,
    )
    return out, state.reshape(per_dev, states, channels)


def solution(mesh):
    placed = (
        P(("groups", "replica"), "tensor"),
        P(("groups", "replica"), "tensor"),
        P(None, "tensor"),
        P("tensor"),
        P("tensor", None),
        P(None, "tensor"),
        P("tensor"),
        P(None, "tensor"),
        P("tensor"),
        P(("groups", "replica"), None, "tensor"),
        P(("groups", "replica"), None, "tensor"),
        P("groups"),
        P("groups"),
        P("groups"),
    )
    return jax.shard_map(
        functools.partial(shards, mesh),
        mesh=mesh,
        in_specs=placed,
        out_specs=(P(("groups", "replica"), "tensor"), P(("groups", "replica"), None, "tensor")),
        check_vma=False,
    )
```

```python
import functools

import jax
import jax.numpy as jnp
from jax import lax
from jax.experimental import pallas as pl
from jax.experimental.pallas import tpu as pltpu
from jax.sharding import PartitionSpec as P

NEW = 32
LANES = 128
MIB = 1024 * 1024
UNROLL = 32
LOG2E = 1.4426950408889634
F32, BF16 = jnp.float32, jnp.bfloat16
NT = (((1,), (1,)), ((), ()))


def silu(v):
    half = 0.5 * v
    return half + half * jnp.tanh(half)


def softplus(v):
    u = jnp.exp2(jnp.abs(v) * -LOG2E)
    return jnp.maximum(v, 0.0) + jnp.where(u < 2.0**-10, u - 0.5 * (u * u), jnp.log(1.0 + u))


def split_index(value, inner):
    assert inner & (inner - 1) == 0
    return value >> (inner.bit_length() - 1), value & (inner - 1)


def pick_rows(values, row_low, count):
    out = jnp.zeros(row_low.shape, jnp.int32)
    for r in range(count):
        out = jnp.where(row_low == r, values[r], out)
    return out


def request_places(dims, ints, me):
    per_dev, n_replica, _, relative = dims
    places, slot_ids, lengths = [], [], []
    for r in range(per_dev):
        request = me * per_dev + r
        place = ints[0][request]
        if relative:
            place = place ^ me
            place = place ^ (place >> 1)
        places.append(place)
        slot_ids.append(ints[1][request])
        lengths.append(ints[2][request])
    return places, slot_ids, lengths


def fetch_rows(target, live, pieces):
    total = None
    for first, value in pieces:
        col = lax.broadcasted_iota(jnp.int32, (target.shape[0], value.shape[0]), 1) + first
        select = jnp.where((col == target) & live, 1.0, 0.0).astype(BF16)
        part = jnp.dot(select, value, preferred_element_type=F32)
        total = part if total is None else total + part
    return total


def pack_kernel(dims, refs_in, refs_out, scratch):
    slots, taps = dims
    ssm_hbm, conv_hbm = refs_in
    block_ref, conv_ref = refs_out
    conv_v, sems = scratch
    states = pltpu.make_async_copy(ssm_hbm, block_ref.at[: ssm_hbm.shape[0]], sems.at[0])
    inputs = pltpu.make_async_copy(conv_hbm, conv_v, sems.at[1])
    states.start()
    inputs.start()
    inputs.wait()
    lines = []
    for slot in range(slots):
        for tap in range(taps):
            line = conv_v[min(tap, taps - 2)].astype(F32)[slot : slot + 1]
            lines.append(line if tap < taps - 1 else jnp.zeros_like(line))
    rows = jnp.concatenate(lines, axis=0).astype(BF16)
    conv_ref[...] = rows
    block_ref[ssm_hbm.shape[0] :, :] = rows
    states.wait()


def project_kernel(dims, refs_in, refs_out, scratch):
    per_dev = dims
    x_hbm, wt_hbm, cw_hbm, cb_hbm = refs_in
    mixed_hbm, head_hbm, part_hbm = refs_out
    x_v, wt_v, cw_v, cb_v, joined, mixed_v, head_v, part_f, part_v, sems, out_sems = scratch
    rows, channels = x_v.shape
    taps = cw_v.shape[0]
    lines = (taps - 1) * per_dev
    pairs = [(cw_hbm, cw_v), (cb_hbm, cb_v)]
    width = min(512, channels)
    chunks = [slice(c * width, (c + 1) * width) for c in range(channels // width)]
    for chunk in chunks:
        pairs += [(x_hbm.at[:, chunk], x_v.at[:, chunk]), (wt_hbm.at[:, chunk], wt_v.at[:, chunk])]
    copies = [pltpu.make_async_copy(src, dst, sems.at[i]) for i, (src, dst) in enumerate(pairs)]
    for copy in copies:
        copy.start()

    joined[:, :lines, :] = jnp.zeros((channels // LANES, lines, LANES), F32)
    copies[0].wait()
    copies[1].wait()
    outs = []
    for c, chunk in enumerate(chunks):
        copies[2 + 2 * c].wait()
        for tile in range(c * width // LANES, (c + 1) * width // LANES):
            lanes = slice(tile * LANES, (tile + 1) * LANES)
            for r in range(per_dev):
                tokens = x_v[r * NEW : (r + 1) * NEW, lanes].astype(F32)
                joined[tile, pl.ds(lines + r, NEW, stride=per_dev), :] = tokens
            weight = [cw_v[k : k + 1, lanes].astype(F32) for k in range(taps)]
            bias = cb_v[:, lanes]
            for first in range(0, rows, LANES):
                summed = bias + joined[tile, first : first + LANES, :] * weight[0]
                for k in range(1, taps):
                    begin = first + k * per_dev
                    summed = summed + joined[tile, begin : begin + LANES, :] * weight[k]
                if first == 0:
                    head_v[:, lanes] = summed[: head_v.shape[0]]
                mixed_v[first : first + LANES, lanes] = silu(summed).astype(BF16)
        copies[3 + 2 * c].wait()
        part = lax.dot_general(wt_v[:, chunk], mixed_v[:, chunk], NT, preferred_element_type=F32)
        if c == 0:
            part_f[...] = part
        else:
            part_f[...] += part
        outs.append(pltpu.make_async_copy(mixed_v.at[:, chunk], mixed_hbm.at[:, chunk], out_sems.at[c]))
        outs[-1].start()
    part_v[...] = part_f[...].astype(BF16)
    for src, dst in ((part_v, part_hbm), (head_v, head_hbm)):
        outs.append(pltpu.make_async_copy(src, dst, out_sems.at[len(outs)]))
        outs[-1].start()
    for copy in outs:
        copy.wait()


def history_kernel(dims, refs_in, refs_out, scratch):
    dims, block, firsts = dims
    per_dev, n_replica, slots, _ = dims
    holder, slot_id, prefix_len, head_ref, part_ref, wt_ref, cw_ref = refs_in[:7]
    pieces = refs_in[7:]
    mixed_ref, fixed_ref = refs_out
    taps = cw_ref.shape[0]
    me = lax.axis_index("replica")
    places, slot_ids, lengths = request_places(dims, (holder, slot_id, prefix_len), me)
    tap, request = split_index(lax.broadcasted_iota(jnp.int32, (per_dev * taps, 1), 0), per_dev)
    starts = [places[r] * block + (block - slots * taps) + slot_ids[r] * taps for r in range(per_dev)]
    target = pick_rows(starts, request, per_dev) + tap
    live = (tap < taps - 1) & (taps - 1 - tap <= pick_rows(lengths, request, per_dev))
    history = fetch_rows(target, live, [(first, ref[...]) for first, ref in zip(firsts, pieces)])
    sums = []
    for t in range(taps):
        summed = head_ref[t * per_dev : (t + 1) * per_dev]
        for k in range(taps - 1 - t):
            weight = cw_ref[k : k + 1].astype(F32)
            summed = summed + history[(t + k) * per_dev : (t + k + 1) * per_dev] * weight
        sums.append(summed)
    mixed = silu(jnp.concatenate(sums, axis=0)).astype(BF16)
    mixed_ref[...] = mixed
    part = lax.dot_general(wt_ref[...], mixed, NT, preferred_element_type=F32)
    fixed_ref[...] = part_ref[...]
    fixed_ref[:, : per_dev * taps] = part.astype(BF16)


def prepare_kernel(dims, refs_in, refs_out, scratch):
    mixed_ref, head_ref, z_ref, al_ref, skip_ref = refs_in
    gate_ref, skipped_ref, rate_ref = refs_out
    rows, channels = z_ref.shape
    head = head_ref.shape[0]
    gate_ref[...] = silu(z_ref[...].astype(F32))
    rate_ref[...] = jnp.exp(al_ref[...]) * (-LOG2E)
    for tile in range(channels // LANES):
        lanes = slice(tile * LANES, (tile + 1) * LANES)
        skipped_ref[tile, :head, :] = skip_ref[:, lanes] * head_ref[:, lanes].astype(F32)
        skipped_ref[tile, head:, :] = skip_ref[:, lanes] * mixed_ref[head:, lanes].astype(F32)


def scan_kernel(dims, refs_in, refs_out, scratch):
    per_dev, n_replica, _, _ = dims
    mixed_ref, head_ref, dtw_ref, dtb_ref, gate_ref, skipped_ref, rate_ref = refs_in[3:10]
    out_hbm, state_hbm = refs_out
    b_tab, c_tab, dt_v, drive_v, start_tm, final_tm, y_v, out_v, state_v, out_sems, int_sems = scratch[:11]
    ints = scratch[11:]
    int_copies = [pltpu.make_async_copy(refs_in[i], ints[i], int_sems.at[i]) for i in range(len(ints))]
    for copy in int_copies:
        copy.start()
    n_pieces = sum(1 for ref in refs_in[10:] if ref.shape[-1] == gate_ref.shape[1])
    parts, pieces = refs_in[10:-n_pieces], refs_in[-n_pieces:]
    rows, channels = gate_ref.shape
    states = rate_ref.shape[0]
    rank = dtw_ref.shape[0]
    head = head_ref.shape[0]

    projected = parts[0][...].astype(F32)
    for part in parts[1:]:
        projected = projected + part[...].astype(F32)
    c_part = projected[rank + states :]
    c_high = c_part.astype(BF16).astype(F32)
    shape = (2 * states, states * LANES)
    term = lax.broadcasted_iota(jnp.int32, shape, 0) & (states - 1)
    lane_group, _ = split_index(lax.broadcasted_iota(jnp.int32, shape, 1), LANES)
    spread = jnp.where(term == lane_group, 1.0, 0.0).astype(BF16)
    c_terms = jnp.concatenate([c_high, c_part - c_high], axis=0).T.astype(BF16)
    projected = projected[: rank + states].T
    dt_low = projected[:, :rank].astype(BF16)
    late = projected[:, rank:]
    n_tiles = channels // LANES
    wide = min(4, n_tiles)
    per_chunk = states * wide // n_tiles
    for c in range(n_tiles // wide):
        for n in range(c * per_chunk, (c + 1) * per_chunk):
            b_tab[n] = jnp.broadcast_to(late[:, n : n + 1], (rows, LANES))
        lanes = slice(c * per_chunk * LANES, (c + 1) * per_chunk * LANES)
        repeated = jnp.dot(c_terms, spread[:, lanes], preferred_element_type=F32)
        for n in range(per_chunk):
            c_tab[c * per_chunk + n] = repeated[:, n * LANES : (n + 1) * LANES]
        weights = dtw_ref[:, c * wide * LANES : (c + 1) * wide * LANES]
        raw = jnp.dot(dt_low, weights, preferred_element_type=F32)
        for j in range(wide):
            tile = c * wide + j
            lanes = slice(tile * LANES, (tile + 1) * LANES)
            for first in range(0, rows, LANES):
                here = slice(first, first + LANES)
                dt = softplus(raw[here, j * LANES : (j + 1) * LANES] + dtb_ref[:, lanes])
                mixed = mixed_ref[here, lanes]
                if first == 0:
                    mixed = jnp.concatenate([head_ref[:, lanes], mixed[head:]], axis=0)
                mixed = mixed.astype(F32)
                dt_v[tile, here, :] = dt
                drive_v[tile, here, :] = dt * mixed

    me = lax.axis_index("replica")
    for copy in int_copies:
        copy.wait()
    places, slot_ids, lengths = request_places(dims, ints, me)
    for r in range(per_dev):
        spot = pl.ds(pl.multiple_of(slot_ids[r] * states, states), states)
        for tile in range(n_tiles):
            lanes = slice(tile * LANES, (tile + 1) * LANES)
            if n_pieces == 1:
                value = pieces[0][places[r], spot, lanes]
            else:
                value = pieces[0][spot, lanes]
                for p in range(1, n_pieces):
                    value = jnp.where(places[r] == p, pieces[p][spot, lanes], value)
            value = value.astype(F32)
            value = jnp.where(lengths[r] > 0, value, jnp.zeros_like(value))
            start_tm[tile, pl.ds(r, states, stride=per_dev), :] = value

    tiles = 2
    half = states // 4
    width = tiles * LANES
    n_groups = n_tiles // tiles

    def out_copies(g):
        lanes = pl.ds(pl.multiple_of(g * width, width), width)
        return [
            pltpu.make_async_copy(src.at[:, lanes], dst.at[:, lanes], out_sems.at[i, g])
            for i, (src, dst) in enumerate(((out_v, out_hbm), (state_v, state_hbm)))
        ]

    def finish(g):
        for j in range(tiles):
            tile = g * tiles + j
            lanes = pl.ds(pl.multiple_of(tile * LANES, LANES), LANES)
            for r in range(per_dev):
                here = slice(r * NEW, (r + 1) * NEW)
                value = y_v[tile, pl.ds(r, NEW, stride=per_dev), :] * gate_ref[here, lanes]
                out_v[here, lanes] = value.astype(BF16)
                final = final_tm[tile, pl.ds(r, states, stride=per_dev), :]
                state_v[r * states : (r + 1) * states, lanes] = final.astype(BF16)

    def scan_group(g):
        group = [g * tiles + j for j in range(tiles)]
        lanes = [pl.ds(pl.multiple_of(tile * LANES, LANES), LANES) for tile in group]
        for first in range(0, states, half):
            ids = range(first, first + half)
            rates = [[jnp.broadcast_to(rate_ref[n : n + 1, lane], (per_dev, LANES)) for n in ids] for lane in lanes]

            def advance(step, state):
                state = list(state)
                for u in range(UNROLL):
                    now = pl.ds(pl.multiple_of((step * UNROLL + u) * per_dev, per_dev), per_dev)
                    dt = [dt_v[tile, now, :] for tile in group]
                    drive = [drive_v[tile, now, :] for tile in group]
                    sums = [None] * tiles
                    for k, n in enumerate(ids):
                        b, c = b_tab[n, now, :], c_tab[n, now, :]
                        for j in range(tiles):
                            i = j * half + k
                            state[i] = jnp.exp2(dt[j] * rates[j][k]) * state[i] + drive[j] * b
                            term = state[i] * c
                            sums[j] = term if sums[j] is None else sums[j] + term
                    for j, tile in enumerate(group):
                        before = skipped_ref[tile, now, :] if first == 0 else y_v[tile, now, :]
                        y_v[tile, now, :] = before + sums[j]
                return tuple(state)

            state = tuple(start_tm[tile, n * per_dev : (n + 1) * per_dev, :] for tile in group for n in ids)
            if NEW == UNROLL:
                state = advance(0, state)
            else:
                state = lax.fori_loop(0, NEW // UNROLL, advance, state)
            for j, tile in enumerate(group):
                for k, n in enumerate(ids):
                    final_tm[tile, n * per_dev : (n + 1) * per_dev, :] = state[j * half + k]

    def one_group(g, carry):
        before = jnp.maximum(g - 1, 0)
        finish(before)
        scan_group(g)

        @pl.when(g > 0)
        def _():
            for copy in out_copies(before):
                copy.start()

        return carry

    final_tm[:tiles] = jnp.zeros((tiles,) + final_tm.shape[1:], F32)
    y_v[:tiles] = jnp.zeros((tiles,) + y_v.shape[1:], F32)
    lax.fori_loop(0, n_groups, one_group, 0)
    finish(n_groups - 1)
    for copy in out_copies(n_groups - 1):
        copy.start()

    def last_wait(g, carry):
        for copy in out_copies(g):
            copy.wait()
        return carry

    lax.fori_loop(0, n_groups, last_wait, 0)


def split_refs(kernel, dims, n_in, n_out):
    def body(*refs):
        kernel(dims, refs[:n_in], refs[n_in : n_in + n_out], refs[n_in + n_out :])

    return body


def call(kernel, dims, name, limit, ins, outs, scratch):
    spaces = {"hbm": pltpu.HBM, "any": pl.ANY, "vmem": pltpu.VMEM, "smem": pltpu.SMEM}
    values = [
        pltpu.with_memory_space_constraint(value, pltpu.HBM) if place == "hbm" else value for value, place in ins
    ]
    return pl.pallas_call(
        split_refs(kernel, dims, len(ins), len(outs)),
        in_specs=[pl.BlockSpec(memory_space=spaces[place]) for _, place in ins],
        out_specs=[pl.BlockSpec(memory_space=spaces[place]) for _, _, place in outs],
        out_shape=[jax.ShapeDtypeStruct(shape, dtype) for shape, dtype, _ in outs],
        scratch_shapes=scratch,
        compiler_params=pltpu.CompilerParams(vmem_limit_bytes=limit * MIB),
        name=name,
    )(*values)


def swap(value, axis, size, mask):
    return lax.ppermute(value, axis, [(i, i ^ mask) for i in range(size)])


def shards(mesh, x_new, z_new, conv_weight, conv_bias, x_proj_weight, dt_proj_weight, dt_bias, a_log, d_skip,
           cache_ssm, cache_conv, holder, slot_id, prefix_len):
    n_replica, n_tensor = mesh.shape["replica"], mesh.shape["tensor"]
    rows, channels = x_new.shape
    per_dev = rows // NEW
    states = a_log.shape[0]
    rank = dt_proj_weight.shape[0]
    taps = conv_weight.shape[0]
    slots = cache_ssm.shape[0]
    out_cols = x_proj_weight.shape[1]
    requests = holder.shape[0]

    vmem, dma = pltpu.VMEM, pltpu.SemaphoreType.DMA
    ssm_rows = slots * states
    rows_all, conv_rows = call(
        pack_kernel, (slots, taps), "pack", 20,
        [(cache_ssm.reshape(ssm_rows, channels), "hbm"), (cache_conv.transpose(1, 0, 2), "hbm")],
        [((ssm_rows + slots * taps, channels), BF16, "vmem"), ((slots * taps, channels), BF16, "vmem")],
        [vmem((taps - 1, slots, channels), BF16), dma((2,))],
    )
    block = rows_all.shape[0]
    relative = n_replica == 4
    if relative:
        far = swap(rows_all, "replica", n_replica, 3)
        near = swap(rows_all, "replica", n_replica, 1)
        conv_two = swap(conv_rows, "replica", n_replica, 2)
        conv_pieces = [rows_all, near, far, conv_two]
        firsts = (0, block, 2 * block, 4 * block - slots * taps)
        ssm_pieces = [rows_all, near, far, swap(far, "replica", n_replica, 1)]
    else:
        ssm_pieces = [lax.all_gather(rows_all, "replica")]
        conv_pieces, firsts = [ssm_pieces[0].reshape(-1, channels)], (0,)

    n_chunks = channels // min(512, channels)
    dims = (per_dev, n_replica, slots, relative)
    head = per_dev * taps
    weights = x_proj_weight.T
    requests = [(holder, "smem"), (slot_id, "smem"), (prefix_len, "smem")]

    mixed, head_sums, part = call(
        project_kernel, per_dev, "conv_project", 40,
        [(x_new, "hbm"), (weights, "hbm"), (conv_weight, "hbm"), (conv_bias[None, :], "hbm")],
        [((rows, channels), BF16, "any"), ((head, channels), F32, "any"), ((out_cols, rows), BF16, "any")],
        [
            vmem((rows, channels), BF16),
            vmem((out_cols, channels), BF16),
            vmem((taps, channels), BF16),
            vmem((1, channels), F32),
            vmem((channels // LANES, rows + taps * per_dev, LANES), F32),
            vmem((rows, channels), BF16),
            vmem((head, channels), F32),
            vmem((out_cols, rows), F32),
            vmem((out_cols, rows), BF16),
            dma((2 + 2 * n_chunks,)),
            dma((n_chunks + 2,)),
        ],
    )
    mixed_head, part = call(
        history_kernel, (dims, block, firsts), "history", 20,
        requests
        + [(value, "vmem") for value in [head_sums, part, weights, conv_weight] + conv_pieces],
        [((head, channels), BF16, "vmem"), ((out_cols, rows), BF16, "vmem")],
        [],
    )
    parts = [part]
    mask = n_tensor // 2
    while mask:
        parts = parts + [swap(value, "tensor", n_tensor, mask) for value in reversed(parts)]
        mask //= 2

    n_tiles = channels // LANES
    prepared = call(
        prepare_kernel, None, "prepare", 40,
        [(value, "vmem") for value in (mixed, mixed_head, z_new, a_log, d_skip[None, :])],
        [((rows, channels), F32, "vmem"), ((n_tiles, rows, LANES), F32, "vmem"), ((states, channels), F32, "vmem")],
        [],
    )
    operands = [mixed, mixed_head, dt_proj_weight, dt_bias[None, :], *prepared]
    out, state = call(
        scan_kernel, dims, "dt_scan_gate", 40,
        [(value, "any") for value, _ in requests] + [(value, "vmem") for value in operands + parts + ssm_pieces],
        [((rows, channels), BF16, "any"), ((per_dev * states, channels), BF16, "any")],
        [
            vmem((states, rows, LANES), F32),
            vmem((states, rows, LANES), F32),
            vmem((n_tiles, rows, LANES), F32),
            vmem((n_tiles, rows, LANES), F32),
            vmem((n_tiles, per_dev * (states + 1), LANES), F32),
            vmem((n_tiles, per_dev * (states + 1), LANES), F32),
            vmem((n_tiles, rows + per_dev, LANES), F32),
            vmem((rows, channels), BF16),
            vmem((per_dev * states, channels), BF16),
            dma((2, n_tiles // 2)),
            dma((3,)),
        ] + [pltpu.SMEM(holder.shape, jnp.int32)] * 3,
    )
    return out, state.reshape(per_dev, states, channels)


def solution(mesh):
    placed = (
        P(("groups", "replica"), "tensor"),
        P(("groups", "replica"), "tensor"),
        P(None, "tensor"),
        P("tensor"),
        P("tensor", None),
        P(None, "tensor"),
        P("tensor"),
        P(None, "tensor"),
        P("tensor"),
        P(("groups", "replica"), None, "tensor"),
        P(("groups", "replica"), None, "tensor"),
        P("groups"),
        P("groups"),
        P("groups"),
    )
    return jax.shard_map(
        functools.partial(shards, mesh),
        mesh=mesh,
        in_specs=placed,
        out_specs=(P(("groups", "replica"), "tensor"), P(("groups", "replica"), None, "tensor")),
        check_vma=False,
    )
```

```python
import functools

import jax
import jax.numpy as jnp
from jax import lax
from jax.experimental import pallas as pl
from jax.experimental.pallas import tpu as pltpu
from jax.sharding import PartitionSpec as P

NEW = 32
LANES = 128
MIB = 1024 * 1024
UNROLL = 32
LOG2E = 1.4426950408889634
F32, BF16 = jnp.float32, jnp.bfloat16
NT = (((1,), (1,)), ((), ()))


def silu(v):
    half = 0.5 * v
    return half + half * jnp.tanh(half)


def softplus(v):
    u = jnp.exp2(jnp.abs(v) * -LOG2E)
    return jnp.maximum(v, 0.0) + jnp.where(u < 2.0**-10, u - 0.5 * (u * u), jnp.log(1.0 + u))


def split_index(value, inner):
    assert inner & (inner - 1) == 0
    return value >> (inner.bit_length() - 1), value & (inner - 1)


def pick_rows(values, row_low, count):
    out = jnp.zeros(row_low.shape, jnp.int32)
    for r in range(count):
        out = jnp.where(row_low == r, values[r], out)
    return out


def request_places(dims, ints, me):
    per_dev, n_replica, _, relative = dims
    places, slot_ids, lengths = [], [], []
    for r in range(per_dev):
        request = me * per_dev + r
        place = ints[0][request]
        if relative:
            place = place ^ me
            place = place ^ (place >> 1)
        places.append(place)
        slot_ids.append(ints[1][request])
        lengths.append(ints[2][request])
    return places, slot_ids, lengths


def fetch_rows(target, live, pieces):
    total = None
    for first, value in pieces:
        col = lax.broadcasted_iota(jnp.int32, (target.shape[0], value.shape[0]), 1) + first
        select = jnp.where((col == target) & live, 1.0, 0.0).astype(BF16)
        part = jnp.dot(select, value, preferred_element_type=F32)
        total = part if total is None else total + part
    return total


def pack_kernel(dims, refs_in, refs_out, scratch):
    slots, taps = dims
    ssm_hbm, conv_hbm = refs_in
    block_ref, conv_ref = refs_out
    conv_v, sems = scratch
    states = pltpu.make_async_copy(ssm_hbm, block_ref.at[: ssm_hbm.shape[0]], sems.at[0])
    inputs = pltpu.make_async_copy(conv_hbm, conv_v, sems.at[1])
    states.start()
    inputs.start()
    inputs.wait()
    lines = []
    for slot in range(slots):
        for tap in range(taps):
            line = conv_v[min(tap, taps - 2)].astype(F32)[slot : slot + 1]
            lines.append(line if tap < taps - 1 else jnp.zeros_like(line))
    rows = jnp.concatenate(lines, axis=0).astype(BF16)
    conv_ref[...] = rows
    block_ref[ssm_hbm.shape[0] :, :] = rows
    states.wait()


def project_kernel(dims, refs_in, refs_out, scratch):
    per_dev = dims
    x_hbm, wt_hbm, cw_hbm, cb_hbm = refs_in
    mixed_hbm, head_hbm, part_hbm = refs_out
    x_v, wt_v, cw_v, cb_v, joined, mixed_v, head_v, part_f, part_v, sems, out_sems = scratch
    rows, channels = x_v.shape
    taps = cw_v.shape[0]
    lines = (taps - 1) * per_dev
    pairs = [(cw_hbm, cw_v), (cb_hbm, cb_v)]
    width = min(512, channels)
    chunks = [slice(c * width, (c + 1) * width) for c in range(channels // width)]
    for chunk in chunks:
        pairs += [(x_hbm.at[:, chunk], x_v.at[:, chunk]), (wt_hbm.at[:, chunk], wt_v.at[:, chunk])]
    copies = [pltpu.make_async_copy(src, dst, sems.at[i]) for i, (src, dst) in enumerate(pairs)]
    for copy in copies:
        copy.start()

    joined[:, :lines, :] = jnp.zeros((channels // LANES, lines, LANES), F32)
    copies[0].wait()
    copies[1].wait()
    outs = []
    for c, chunk in enumerate(chunks):
        copies[2 + 2 * c].wait()
        for tile in range(c * width // LANES, (c + 1) * width // LANES):
            lanes = slice(tile * LANES, (tile + 1) * LANES)
            for r in range(per_dev):
                tokens = x_v[r * NEW : (r + 1) * NEW, lanes].astype(F32)
                joined[tile, pl.ds(lines + r, NEW, stride=per_dev), :] = tokens
            weight = [cw_v[k : k + 1, lanes].astype(F32) for k in range(taps)]
            bias = cb_v[:, lanes]
            for first in range(0, rows, LANES):
                summed = bias + joined[tile, first : first + LANES, :] * weight[0]
                for k in range(1, taps):
                    begin = first + k * per_dev
                    summed = summed + joined[tile, begin : begin + LANES, :] * weight[k]
                if first == 0:
                    head_v[:, lanes] = summed[: head_v.shape[0]]
                mixed_v[first : first + LANES, lanes] = silu(summed).astype(BF16)
        copies[3 + 2 * c].wait()
        part = lax.dot_general(wt_v[:, chunk], mixed_v[:, chunk], NT, preferred_element_type=F32)
        if c == 0:
            part_f[...] = part
        else:
            part_f[...] += part
        outs.append(pltpu.make_async_copy(mixed_v.at[:, chunk], mixed_hbm.at[:, chunk], out_sems.at[c]))
        outs[-1].start()
    part_v[...] = part_f[...].astype(BF16)
    for src, dst in ((part_v, part_hbm), (head_v, head_hbm)):
        outs.append(pltpu.make_async_copy(src, dst, out_sems.at[len(outs)]))
        outs[-1].start()
    for copy in outs:
        copy.wait()


def history_kernel(dims, refs_in, refs_out, scratch):
    dims, block, firsts = dims
    per_dev, n_replica, slots, _ = dims
    holder, slot_id, prefix_len, head_ref, part_ref, wt_ref, cw_ref = refs_in[:7]
    pieces = refs_in[7:]
    mixed_ref, fixed_ref = refs_out
    taps = cw_ref.shape[0]
    me = lax.axis_index("replica")
    places, slot_ids, lengths = request_places(dims, (holder, slot_id, prefix_len), me)
    tap, request = split_index(lax.broadcasted_iota(jnp.int32, (per_dev * taps, 1), 0), per_dev)
    starts = [places[r] * block + (block - slots * taps) + slot_ids[r] * taps for r in range(per_dev)]
    target = pick_rows(starts, request, per_dev) + tap
    live = (tap < taps - 1) & (taps - 1 - tap <= pick_rows(lengths, request, per_dev))
    history = fetch_rows(target, live, [(first, ref[...]) for first, ref in zip(firsts, pieces)])
    sums = []
    for t in range(taps):
        summed = head_ref[t * per_dev : (t + 1) * per_dev]
        for k in range(taps - 1 - t):
            weight = cw_ref[k : k + 1].astype(F32)
            summed = summed + history[(t + k) * per_dev : (t + k + 1) * per_dev] * weight
        sums.append(summed)
    mixed = silu(jnp.concatenate(sums, axis=0)).astype(BF16)
    mixed_ref[...] = mixed
    part = lax.dot_general(wt_ref[...], mixed, NT, preferred_element_type=F32)
    fixed_ref[...] = part_ref[...]
    fixed_ref[:, : per_dev * taps] = part.astype(BF16)


def prepare_kernel(dims, refs_in, refs_out, scratch):
    mixed_ref, head_ref, z_ref, al_ref, skip_ref = refs_in
    gate_ref, skipped_ref, rate_ref = refs_out
    rows, channels = z_ref.shape
    head = head_ref.shape[0]
    gate_ref[...] = silu(z_ref[...].astype(F32))
    rate_ref[...] = jnp.exp(al_ref[...]) * (-LOG2E)
    for tile in range(channels // LANES):
        lanes = slice(tile * LANES, (tile + 1) * LANES)
        skipped_ref[tile, :head, :] = skip_ref[:, lanes] * head_ref[:, lanes].astype(F32)
        skipped_ref[tile, head:, :] = skip_ref[:, lanes] * mixed_ref[head:, lanes].astype(F32)


def scan_kernel(dims, refs_in, refs_out, scratch):
    per_dev, n_replica, _, _ = dims
    mixed_ref, head_ref, dtw_ref, dtb_ref, gate_ref, skipped_ref, rate_ref = refs_in[3:10]
    out_hbm, state_hbm = refs_out
    b_tab, c_tab, dt_v, drive_v, start_tm, final_tm, y_v, out_v, state_v, out_sems, int_sems = scratch[:11]
    ints = scratch[11:]
    int_copies = [pltpu.make_async_copy(refs_in[i], ints[i], int_sems.at[i]) for i in range(len(ints))]
    for copy in int_copies:
        copy.start()
    n_pieces = sum(1 for ref in refs_in[10:] if ref.shape[-1] == gate_ref.shape[1])
    parts, pieces = refs_in[10:-n_pieces], refs_in[-n_pieces:]
    rows, channels = gate_ref.shape
    states = rate_ref.shape[0]
    rank = dtw_ref.shape[0]
    head = head_ref.shape[0]

    me = lax.axis_index("replica")
    for copy in int_copies:
        copy.wait()
    places, slot_ids, lengths = request_places(dims, ints, me)
    projected = parts[0][...].astype(F32)
    for part in parts[1:]:
        projected = projected + part[...].astype(F32)
    c_part = projected[rank + states :]
    c_high = c_part.astype(BF16).astype(F32)
    shape = (2 * states, states * LANES)
    term = lax.broadcasted_iota(jnp.int32, shape, 0) & (states - 1)
    lane_group, _ = split_index(lax.broadcasted_iota(jnp.int32, shape, 1), LANES)
    spread = jnp.where(term == lane_group, 1.0, 0.0).astype(BF16)
    c_terms = jnp.concatenate([c_high, c_part - c_high], axis=0).T.astype(BF16)
    projected = projected[: rank + states].T
    dt_low = projected[:, :rank].astype(BF16)
    late = projected[:, rank:]
    n_tiles = channels // LANES
    wide = min(4, n_tiles)
    per_chunk = states * wide // n_tiles
    for c in range(n_tiles // wide):
        for r in range(c * per_dev * wide // n_tiles, (c + 1) * per_dev * wide // n_tiles):
            spot = pl.ds(pl.multiple_of(slot_ids[r] * states, states), states)
            for tile in range(n_tiles):
                lanes = slice(tile * LANES, (tile + 1) * LANES)
                if n_pieces == 1:
                    value = pieces[0][places[r], spot, lanes]
                else:
                    value = pieces[0][spot, lanes]
                    for p in range(1, n_pieces):
                        value = jnp.where(places[r] == p, pieces[p][spot, lanes], value)
                value = value.astype(F32)
                value = jnp.where(lengths[r] > 0, value, jnp.zeros_like(value))
                start_tm[tile, pl.ds(r, states, stride=per_dev), :] = value
        for n in range(c * per_chunk, (c + 1) * per_chunk):
            b_tab[n] = jnp.broadcast_to(late[:, n : n + 1], (rows, LANES))
        lanes = slice(c * per_chunk * LANES, (c + 1) * per_chunk * LANES)
        repeated = jnp.dot(c_terms, spread[:, lanes], preferred_element_type=F32)
        for n in range(per_chunk):
            c_tab[c * per_chunk + n] = repeated[:, n * LANES : (n + 1) * LANES]
        weights = dtw_ref[:, c * wide * LANES : (c + 1) * wide * LANES]
        raw = jnp.dot(dt_low, weights, preferred_element_type=F32)
        for j in range(wide):
            tile = c * wide + j
            lanes = slice(tile * LANES, (tile + 1) * LANES)
            for first in range(0, rows, LANES):
                here = slice(first, first + LANES)
                dt = softplus(raw[here, j * LANES : (j + 1) * LANES] + dtb_ref[:, lanes])
                mixed = mixed_ref[here, lanes]
                if first == 0:
                    mixed = jnp.concatenate([head_ref[:, lanes], mixed[head:]], axis=0)
                mixed = mixed.astype(F32)
                dt_v[tile, here, :] = dt
                drive_v[tile, here, :] = dt * mixed

    tiles = 2
    half = states // 4
    width = tiles * LANES
    n_groups = n_tiles // tiles

    def out_copies(g):
        lanes = pl.ds(pl.multiple_of(g * width, width), width)
        return [
            pltpu.make_async_copy(src.at[:, lanes], dst.at[:, lanes], out_sems.at[i, g])
            for i, (src, dst) in enumerate(((out_v, out_hbm), (state_v, state_hbm)))
        ]

    def finish(g):
        for j in range(tiles):
            tile = g * tiles + j
            lanes = pl.ds(pl.multiple_of(tile * LANES, LANES), LANES)
            for r in range(per_dev):
                here = slice(r * NEW, (r + 1) * NEW)
                value = y_v[tile, pl.ds(r, NEW, stride=per_dev), :] * gate_ref[here, lanes]
                out_v[here, lanes] = value.astype(BF16)
                final = final_tm[tile, pl.ds(r, states, stride=per_dev), :]
                state_v[r * states : (r + 1) * states, lanes] = final.astype(BF16)

    def scan_group(g):
        group = [g * tiles + j for j in range(tiles)]
        lanes = [pl.ds(pl.multiple_of(tile * LANES, LANES), LANES) for tile in group]
        for first in range(0, states, half):
            ids = range(first, first + half)
            rates = [[jnp.broadcast_to(rate_ref[n : n + 1, lane], (per_dev, LANES)) for n in ids] for lane in lanes]

            def advance(step, state):
                state = list(state)
                for u in range(UNROLL):
                    now = pl.ds(pl.multiple_of((step * UNROLL + u) * per_dev, per_dev), per_dev)
                    dt = [dt_v[tile, now, :] for tile in group]
                    drive = [drive_v[tile, now, :] for tile in group]
                    sums = [None] * tiles
                    for k, n in enumerate(ids):
                        b, c = b_tab[n, now, :], c_tab[n, now, :]
                        for j in range(tiles):
                            i = j * half + k
                            state[i] = jnp.exp2(dt[j] * rates[j][k]) * state[i] + drive[j] * b
                            term = state[i] * c
                            sums[j] = term if sums[j] is None else sums[j] + term
                    for j, tile in enumerate(group):
                        before = skipped_ref[tile, now, :] if first == 0 else y_v[tile, now, :]
                        y_v[tile, now, :] = before + sums[j]
                return tuple(state)

            state = tuple(start_tm[tile, n * per_dev : (n + 1) * per_dev, :] for tile in group for n in ids)
            if NEW == UNROLL:
                state = advance(0, state)
            else:
                state = lax.fori_loop(0, NEW // UNROLL, advance, state)
            for j, tile in enumerate(group):
                for k, n in enumerate(ids):
                    final_tm[tile, n * per_dev : (n + 1) * per_dev, :] = state[j * half + k]

    def one_group(g, carry):
        before = jnp.maximum(g - 1, 0)
        finish(before)
        scan_group(g)

        @pl.when(g > 0)
        def _():
            for copy in out_copies(before):
                copy.start()

        return carry

    final_tm[:tiles] = jnp.zeros((tiles,) + final_tm.shape[1:], F32)
    y_v[:tiles] = jnp.zeros((tiles,) + y_v.shape[1:], F32)
    lax.fori_loop(0, n_groups, one_group, 0)
    finish(n_groups - 1)
    for copy in out_copies(n_groups - 1):
        copy.start()

    def last_wait(g, carry):
        for copy in out_copies(g):
            copy.wait()
        return carry

    lax.fori_loop(0, n_groups, last_wait, 0)


def split_refs(kernel, dims, n_in, n_out):
    def body(*refs):
        kernel(dims, refs[:n_in], refs[n_in : n_in + n_out], refs[n_in + n_out :])

    return body


def call(kernel, dims, name, limit, ins, outs, scratch):
    spaces = {"hbm": pltpu.HBM, "any": pl.ANY, "vmem": pltpu.VMEM, "smem": pltpu.SMEM}
    values = [
        pltpu.with_memory_space_constraint(value, pltpu.HBM) if place == "hbm" else value for value, place in ins
    ]
    return pl.pallas_call(
        split_refs(kernel, dims, len(ins), len(outs)),
        in_specs=[pl.BlockSpec(memory_space=spaces[place]) for _, place in ins],
        out_specs=[pl.BlockSpec(memory_space=spaces[place]) for _, _, place in outs],
        out_shape=[jax.ShapeDtypeStruct(shape, dtype) for shape, dtype, _ in outs],
        scratch_shapes=scratch,
        compiler_params=pltpu.CompilerParams(vmem_limit_bytes=limit * MIB),
        name=name,
    )(*values)


def swap(value, axis, size, mask):
    return lax.ppermute(value, axis, [(i, i ^ mask) for i in range(size)])


def shards(mesh, x_new, z_new, conv_weight, conv_bias, x_proj_weight, dt_proj_weight, dt_bias, a_log, d_skip,
           cache_ssm, cache_conv, holder, slot_id, prefix_len):
    n_replica, n_tensor = mesh.shape["replica"], mesh.shape["tensor"]
    rows, channels = x_new.shape
    per_dev = rows // NEW
    states = a_log.shape[0]
    rank = dt_proj_weight.shape[0]
    taps = conv_weight.shape[0]
    slots = cache_ssm.shape[0]
    out_cols = x_proj_weight.shape[1]
    requests = holder.shape[0]

    vmem, dma = pltpu.VMEM, pltpu.SemaphoreType.DMA
    ssm_rows = slots * states
    rows_all, conv_rows = call(
        pack_kernel, (slots, taps), "pack", 20,
        [(cache_ssm.reshape(ssm_rows, channels), "hbm"), (cache_conv.transpose(1, 0, 2), "hbm")],
        [((ssm_rows + slots * taps, channels), BF16, "vmem"), ((slots * taps, channels), BF16, "vmem")],
        [vmem((taps - 1, slots, channels), BF16), dma((2,))],
    )
    block = rows_all.shape[0]
    relative = n_replica == 4
    if relative:
        far = swap(rows_all, "replica", n_replica, 3)
        near = swap(rows_all, "replica", n_replica, 1)
        conv_two = swap(conv_rows, "replica", n_replica, 2)
        conv_pieces = [rows_all, near, far, conv_two]
        firsts = (0, block, 2 * block, 4 * block - slots * taps)
        ssm_pieces = [rows_all, near, far, swap(far, "replica", n_replica, 1)]
    else:
        ssm_pieces = [lax.all_gather(rows_all, "replica")]
        conv_pieces, firsts = [ssm_pieces[0].reshape(-1, channels)], (0,)

    n_chunks = channels // min(512, channels)
    dims = (per_dev, n_replica, slots, relative)
    head = per_dev * taps
    weights = x_proj_weight.T
    requests = [(holder, "smem"), (slot_id, "smem"), (prefix_len, "smem")]

    mixed, head_sums, part = call(
        project_kernel, per_dev, "conv_project", 40,
        [(x_new, "hbm"), (weights, "hbm"), (conv_weight, "hbm"), (conv_bias[None, :], "hbm")],
        [((rows, channels), BF16, "any"), ((head, channels), F32, "any"), ((out_cols, rows), BF16, "any")],
        [
            vmem((rows, channels), BF16),
            vmem((out_cols, channels), BF16),
            vmem((taps, channels), BF16),
            vmem((1, channels), F32),
            vmem((channels // LANES, rows + taps * per_dev, LANES), F32),
            vmem((rows, channels), BF16),
            vmem((head, channels), F32),
            vmem((out_cols, rows), F32),
            vmem((out_cols, rows), BF16),
            dma((2 + 2 * n_chunks,)),
            dma((n_chunks + 2,)),
        ],
    )
    mixed_head, part = call(
        history_kernel, (dims, block, firsts), "history", 20,
        requests
        + [(value, "vmem") for value in [head_sums, part, weights, conv_weight] + conv_pieces],
        [((head, channels), BF16, "vmem"), ((out_cols, rows), BF16, "vmem")],
        [],
    )
    parts = [part]
    mask = n_tensor // 2
    while mask:
        parts = parts + [swap(value, "tensor", n_tensor, mask) for value in reversed(parts)]
        mask //= 2

    n_tiles = channels // LANES
    prepared = call(
        prepare_kernel, None, "prepare", 40,
        [(value, "vmem") for value in (mixed, mixed_head, z_new, a_log, d_skip[None, :])],
        [((rows, channels), F32, "vmem"), ((n_tiles, rows, LANES), F32, "vmem"), ((states, channels), F32, "vmem")],
        [],
    )
    operands = [mixed, mixed_head, dt_proj_weight, dt_bias[None, :], *prepared]
    out, state = call(
        scan_kernel, dims, "dt_scan_gate", 40,
        [(value, "any") for value, _ in requests] + [(value, "vmem") for value in operands + parts + ssm_pieces],
        [((rows, channels), BF16, "any"), ((per_dev * states, channels), BF16, "any")],
        [
            vmem((states, rows, LANES), F32),
            vmem((states, rows, LANES), F32),
            vmem((n_tiles, rows, LANES), F32),
            vmem((n_tiles, rows, LANES), F32),
            vmem((n_tiles, per_dev * (states + 1), LANES), F32),
            vmem((n_tiles, per_dev * (states + 1), LANES), F32),
            vmem((n_tiles, rows + per_dev, LANES), F32),
            vmem((rows, channels), BF16),
            vmem((per_dev * states, channels), BF16),
            dma((2, n_tiles // 2)),
            dma((3,)),
        ] + [pltpu.SMEM(holder.shape, jnp.int32)] * 3,
    )
    return out, state.reshape(per_dev, states, channels)


def solution(mesh):
    placed = (
        P(("groups", "replica"), "tensor"),
        P(("groups", "replica"), "tensor"),
        P(None, "tensor"),
        P("tensor"),
        P("tensor", None),
        P(None, "tensor"),
        P("tensor"),
        P(None, "tensor"),
        P("tensor"),
        P(("groups", "replica"), None, "tensor"),
        P(("groups", "replica"), None, "tensor"),
        P("groups"),
        P("groups"),
        P("groups"),
    )
    return jax.shard_map(
        functools.partial(shards, mesh),
        mesh=mesh,
        in_specs=placed,
        out_specs=(P(("groups", "replica"), "tensor"), P(("groups", "replica"), None, "tensor")),
        check_vma=False,
    )
```

```python
import functools

import jax
import jax.numpy as jnp
from jax import lax
from jax.experimental import pallas as pl
from jax.experimental.pallas import tpu as pltpu
from jax.sharding import PartitionSpec as P

NEW = 32
LANES = 128
MIB = 1024 * 1024
UNROLL = 32
LOG2E = 1.4426950408889634
F32, BF16 = jnp.float32, jnp.bfloat16
NT = (((1,), (1,)), ((), ()))


def silu(v):
    half = 0.5 * v
    return half + half * jnp.tanh(half)


def softplus(v):
    u = jnp.exp2(jnp.abs(v) * -LOG2E)
    return jnp.maximum(v, 0.0) + jnp.where(u < 2.0**-10, u - 0.5 * (u * u), jnp.log(1.0 + u))


def split_index(value, inner):
    assert inner & (inner - 1) == 0
    return value >> (inner.bit_length() - 1), value & (inner - 1)


def pick_rows(values, row_low, count):
    out = jnp.zeros(row_low.shape, jnp.int32)
    for r in range(count):
        out = jnp.where(row_low == r, values[r], out)
    return out


def request_places(dims, ints, me):
    per_dev, n_replica, _, relative = dims
    places, slot_ids, lengths = [], [], []
    for r in range(per_dev):
        request = me * per_dev + r
        place = ints[0][request]
        if relative:
            place = place ^ me
            place = place ^ (place >> 1)
        places.append(place)
        slot_ids.append(ints[1][request])
        lengths.append(ints[2][request])
    return places, slot_ids, lengths


def fetch_rows(target, live, pieces):
    total = None
    for first, value in pieces:
        col = lax.broadcasted_iota(jnp.int32, (target.shape[0], value.shape[0]), 1) + first
        select = jnp.where((col == target) & live, 1.0, 0.0).astype(BF16)
        part = jnp.dot(select, value, preferred_element_type=F32)
        total = part if total is None else total + part
    return total


def pack_kernel(dims, refs_in, refs_out, scratch):
    slots, taps = dims
    ssm_hbm, conv_hbm = refs_in
    block_ref, conv_ref = refs_out
    conv_v, sems = scratch
    states = pltpu.make_async_copy(ssm_hbm, block_ref.at[: ssm_hbm.shape[0]], sems.at[0])
    inputs = pltpu.make_async_copy(conv_hbm, conv_v, sems.at[1])
    states.start()
    inputs.start()
    inputs.wait()
    lines = []
    for slot in range(slots):
        for tap in range(taps):
            line = conv_v[min(tap, taps - 2)].astype(F32)[slot : slot + 1]
            lines.append(line if tap < taps - 1 else jnp.zeros_like(line))
    rows = jnp.concatenate(lines, axis=0).astype(BF16)
    conv_ref[...] = rows
    block_ref[ssm_hbm.shape[0] :, :] = rows
    states.wait()


def project_kernel(dims, refs_in, refs_out, scratch):
    dims, block = dims
    per_dev, _, slots, _ = dims
    x_hbm, wt_hbm, cw_hbm, cb_hbm = refs_in[:4]
    mixed_hbm, head_hbm, part_hbm, target_ref = refs_out
    x_v, wt_v, cw_v, cb_v, joined, mixed_v, head_v, part_f, part_v, sems, out_sems = scratch
    rows, channels = x_v.shape
    taps = cw_v.shape[0]
    lines = (taps - 1) * per_dev
    pairs = [(cw_hbm, cw_v), (cb_hbm, cb_v)]
    width = min(512, channels)
    chunks = [slice(c * width, (c + 1) * width) for c in range(channels // width)]
    for chunk in chunks:
        pairs += [(x_hbm.at[:, chunk], x_v.at[:, chunk]), (wt_hbm.at[:, chunk], wt_v.at[:, chunk])]
    copies = [pltpu.make_async_copy(src, dst, sems.at[i]) for i, (src, dst) in enumerate(pairs)]
    for copy in copies:
        copy.start()

    me = lax.axis_index("replica")
    places, slot_ids, lengths = request_places(dims, refs_in[4:], me)
    tap, request = split_index(lax.broadcasted_iota(jnp.int32, target_ref.shape, 0), per_dev)
    starts = [places[r] * block + (block - slots * taps) + slot_ids[r] * taps for r in range(per_dev)]
    live = (tap < taps - 1) & (taps - 1 - tap <= pick_rows(lengths, request, per_dev))
    target_ref[...] = jnp.where(live, pick_rows(starts, request, per_dev) + tap, -1)

    joined[:, :lines, :] = jnp.zeros((channels // LANES, lines, LANES), F32)
    copies[0].wait()
    copies[1].wait()
    outs = []
    for c, chunk in enumerate(chunks):
        copies[2 + 2 * c].wait()
        for tile in range(c * width // LANES, (c + 1) * width // LANES):
            lanes = slice(tile * LANES, (tile + 1) * LANES)
            for r in range(per_dev):
                tokens = x_v[r * NEW : (r + 1) * NEW, lanes].astype(F32)
                joined[tile, pl.ds(lines + r, NEW, stride=per_dev), :] = tokens
            weight = [cw_v[k : k + 1, lanes].astype(F32) for k in range(taps)]
            bias = cb_v[:, lanes]
            for first in range(0, rows, LANES):
                summed = bias + joined[tile, first : first + LANES, :] * weight[0]
                for k in range(1, taps):
                    begin = first + k * per_dev
                    summed = summed + joined[tile, begin : begin + LANES, :] * weight[k]
                if first == 0:
                    head_v[:, lanes] = summed[: head_v.shape[0]]
                mixed_v[first : first + LANES, lanes] = silu(summed).astype(BF16)
        copies[3 + 2 * c].wait()
        part = lax.dot_general(wt_v[:, chunk], mixed_v[:, chunk], NT, preferred_element_type=F32)
        if c == 0:
            part_f[...] = part
        else:
            part_f[...] += part
        outs.append(pltpu.make_async_copy(mixed_v.at[:, chunk], mixed_hbm.at[:, chunk], out_sems.at[c]))
        outs[-1].start()
    part_v[...] = part_f[...].astype(BF16)
    for src, dst in ((part_v, part_hbm), (head_v, head_hbm)):
        outs.append(pltpu.make_async_copy(src, dst, out_sems.at[len(outs)]))
        outs[-1].start()
    for copy in outs:
        copy.wait()


def history_kernel(dims, refs_in, refs_out, scratch):
    per_dev, firsts = dims
    target_ref, head_ref, part_ref, wt_ref, cw_ref = refs_in[:5]
    pieces = refs_in[5:]
    mixed_ref, fixed_ref = refs_out
    taps = cw_ref.shape[0]
    target = target_ref[:, :1]
    history = fetch_rows(target, target >= 0, [(first, ref[...]) for first, ref in zip(firsts, pieces)])
    sums = []
    for t in range(taps):
        summed = head_ref[t * per_dev : (t + 1) * per_dev]
        for k in range(taps - 1 - t):
            weight = cw_ref[k : k + 1].astype(F32)
            summed = summed + history[(t + k) * per_dev : (t + k + 1) * per_dev] * weight
        sums.append(summed)
    mixed = silu(jnp.concatenate(sums, axis=0)).astype(BF16)
    mixed_ref[...] = mixed
    part = lax.dot_general(wt_ref[...], mixed, NT, preferred_element_type=F32)
    fixed_ref[...] = part_ref[...]
    fixed_ref[:, : per_dev * taps] = part.astype(BF16)


def prepare_kernel(dims, refs_in, refs_out, scratch):
    mixed_ref, head_ref, z_ref, al_ref, skip_ref = refs_in
    gate_ref, skipped_ref, rate_ref = refs_out
    rows, channels = z_ref.shape
    head = head_ref.shape[0]
    gate_ref[...] = silu(z_ref[...].astype(F32))
    rate_ref[...] = jnp.exp(al_ref[...]) * (-LOG2E)
    for tile in range(channels // LANES):
        lanes = slice(tile * LANES, (tile + 1) * LANES)
        skipped_ref[tile, :head, :] = skip_ref[:, lanes] * head_ref[:, lanes].astype(F32)
        skipped_ref[tile, head:, :] = skip_ref[:, lanes] * mixed_ref[head:, lanes].astype(F32)


def scan_kernel(dims, refs_in, refs_out, scratch):
    per_dev, n_replica, _, _ = dims
    mixed_ref, head_ref, dtw_ref, dtb_ref, gate_ref, skipped_ref, rate_ref = refs_in[3:10]
    out_hbm, state_hbm = refs_out
    b_tab, c_tab, dt_v, drive_v, start_tm, final_tm, y_v, out_v, state_v, out_sems, int_sems = scratch[:11]
    ints = scratch[11:]
    int_copies = [pltpu.make_async_copy(refs_in[i], ints[i], int_sems.at[i]) for i in range(len(ints))]
    for copy in int_copies:
        copy.start()
    n_pieces = sum(1 for ref in refs_in[10:] if ref.shape[-1] == gate_ref.shape[1])
    parts, pieces = refs_in[10:-n_pieces], refs_in[-n_pieces:]
    rows, channels = gate_ref.shape
    states = rate_ref.shape[0]
    rank = dtw_ref.shape[0]
    head = head_ref.shape[0]

    projected = parts[0][...].astype(F32)
    for part in parts[1:]:
        projected = projected + part[...].astype(F32)
    c_part = projected[rank + states :]
    c_high = c_part.astype(BF16).astype(F32)
    shape = (2 * states, states * LANES)
    term = lax.broadcasted_iota(jnp.int32, shape, 0) & (states - 1)
    lane_group, _ = split_index(lax.broadcasted_iota(jnp.int32, shape, 1), LANES)
    spread = jnp.where(term == lane_group, 1.0, 0.0).astype(BF16)
    c_terms = jnp.concatenate([c_high, c_part - c_high], axis=0).T.astype(BF16)
    projected = projected[: rank + states].T
    dt_low = projected[:, :rank].astype(BF16)
    late = projected[:, rank:]
    n_tiles = channels // LANES
    wide = min(2, n_tiles)
    per_chunk = states * wide // n_tiles
    for c in range(n_tiles // wide):
        for n in range(c * per_chunk, (c + 1) * per_chunk):
            b_tab[n] = jnp.broadcast_to(late[:, n : n + 1], (rows, LANES))
        lanes = slice(c * per_chunk * LANES, (c + 1) * per_chunk * LANES)
        repeated = jnp.dot(c_terms, spread[:, lanes], preferred_element_type=F32)
        for n in range(per_chunk):
            c_tab[c * per_chunk + n] = repeated[:, n * LANES : (n + 1) * LANES]
        weights = dtw_ref[:, c * wide * LANES : (c + 1) * wide * LANES]
        raw = jnp.dot(dt_low, weights, preferred_element_type=F32)
        for j in range(wide):
            tile = c * wide + j
            lanes = slice(tile * LANES, (tile + 1) * LANES)
            for first in range(0, rows, LANES):
                here = slice(first, first + LANES)
                dt = softplus(raw[here, j * LANES : (j + 1) * LANES] + dtb_ref[:, lanes])
                mixed = mixed_ref[here, lanes]
                if first == 0:
                    mixed = jnp.concatenate([head_ref[:, lanes], mixed[head:]], axis=0)
                mixed = mixed.astype(F32)
                dt_v[tile, here, :] = dt
                drive_v[tile, here, :] = dt * mixed

    me = lax.axis_index("replica")
    for copy in int_copies:
        copy.wait()
    places, slot_ids, lengths = request_places(dims, ints, me)
    for r in range(per_dev):
        spot = pl.ds(pl.multiple_of(slot_ids[r] * states, states), states)
        for tile in range(n_tiles):
            lanes = slice(tile * LANES, (tile + 1) * LANES)
            if n_pieces == 1:
                value = pieces[0][places[r], spot, lanes]
            else:
                value = pieces[0][spot, lanes]
                for p in range(1, n_pieces):
                    value = jnp.where(places[r] == p, pieces[p][spot, lanes], value)
            value = value.astype(F32)
            value = jnp.where(lengths[r] > 0, value, jnp.zeros_like(value))
            start_tm[tile, pl.ds(r, states, stride=per_dev), :] = value

    tiles = 2
    half = states // 4
    width = tiles * LANES
    n_groups = n_tiles // tiles

    def out_copies(g):
        lanes = pl.ds(pl.multiple_of(g * width, width), width)
        return [
            pltpu.make_async_copy(src.at[:, lanes], dst.at[:, lanes], out_sems.at[i, g])
            for i, (src, dst) in enumerate(((out_v, out_hbm), (state_v, state_hbm)))
        ]

    def finish(g):
        for j in range(tiles):
            tile = g * tiles + j
            lanes = pl.ds(pl.multiple_of(tile * LANES, LANES), LANES)
            for r in range(per_dev):
                here = slice(r * NEW, (r + 1) * NEW)
                value = y_v[tile, pl.ds(r, NEW, stride=per_dev), :] * gate_ref[here, lanes]
                out_v[here, lanes] = value.astype(BF16)
                final = final_tm[tile, pl.ds(r, states, stride=per_dev), :]
                state_v[r * states : (r + 1) * states, lanes] = final.astype(BF16)

    def scan_group(g):
        group = [g * tiles + j for j in range(tiles)]
        lanes = [pl.ds(pl.multiple_of(tile * LANES, LANES), LANES) for tile in group]
        for first in range(0, states, half):
            ids = range(first, first + half)
            rates = [[jnp.broadcast_to(rate_ref[n : n + 1, lane], (per_dev, LANES)) for n in ids] for lane in lanes]

            def advance(step, state):
                state = list(state)
                for u in range(UNROLL):
                    now = pl.ds(pl.multiple_of((step * UNROLL + u) * per_dev, per_dev), per_dev)
                    dt = [dt_v[tile, now, :] for tile in group]
                    drive = [drive_v[tile, now, :] for tile in group]
                    sums = [None] * tiles
                    for k, n in enumerate(ids):
                        b, c = b_tab[n, now, :], c_tab[n, now, :]
                        for j in range(tiles):
                            i = j * half + k
                            state[i] = jnp.exp2(dt[j] * rates[j][k]) * state[i] + drive[j] * b
                            term = state[i] * c
                            sums[j] = term if sums[j] is None else sums[j] + term
                    for j, tile in enumerate(group):
                        before = skipped_ref[tile, now, :] if first == 0 else y_v[tile, now, :]
                        y_v[tile, now, :] = before + sums[j]
                return tuple(state)

            state = tuple(start_tm[tile, n * per_dev : (n + 1) * per_dev, :] for tile in group for n in ids)
            if NEW == UNROLL:
                state = advance(0, state)
            else:
                state = lax.fori_loop(0, NEW // UNROLL, advance, state)
            for j, tile in enumerate(group):
                for k, n in enumerate(ids):
                    final_tm[tile, n * per_dev : (n + 1) * per_dev, :] = state[j * half + k]

    def one_group(g, carry):
        before = jnp.maximum(g - 1, 0)
        finish(before)
        scan_group(g)

        @pl.when(g > 0)
        def _():
            for copy in out_copies(before):
                copy.start()

        return carry

    final_tm[:tiles] = jnp.zeros((tiles,) + final_tm.shape[1:], F32)
    y_v[:tiles] = jnp.zeros((tiles,) + y_v.shape[1:], F32)
    lax.fori_loop(0, n_groups, one_group, 0)
    finish(n_groups - 1)
    for copy in out_copies(n_groups - 1):
        copy.start()

    def last_wait(g, carry):
        for copy in out_copies(g):
            copy.wait()
        return carry

    lax.fori_loop(0, n_groups, last_wait, 0)


def split_refs(kernel, dims, n_in, n_out):
    def body(*refs):
        kernel(dims, refs[:n_in], refs[n_in : n_in + n_out], refs[n_in + n_out :])

    return body


def call(kernel, dims, name, limit, ins, outs, scratch):
    spaces = {"hbm": pltpu.HBM, "any": pl.ANY, "vmem": pltpu.VMEM, "smem": pltpu.SMEM}
    values = [
        pltpu.with_memory_space_constraint(value, pltpu.HBM) if place == "hbm" else value for value, place in ins
    ]
    return pl.pallas_call(
        split_refs(kernel, dims, len(ins), len(outs)),
        in_specs=[pl.BlockSpec(memory_space=spaces[place]) for _, place in ins],
        out_specs=[pl.BlockSpec(memory_space=spaces[place]) for _, _, place in outs],
        out_shape=[jax.ShapeDtypeStruct(shape, dtype) for shape, dtype, _ in outs],
        scratch_shapes=scratch,
        compiler_params=pltpu.CompilerParams(vmem_limit_bytes=limit * MIB),
        name=name,
    )(*values)


def swap(value, axis, size, mask):
    return lax.ppermute(value, axis, [(i, i ^ mask) for i in range(size)])


def shards(mesh, x_new, z_new, conv_weight, conv_bias, x_proj_weight, dt_proj_weight, dt_bias, a_log, d_skip,
           cache_ssm, cache_conv, holder, slot_id, prefix_len):
    n_replica, n_tensor = mesh.shape["replica"], mesh.shape["tensor"]
    rows, channels = x_new.shape
    per_dev = rows // NEW
    states = a_log.shape[0]
    rank = dt_proj_weight.shape[0]
    taps = conv_weight.shape[0]
    slots = cache_ssm.shape[0]
    out_cols = x_proj_weight.shape[1]
    requests = holder.shape[0]

    vmem, dma = pltpu.VMEM, pltpu.SemaphoreType.DMA
    ssm_rows = slots * states
    rows_all, conv_rows = call(
        pack_kernel, (slots, taps), "pack", 20,
        [(cache_ssm.reshape(ssm_rows, channels), "hbm"), (cache_conv.transpose(1, 0, 2), "hbm")],
        [((ssm_rows + slots * taps, channels), BF16, "vmem"), ((slots * taps, channels), BF16, "vmem")],
        [vmem((taps - 1, slots, channels), BF16), dma((2,))],
    )
    block = rows_all.shape[0]
    relative = n_replica == 4
    if relative:
        far = swap(rows_all, "replica", n_replica, 3)
        near = swap(rows_all, "replica", n_replica, 1)
        conv_two = swap(conv_rows, "replica", n_replica, 2)
        conv_pieces = [rows_all, near, far, conv_two]
        firsts = (0, block, 2 * block, 4 * block - slots * taps)
        ssm_pieces = [rows_all, near, far, swap(far, "replica", n_replica, 1)]
    else:
        ssm_pieces = [lax.all_gather(rows_all, "replica")]
        conv_pieces, firsts = [ssm_pieces[0].reshape(-1, channels)], (0,)

    n_chunks = channels // min(512, channels)
    dims = (per_dev, n_replica, slots, relative)
    head = per_dev * taps
    weights = x_proj_weight.T
    requests = [(holder, "smem"), (slot_id, "smem"), (prefix_len, "smem")]

    mixed, head_sums, part, target = call(
        project_kernel, (dims, block), "conv_project", 40,
        [(x_new, "hbm"), (weights, "hbm"), (conv_weight, "hbm"), (conv_bias[None, :], "hbm")] + requests,
        [((rows, channels), BF16, "any"), ((head, channels), F32, "any"), ((out_cols, rows), BF16, "any"),
         ((head, LANES), jnp.int32, "vmem")],
        [
            vmem((rows, channels), BF16),
            vmem((out_cols, channels), BF16),
            vmem((taps, channels), BF16),
            vmem((1, channels), F32),
            vmem((channels // LANES, rows + taps * per_dev, LANES), F32),
            vmem((rows, channels), BF16),
            vmem((head, channels), F32),
            vmem((out_cols, rows), F32),
            vmem((out_cols, rows), BF16),
            dma((2 + 2 * n_chunks,)),
            dma((n_chunks + 2,)),
        ],
    )
    mixed_head, part = call(
        history_kernel, (per_dev, firsts), "history", 20,
        [(value, "vmem") for value in [target, head_sums, part, weights, conv_weight] + conv_pieces],
        [((head, channels), BF16, "vmem"), ((out_cols, rows), BF16, "vmem")],
        [],
    )
    parts = [part]
    mask = n_tensor // 2
    while mask:
        parts = parts + [swap(value, "tensor", n_tensor, mask) for value in reversed(parts)]
        mask //= 2

    n_tiles = channels // LANES
    prepared = call(
        prepare_kernel, None, "prepare", 40,
        [(value, "vmem") for value in (mixed, mixed_head, z_new, a_log, d_skip[None, :])],
        [((rows, channels), F32, "vmem"), ((n_tiles, rows, LANES), F32, "vmem"), ((states, channels), F32, "vmem")],
        [],
    )
    operands = [mixed, mixed_head, dt_proj_weight, dt_bias[None, :], *prepared]
    out, state = call(
        scan_kernel, dims, "dt_scan_gate", 40,
        [(value, "any") for value, _ in requests] + [(value, "vmem") for value in operands + parts + ssm_pieces],
        [((rows, channels), BF16, "any"), ((per_dev * states, channels), BF16, "any")],
        [
            vmem((states, rows, LANES), F32),
            vmem((states, rows, LANES), F32),
            vmem((n_tiles, rows, LANES), F32),
            vmem((n_tiles, rows, LANES), F32),
            vmem((n_tiles, per_dev * (states + 1), LANES), F32),
            vmem((n_tiles, per_dev * (states + 1), LANES), F32),
            vmem((n_tiles, rows + per_dev, LANES), F32),
            vmem((rows, channels), BF16),
            vmem((per_dev * states, channels), BF16),
            dma((2, n_tiles // 2)),
            dma((3,)),
        ] + [pltpu.SMEM(holder.shape, jnp.int32)] * 3,
    )
    return out, state.reshape(per_dev, states, channels)


def solution(mesh):
    placed = (
        P(("groups", "replica"), "tensor"),
        P(("groups", "replica"), "tensor"),
        P(None, "tensor"),
        P("tensor"),
        P("tensor", None),
        P(None, "tensor"),
        P("tensor"),
        P(None, "tensor"),
        P("tensor"),
        P(("groups", "replica"), None, "tensor"),
        P(("groups", "replica"), None, "tensor"),
        P("groups"),
        P("groups"),
        P("groups"),
    )
    return jax.shard_map(
        functools.partial(shards, mesh),
        mesh=mesh,
        in_specs=placed,
        out_specs=(P(("groups", "replica"), "tensor"), P(("groups", "replica"), None, "tensor")),
        check_vma=False,
    )
```

```python
import functools

import jax
import jax.numpy as jnp
from jax import lax
from jax.experimental import pallas as pl
from jax.experimental.pallas import tpu as pltpu
from jax.sharding import PartitionSpec as P

NEW = 32
LANES = 128
MIB = 1024 * 1024
UNROLL = 32
LOG2E = 1.4426950408889634
F32, BF16 = jnp.float32, jnp.bfloat16
NT = (((1,), (1,)), ((), ()))


def silu(v):
    half = 0.5 * v
    return half + half * jnp.tanh(half)


def softplus(v):
    u = jnp.exp2(jnp.abs(v) * -LOG2E)
    return jnp.maximum(v, 0.0) + jnp.where(u < 2.0**-10, u - 0.5 * (u * u), jnp.log(1.0 + u))


def split_index(value, inner):
    assert inner & (inner - 1) == 0
    return value >> (inner.bit_length() - 1), value & (inner - 1)


def pick_rows(values, row_low, count):
    out = jnp.zeros(row_low.shape, jnp.int32)
    for r in range(count):
        out = jnp.where(row_low == r, values[r], out)
    return out


def request_places(dims, ints, me):
    per_dev, n_replica, _, relative = dims
    places, slot_ids, lengths = [], [], []
    for r in range(per_dev):
        request = me * per_dev + r
        place = ints[0][request]
        if relative:
            place = place ^ me
            place = place ^ (place >> 1)
        places.append(place)
        slot_ids.append(ints[1][request])
        lengths.append(ints[2][request])
    return places, slot_ids, lengths


def fetch_rows(target, live, pieces):
    total = None
    for first, value in pieces:
        col = lax.broadcasted_iota(jnp.int32, (target.shape[0], value.shape[0]), 1) + first
        select = jnp.where((col == target) & live, 1.0, 0.0).astype(BF16)
        part = jnp.dot(select, value, preferred_element_type=F32)
        total = part if total is None else total + part
    return total


def pack_kernel(dims, refs_in, refs_out, scratch):
    slots, taps = dims
    ssm_hbm, conv_hbm = refs_in
    block_ref, conv_ref = refs_out
    conv_v, sems = scratch
    states = pltpu.make_async_copy(ssm_hbm, block_ref.at[: ssm_hbm.shape[0]], sems.at[0])
    inputs = pltpu.make_async_copy(conv_hbm, conv_v, sems.at[1])
    states.start()
    inputs.start()
    inputs.wait()
    lines = []
    for slot in range(slots):
        for tap in range(taps):
            line = conv_v[min(tap, taps - 2)].astype(F32)[slot : slot + 1]
            lines.append(line if tap < taps - 1 else jnp.zeros_like(line))
    rows = jnp.concatenate(lines, axis=0).astype(BF16)
    conv_ref[...] = rows
    block_ref[ssm_hbm.shape[0] :, :] = rows
    states.wait()


def project_kernel(dims, refs_in, refs_out, scratch):
    dims, block = dims
    per_dev, _, slots, _ = dims
    x_hbm, wt_hbm, cw_hbm, cb_hbm = refs_in[:4]
    mixed_hbm, head_hbm, part_hbm, target_ref = refs_out
    x_v, wt_v, cw_v, cb_v, joined, mixed_v, head_v, part_f, part_v, sems, out_sems, int_sems = scratch[:12]
    ints = scratch[12:]
    int_copies = [pltpu.make_async_copy(refs_in[4 + i], ints[i], int_sems.at[i]) for i in range(len(ints))]
    rows, channels = x_v.shape
    taps = cw_v.shape[0]
    lines = (taps - 1) * per_dev
    pairs = [(cw_hbm, cw_v), (cb_hbm, cb_v)]
    width = min(512, channels)
    chunks = [slice(c * width, (c + 1) * width) for c in range(channels // width)]
    for chunk in chunks:
        pairs += [(x_hbm.at[:, chunk], x_v.at[:, chunk]), (wt_hbm.at[:, chunk], wt_v.at[:, chunk])]
    copies = [pltpu.make_async_copy(src, dst, sems.at[i]) for i, (src, dst) in enumerate(pairs)]
    for copy in copies + int_copies:
        copy.start()

    joined[:, :lines, :] = jnp.zeros((channels // LANES, lines, LANES), F32)
    copies[0].wait()
    copies[1].wait()
    outs = []
    for c, chunk in enumerate(chunks):
        copies[2 + 2 * c].wait()
        for tile in range(c * width // LANES, (c + 1) * width // LANES):
            lanes = slice(tile * LANES, (tile + 1) * LANES)
            for r in range(per_dev):
                tokens = x_v[r * NEW : (r + 1) * NEW, lanes].astype(F32)
                joined[tile, pl.ds(lines + r, NEW, stride=per_dev), :] = tokens
            weight = [cw_v[k : k + 1, lanes].astype(F32) for k in range(taps)]
            bias = cb_v[:, lanes]
            for first in range(0, rows, LANES):
                summed = bias + joined[tile, first : first + LANES, :] * weight[0]
                for k in range(1, taps):
                    begin = first + k * per_dev
                    summed = summed + joined[tile, begin : begin + LANES, :] * weight[k]
                if first == 0:
                    head_v[:, lanes] = summed[: head_v.shape[0]]
                mixed_v[first : first + LANES, lanes] = silu(summed).astype(BF16)
        copies[3 + 2 * c].wait()
        part = lax.dot_general(wt_v[:, chunk], mixed_v[:, chunk], NT, preferred_element_type=F32)
        if c == 0:
            part_f[...] = part
        else:
            part_f[...] += part
        outs.append(pltpu.make_async_copy(mixed_v.at[:, chunk], mixed_hbm.at[:, chunk], out_sems.at[c]))
        outs[-1].start()
    for copy in int_copies:
        copy.wait()
    me = lax.axis_index("replica")
    places, slot_ids, lengths = request_places(dims, ints, me)
    tap, request = split_index(lax.broadcasted_iota(jnp.int32, target_ref.shape, 0), per_dev)
    starts = [places[r] * block + (block - slots * taps) + slot_ids[r] * taps for r in range(per_dev)]
    live = (tap < taps - 1) & (taps - 1 - tap <= pick_rows(lengths, request, per_dev))
    target_ref[...] = jnp.where(live, pick_rows(starts, request, per_dev) + tap, -1)
    part_v[...] = part_f[...].astype(BF16)
    for src, dst in ((part_v, part_hbm), (head_v, head_hbm)):
        outs.append(pltpu.make_async_copy(src, dst, out_sems.at[len(outs)]))
        outs[-1].start()
    for copy in outs:
        copy.wait()


def history_kernel(dims, refs_in, refs_out, scratch):
    per_dev, firsts = dims
    target_ref, head_ref, part_ref, wt_ref, cw_ref = refs_in[:5]
    pieces = refs_in[5:]
    mixed_ref, fixed_ref = refs_out
    taps = cw_ref.shape[0]
    target = target_ref[:, :1]
    history = fetch_rows(target, target >= 0, [(first, ref[...]) for first, ref in zip(firsts, pieces)])
    sums = []
    for t in range(taps):
        summed = head_ref[t * per_dev : (t + 1) * per_dev]
        for k in range(taps - 1 - t):
            weight = cw_ref[k : k + 1].astype(F32)
            summed = summed + history[(t + k) * per_dev : (t + k + 1) * per_dev] * weight
        sums.append(summed)
    mixed = silu(jnp.concatenate(sums, axis=0)).astype(BF16)
    mixed_ref[...] = mixed
    part = lax.dot_general(wt_ref[...], mixed, NT, preferred_element_type=F32)
    fixed_ref[...] = part_ref[...]
    fixed_ref[:, : per_dev * taps] = part.astype(BF16)


def prepare_kernel(dims, refs_in, refs_out, scratch):
    mixed_ref, head_ref, z_ref, al_ref, skip_ref = refs_in
    gate_ref, skipped_ref, rate_ref = refs_out
    rows, channels = z_ref.shape
    head = head_ref.shape[0]
    gate_ref[...] = silu(z_ref[...].astype(F32))
    rate_ref[...] = jnp.exp(al_ref[...]) * (-LOG2E)
    for tile in range(channels // LANES):
        lanes = slice(tile * LANES, (tile + 1) * LANES)
        skipped_ref[tile, :head, :] = skip_ref[:, lanes] * head_ref[:, lanes].astype(F32)
        skipped_ref[tile, head:, :] = skip_ref[:, lanes] * mixed_ref[head:, lanes].astype(F32)


def scan_kernel(dims, refs_in, refs_out, scratch):
    per_dev, n_replica, _, _ = dims
    mixed_ref, head_ref, dtw_ref, dtb_ref, gate_ref, skipped_ref, rate_ref = refs_in[3:10]
    out_hbm, state_hbm = refs_out
    b_tab, c_tab, dt_v, drive_v, start_tm, final_tm, y_v, out_v, state_v, out_sems, int_sems = scratch[:11]
    ints = scratch[11:]
    int_copies = [pltpu.make_async_copy(refs_in[i], ints[i], int_sems.at[i]) for i in range(len(ints))]
    for copy in int_copies:
        copy.start()
    n_pieces = sum(1 for ref in refs_in[10:] if ref.shape[-1] == gate_ref.shape[1])
    parts, pieces = refs_in[10:-n_pieces], refs_in[-n_pieces:]
    rows, channels = gate_ref.shape
    states = rate_ref.shape[0]
    rank = dtw_ref.shape[0]
    head = head_ref.shape[0]

    projected = parts[0][...].astype(F32)
    for part in parts[1:]:
        projected = projected + part[...].astype(F32)
    c_part = projected[rank + states :]
    c_high = c_part.astype(BF16).astype(F32)
    shape = (2 * states, states * LANES)
    term = lax.broadcasted_iota(jnp.int32, shape, 0) & (states - 1)
    lane_group, _ = split_index(lax.broadcasted_iota(jnp.int32, shape, 1), LANES)
    spread = jnp.where(term == lane_group, 1.0, 0.0).astype(BF16)
    c_terms = jnp.concatenate([c_high, c_part - c_high], axis=0).T.astype(BF16)
    projected = projected[: rank + states].T
    dt_low = projected[:, :rank].astype(BF16)
    late = projected[:, rank:]
    n_tiles = channels // LANES
    wide = min(2, n_tiles)
    per_chunk = states * wide // n_tiles
    for c in range(n_tiles // wide):
        for n in range(c * per_chunk, (c + 1) * per_chunk):
            b_tab[n] = jnp.broadcast_to(late[:, n : n + 1], (rows, LANES))
        lanes = slice(c * per_chunk * LANES, (c + 1) * per_chunk * LANES)
        repeated = jnp.dot(c_terms, spread[:, lanes], preferred_element_type=F32)
        for n in range(per_chunk):
            c_tab[c * per_chunk + n] = repeated[:, n * LANES : (n + 1) * LANES]
        weights = dtw_ref[:, c * wide * LANES : (c + 1) * wide * LANES]
        raw = jnp.dot(dt_low, weights, preferred_element_type=F32)
        for j in range(wide):
            tile = c * wide + j
            lanes = slice(tile * LANES, (tile + 1) * LANES)
            for first in range(0, rows, LANES):
                here = slice(first, first + LANES)
                dt = softplus(raw[here, j * LANES : (j + 1) * LANES] + dtb_ref[:, lanes])
                mixed = mixed_ref[here, lanes]
                if first == 0:
                    mixed = jnp.concatenate([head_ref[:, lanes], mixed[head:]], axis=0)
                mixed = mixed.astype(F32)
                dt_v[tile, here, :] = dt
                drive_v[tile, here, :] = dt * mixed

    me = lax.axis_index("replica")
    for copy in int_copies:
        copy.wait()
    places, slot_ids, lengths = request_places(dims, ints, me)
    for r in range(per_dev):
        spot = pl.ds(pl.multiple_of(slot_ids[r] * states, states), states)
        for tile in range(n_tiles):
            lanes = slice(tile * LANES, (tile + 1) * LANES)
            if n_pieces == 1:
                value = pieces[0][places[r], spot, lanes]
            else:
                value = pieces[0][spot, lanes]
                for p in range(1, n_pieces):
                    value = jnp.where(places[r] == p, pieces[p][spot, lanes], value)
            value = value.astype(F32)
            value = jnp.where(lengths[r] > 0, value, jnp.zeros_like(value))
            start_tm[tile, pl.ds(r, states, stride=per_dev), :] = value

    tiles = 2
    half = states // 4
    width = tiles * LANES
    n_groups = n_tiles // tiles

    def out_copies(g):
        lanes = pl.ds(pl.multiple_of(g * width, width), width)
        return [
            pltpu.make_async_copy(src.at[:, lanes], dst.at[:, lanes], out_sems.at[i, g])
            for i, (src, dst) in enumerate(((out_v, out_hbm), (state_v, state_hbm)))
        ]

    def finish(g):
        for j in range(tiles):
            tile = g * tiles + j
            lanes = pl.ds(pl.multiple_of(tile * LANES, LANES), LANES)
            for r in range(per_dev):
                here = slice(r * NEW, (r + 1) * NEW)
                value = y_v[tile, pl.ds(r, NEW, stride=per_dev), :] * gate_ref[here, lanes]
                out_v[here, lanes] = value.astype(BF16)
                final = final_tm[tile, pl.ds(r, states, stride=per_dev), :]
                state_v[r * states : (r + 1) * states, lanes] = final.astype(BF16)

    def scan_group(g):
        group = [g * tiles + j for j in range(tiles)]
        lanes = [pl.ds(pl.multiple_of(tile * LANES, LANES), LANES) for tile in group]
        for first in range(0, states, half):
            ids = range(first, first + half)
            rates = [[jnp.broadcast_to(rate_ref[n : n + 1, lane], (per_dev, LANES)) for n in ids] for lane in lanes]

            def advance(step, state):
                state = list(state)
                for u in range(UNROLL):
                    now = pl.ds(pl.multiple_of((step * UNROLL + u) * per_dev, per_dev), per_dev)
                    dt = [dt_v[tile, now, :] for tile in group]
                    drive = [drive_v[tile, now, :] for tile in group]
                    sums = [None] * tiles
                    for k, n in enumerate(ids):
                        b, c = b_tab[n, now, :], c_tab[n, now, :]
                        for j in range(tiles):
                            i = j * half + k
                            state[i] = jnp.exp2(dt[j] * rates[j][k]) * state[i] + drive[j] * b
                            term = state[i] * c
                            sums[j] = term if sums[j] is None else sums[j] + term
                    for j, tile in enumerate(group):
                        before = skipped_ref[tile, now, :] if first == 0 else y_v[tile, now, :]
                        y_v[tile, now, :] = before + sums[j]
                return tuple(state)

            state = tuple(start_tm[tile, n * per_dev : (n + 1) * per_dev, :] for tile in group for n in ids)
            if NEW == UNROLL:
                state = advance(0, state)
            else:
                state = lax.fori_loop(0, NEW // UNROLL, advance, state)
            for j, tile in enumerate(group):
                for k, n in enumerate(ids):
                    final_tm[tile, n * per_dev : (n + 1) * per_dev, :] = state[j * half + k]

    def one_group(g, carry):
        before = jnp.maximum(g - 1, 0)
        finish(before)
        scan_group(g)

        @pl.when(g > 0)
        def _():
            for copy in out_copies(before):
                copy.start()

        return carry

    final_tm[:tiles] = jnp.zeros((tiles,) + final_tm.shape[1:], F32)
    y_v[:tiles] = jnp.zeros((tiles,) + y_v.shape[1:], F32)
    lax.fori_loop(0, n_groups, one_group, 0)
    finish(n_groups - 1)
    for copy in out_copies(n_groups - 1):
        copy.start()

    def last_wait(g, carry):
        for copy in out_copies(g):
            copy.wait()
        return carry

    lax.fori_loop(0, n_groups, last_wait, 0)


def split_refs(kernel, dims, n_in, n_out):
    def body(*refs):
        kernel(dims, refs[:n_in], refs[n_in : n_in + n_out], refs[n_in + n_out :])

    return body


def call(kernel, dims, name, limit, ins, outs, scratch):
    spaces = {"hbm": pltpu.HBM, "any": pl.ANY, "vmem": pltpu.VMEM, "smem": pltpu.SMEM}
    values = [
        pltpu.with_memory_space_constraint(value, pltpu.HBM) if place == "hbm" else value for value, place in ins
    ]
    return pl.pallas_call(
        split_refs(kernel, dims, len(ins), len(outs)),
        in_specs=[pl.BlockSpec(memory_space=spaces[place]) for _, place in ins],
        out_specs=[pl.BlockSpec(memory_space=spaces[place]) for _, _, place in outs],
        out_shape=[jax.ShapeDtypeStruct(shape, dtype) for shape, dtype, _ in outs],
        scratch_shapes=scratch,
        compiler_params=pltpu.CompilerParams(vmem_limit_bytes=limit * MIB),
        name=name,
    )(*values)


def swap(value, axis, size, mask):
    return lax.ppermute(value, axis, [(i, i ^ mask) for i in range(size)])


def shards(mesh, x_new, z_new, conv_weight, conv_bias, x_proj_weight, dt_proj_weight, dt_bias, a_log, d_skip,
           cache_ssm, cache_conv, holder, slot_id, prefix_len):
    n_replica, n_tensor = mesh.shape["replica"], mesh.shape["tensor"]
    rows, channels = x_new.shape
    per_dev = rows // NEW
    states = a_log.shape[0]
    rank = dt_proj_weight.shape[0]
    taps = conv_weight.shape[0]
    slots = cache_ssm.shape[0]
    out_cols = x_proj_weight.shape[1]
    requests = holder.shape[0]

    vmem, dma = pltpu.VMEM, pltpu.SemaphoreType.DMA
    ssm_rows = slots * states
    rows_all, conv_rows = call(
        pack_kernel, (slots, taps), "pack", 20,
        [(cache_ssm.reshape(ssm_rows, channels), "hbm"), (cache_conv.transpose(1, 0, 2), "hbm")],
        [((ssm_rows + slots * taps, channels), BF16, "vmem"), ((slots * taps, channels), BF16, "vmem")],
        [vmem((taps - 1, slots, channels), BF16), dma((2,))],
    )
    block = rows_all.shape[0]
    relative = n_replica == 4
    if relative:
        far = swap(rows_all, "replica", n_replica, 3)
        near = swap(rows_all, "replica", n_replica, 1)
        conv_two = swap(conv_rows, "replica", n_replica, 2)
        conv_pieces = [rows_all, near, far, conv_two]
        firsts = (0, block, 2 * block, 4 * block - slots * taps)
        ssm_pieces = [rows_all, near, far, swap(far, "replica", n_replica, 1)]
    else:
        ssm_pieces = [lax.all_gather(rows_all, "replica")]
        conv_pieces, firsts = [ssm_pieces[0].reshape(-1, channels)], (0,)

    n_chunks = channels // min(512, channels)
    dims = (per_dev, n_replica, slots, relative)
    head = per_dev * taps
    weights = x_proj_weight.T
    requests = [(holder, "smem"), (slot_id, "smem"), (prefix_len, "smem")]

    mixed, head_sums, part, target = call(
        project_kernel, (dims, block), "conv_project", 40,
        [(x_new, "hbm"), (weights, "hbm"), (conv_weight, "hbm"), (conv_bias[None, :], "hbm")]
        + [(value, "hbm") for value, _ in requests],
        [((rows, channels), BF16, "any"), ((head, channels), F32, "any"), ((out_cols, rows), BF16, "any"),
         ((head, LANES), jnp.int32, "vmem")],
        [
            vmem((rows, channels), BF16),
            vmem((out_cols, channels), BF16),
            vmem((taps, channels), BF16),
            vmem((1, channels), F32),
            vmem((channels // LANES, rows + taps * per_dev, LANES), F32),
            vmem((rows, channels), BF16),
            vmem((head, channels), F32),
            vmem((out_cols, rows), F32),
            vmem((out_cols, rows), BF16),
            dma((2 + 2 * n_chunks,)),
            dma((n_chunks + 2,)),
            dma((3,)),
        ] + [pltpu.SMEM(holder.shape, jnp.int32)] * 3,
    )
    mixed_head, part = call(
        history_kernel, (per_dev, firsts), "history", 20,
        [(value, "vmem") for value in [target, head_sums, part, weights, conv_weight] + conv_pieces],
        [((head, channels), BF16, "vmem"), ((out_cols, rows), BF16, "vmem")],
        [],
    )
    parts = [part]
    mask = n_tensor // 2
    while mask:
        parts = parts + [swap(value, "tensor", n_tensor, mask) for value in reversed(parts)]
        mask //= 2

    n_tiles = channels // LANES
    prepared = call(
        prepare_kernel, None, "prepare", 40,
        [(value, "vmem") for value in (mixed, mixed_head, z_new, a_log, d_skip[None, :])],
        [((rows, channels), F32, "vmem"), ((n_tiles, rows, LANES), F32, "vmem"), ((states, channels), F32, "vmem")],
        [],
    )
    operands = [mixed, mixed_head, dt_proj_weight, dt_bias[None, :], *prepared]
    out, state = call(
        scan_kernel, dims, "dt_scan_gate", 40,
        [(value, "any") for value, _ in requests] + [(value, "vmem") for value in operands + parts + ssm_pieces],
        [((rows, channels), BF16, "any"), ((per_dev * states, channels), BF16, "any")],
        [
            vmem((states, rows, LANES), F32),
            vmem((states, rows, LANES), F32),
            vmem((n_tiles, rows, LANES), F32),
            vmem((n_tiles, rows, LANES), F32),
            vmem((n_tiles, per_dev * (states + 1), LANES), F32),
            vmem((n_tiles, per_dev * (states + 1), LANES), F32),
            vmem((n_tiles, rows + per_dev, LANES), F32),
            vmem((rows, channels), BF16),
            vmem((per_dev * states, channels), BF16),
            dma((2, n_tiles // 2)),
            dma((3,)),
        ] + [pltpu.SMEM(holder.shape, jnp.int32)] * 3,
    )
    return out, state.reshape(per_dev, states, channels)


def solution(mesh):
    placed = (
        P(("groups", "replica"), "tensor"),
        P(("groups", "replica"), "tensor"),
        P(None, "tensor"),
        P("tensor"),
        P("tensor", None),
        P(None, "tensor"),
        P("tensor"),
        P(None, "tensor"),
        P("tensor"),
        P(("groups", "replica"), None, "tensor"),
        P(("groups", "replica"), None, "tensor"),
        P("groups"),
        P("groups"),
        P("groups"),
    )
    return jax.shard_map(
        functools.partial(shards, mesh),
        mesh=mesh,
        in_specs=placed,
        out_specs=(P(("groups", "replica"), "tensor"), P(("groups", "replica"), None, "tensor")),
        check_vma=False,
    )
```

```python
import functools

import jax
import jax.numpy as jnp
from jax import lax
from jax.experimental import pallas as pl
from jax.experimental.pallas import tpu as pltpu
from jax.sharding import PartitionSpec as P

NEW = 32
LANES = 128
MIB = 1024 * 1024
UNROLL = 32
LOG2E = 1.4426950408889634
F32, BF16 = jnp.float32, jnp.bfloat16
NT = (((1,), (1,)), ((), ()))


def silu(v):
    half = 0.5 * v
    return half + half * jnp.tanh(half)


def softplus(v):
    u = jnp.exp2(jnp.abs(v) * -LOG2E)
    return jnp.maximum(v, 0.0) + jnp.where(u < 2.0**-10, u - 0.5 * (u * u), jnp.log(1.0 + u))


def split_index(value, inner):
    assert inner & (inner - 1) == 0
    return value >> (inner.bit_length() - 1), value & (inner - 1)


def pick_rows(values, row_low, count):
    out = jnp.zeros(row_low.shape, jnp.int32)
    for r in range(count):
        out = jnp.where(row_low == r, values[r], out)
    return out


def request_places(dims, ints, me):
    per_dev, n_replica, _, relative = dims
    places, slot_ids, lengths = [], [], []
    for r in range(per_dev):
        request = me * per_dev + r
        place = ints[0][request]
        if relative:
            place = place ^ me
            place = place ^ (place >> 1)
        places.append(place)
        slot_ids.append(ints[1][request])
        lengths.append(ints[2][request])
    return places, slot_ids, lengths


def fetch_rows(target, live, pieces):
    total = None
    for first, value in pieces:
        col = lax.broadcasted_iota(jnp.int32, (target.shape[0], value.shape[0]), 1) + first
        select = jnp.where((col == target) & live, 1.0, 0.0).astype(BF16)
        part = jnp.dot(select, value, preferred_element_type=F32)
        total = part if total is None else total + part
    return total


def pack_kernel(dims, refs_in, refs_out, scratch):
    slots, taps = dims
    ssm_hbm, conv_hbm = refs_in
    block_ref, conv_ref = refs_out
    conv_v, sems = scratch
    states = pltpu.make_async_copy(ssm_hbm, block_ref.at[: ssm_hbm.shape[0]], sems.at[0])
    inputs = pltpu.make_async_copy(conv_hbm, conv_v, sems.at[1])
    states.start()
    inputs.start()
    inputs.wait()
    lines = []
    for slot in range(slots):
        for tap in range(taps):
            line = conv_v[min(tap, taps - 2)].astype(F32)[slot : slot + 1]
            lines.append(line if tap < taps - 1 else jnp.zeros_like(line))
    rows = jnp.concatenate(lines, axis=0).astype(BF16)
    conv_ref[...] = rows
    block_ref[ssm_hbm.shape[0] :, :] = rows
    states.wait()


def project_kernel(dims, refs_in, refs_out, scratch):
    dims, block = dims
    per_dev, _, slots, _ = dims
    x_hbm, wt_hbm, cw_hbm, cb_hbm = refs_in[:4]
    mixed_hbm, head_hbm, part_hbm, target_ref = refs_out
    x_v, wt_v, cw_v, cb_v, joined, mixed_v, head_v, part_f, part_v, sems, out_sems, int_sems = scratch[:12]
    ints = scratch[12:]
    int_copies = [pltpu.make_async_copy(refs_in[4 + i], ints[i], int_sems.at[i]) for i in range(len(ints))]
    rows, channels = x_v.shape
    taps = cw_v.shape[0]
    lines = (taps - 1) * per_dev
    pairs = [(cw_hbm, cw_v), (cb_hbm, cb_v)]
    width = min(512, channels)
    chunks = [slice(c * width, (c + 1) * width) for c in range(channels // width)]
    for chunk in chunks:
        pairs += [(x_hbm.at[:, chunk], x_v.at[:, chunk]), (wt_hbm.at[:, chunk], wt_v.at[:, chunk])]
    copies = [pltpu.make_async_copy(src, dst, sems.at[i]) for i, (src, dst) in enumerate(pairs)]
    for copy in copies + int_copies:
        copy.start()

    joined[:, :lines, :] = jnp.zeros((channels // LANES, lines, LANES), F32)
    copies[0].wait()
    copies[1].wait()
    outs = []
    for c, chunk in enumerate(chunks):
        copies[2 + 2 * c].wait()
        for tile in range(c * width // LANES, (c + 1) * width // LANES):
            lanes = slice(tile * LANES, (tile + 1) * LANES)
            for r in range(per_dev):
                tokens = x_v[r * NEW : (r + 1) * NEW, lanes].astype(F32)
                joined[tile, pl.ds(lines + r, NEW, stride=per_dev), :] = tokens
            weight = [cw_v[k : k + 1, lanes].astype(F32) for k in range(taps)]
            bias = cb_v[:, lanes]
            for first in range(0, rows, LANES):
                summed = bias + joined[tile, first : first + LANES, :] * weight[0]
                for k in range(1, taps):
                    begin = first + k * per_dev
                    summed = summed + joined[tile, begin : begin + LANES, :] * weight[k]
                if first == 0:
                    head_v[:, lanes] = summed[: head_v.shape[0]]
                mixed_v[first : first + LANES, lanes] = silu(summed).astype(BF16)
        copies[3 + 2 * c].wait()
        part = lax.dot_general(wt_v[:, chunk], mixed_v[:, chunk], NT, preferred_element_type=F32)
        if c == 0:
            part_f[...] = part
        else:
            part_f[...] += part
        outs.append(pltpu.make_async_copy(mixed_v.at[:, chunk], mixed_hbm.at[:, chunk], out_sems.at[c]))
        outs[-1].start()
    for copy in int_copies:
        copy.wait()
    me = lax.axis_index("replica")
    places, slot_ids, lengths = request_places(dims, ints, me)
    tap, request = split_index(lax.broadcasted_iota(jnp.int32, target_ref.shape, 0), per_dev)
    starts = [places[r] * block + (block - slots * taps) + slot_ids[r] * taps for r in range(per_dev)]
    live = (tap < taps - 1) & (taps - 1 - tap <= pick_rows(lengths, request, per_dev))
    target_ref[...] = jnp.where(live, pick_rows(starts, request, per_dev) + tap, -1)
    part_v[...] = part_f[...].astype(BF16)
    for src, dst in ((part_v, part_hbm), (head_v, head_hbm)):
        outs.append(pltpu.make_async_copy(src, dst, out_sems.at[len(outs)]))
        outs[-1].start()
    for copy in outs:
        copy.wait()


def history_kernel(dims, refs_in, refs_out, scratch):
    per_dev, firsts = dims
    target_ref, head_ref, part_ref, wt_ref, cw_ref = refs_in[:5]
    pieces = refs_in[5:]
    mixed_ref, fixed_ref = refs_out
    taps = cw_ref.shape[0]
    target = target_ref[:, :1]
    history = fetch_rows(target, target >= 0, [(first, ref[...]) for first, ref in zip(firsts, pieces)])
    sums = []
    for t in range(taps):
        summed = head_ref[t * per_dev : (t + 1) * per_dev]
        for k in range(taps - 1 - t):
            weight = cw_ref[k : k + 1].astype(F32)
            summed = summed + history[(t + k) * per_dev : (t + k + 1) * per_dev] * weight
        sums.append(summed)
    mixed = silu(jnp.concatenate(sums, axis=0)).astype(BF16)
    mixed_ref[...] = mixed
    part = lax.dot_general(wt_ref[...], mixed, NT, preferred_element_type=F32)
    fixed_ref[...] = part_ref[...]
    fixed_ref[:, : per_dev * taps] = part.astype(BF16)


def prepare_kernel(dims, refs_in, refs_out, scratch):
    mixed_ref, head_ref, z_ref, al_ref, skip_ref = refs_in
    gate_ref, skipped_ref, rate_ref = refs_out
    rows, channels = z_ref.shape
    head = head_ref.shape[0]
    gate_ref[...] = silu(z_ref[...].astype(F32))
    rate_ref[...] = jnp.exp(al_ref[...]) * (-LOG2E)
    for tile in range(channels // LANES):
        lanes = slice(tile * LANES, (tile + 1) * LANES)
        skipped_ref[tile, :head, :] = skip_ref[:, lanes] * head_ref[:, lanes].astype(F32)
        skipped_ref[tile, head:, :] = skip_ref[:, lanes] * mixed_ref[head:, lanes].astype(F32)


def scan_kernel(dims, refs_in, refs_out, scratch):
    per_dev, n_replica, _, _ = dims
    mixed_ref, head_ref, dtw_ref, dtb_ref, gate_ref, skipped_ref, rate_ref = refs_in[3:10]
    out_hbm, state_hbm = refs_out
    b_tab, c_tab, dt_v, drive_v, start_tm, final_rm, y_v, y_rm, out_v, state_v, out_sems, int_sems = scratch[:12]
    ints = scratch[12:]
    int_copies = [pltpu.make_async_copy(refs_in[i], ints[i], int_sems.at[i]) for i in range(len(ints))]
    for copy in int_copies:
        copy.start()
    n_pieces = sum(1 for ref in refs_in[10:] if ref.shape[-1] == gate_ref.shape[1])
    parts, pieces = refs_in[10:-n_pieces], refs_in[-n_pieces:]
    rows, channels = gate_ref.shape
    states = rate_ref.shape[0]
    rank = dtw_ref.shape[0]
    head = head_ref.shape[0]

    projected = parts[0][...].astype(F32)
    for part in parts[1:]:
        projected = projected + part[...].astype(F32)
    c_part = projected[rank + states :]
    c_high = c_part.astype(BF16).astype(F32)
    shape = (2 * states, states * LANES)
    term = lax.broadcasted_iota(jnp.int32, shape, 0) & (states - 1)
    lane_group, _ = split_index(lax.broadcasted_iota(jnp.int32, shape, 1), LANES)
    spread = jnp.where(term == lane_group, 1.0, 0.0).astype(BF16)
    c_terms = jnp.concatenate([c_high, c_part - c_high], axis=0).T.astype(BF16)
    projected = projected[: rank + states].T
    dt_low = projected[:, :rank].astype(BF16)
    late = projected[:, rank:]
    n_tiles = channels // LANES
    wide = min(2, n_tiles)
    per_chunk = states * wide // n_tiles
    for c in range(n_tiles // wide):
        for n in range(c * per_chunk, (c + 1) * per_chunk):
            b_tab[n] = jnp.broadcast_to(late[:, n : n + 1], (rows, LANES))
        lanes = slice(c * per_chunk * LANES, (c + 1) * per_chunk * LANES)
        repeated = jnp.dot(c_terms, spread[:, lanes], preferred_element_type=F32)
        for n in range(per_chunk):
            c_tab[c * per_chunk + n] = repeated[:, n * LANES : (n + 1) * LANES]
        weights = dtw_ref[:, c * wide * LANES : (c + 1) * wide * LANES]
        raw = jnp.dot(dt_low, weights, preferred_element_type=F32)
        for j in range(wide):
            tile = c * wide + j
            lanes = slice(tile * LANES, (tile + 1) * LANES)
            for first in range(0, rows, LANES):
                here = slice(first, first + LANES)
                dt = softplus(raw[here, j * LANES : (j + 1) * LANES] + dtb_ref[:, lanes])
                mixed = mixed_ref[here, lanes]
                if first == 0:
                    mixed = jnp.concatenate([head_ref[:, lanes], mixed[head:]], axis=0)
                mixed = mixed.astype(F32)
                dt_v[tile, here, :] = dt
                drive_v[tile, here, :] = dt * mixed

    me = lax.axis_index("replica")
    for copy in int_copies:
        copy.wait()
    places, slot_ids, lengths = request_places(dims, ints, me)
    for r in range(per_dev):
        spot = pl.ds(pl.multiple_of(slot_ids[r] * states, states), states)
        for tile in range(n_tiles):
            lanes = slice(tile * LANES, (tile + 1) * LANES)
            if n_pieces == 1:
                value = pieces[0][places[r], spot, lanes]
            else:
                value = pieces[0][spot, lanes]
                for p in range(1, n_pieces):
                    value = jnp.where(places[r] == p, pieces[p][spot, lanes], value)
            value = value.astype(F32)
            value = jnp.where(lengths[r] > 0, value, jnp.zeros_like(value))
            start_tm[tile, pl.ds(r, states, stride=per_dev), :] = value

    tiles = 2
    half = states // 4
    width = tiles * LANES
    n_groups = n_tiles // tiles

    def out_copies(g):
        lanes = pl.ds(pl.multiple_of(g * width, width), width)
        return [
            pltpu.make_async_copy(src.at[:, lanes], dst.at[:, lanes], out_sems.at[i, g])
            for i, (src, dst) in enumerate(((out_v, out_hbm), (state_v, state_hbm)))
        ]

    def finish(g):
        for j in range(tiles):
            tile = g * tiles + j
            lanes = pl.ds(pl.multiple_of(tile * LANES, LANES), LANES)
            for r in range(per_dev):
                here = slice(r * NEW, (r + 1) * NEW)
                out_v[here, lanes] = (y_rm[tile, here, :] * gate_ref[here, lanes]).astype(BF16)
                here = slice(r * states, (r + 1) * states)
                state_v[here, lanes] = final_rm[tile, here, :].astype(BF16)

    def scan_group(g):
        group = [g * tiles + j for j in range(tiles)]
        lanes = [pl.ds(pl.multiple_of(tile * LANES, LANES), LANES) for tile in group]
        for first in range(0, states, half):
            ids = range(first, first + half)
            rates = [[jnp.broadcast_to(rate_ref[n : n + 1, lane], (per_dev, LANES)) for n in ids] for lane in lanes]

            def advance(step, state):
                state = list(state)
                for u in range(UNROLL):
                    now = pl.ds(pl.multiple_of((step * UNROLL + u) * per_dev, per_dev), per_dev)
                    dt = [dt_v[tile, now, :] for tile in group]
                    drive = [drive_v[tile, now, :] for tile in group]
                    sums = [None] * tiles
                    for k, n in enumerate(ids):
                        b, c = b_tab[n, now, :], c_tab[n, now, :]
                        for j in range(tiles):
                            i = j * half + k
                            state[i] = jnp.exp2(dt[j] * rates[j][k]) * state[i] + drive[j] * b
                            term = state[i] * c
                            sums[j] = term if sums[j] is None else sums[j] + term
                    for j, tile in enumerate(group):
                        before = skipped_ref[tile, now, :] if first == 0 else y_v[tile, now, :]
                        if first + half < states:
                            y_v[tile, now, :] = before + sums[j]
                        else:
                            y_rm[tile, pl.ds(step * UNROLL + u, per_dev, stride=NEW), :] = before + sums[j]
                return tuple(state)

            state = tuple(start_tm[tile, n * per_dev : (n + 1) * per_dev, :] for tile in group for n in ids)
            if NEW == UNROLL:
                state = advance(0, state)
            else:
                state = lax.fori_loop(0, NEW // UNROLL, advance, state)
            for j, tile in enumerate(group):
                for k, n in enumerate(ids):
                    final_rm[tile, pl.ds(n, per_dev, stride=states), :] = state[j * half + k]

    def one_group(g, carry):
        before = jnp.maximum(g - 1, 0)
        finish(before)
        scan_group(g)

        @pl.when(g > 0)
        def _():
            for copy in out_copies(before):
                copy.start()

        return carry

    final_rm[:tiles] = jnp.zeros((tiles,) + final_rm.shape[1:], F32)
    y_rm[:tiles] = jnp.zeros((tiles,) + y_rm.shape[1:], F32)
    lax.fori_loop(0, n_groups, one_group, 0)
    finish(n_groups - 1)
    for copy in out_copies(n_groups - 1):
        copy.start()

    def last_wait(g, carry):
        for copy in out_copies(g):
            copy.wait()
        return carry

    lax.fori_loop(0, n_groups, last_wait, 0)


def split_refs(kernel, dims, n_in, n_out):
    def body(*refs):
        kernel(dims, refs[:n_in], refs[n_in : n_in + n_out], refs[n_in + n_out :])

    return body


def call(kernel, dims, name, limit, ins, outs, scratch):
    spaces = {"hbm": pltpu.HBM, "any": pl.ANY, "vmem": pltpu.VMEM, "smem": pltpu.SMEM}
    values = [
        pltpu.with_memory_space_constraint(value, pltpu.HBM) if place == "hbm" else value for value, place in ins
    ]
    return pl.pallas_call(
        split_refs(kernel, dims, len(ins), len(outs)),
        in_specs=[pl.BlockSpec(memory_space=spaces[place]) for _, place in ins],
        out_specs=[pl.BlockSpec(memory_space=spaces[place]) for _, _, place in outs],
        out_shape=[jax.ShapeDtypeStruct(shape, dtype) for shape, dtype, _ in outs],
        scratch_shapes=scratch,
        compiler_params=pltpu.CompilerParams(vmem_limit_bytes=limit * MIB),
        name=name,
    )(*values)


def swap(value, axis, size, mask):
    return lax.ppermute(value, axis, [(i, i ^ mask) for i in range(size)])


def shards(mesh, x_new, z_new, conv_weight, conv_bias, x_proj_weight, dt_proj_weight, dt_bias, a_log, d_skip,
           cache_ssm, cache_conv, holder, slot_id, prefix_len):
    n_replica, n_tensor = mesh.shape["replica"], mesh.shape["tensor"]
    rows, channels = x_new.shape
    per_dev = rows // NEW
    states = a_log.shape[0]
    rank = dt_proj_weight.shape[0]
    taps = conv_weight.shape[0]
    slots = cache_ssm.shape[0]
    out_cols = x_proj_weight.shape[1]
    requests = holder.shape[0]

    vmem, dma = pltpu.VMEM, pltpu.SemaphoreType.DMA
    ssm_rows = slots * states
    rows_all, conv_rows = call(
        pack_kernel, (slots, taps), "pack", 20,
        [(cache_ssm.reshape(ssm_rows, channels), "hbm"), (cache_conv.transpose(1, 0, 2), "hbm")],
        [((ssm_rows + slots * taps, channels), BF16, "vmem"), ((slots * taps, channels), BF16, "vmem")],
        [vmem((taps - 1, slots, channels), BF16), dma((2,))],
    )
    block = rows_all.shape[0]
    relative = n_replica == 4
    if relative:
        far = swap(rows_all, "replica", n_replica, 3)
        near = swap(rows_all, "replica", n_replica, 1)
        conv_two = swap(conv_rows, "replica", n_replica, 2)
        conv_pieces = [rows_all, near, far, conv_two]
        firsts = (0, block, 2 * block, 4 * block - slots * taps)
        ssm_pieces = [rows_all, near, far, swap(far, "replica", n_replica, 1)]
    else:
        ssm_pieces = [lax.all_gather(rows_all, "replica")]
        conv_pieces, firsts = [ssm_pieces[0].reshape(-1, channels)], (0,)

    n_chunks = channels // min(512, channels)
    dims = (per_dev, n_replica, slots, relative)
    head = per_dev * taps
    weights = x_proj_weight.T
    requests = [(holder, "smem"), (slot_id, "smem"), (prefix_len, "smem")]

    mixed, head_sums, part, target = call(
        project_kernel, (dims, block), "conv_project", 40,
        [(x_new, "hbm"), (weights, "hbm"), (conv_weight, "hbm"), (conv_bias[None, :], "hbm")]
        + [(value, "hbm") for value, _ in requests],
        [((rows, channels), BF16, "any"), ((head, channels), F32, "any"), ((out_cols, rows), BF16, "any"),
         ((head, LANES), jnp.int32, "vmem")],
        [
            vmem((rows, channels), BF16),
            vmem((out_cols, channels), BF16),
            vmem((taps, channels), BF16),
            vmem((1, channels), F32),
            vmem((channels // LANES, rows + taps * per_dev, LANES), F32),
            vmem((rows, channels), BF16),
            vmem((head, channels), F32),
            vmem((out_cols, rows), F32),
            vmem((out_cols, rows), BF16),
            dma((2 + 2 * n_chunks,)),
            dma((n_chunks + 2,)),
            dma((3,)),
        ] + [pltpu.SMEM(holder.shape, jnp.int32)] * 3,
    )
    mixed_head, part = call(
        history_kernel, (per_dev, firsts), "history", 20,
        [(value, "vmem") for value in [target, head_sums, part, weights, conv_weight] + conv_pieces],
        [((head, channels), BF16, "vmem"), ((out_cols, rows), BF16, "vmem")],
        [],
    )
    parts = [part]
    mask = n_tensor // 2
    while mask:
        parts = parts + [swap(value, "tensor", n_tensor, mask) for value in reversed(parts)]
        mask //= 2

    n_tiles = channels // LANES
    prepared = call(
        prepare_kernel, None, "prepare", 40,
        [(value, "vmem") for value in (mixed, mixed_head, z_new, a_log, d_skip[None, :])],
        [((rows, channels), F32, "vmem"), ((n_tiles, rows, LANES), F32, "vmem"), ((states, channels), F32, "vmem")],
        [],
    )
    operands = [mixed, mixed_head, dt_proj_weight, dt_bias[None, :], *prepared]
    out, state = call(
        scan_kernel, dims, "dt_scan_gate", 40,
        [(value, "any") for value, _ in requests] + [(value, "vmem") for value in operands + parts + ssm_pieces],
        [((rows, channels), BF16, "any"), ((per_dev * states, channels), BF16, "any")],
        [
            vmem((states, rows, LANES), F32),
            vmem((states, rows, LANES), F32),
            vmem((n_tiles, rows, LANES), F32),
            vmem((n_tiles, rows, LANES), F32),
            vmem((n_tiles, per_dev * (states + 1), LANES), F32),
            vmem((n_tiles, (per_dev + 1) * states, LANES), F32),
            vmem((n_tiles, rows, LANES), F32),
            vmem((n_tiles, rows + NEW, LANES), F32),
            vmem((rows, channels), BF16),
            vmem((per_dev * states, channels), BF16),
            dma((2, n_tiles // 2)),
            dma((3,)),
        ] + [pltpu.SMEM(holder.shape, jnp.int32)] * 3,
    )
    return out, state.reshape(per_dev, states, channels)


def solution(mesh):
    placed = (
        P(("groups", "replica"), "tensor"),
        P(("groups", "replica"), "tensor"),
        P(None, "tensor"),
        P("tensor"),
        P("tensor", None),
        P(None, "tensor"),
        P("tensor"),
        P(None, "tensor"),
        P("tensor"),
        P(("groups", "replica"), None, "tensor"),
        P(("groups", "replica"), None, "tensor"),
        P("groups"),
        P("groups"),
        P("groups"),
    )
    return jax.shard_map(
        functools.partial(shards, mesh),
        mesh=mesh,
        in_specs=placed,
        out_specs=(P(("groups", "replica"), "tensor"), P(("groups", "replica"), None, "tensor")),
        check_vma=False,
    )
```

```python
import functools

import jax
import jax.numpy as jnp
from jax import lax
from jax.experimental import pallas as pl
from jax.experimental.pallas import tpu as pltpu
from jax.sharding import PartitionSpec as P

NEW = 32
LANES = 128
MIB = 1024 * 1024
UNROLL = 32
LOG2E = 1.4426950408889634
F32, BF16 = jnp.float32, jnp.bfloat16
NT = (((1,), (1,)), ((), ()))


def silu(v):
    half = 0.5 * v
    return half + half * jnp.tanh(half)


def softplus(v):
    u = jnp.exp2(jnp.abs(v) * -LOG2E)
    return jnp.maximum(v, 0.0) + jnp.where(u < 2.0**-10, u - 0.5 * (u * u), jnp.log(1.0 + u))


def split_index(value, inner):
    assert inner & (inner - 1) == 0
    return value >> (inner.bit_length() - 1), value & (inner - 1)


def pick_rows(values, row_low, count):
    out = jnp.zeros(row_low.shape, jnp.int32)
    for r in range(count):
        out = jnp.where(row_low == r, values[r], out)
    return out


def request_places(dims, ints, me):
    per_dev, n_replica, _, relative = dims
    places, slot_ids, lengths = [], [], []
    for r in range(per_dev):
        request = me * per_dev + r
        place = ints[0][request]
        if relative:
            place = place ^ me
            place = place ^ (place >> 1)
        places.append(place)
        slot_ids.append(ints[1][request])
        lengths.append(ints[2][request])
    return places, slot_ids, lengths


def fetch_rows(target, live, pieces):
    total = None
    for first, value in pieces:
        col = lax.broadcasted_iota(jnp.int32, (target.shape[0], value.shape[0]), 1) + first
        select = jnp.where((col == target) & live, 1.0, 0.0).astype(BF16)
        part = jnp.dot(select, value, preferred_element_type=F32)
        total = part if total is None else total + part
    return total


def pack_kernel(dims, refs_in, refs_out, scratch):
    slots, taps = dims
    ssm_hbm, conv_hbm = refs_in
    block_ref, conv_ref = refs_out
    conv_v, sems = scratch
    states = pltpu.make_async_copy(ssm_hbm, block_ref.at[: ssm_hbm.shape[0]], sems.at[0])
    inputs = pltpu.make_async_copy(conv_hbm, conv_v, sems.at[1])
    states.start()
    inputs.start()
    inputs.wait()
    lines = []
    for slot in range(slots):
        for tap in range(taps):
            line = conv_v[min(tap, taps - 2)].astype(F32)[slot : slot + 1]
            lines.append(line if tap < taps - 1 else jnp.zeros_like(line))
    rows = jnp.concatenate(lines, axis=0).astype(BF16)
    conv_ref[...] = rows
    block_ref[ssm_hbm.shape[0] :, :] = rows
    states.wait()


def project_kernel(dims, refs_in, refs_out, scratch):
    dims, block = dims
    per_dev, _, slots, _ = dims
    x_hbm, wt_hbm, cw_hbm, cb_hbm = refs_in[:4]
    mixed_hbm, head_hbm, part_hbm, target_ref = refs_out
    x_v, wt_v, cw_v, cb_v, joined, mixed_v, head_v, part_f, part_v, sems, out_sems, int_sems = scratch[:12]
    ints = scratch[12:]
    int_copies = [pltpu.make_async_copy(refs_in[4 + i], ints[i], int_sems.at[i]) for i in range(len(ints))]
    rows, channels = x_v.shape
    taps = cw_v.shape[0]
    lines = (taps - 1) * per_dev
    pairs = [(cw_hbm, cw_v), (cb_hbm, cb_v)]
    width = min(512, channels)
    chunks = [slice(c * width, (c + 1) * width) for c in range(channels // width)]
    for chunk in chunks:
        pairs += [(x_hbm.at[:, chunk], x_v.at[:, chunk]), (wt_hbm.at[:, chunk], wt_v.at[:, chunk])]
    copies = [pltpu.make_async_copy(src, dst, sems.at[i]) for i, (src, dst) in enumerate(pairs)]
    for copy in copies + int_copies:
        copy.start()

    joined[:, :lines, :] = jnp.zeros((channels // LANES, lines, LANES), F32)
    copies[0].wait()
    copies[1].wait()
    outs = []
    for c, chunk in enumerate(chunks):
        copies[2 + 2 * c].wait()
        for tile in range(c * width // LANES, (c + 1) * width // LANES):
            lanes = slice(tile * LANES, (tile + 1) * LANES)
            for r in range(per_dev):
                tokens = x_v[r * NEW : (r + 1) * NEW, lanes].astype(F32)
                joined[tile, pl.ds(lines + r, NEW, stride=per_dev), :] = tokens
            weight = [cw_v[k : k + 1, lanes].astype(F32) for k in range(taps)]
            bias = cb_v[:, lanes]
            for first in range(0, rows, LANES):
                summed = bias + joined[tile, first : first + LANES, :] * weight[0]
                for k in range(1, taps):
                    begin = first + k * per_dev
                    summed = summed + joined[tile, begin : begin + LANES, :] * weight[k]
                if first == 0:
                    head_v[:, lanes] = summed[: head_v.shape[0]]
                mixed_v[first : first + LANES, lanes] = silu(summed).astype(BF16)
        copies[3 + 2 * c].wait()
        part = lax.dot_general(wt_v[:, chunk], mixed_v[:, chunk], NT, preferred_element_type=F32)
        if c == 0:
            part_f[...] = part
        else:
            part_f[...] += part
        outs.append(pltpu.make_async_copy(mixed_v.at[:, chunk], mixed_hbm.at[:, chunk], out_sems.at[c]))
        outs[-1].start()
    for copy in int_copies:
        copy.wait()
    me = lax.axis_index("replica")
    places, slot_ids, lengths = request_places(dims, ints, me)
    tap, request = split_index(lax.broadcasted_iota(jnp.int32, target_ref.shape, 0), per_dev)
    starts = [places[r] * block + (block - slots * taps) + slot_ids[r] * taps for r in range(per_dev)]
    live = (tap < taps - 1) & (taps - 1 - tap <= pick_rows(lengths, request, per_dev))
    target_ref[...] = jnp.where(live, pick_rows(starts, request, per_dev) + tap, -1)
    part_v[...] = part_f[...].astype(BF16)
    for src, dst in ((part_v, part_hbm), (head_v, head_hbm)):
        outs.append(pltpu.make_async_copy(src, dst, out_sems.at[len(outs)]))
        outs[-1].start()
    for copy in outs:
        copy.wait()


def history_kernel(dims, refs_in, refs_out, scratch):
    per_dev, firsts = dims
    target_ref, head_ref, part_ref, wt_ref, cw_ref = refs_in[:5]
    pieces = refs_in[5:]
    mixed_ref, fixed_ref = refs_out
    taps = cw_ref.shape[0]
    target = target_ref[:, :1]
    history = fetch_rows(target, target >= 0, [(first, ref[...]) for first, ref in zip(firsts, pieces)])
    sums = []
    for t in range(taps):
        summed = head_ref[t * per_dev : (t + 1) * per_dev]
        for k in range(taps - 1 - t):
            weight = cw_ref[k : k + 1].astype(F32)
            summed = summed + history[(t + k) * per_dev : (t + k + 1) * per_dev] * weight
        sums.append(summed)
    mixed = silu(jnp.concatenate(sums, axis=0)).astype(BF16)
    mixed_ref[...] = mixed
    part = lax.dot_general(wt_ref[...], mixed, NT, preferred_element_type=F32)
    fixed_ref[...] = part_ref[...]
    fixed_ref[:, : per_dev * taps] = part.astype(BF16)


def prepare_kernel(dims, refs_in, refs_out, scratch):
    mixed_ref, head_ref, z_ref, al_ref, skip_ref = refs_in
    gate_ref, skipped_ref, rate_ref = refs_out
    rows, channels = z_ref.shape
    head = head_ref.shape[0]
    gate_ref[...] = silu(z_ref[...].astype(F32))
    rate_ref[...] = jnp.exp(al_ref[...]) * (-LOG2E)
    for tile in range(channels // LANES):
        lanes = slice(tile * LANES, (tile + 1) * LANES)
        skipped_ref[tile, :head, :] = skip_ref[:, lanes] * head_ref[:, lanes].astype(F32)
        skipped_ref[tile, head:, :] = skip_ref[:, lanes] * mixed_ref[head:, lanes].astype(F32)


def scan_kernel(dims, refs_in, refs_out, scratch):
    per_dev, n_replica, _, _ = dims
    mixed_ref, head_ref, dtw_ref, dtb_ref, gate_ref, skipped_ref, rate_ref = refs_in[3:10]
    out_hbm, state_hbm = refs_out
    b_tab, c_tab, dt_v, drive_v, start_rm, final_tm, y_v, out_v, state_v, out_sems, int_sems = scratch[:11]
    ints = scratch[11:]
    int_copies = [pltpu.make_async_copy(refs_in[i], ints[i], int_sems.at[i]) for i in range(len(ints))]
    for copy in int_copies:
        copy.start()
    n_pieces = sum(1 for ref in refs_in[10:] if ref.shape[-1] == gate_ref.shape[1])
    parts, pieces = refs_in[10:-n_pieces], refs_in[-n_pieces:]
    rows, channels = gate_ref.shape
    states = rate_ref.shape[0]
    rank = dtw_ref.shape[0]
    head = head_ref.shape[0]

    projected = parts[0][...].astype(F32)
    for part in parts[1:]:
        projected = projected + part[...].astype(F32)
    c_part = projected[rank + states :]
    c_high = c_part.astype(BF16).astype(F32)
    shape = (2 * states, states * LANES)
    term = lax.broadcasted_iota(jnp.int32, shape, 0) & (states - 1)
    lane_group, _ = split_index(lax.broadcasted_iota(jnp.int32, shape, 1), LANES)
    spread = jnp.where(term == lane_group, 1.0, 0.0).astype(BF16)
    c_terms = jnp.concatenate([c_high, c_part - c_high], axis=0).T.astype(BF16)
    projected = projected[: rank + states].T
    dt_low = projected[:, :rank].astype(BF16)
    late = projected[:, rank:]
    n_tiles = channels // LANES
    wide = min(2, n_tiles)
    per_chunk = states * wide // n_tiles
    for c in range(n_tiles // wide):
        for n in range(c * per_chunk, (c + 1) * per_chunk):
            b_tab[n] = jnp.broadcast_to(late[:, n : n + 1], (rows, LANES))
        lanes = slice(c * per_chunk * LANES, (c + 1) * per_chunk * LANES)
        repeated = jnp.dot(c_terms, spread[:, lanes], preferred_element_type=F32)
        for n in range(per_chunk):
            c_tab[c * per_chunk + n] = repeated[:, n * LANES : (n + 1) * LANES]
        weights = dtw_ref[:, c * wide * LANES : (c + 1) * wide * LANES]
        raw = jnp.dot(dt_low, weights, preferred_element_type=F32)
        for j in range(wide):
            tile = c * wide + j
            lanes = slice(tile * LANES, (tile + 1) * LANES)
            for first in range(0, rows, LANES):
                here = slice(first, first + LANES)
                dt = softplus(raw[here, j * LANES : (j + 1) * LANES] + dtb_ref[:, lanes])
                mixed = mixed_ref[here, lanes]
                if first == 0:
                    mixed = jnp.concatenate([head_ref[:, lanes], mixed[head:]], axis=0)
                mixed = mixed.astype(F32)
                dt_v[tile, here, :] = dt
                drive_v[tile, here, :] = dt * mixed

    me = lax.axis_index("replica")
    for copy in int_copies:
        copy.wait()
    places, slot_ids, lengths = request_places(dims, ints, me)
    for r in range(per_dev):
        spot = pl.ds(pl.multiple_of(slot_ids[r] * states, states), states)
        for tile in range(n_tiles):
            lanes = slice(tile * LANES, (tile + 1) * LANES)
            if n_pieces == 1:
                value = pieces[0][places[r], spot, lanes]
            else:
                value = pieces[0][spot, lanes]
                for p in range(1, n_pieces):
                    value = jnp.where(places[r] == p, pieces[p][spot, lanes], value)
            value = value.astype(F32)
            value = jnp.where(lengths[r] > 0, value, jnp.zeros_like(value))
            start_rm[tile, r * states : (r + 1) * states, :] = value

    tiles = 2
    half = states // 4
    width = tiles * LANES
    n_groups = n_tiles // tiles

    def out_copies(g):
        lanes = pl.ds(pl.multiple_of(g * width, width), width)
        return [
            pltpu.make_async_copy(src.at[:, lanes], dst.at[:, lanes], out_sems.at[i, g])
            for i, (src, dst) in enumerate(((out_v, out_hbm), (state_v, state_hbm)))
        ]

    def finish(g):
        for j in range(tiles):
            tile = g * tiles + j
            lanes = pl.ds(pl.multiple_of(tile * LANES, LANES), LANES)
            for r in range(per_dev):
                here = slice(r * NEW, (r + 1) * NEW)
                value = y_v[tile, pl.ds(r, NEW, stride=per_dev), :] * gate_ref[here, lanes]
                out_v[here, lanes] = value.astype(BF16)
                final = final_tm[tile, pl.ds(r, states, stride=per_dev), :]
                state_v[r * states : (r + 1) * states, lanes] = final.astype(BF16)

    def scan_group(g):
        group = [g * tiles + j for j in range(tiles)]
        lanes = [pl.ds(pl.multiple_of(tile * LANES, LANES), LANES) for tile in group]
        for first in range(0, states, half):
            ids = range(first, first + half)
            rates = [[jnp.broadcast_to(rate_ref[n : n + 1, lane], (per_dev, LANES)) for n in ids] for lane in lanes]

            def advance(step, state):
                state = list(state)
                for u in range(UNROLL):
                    now = pl.ds(pl.multiple_of((step * UNROLL + u) * per_dev, per_dev), per_dev)
                    dt = [dt_v[tile, now, :] for tile in group]
                    drive = [drive_v[tile, now, :] for tile in group]
                    sums = [None] * tiles
                    for k, n in enumerate(ids):
                        b, c = b_tab[n, now, :], c_tab[n, now, :]
                        for j in range(tiles):
                            i = j * half + k
                            state[i] = jnp.exp2(dt[j] * rates[j][k]) * state[i] + drive[j] * b
                            term = state[i] * c
                            sums[j] = term if sums[j] is None else sums[j] + term
                    for j, tile in enumerate(group):
                        before = skipped_ref[tile, now, :] if first == 0 else y_v[tile, now, :]
                        y_v[tile, now, :] = before + sums[j]
                return tuple(state)

            state = tuple(start_rm[tile, pl.ds(n, per_dev, stride=states), :] for tile in group for n in ids)
            if NEW == UNROLL:
                state = advance(0, state)
            else:
                state = lax.fori_loop(0, NEW // UNROLL, advance, state)
            for j, tile in enumerate(group):
                for k, n in enumerate(ids):
                    final_tm[tile, n * per_dev : (n + 1) * per_dev, :] = state[j * half + k]

    def one_group(g, carry):
        before = jnp.maximum(g - 1, 0)
        finish(before)
        scan_group(g)

        @pl.when(g > 0)
        def _():
            for copy in out_copies(before):
                copy.start()

        return carry

    final_tm[:tiles] = jnp.zeros((tiles,) + final_tm.shape[1:], F32)
    y_v[:tiles] = jnp.zeros((tiles,) + y_v.shape[1:], F32)
    lax.fori_loop(0, n_groups, one_group, 0)
    finish(n_groups - 1)
    for copy in out_copies(n_groups - 1):
        copy.start()

    def last_wait(g, carry):
        for copy in out_copies(g):
            copy.wait()
        return carry

    lax.fori_loop(0, n_groups, last_wait, 0)


def split_refs(kernel, dims, n_in, n_out):
    def body(*refs):
        kernel(dims, refs[:n_in], refs[n_in : n_in + n_out], refs[n_in + n_out :])

    return body


def call(kernel, dims, name, limit, ins, outs, scratch):
    spaces = {"hbm": pltpu.HBM, "any": pl.ANY, "vmem": pltpu.VMEM, "smem": pltpu.SMEM}
    values = [
        pltpu.with_memory_space_constraint(value, pltpu.HBM) if place == "hbm" else value for value, place in ins
    ]
    return pl.pallas_call(
        split_refs(kernel, dims, len(ins), len(outs)),
        in_specs=[pl.BlockSpec(memory_space=spaces[place]) for _, place in ins],
        out_specs=[pl.BlockSpec(memory_space=spaces[place]) for _, _, place in outs],
        out_shape=[jax.ShapeDtypeStruct(shape, dtype) for shape, dtype, _ in outs],
        scratch_shapes=scratch,
        compiler_params=pltpu.CompilerParams(vmem_limit_bytes=limit * MIB),
        name=name,
    )(*values)


def swap(value, axis, size, mask):
    return lax.ppermute(value, axis, [(i, i ^ mask) for i in range(size)])


def shards(mesh, x_new, z_new, conv_weight, conv_bias, x_proj_weight, dt_proj_weight, dt_bias, a_log, d_skip,
           cache_ssm, cache_conv, holder, slot_id, prefix_len):
    n_replica, n_tensor = mesh.shape["replica"], mesh.shape["tensor"]
    rows, channels = x_new.shape
    per_dev = rows // NEW
    states = a_log.shape[0]
    rank = dt_proj_weight.shape[0]
    taps = conv_weight.shape[0]
    slots = cache_ssm.shape[0]
    out_cols = x_proj_weight.shape[1]
    requests = holder.shape[0]

    vmem, dma = pltpu.VMEM, pltpu.SemaphoreType.DMA
    ssm_rows = slots * states
    rows_all, conv_rows = call(
        pack_kernel, (slots, taps), "pack", 20,
        [(cache_ssm.reshape(ssm_rows, channels), "hbm"), (cache_conv.transpose(1, 0, 2), "hbm")],
        [((ssm_rows + slots * taps, channels), BF16, "vmem"), ((slots * taps, channels), BF16, "vmem")],
        [vmem((taps - 1, slots, channels), BF16), dma((2,))],
    )
    block = rows_all.shape[0]
    relative = n_replica == 4
    if relative:
        far = swap(rows_all, "replica", n_replica, 3)
        near = swap(rows_all, "replica", n_replica, 1)
        conv_two = swap(conv_rows, "replica", n_replica, 2)
        conv_pieces = [rows_all, near, far, conv_two]
        firsts = (0, block, 2 * block, 4 * block - slots * taps)
        ssm_pieces = [rows_all, near, far, swap(far, "replica", n_replica, 1)]
    else:
        ssm_pieces = [lax.all_gather(rows_all, "replica")]
        conv_pieces, firsts = [ssm_pieces[0].reshape(-1, channels)], (0,)

    n_chunks = channels // min(512, channels)
    dims = (per_dev, n_replica, slots, relative)
    head = per_dev * taps
    weights = x_proj_weight.T
    requests = [(holder, "smem"), (slot_id, "smem"), (prefix_len, "smem")]

    mixed, head_sums, part, target = call(
        project_kernel, (dims, block), "conv_project", 40,
        [(x_new, "hbm"), (weights, "hbm"), (conv_weight, "hbm"), (conv_bias[None, :], "hbm")]
        + [(value, "hbm") for value, _ in requests],
        [((rows, channels), BF16, "any"), ((head, channels), F32, "any"), ((out_cols, rows), BF16, "any"),
         ((head, LANES), jnp.int32, "vmem")],
        [
            vmem((rows, channels), BF16),
            vmem((out_cols, channels), BF16),
            vmem((taps, channels), BF16),
            vmem((1, channels), F32),
            vmem((channels // LANES, rows + taps * per_dev, LANES), F32),
            vmem((rows, channels), BF16),
            vmem((head, channels), F32),
            vmem((out_cols, rows), F32),
            vmem((out_cols, rows), BF16),
            dma((2 + 2 * n_chunks,)),
            dma((n_chunks + 2,)),
            dma((3,)),
        ] + [pltpu.SMEM(holder.shape, jnp.int32)] * 3,
    )
    mixed_head, part = call(
        history_kernel, (per_dev, firsts), "history", 20,
        [(value, "vmem") for value in [target, head_sums, part, weights, conv_weight] + conv_pieces],
        [((head, channels), BF16, "vmem"), ((out_cols, rows), BF16, "vmem")],
        [],
    )
    parts = [part]
    mask = n_tensor // 2
    while mask:
        parts = parts + [swap(value, "tensor", n_tensor, mask) for value in reversed(parts)]
        mask //= 2

    n_tiles = channels // LANES
    prepared = call(
        prepare_kernel, None, "prepare", 40,
        [(value, "vmem") for value in (mixed, mixed_head, z_new, a_log, d_skip[None, :])],
        [((rows, channels), F32, "vmem"), ((n_tiles, rows, LANES), F32, "vmem"), ((states, channels), F32, "vmem")],
        [],
    )
    operands = [mixed, mixed_head, dt_proj_weight, dt_bias[None, :], *prepared]
    out, state = call(
        scan_kernel, dims, "dt_scan_gate", 40,
        [(value, "any") for value, _ in requests] + [(value, "vmem") for value in operands + parts + ssm_pieces],
        [((rows, channels), BF16, "any"), ((per_dev * states, channels), BF16, "any")],
        [
            vmem((states, rows, LANES), F32),
            vmem((states, rows, LANES), F32),
            vmem((n_tiles, rows, LANES), F32),
            vmem((n_tiles, rows, LANES), F32),
            vmem((n_tiles, (per_dev + 1) * states, LANES), F32),
            vmem((n_tiles, per_dev * (states + 1), LANES), F32),
            vmem((n_tiles, rows + per_dev, LANES), F32),
            vmem((rows, channels), BF16),
            vmem((per_dev * states, channels), BF16),
            dma((2, n_tiles // 2)),
            dma((3,)),
        ] + [pltpu.SMEM(holder.shape, jnp.int32)] * 3,
    )
    return out, state.reshape(per_dev, states, channels)


def solution(mesh):
    placed = (
        P(("groups", "replica"), "tensor"),
        P(("groups", "replica"), "tensor"),
        P(None, "tensor"),
        P("tensor"),
        P("tensor", None),
        P(None, "tensor"),
        P("tensor"),
        P(None, "tensor"),
        P("tensor"),
        P(("groups", "replica"), None, "tensor"),
        P(("groups", "replica"), None, "tensor"),
        P("groups"),
        P("groups"),
        P("groups"),
    )
    return jax.shard_map(
        functools.partial(shards, mesh),
        mesh=mesh,
        in_specs=placed,
        out_specs=(P(("groups", "replica"), "tensor"), P(("groups", "replica"), None, "tensor")),
        check_vma=False,
    )
```

```python
import functools

import jax
import jax.numpy as jnp
from jax import lax
from jax.experimental import pallas as pl
from jax.experimental.pallas import tpu as pltpu
from jax.sharding import PartitionSpec as P

NEW = 32
LANES = 128
MIB = 1024 * 1024
UNROLL = 16
LOG2E = 1.4426950408889634
F32, BF16 = jnp.float32, jnp.bfloat16
NT = (((1,), (1,)), ((), ()))


def silu(v):
    half = 0.5 * v
    return half + half * jnp.tanh(half)


def softplus(v):
    u = jnp.exp2(jnp.abs(v) * -LOG2E)
    return jnp.maximum(v, 0.0) + jnp.where(u < 2.0**-10, u - 0.5 * (u * u), jnp.log(1.0 + u))


def split_index(value, inner):
    assert inner & (inner - 1) == 0
    return value >> (inner.bit_length() - 1), value & (inner - 1)


def pick_rows(values, row_low, count):
    out = jnp.zeros(row_low.shape, jnp.int32)
    for r in range(count):
        out = jnp.where(row_low == r, values[r], out)
    return out


def request_places(dims, ints, me):
    per_dev, n_replica, _, relative = dims
    places, slot_ids, lengths = [], [], []
    for r in range(per_dev):
        request = me * per_dev + r
        place = ints[0][request]
        if relative:
            place = place ^ me
            place = place ^ (place >> 1)
        places.append(place)
        slot_ids.append(ints[1][request])
        lengths.append(ints[2][request])
    return places, slot_ids, lengths


def fetch_rows(target, live, pieces):
    total = None
    for first, value in pieces:
        col = lax.broadcasted_iota(jnp.int32, (target.shape[0], value.shape[0]), 1) + first
        select = jnp.where((col == target) & live, 1.0, 0.0).astype(BF16)
        part = jnp.dot(select, value, preferred_element_type=F32)
        total = part if total is None else total + part
    return total


def pack_kernel(dims, refs_in, refs_out, scratch):
    slots, taps = dims
    ssm_hbm, conv_hbm = refs_in
    block_ref, conv_ref = refs_out
    conv_v, sems = scratch
    states = pltpu.make_async_copy(ssm_hbm, block_ref.at[: ssm_hbm.shape[0]], sems.at[0])
    inputs = pltpu.make_async_copy(conv_hbm, conv_v, sems.at[1])
    states.start()
    inputs.start()
    inputs.wait()
    lines = []
    for slot in range(slots):
        for tap in range(taps):
            line = conv_v[min(tap, taps - 2)].astype(F32)[slot : slot + 1]
            lines.append(line if tap < taps - 1 else jnp.zeros_like(line))
    rows = jnp.concatenate(lines, axis=0).astype(BF16)
    conv_ref[...] = rows
    block_ref[ssm_hbm.shape[0] :, :] = rows
    states.wait()


def project_kernel(dims, refs_in, refs_out, scratch):
    dims, block = dims
    per_dev, _, slots, _ = dims
    x_hbm, wt_hbm, cw_hbm, cb_hbm = refs_in[:4]
    mixed_hbm, head_hbm, part_hbm, target_ref = refs_out
    x_v, wt_v, cw_v, cb_v, joined, mixed_v, head_v, part_f, part_v, sems, out_sems = scratch
    rows, channels = x_v.shape
    taps = cw_v.shape[0]
    lines = (taps - 1) * per_dev
    pairs = [(cw_hbm, cw_v), (cb_hbm, cb_v)]
    width = min(512, channels)
    chunks = [slice(c * width, (c + 1) * width) for c in range(channels // width)]
    for chunk in chunks:
        pairs += [(x_hbm.at[:, chunk], x_v.at[:, chunk]), (wt_hbm.at[:, chunk], wt_v.at[:, chunk])]
    copies = [pltpu.make_async_copy(src, dst, sems.at[i]) for i, (src, dst) in enumerate(pairs)]
    for copy in copies:
        copy.start()

    me = lax.axis_index("replica")
    places, slot_ids, lengths = request_places(dims, refs_in[4:], me)
    tap, request = split_index(lax.broadcasted_iota(jnp.int32, target_ref.shape, 0), per_dev)
    starts = [places[r] * block + (block - slots * taps) + slot_ids[r] * taps for r in range(per_dev)]
    live = (tap < taps - 1) & (taps - 1 - tap <= pick_rows(lengths, request, per_dev))
    target_ref[...] = jnp.where(live, pick_rows(starts, request, per_dev) + tap, -1)

    joined[:, :lines, :] = jnp.zeros((channels // LANES, lines, LANES), F32)
    copies[0].wait()
    copies[1].wait()
    outs = []
    for c, chunk in enumerate(chunks):
        copies[2 + 2 * c].wait()
        for tile in range(c * width // LANES, (c + 1) * width // LANES):
            lanes = slice(tile * LANES, (tile + 1) * LANES)
            for r in range(per_dev):
                tokens = x_v[r * NEW : (r + 1) * NEW, lanes].astype(F32)
                joined[tile, pl.ds(lines + r, NEW, stride=per_dev), :] = tokens
            weight = [cw_v[k : k + 1, lanes].astype(F32) for k in range(taps)]
            bias = cb_v[:, lanes]
            for first in range(0, rows, LANES):
                summed = bias + joined[tile, first : first + LANES, :] * weight[0]
                for k in range(1, taps):
                    begin = first + k * per_dev
                    summed = summed + joined[tile, begin : begin + LANES, :] * weight[k]
                if first == 0:
                    head_v[:, lanes] = summed[: head_v.shape[0]]
                mixed_v[first : first + LANES, lanes] = silu(summed).astype(BF16)
        copies[3 + 2 * c].wait()
        part = lax.dot_general(wt_v[:, chunk], mixed_v[:, chunk], NT, preferred_element_type=F32)
        if c == 0:
            part_f[...] = part
        else:
            part_f[...] += part
        outs.append(pltpu.make_async_copy(mixed_v.at[:, chunk], mixed_hbm.at[:, chunk], out_sems.at[c]))
        outs[-1].start()
    part_v[...] = part_f[...].astype(BF16)
    for src, dst in ((part_v, part_hbm), (head_v, head_hbm)):
        outs.append(pltpu.make_async_copy(src, dst, out_sems.at[len(outs)]))
        outs[-1].start()
    for copy in outs:
        copy.wait()


def history_kernel(dims, refs_in, refs_out, scratch):
    per_dev, firsts = dims
    target_ref, head_ref, part_ref, wt_ref, cw_ref = refs_in[:5]
    pieces = refs_in[5:]
    mixed_ref, fixed_ref = refs_out
    taps = cw_ref.shape[0]
    target = target_ref[:, :1]
    history = fetch_rows(target, target >= 0, [(first, ref[...]) for first, ref in zip(firsts, pieces)])
    sums = []
    for t in range(taps):
        summed = head_ref[t * per_dev : (t + 1) * per_dev]
        for k in range(taps - 1 - t):
            weight = cw_ref[k : k + 1].astype(F32)
            summed = summed + history[(t + k) * per_dev : (t + k + 1) * per_dev] * weight
        sums.append(summed)
    mixed = silu(jnp.concatenate(sums, axis=0)).astype(BF16)
    mixed_ref[...] = mixed
    part = lax.dot_general(wt_ref[...], mixed, NT, preferred_element_type=F32)
    fixed_ref[...] = part_ref[...]
    fixed_ref[:, : per_dev * taps] = part.astype(BF16)


def prepare_kernel(dims, refs_in, refs_out, scratch):
    mixed_ref, head_ref, z_ref, al_ref, skip_ref = refs_in
    gate_ref, skipped_ref, rate_ref = refs_out
    rows, channels = z_ref.shape
    head = head_ref.shape[0]
    gate_ref[...] = silu(z_ref[...].astype(F32))
    rate_ref[...] = jnp.exp(al_ref[...]) * (-LOG2E)
    for tile in range(channels // LANES):
        lanes = slice(tile * LANES, (tile + 1) * LANES)
        skipped_ref[tile, :head, :] = skip_ref[:, lanes] * head_ref[:, lanes].astype(F32)
        skipped_ref[tile, head:, :] = skip_ref[:, lanes] * mixed_ref[head:, lanes].astype(F32)


def scan_kernel(dims, refs_in, refs_out, scratch):
    per_dev, n_replica, _, _ = dims
    mixed_ref, head_ref, dtw_ref, dtb_ref, gate_ref, skipped_ref, rate_ref = refs_in[3:10]
    out_hbm, state_hbm = refs_out
    b_tab, c_tab, dt_v, drive_v, start_tm, final_tm, y_v, out_v, state_v, out_sems, int_sems = scratch[:11]
    ints = scratch[11:]
    int_copies = [pltpu.make_async_copy(refs_in[i], ints[i], int_sems.at[i]) for i in range(len(ints))]
    for copy in int_copies:
        copy.start()
    n_pieces = sum(1 for ref in refs_in[10:] if ref.shape[-1] == gate_ref.shape[1])
    parts, pieces = refs_in[10:-n_pieces], refs_in[-n_pieces:]
    rows, channels = gate_ref.shape
    states = rate_ref.shape[0]
    rank = dtw_ref.shape[0]
    head = head_ref.shape[0]

    projected = parts[0][...].astype(F32)
    for part in parts[1:]:
        projected = projected + part[...].astype(F32)
    c_part = projected[rank + states :]
    c_high = c_part.astype(BF16).astype(F32)
    shape = (2 * states, states * LANES)
    term = lax.broadcasted_iota(jnp.int32, shape, 0) & (states - 1)
    lane_group, _ = split_index(lax.broadcasted_iota(jnp.int32, shape, 1), LANES)
    spread = jnp.where(term == lane_group, 1.0, 0.0).astype(BF16)
    c_terms = jnp.concatenate([c_high, c_part - c_high], axis=0).T.astype(BF16)
    projected = projected[: rank + states].T
    dt_low = projected[:, :rank].astype(BF16)
    late = projected[:, rank:]
    n_tiles = channels // LANES
    wide = min(2, n_tiles)
    per_chunk = states * wide // n_tiles
    for c in range(n_tiles // wide):
        for n in range(c * per_chunk, (c + 1) * per_chunk):
            b_tab[n] = jnp.broadcast_to(late[:, n : n + 1], (rows, LANES))
        lanes = slice(c * per_chunk * LANES, (c + 1) * per_chunk * LANES)
        repeated = jnp.dot(c_terms, spread[:, lanes], preferred_element_type=F32)
        for n in range(per_chunk):
            c_tab[c * per_chunk + n] = repeated[:, n * LANES : (n + 1) * LANES]
        weights = dtw_ref[:, c * wide * LANES : (c + 1) * wide * LANES]
        raw = jnp.dot(dt_low, weights, preferred_element_type=F32)
        for j in range(wide):
            tile = c * wide + j
            lanes = slice(tile * LANES, (tile + 1) * LANES)
            for first in range(0, rows, LANES):
                here = slice(first, first + LANES)
                dt = softplus(raw[here, j * LANES : (j + 1) * LANES] + dtb_ref[:, lanes])
                mixed = mixed_ref[here, lanes]
                if first == 0:
                    mixed = jnp.concatenate([head_ref[:, lanes], mixed[head:]], axis=0)
                mixed = mixed.astype(F32)
                dt_v[tile, here, :] = dt
                drive_v[tile, here, :] = dt * mixed

    me = lax.axis_index("replica")
    for copy in int_copies:
        copy.wait()
    places, slot_ids, lengths = request_places(dims, ints, me)
    for r in range(per_dev):
        spot = pl.ds(pl.multiple_of(slot_ids[r] * states, states), states)
        for tile in range(n_tiles):
            lanes = slice(tile * LANES, (tile + 1) * LANES)
            if n_pieces == 1:
                value = pieces[0][places[r], spot, lanes]
            else:
                value = pieces[0][spot, lanes]
                for p in range(1, n_pieces):
                    value = jnp.where(places[r] == p, pieces[p][spot, lanes], value)
            value = value.astype(F32)
            value = jnp.where(lengths[r] > 0, value, jnp.zeros_like(value))
            start_tm[tile, pl.ds(r, states, stride=per_dev), :] = value

    tiles = 2
    half = states // 4
    width = tiles * LANES
    n_groups = n_tiles // tiles

    def out_copies(g):
        lanes = pl.ds(pl.multiple_of(g * width, width), width)
        return [
            pltpu.make_async_copy(src.at[:, lanes], dst.at[:, lanes], out_sems.at[i, g])
            for i, (src, dst) in enumerate(((out_v, out_hbm), (state_v, state_hbm)))
        ]

    def finish(g):
        for j in range(tiles):
            tile = g * tiles + j
            lanes = pl.ds(pl.multiple_of(tile * LANES, LANES), LANES)
            for r in range(per_dev):
                here = slice(r * NEW, (r + 1) * NEW)
                value = y_v[tile, pl.ds(r, NEW, stride=per_dev), :] * gate_ref[here, lanes]
                out_v[here, lanes] = value.astype(BF16)
                final = final_tm[tile, pl.ds(r, states, stride=per_dev), :]
                state_v[r * states : (r + 1) * states, lanes] = final.astype(BF16)

    def scan_group(g):
        group = [g * tiles + j for j in range(tiles)]
        lanes = [pl.ds(pl.multiple_of(tile * LANES, LANES), LANES) for tile in group]
        for first in range(0, states, half):
            ids = range(first, first + half)
            rates = [[jnp.broadcast_to(rate_ref[n : n + 1, lane], (per_dev, LANES)) for n in ids] for lane in lanes]

            def advance(step, state):
                state = list(state)
                for u in range(UNROLL):
                    now = pl.ds(pl.multiple_of((step * UNROLL + u) * per_dev, per_dev), per_dev)
                    dt = [dt_v[tile, now, :] for tile in group]
                    drive = [drive_v[tile, now, :] for tile in group]
                    sums = [None] * tiles
                    for k, n in enumerate(ids):
                        b, c = b_tab[n, now, :], c_tab[n, now, :]
                        for j in range(tiles):
                            i = j * half + k
                            state[i] = jnp.exp2(dt[j] * rates[j][k]) * state[i] + drive[j] * b
                            term = state[i] * c
                            sums[j] = term if sums[j] is None else sums[j] + term
                    for j, tile in enumerate(group):
                        before = skipped_ref[tile, now, :] if first == 0 else y_v[tile, now, :]
                        y_v[tile, now, :] = before + sums[j]
                return tuple(state)

            state = tuple(start_tm[tile, n * per_dev : (n + 1) * per_dev, :] for tile in group for n in ids)
            if NEW == UNROLL:
                state = advance(0, state)
            else:
                state = lax.fori_loop(0, NEW // UNROLL, advance, state)
            for j, tile in enumerate(group):
                for k, n in enumerate(ids):
                    final_tm[tile, n * per_dev : (n + 1) * per_dev, :] = state[j * half + k]

    def one_group(g, carry):
        before = jnp.maximum(g - 1, 0)
        finish(before)
        scan_group(g)

        @pl.when(g > 0)
        def _():
            for copy in out_copies(before):
                copy.start()

        return carry

    final_tm[:tiles] = jnp.zeros((tiles,) + final_tm.shape[1:], F32)
    y_v[:tiles] = jnp.zeros((tiles,) + y_v.shape[1:], F32)
    lax.fori_loop(0, n_groups, one_group, 0)
    finish(n_groups - 1)
    for copy in out_copies(n_groups - 1):
        copy.start()

    def last_wait(g, carry):
        for copy in out_copies(g):
            copy.wait()
        return carry

    lax.fori_loop(0, n_groups, last_wait, 0)


def split_refs(kernel, dims, n_in, n_out):
    def body(*refs):
        kernel(dims, refs[:n_in], refs[n_in : n_in + n_out], refs[n_in + n_out :])

    return body


def call(kernel, dims, name, limit, ins, outs, scratch):
    spaces = {"hbm": pltpu.HBM, "any": pl.ANY, "vmem": pltpu.VMEM, "smem": pltpu.SMEM}
    values = [
        pltpu.with_memory_space_constraint(value, pltpu.HBM) if place == "hbm" else value for value, place in ins
    ]
    return pl.pallas_call(
        split_refs(kernel, dims, len(ins), len(outs)),
        in_specs=[pl.BlockSpec(memory_space=spaces[place]) for _, place in ins],
        out_specs=[pl.BlockSpec(memory_space=spaces[place]) for _, _, place in outs],
        out_shape=[jax.ShapeDtypeStruct(shape, dtype) for shape, dtype, _ in outs],
        scratch_shapes=scratch,
        compiler_params=pltpu.CompilerParams(vmem_limit_bytes=limit * MIB),
        name=name,
    )(*values)


def swap(value, axis, size, mask):
    return lax.ppermute(value, axis, [(i, i ^ mask) for i in range(size)])


def shards(mesh, x_new, z_new, conv_weight, conv_bias, x_proj_weight, dt_proj_weight, dt_bias, a_log, d_skip,
           cache_ssm, cache_conv, holder, slot_id, prefix_len):
    n_replica, n_tensor = mesh.shape["replica"], mesh.shape["tensor"]
    rows, channels = x_new.shape
    per_dev = rows // NEW
    states = a_log.shape[0]
    rank = dt_proj_weight.shape[0]
    taps = conv_weight.shape[0]
    slots = cache_ssm.shape[0]
    out_cols = x_proj_weight.shape[1]
    requests = holder.shape[0]

    vmem, dma = pltpu.VMEM, pltpu.SemaphoreType.DMA
    ssm_rows = slots * states
    rows_all, conv_rows = call(
        pack_kernel, (slots, taps), "pack", 20,
        [(cache_ssm.reshape(ssm_rows, channels), "hbm"), (cache_conv.transpose(1, 0, 2), "hbm")],
        [((ssm_rows + slots * taps, channels), BF16, "vmem"), ((slots * taps, channels), BF16, "vmem")],
        [vmem((taps - 1, slots, channels), BF16), dma((2,))],
    )
    block = rows_all.shape[0]
    relative = n_replica == 4
    if relative:
        far = swap(rows_all, "replica", n_replica, 3)
        near = swap(rows_all, "replica", n_replica, 1)
        conv_two = swap(conv_rows, "replica", n_replica, 2)
        conv_pieces = [rows_all, near, far, conv_two]
        firsts = (0, block, 2 * block, 4 * block - slots * taps)
        ssm_pieces = [rows_all, near, far, swap(far, "replica", n_replica, 1)]
    else:
        ssm_pieces = [lax.all_gather(rows_all, "replica")]
        conv_pieces, firsts = [ssm_pieces[0].reshape(-1, channels)], (0,)

    n_chunks = channels // min(512, channels)
    dims = (per_dev, n_replica, slots, relative)
    head = per_dev * taps
    weights = x_proj_weight.T
    requests = [(holder, "smem"), (slot_id, "smem"), (prefix_len, "smem")]

    mixed, head_sums, part, target = call(
        project_kernel, (dims, block), "conv_project", 40,
        [(x_new, "hbm"), (weights, "hbm"), (conv_weight, "hbm"), (conv_bias[None, :], "hbm")] + requests,
        [((rows, channels), BF16, "any"), ((head, channels), F32, "any"), ((out_cols, rows), BF16, "any"),
         ((head, LANES), jnp.int32, "vmem")],
        [
            vmem((rows, channels), BF16),
            vmem((out_cols, channels), BF16),
            vmem((taps, channels), BF16),
            vmem((1, channels), F32),
            vmem((channels // LANES, rows + taps * per_dev, LANES), F32),
            vmem((rows, channels), BF16),
            vmem((head, channels), F32),
            vmem((out_cols, rows), F32),
            vmem((out_cols, rows), BF16),
            dma((2 + 2 * n_chunks,)),
            dma((n_chunks + 2,)),
        ],
    )
    mixed_head, part = call(
        history_kernel, (per_dev, firsts), "history", 20,
        [(value, "vmem") for value in [target, head_sums, part, weights, conv_weight] + conv_pieces],
        [((head, channels), BF16, "vmem"), ((out_cols, rows), BF16, "vmem")],
        [],
    )
    parts = [part]
    mask = n_tensor // 2
    while mask:
        parts = parts + [swap(value, "tensor", n_tensor, mask) for value in reversed(parts)]
        mask //= 2

    n_tiles = channels // LANES
    prepared = call(
        prepare_kernel, None, "prepare", 40,
        [(value, "vmem") for value in (mixed, mixed_head, z_new, a_log, d_skip[None, :])],
        [((rows, channels), F32, "vmem"), ((n_tiles, rows, LANES), F32, "vmem"), ((states, channels), F32, "vmem")],
        [],
    )
    operands = [mixed, mixed_head, dt_proj_weight, dt_bias[None, :], *prepared]
    out, state = call(
        scan_kernel, dims, "dt_scan_gate", 40,
        [(value, "any") for value, _ in requests] + [(value, "vmem") for value in operands + parts + ssm_pieces],
        [((rows, channels), BF16, "any"), ((per_dev * states, channels), BF16, "any")],
        [
            vmem((states, rows, LANES), F32),
            vmem((states, rows, LANES), F32),
            vmem((n_tiles, rows, LANES), F32),
            vmem((n_tiles, rows, LANES), F32),
            vmem((n_tiles, per_dev * (states + 1), LANES), F32),
            vmem((n_tiles, per_dev * (states + 1), LANES), F32),
            vmem((n_tiles, rows + per_dev, LANES), F32),
            vmem((rows, channels), BF16),
            vmem((per_dev * states, channels), BF16),
            dma((2, n_tiles // 2)),
            dma((3,)),
        ] + [pltpu.SMEM(holder.shape, jnp.int32)] * 3,
    )
    return out, state.reshape(per_dev, states, channels)


def solution(mesh):
    placed = (
        P(("groups", "replica"), "tensor"),
        P(("groups", "replica"), "tensor"),
        P(None, "tensor"),
        P("tensor"),
        P("tensor", None),
        P(None, "tensor"),
        P("tensor"),
        P(None, "tensor"),
        P("tensor"),
        P(("groups", "replica"), None, "tensor"),
        P(("groups", "replica"), None, "tensor"),
        P("groups"),
        P("groups"),
        P("groups"),
    )
    return jax.shard_map(
        functools.partial(shards, mesh),
        mesh=mesh,
        in_specs=placed,
        out_specs=(P(("groups", "replica"), "tensor"), P(("groups", "replica"), None, "tensor")),
        check_vma=False,
    )
```
